128 devices in a mesh: pts: 8 (over y, x_lo), py: 4 (over z), pz: 4 (over x_hi, core).
Axes of the slice: x: 4 (x_hi: 2, x_lo: 2; x = x_hi * 2 + x_lo), y: 4, z: 4, core: 2. Of those that a mesh axis runs over, the one named last changes fastest.
Arguments:
- xi_map: float32 [256, 256, 256], P('py', 'pz'), may hold values from -6 to 6
- basis: bfloat16 [3, 256, 256, 256], P(None, 'py', 'pz'), may hold values from -6 to 6
- point_index: int32 [16, 3], P('pts'), may hold values from 0 to 2, as said below
- conc_start: float32 [256, 256, 256], P(None, ('py', 'pz')), may hold values from 0.05 to 1
- well_mask: int32 [256, 256], replicated, may hold values 0 or 1
- profile: float32 [256], replicated, may hold values from 0.5 to 2
Outputs:
- expected_conc: float32 [256, 256, 256], P('pts', ('py', 'pz'))
The draws below stay inside these ranges and needn't reach their ends.
Inputs may be any that keep to these rules, and one draw needn't show every extreme that they name: `point_index`: no two rows are equal; some row is all 0 and some row is all 2.
All inputs are finite; a program needn't handle non-finite values.
Results may differ from the reference program's by a relative error of at most 0.0003.
Values sent between devices are 32-bit elements; how exact they have to be, the bound alone decides.
A program may use at most 192 MiB of HBM per device.

```python
import math
import jax
import jax.numpy as jnp
from jax import lax

G = 256
KAPPA = 8
R = 3
NODES = 3
POINTS = 16
STEPS = 4


def draw_point_index(key, part):
    key = jax.random.fold_in(key, 11)
    key_perm, key_roll = jax.random.split(key)
    grid_count = NODES ** R
    inner = jax.random.permutation(key_perm, grid_count - 2) + 1
    chosen = jnp.concatenate([jnp.array([0, grid_count - 1], jnp.int32), inner[:POINTS - 2].astype(jnp.int32)])
    offset = jax.random.randint(key_roll, (), 0, POINTS)
    chosen = jnp.roll(chosen, offset)
    powers = jnp.array([NODES ** r for r in range(R)], jnp.int32)
    return (chosen[:, None] // powers[None, :] % NODES).astype(jnp.int32)


def set_ends(entries, rng, low, largest):
    place = [jax.random.randint(jax.random.fold_in(rng, axis), (), 0, length) for axis, length in enumerate(entries.shape)]
    widest = entries.shape.index(max(entries.shape))
    beside = place[:widest] + [(place[widest] + 1) % entries.shape[widest]] + place[widest + 1:]
    return entries.at[tuple(place)].set(low).at[tuple(beside)].set(largest)


def levels(rng, extent, pieces, least, largest):
    def one(dim, blocks):
        heights = jax.random.uniform(jax.random.fold_in(jax.random.fold_in(rng, 6), dim), (blocks,), jnp.float32, least / len(pieces), largest / len(pieces))
        return jnp.repeat(jnp.exp(heights), extent[dim] // blocks).reshape((-1,) + (1,) * (len(extent) - dim - 1))

    gain = one(*pieces[0])
    for cut in pieces[1:]:
        gain = gain * one(*cut)
    return gain


def bell_draw(key, extent, spread, limit, shards=(), held_as=jnp.bfloat16):
    values = jax.random.normal(key, extent, jnp.float32) * spread
    if len(shards) > 0:
        values = levels(key, extent, shards, -0.22, 0.18) * values
    return jnp.clip(values, min=-limit, max=limit).astype(held_as)


def setup_inputs(seed: int = 0) -> dict:
    keys = jax.random.split(jax.random.key(seed), 7)
    xi_map = bell_draw(keys[0], (G, G, G), 1.0, 6.0, ((0, 4), (1, 4)), jnp.float32)
    basis = bell_draw(keys[1], (R, G, G, G), 1.0, 6.0, ((1, 4), (2, 4)))
    point_index = draw_point_index(jax.random.fold_in(keys[6], 71), 0)
    conc_start = jnp.clip(jnp.exp(math.log(1.0) - 2.9957323 * jax.random.uniform(keys[3], (G, G, G), jnp.float32) ** levels(keys[3], (G, G, G), ((1, 16),), -0.2, 0.2)), 0.05, 1.0)
    well_mask = set_ends((jax.random.randint(keys[4], (G, G), 0, 16) < 1).astype(jnp.int32), jax.random.fold_in(keys[4], 1), 0, 1)
    profile = jnp.clip(jax.random.uniform(keys[5], (G,), jnp.float32, 0.5, 2.0), 0.5, 2.0)
    return {"xi_map": xi_map, "basis": basis, "point_index": point_index, "conc_start": conc_start, "well_mask": well_mask, "profile": profile}


hermite_nodes = (-1.7320508075688772, 0.0, 1.7320508075688772)
hermite_weights = (0.16666666666666666, 0.6666666666666666, 0.16666666666666666)
courant_rates = (0.4, 0.25, 0.25)
inflow_rate = 0.5

def synth_table(count):
    spots = jnp.arange(count, dtype=jnp.float32)
    table = jnp.sqrt(2.0 / count) * jnp.cos(jnp.pi * (spots[:, None] + 0.5) * spots[None, :] / count)
    scaler = jnp.where(jnp.arange(count) == 0, jnp.sqrt(0.5), 1.0).astype(jnp.float32)
    return (table * scaler[None, :]).astype(jnp.float32)

def amplitude(modes_a, modes_b, modes_c, count, kappa):
    square = modes_a[:, None, None] ** 2 + modes_b[None, :, None] ** 2 + modes_c[None, None, :] ** 2
    front = 0.9 * (count / kappa) ** 1.5
    return (front / (1.0 + square / (kappa * kappa))).astype(jnp.float32)

def lookup(index, table):
    hits = (index[..., None] == jnp.arange(len(table))[None, None, :]).astype(jnp.float32)
    return lax.optimization_barrier(jnp.sum(hits * jnp.asarray(table, jnp.float32)[None, None, :], axis=-1))

def synthesize(field, table):
    hp = lax.Precision.HIGHEST
    field = jnp.einsum('ck,xyk->xyc', table, field, precision=hp)
    field = jnp.einsum('bk,xkz->xbz', table, field, precision=hp)
    return jnp.einsum('ak,kyz->ayz', table, field, precision=hp)

def advance(conc, speed, source):
    for step in range(STEPS):
        flux = speed * conc
        zero_a = jnp.zeros_like(flux[:1])
        prev_a = jnp.concatenate([zero_a, flux[:-1]], axis=0)
        prev_b = jnp.concatenate([jnp.zeros_like(flux[:, :1]), flux[:, :-1]], axis=1)
        prev_c = jnp.concatenate([jnp.zeros_like(flux[:, :, :1]), flux[:, :, :-1]], axis=2)
        conc = conc - 0.9 * flux + courant_rates[0] * prev_a + courant_rates[1] * prev_b + courant_rates[2] * prev_c + source
    return conc

def reference(xi_map, basis, point_index, conc_start, well_mask, profile):
    table = synth_table(G)
    modes = jnp.arange(G, dtype=jnp.float32)
    amp = amplitude(modes, modes, modes, G, KAPPA * 1.0)
    centre = synthesize(amp * xi_map, table)
    directions = [synthesize(amp * basis[r].astype(jnp.float32), table) for r in range(R)]
    nodes = lookup(point_index, hermite_nodes)
    weights = jnp.prod(lookup(point_index, hermite_weights), axis=1)
    source = inflow_rate * well_mask.astype(jnp.float32)[:, :, None] * profile[None, None, :]

    def one_point(carry, which):
        logperm = centre
        for r in range(R):
            logperm = logperm + nodes[which, r] * directions[r]
        speed = jax.nn.sigmoid(logperm)
        conc = advance(conc_start, speed, source)
        return (carry + weights[which] * conc, None)
    total, unused = lax.scan(one_point, jnp.zeros((G, G, G), jnp.float32), jnp.arange(POINTS))
    return total
```

```python
import functools

import jax
import jax.numpy as jnp
import ml_dtypes
import numpy as np
from jax import lax
from jax.experimental import pallas as pl
from jax.experimental.pallas import tpu as pltpu
from jax.sharding import PartitionSpec as P

MESH = pl.DeviceIdType.MESH
STEPS = 4
POINTS = 16
G = 256
NROUND = 10
ROOT3 = 1.7320508075688772
F32 = jnp.float32
BF16 = jnp.bfloat16
NT = (((1,), (1,)), ((), ()))


def split_table(table):
    table = np.asarray(table, np.float64)
    high = table.astype(np.float32).astype(ml_dtypes.bfloat16)
    low = (table - high.astype(np.float64)).astype(np.float32).astype(ml_dtypes.bfloat16)
    return high, low


def tables():
    spots = np.arange(G, dtype=np.float64)
    full = np.sqrt(2.0 / G) * np.cos(np.pi * (spots[:, None] + 0.5) * spots[None, :] / G)
    full[:, 0] *= np.sqrt(0.5)
    tz = np.zeros((G + 64, G))
    tz[4 : 4 + G] = full
    cy = np.zeros((8, 5, 8, G))
    for u in range(8):
        for t in range(5):
            for q in range(8):
                y = 32 * u - 8 + 5 * q + t
                if y >= 0:
                    cy[u, t, q] = full[y]
    cx = 0.5 * np.concatenate([full[0::2], full[1::2]], axis=0).T
    return split_table(tz), split_table(cy.reshape(320, G)), split_table(cx)


def halves(value):
    high = value.astype(BF16)
    low = (value - high.astype(F32)).astype(BF16)
    return high, low


def kernel(
    nodes,
    prof,
    xi,
    basis,
    tz,
    cy,
    cx,
    cz,
    mask,
    out,
    share,
    got1,
    rows2,
    got2,
    conc0,
    fields,
    carry,
    plane,
    wave,
    s1,
    r1,
    own1,
    s2,
    r2,
    own2,
    sc,
    rc,
):
    pts = lax.axis_index("pts")
    i = lax.axis_index("py")
    pz = lax.axis_index("pz")
    yy, x_lo = pts // 2, pts % 2
    h, c = pz // 2, pz % 2
    xt = (x_lo + h) % 2
    u = 2 * i + c

    def at(i_, h_, c_):
        return {"pts": 2 * yy + (xt + h_) % 2, "py": i_, "pz": 2 * h_ + c_}

    barrier = pltpu.get_barrier_semaphore()
    for di in range(4):
        for dh in range(2):
            for dc in range(2):
                if di + dh + dc > 0:
                    pl.semaphore_signal(
                        barrier,
                        inc=1,
                        device_id=at((i + di) % 4, (h + dh) % 2, (c + dc) % 2),
                        device_id_type=MESH,
                    )
    pl.semaphore_wait(barrier, 15)

    def slab_copy(to_h):
        return pltpu.make_async_remote_copy(
            src_ref=cz.at[:, pl.ds(16 * to_h, 20)],
            dst_ref=conc0.at[:, :, pl.ds(pl.multiple_of(8 + 16 * c, 8), 16)],
            send_sem=sc.at[to_h],
            recv_sem=rc.at[c],
            device_id=at(i, to_h, h),
            device_id_type=MESH,
        )

    def slab_local(to_h):
        return pltpu.make_async_copy(
            cz.at[:, pl.ds(16 * to_h, 20)],
            conc0.at[:, :, pl.ds(pl.multiple_of(8 + 16 * c, 8), 16)],
            rc.at[c],
        )

    above = 2 * i + h + 1

    def halo_copy(to_h):
        return pltpu.make_async_remote_copy(
            src_ref=cz.at[:, pl.ds(16 * to_h, 20), pl.ds(8, 8)],
            dst_ref=conc0.at[:, :, pl.ds(0, 8)],
            send_sem=sc.at[2 + to_h],
            recv_sem=rc.at[2],
            device_id=at((above // 2) % 4, to_h, above % 2),
            device_id_type=MESH,
        )

    def halo_local(to_h):
        return pltpu.make_async_copy(
            cz.at[:, pl.ds(16 * to_h, 20), pl.ds(8, 8)], conc0.at[:, :, pl.ds(0, 8)], rc.at[2]
        )

    def slab_here(to_h):
        return jnp.logical_and(h == to_h, c == to_h)

    def halo_some():
        return jnp.logical_and(c == 1, above < 8)

    def halo_here(to_h):
        return (h == 0) if to_h == 0 else None

    for to_h in range(2):

        @pl.when(slab_here(to_h))
        def _():
            slab_local(to_h).start()

        @pl.when(jnp.logical_not(slab_here(to_h)))
        def _():
            slab_copy(to_h).start()

    @pl.when(jnp.logical_and(halo_some(), h == 0))
    def _():
        halo_local(0).start()

    @pl.when(jnp.logical_and(halo_some(), h == 1))
    def _():
        halo_copy(0).start()

    @pl.when(halo_some())
    def _():
        halo_copy(1).start()

    @pl.when(u == 0)
    def _():
        conc0[:, :, 0:8, :] = jnp.zeros((2, 20, 8, 128), F32)

    spot_b = (lax.broadcasted_iota(jnp.int32, (64, G), 0) + 64 * pz).astype(F32)
    spot_c = lax.broadcasted_iota(jnp.int32, (64, G), 1).astype(F32)
    wave[...] = 64.0 + spot_b * spot_b + spot_c * spot_c
    front = 64.0 * 0.9 * (32.0**1.5)

    def stage(step, _):
        amps = []
        for part in range(2):
            for half in range(2):
                a = (64 * i + 2 * step + part + 32 * half).astype(F32)
                amps.append(front / (wave[...] + a * a))
        for f in range(4):
            parts = []
            for part in range(2):
                for half in range(2):
                    row = 2 * step + part + 32 * half
                    value = xi[row] if f == 0 else basis[f - 1, row].astype(F32)
                    parts.append(value * amps[2 * part + half])
            high, low = halves(jnp.concatenate(parts, axis=0))
            both = lax.dot_general(tz[...], high, NT, preferred_element_type=F32)
            rest = lax.dot_general(tz[0:48], low, NT, preferred_element_type=F32)
            total = both[0:40] + both[48:88] + rest[0:40]
            for part in range(2):
                share[pl.ds(32 * f + 2 * step + part, 40, stride=128), :] = total[
                    :, 128 * part : 128 * part + 128
                ]
        return 0

    lax.fori_loop(0, 16, stage, 0)

    def first(k, d):
        to_h, to_c = (h + d // 2) % 2, (c + d % 2) % 2
        return pltpu.make_async_remote_copy(
            src_ref=share.at[pl.ds(pl.multiple_of((16 * to_h + 2 * k + to_c) * 128, 128), 128)],
            dst_ref=got1.at[k, pz],
            send_sem=s1.at[k, d],
            recv_sem=r1.at[k, d],
            device_id=at(i, to_h, to_c),
            device_id_type=MESH,
        )

    def first_own(k):
        return pltpu.make_async_copy(
            share.at[pl.ds(pl.multiple_of((16 * h + 2 * k + c) * 128, 128), 128)], got1.at[k, pz], own1.at[k]
        )

    def send_first(k, _):
        for d in (2, 3, 1):
            first(k, d).start()
        first_own(k).start()
        return 0

    lax.fori_loop(0, NROUND, send_first, 0)

    def second(k, d):
        to_i, to_c = (i + d // 2) % 4, (c + d % 2) % 2
        return pltpu.make_async_remote_copy(
            src_ref=rows2.at[k, 2 * to_i + to_c],
            dst_ref=got2.at[k, c, i],
            send_sem=s2.at[k, d],
            recv_sem=r2.at[k, d],
            device_id=at(to_i, h, to_c),
            device_id_type=MESH,
        )

    def second_own(k):
        return pltpu.make_async_copy(rows2.at[k, u], got2.at[k, c, i], own2.at[k])

    lane = lax.broadcasted_iota(jnp.int32, (128, 128), 1)
    lane_low = lane < 64
    lane8 = lax.broadcasted_iota(jnp.int32, (8, 128), 1)
    lane_some = lane8 > 0
    lane40 = lax.broadcasted_iota(jnp.int32, (40, 128), 1) < 64

    def b_contraction(k):
        for d in range(1, 4):
            first(k, d).wait_recv()
        first_own(k).wait()
        sides = [[], []]
        for pair in range(2):
            one, two = got1[k, 2 * pair], got1[k, 2 * pair + 1]
            sides[0].append(jnp.where(lane_low, one, pltpu.roll(two, 64, 1)))
            sides[1].append(jnp.where(lane_low, pltpu.roll(one, 64, 1), two))
        both = [jnp.concatenate(side, axis=1) for side in sides]
        rows = []
        for f in range(4):
            rows += [both[0][32 * f : 32 * f + 32], both[1][32 * f : 32 * f + 32]]
        high, low = halves(jnp.concatenate(rows, axis=0))
        for part in range(2):
            top = lax.dot_general(
                cy[160 * part : 160 * part + 160], high, NT, preferred_element_type=F32
            )
            top += lax.dot_general(
                cy[320 + 160 * part : 480 + 160 * part], high, NT, preferred_element_type=F32
            )
            top += lax.dot_general(
                cy[160 * part : 160 * part + 160], low, NT, preferred_element_type=F32
            )
            for slab in range(4):
                rows2[k, 4 * part + slab] = top[40 * slab : 40 * slab + 40]
        for d in (4, 5, 2, 6, 3, 7, 1):
            second(k, d).start()
        second_own(k).start()

    def a_contraction(k):
        for d in range(1, 8):
            second(k, d).wait_recv()
        second_own(k).wait()
        for core in range(2):
            rows = []
            for pair in range(2):
                cols = [[], []]
                for group in range(2):
                    one = got2[k, core, 2 * group, :, 128 * pair : 128 * pair + 128]
                    two = got2[k, core, 2 * group + 1, :, 128 * pair : 128 * pair + 128]
                    cols[0].append(jnp.where(lane40, one, pltpu.roll(two, 64, 1)))
                    cols[1].append(jnp.where(lane40, pltpu.roll(one, 64, 1), two))
                rows += [jnp.concatenate(col, axis=1) for col in cols]
            high, low = halves(jnp.concatenate(rows, axis=0))
            total = jnp.dot(high, cx[0:256], preferred_element_type=F32)
            total += jnp.dot(high, cx[256:512], preferred_element_type=F32)
            total += jnp.dot(low, cx[0:256], preferred_element_type=F32)
            fields[core] = total

    tiles = [(t, v) for t in range(5) for v in range(2)]

    def transport(k, core):
        zz = 2 * k + core
        well = prof[zz]
        for t, v in tiles:
            plane[0, t, v] = conc0[v, zz, pl.ds(t, 8, stride=5), :]
            plane[1, t, v] = mask[v, 8 * t : 8 * t + 8, :] * well

        def one_point(n, total):
            node = [nodes[4 * n + r] for r in range(3)]
            weight = nodes[4 * n + 3]
            speed, keep, conc = {}, {}, {}
            for t, v in tiles:
                logs = [
                    fields[core, 40 * f + 8 * t : 40 * f + 8 * t + 8, 128 * v : 128 * v + 128]
                    for f in range(4)
                ]
                value = logs[0] + node[0] * logs[1] + node[1] * logs[2] + node[2] * logs[3]
                value = jnp.tanh(value)
                speed[t, v] = 0.125 + 0.125 * value
                keep[t, v] = 0.55 - 0.45 * value
                conc[t, v] = plane[0, t, v]
            for step in range(STEPS):
                flux = {tv: speed[tv] * conc[tv] for tv in tiles}
                for t, v in tiles:
                    behind = carry[n, step, t, v]
                    carry[n, step, t, v] = flux[t, v]
                    prev_b = flux[t - 1, v] if t > 0 else pltpu.roll(flux[4, v], 1, 0)
                    prev_a = (
                        flux[t, 0]
                        if v == 1
                        else jnp.where(lane_some, pltpu.roll(flux[t, 1], 1, 1), 0.0)
                    )
                    conc[t, v] = (
                        keep[t, v] * conc[t, v]
                        + plane[1, t, v]
                        + behind
                        + prev_b
                        + 1.6 * prev_a
                    )
            return tuple(old + weight * conc[tv] for old, tv in zip(total, tiles))

        total = lax.fori_loop(
            0, POINTS, one_point, tuple(jnp.zeros((8, 128), F32) for _ in tiles)
        )
        back = jnp.maximum(zz - 4, 0)
        for value, (t, v) in zip(total, tiles):
            out[v, back, pl.ds(t, 8, stride=5), :] = value

    carry[...] = jnp.zeros(carry.shape, F32)
    lag = 2

    def wait_conc():
        for core in range(2):
            slab = pltpu.make_async_copy(
                cz.at[:, pl.ds(0, 20)], conc0.at[:, :, pl.ds(8 + 16 * core, 16)], rc.at[core]
            )
            slab.wait()

        @pl.when(u > 0)
        def _():
            pltpu.make_async_copy(
                cz.at[:, pl.ds(0, 20), pl.ds(8, 8)], conc0.at[:, :, pl.ds(0, 8)], rc.at[2]
            ).wait()

    def rounds(step, _):
        @pl.when(step < NROUND)
        def _():
            b_contraction(step)

        @pl.when(step >= lag)
        def _():
            a_contraction(step - lag)
            for core in range(2):
                transport(step - lag, core)

        return 0

    wait_conc()
    lax.fori_loop(0, NROUND + lag, rounds, 0)

    def drain(k, _):
        for d in range(1, 4):
            first(k, d).wait_send()
        for d in range(1, 8):
            second(k, d).wait_send()
        return 0

    lax.fori_loop(0, NROUND, drain, 0)
    for to_h in range(2):

        @pl.when(jnp.logical_not(slab_here(to_h)))
        def _():
            slab_copy(to_h).wait_send()

    @pl.when(jnp.logical_and(halo_some(), h == 1))
    def _():
        halo_copy(0).wait_send()

    @pl.when(halo_some())
    def _():
        halo_copy(1).wait_send()


def lookup(index, low, mid, high):
    return jnp.where(index == 0, low, jnp.where(index == 1, mid, high)).astype(F32)


def local(xi_map, basis, point_index, conc_start, well_mask, profile):
    (tz_hi, tz_lo), (cy_hi, cy_lo), (cx_hi, cx_lo) = tables()
    pts = lax.axis_index("pts")
    i = lax.axis_index("py")
    pz = lax.axis_index("pz")
    yy, x_lo = pts // 2, pts % 2
    h, c = pz // 2, pz % 2
    xt = (x_lo + h) % 2
    g = 2 * yy + xt
    u = 2 * i + c

    index = lax.all_gather(point_index, "pts", axis=0, tiled=True)
    nodes = lookup(index, -ROOT3, 0.0, ROOT3)
    weights = jnp.prod(lookup(index, 1.0 / 6.0, 2.0 / 3.0, 1.0 / 6.0), axis=1)
    nodes = jnp.concatenate([nodes, weights[:, None]], axis=1).reshape(-1)

    tz = jnp.concatenate(
        [lax.dynamic_slice_in_dim(jnp.asarray(part), 32 * g, 48, 0) for part in (tz_hi, tz_lo)], axis=0
    )
    cy = jnp.concatenate([cy_hi, cy_lo], axis=0)
    cx = jnp.concatenate([cx_hi, cx_lo], axis=0)

    prof = 0.5 * lax.dynamic_slice_in_dim(jnp.pad(profile, (4, 0)), 16 * (2 * g + h), 20, 0)
    mask = lax.dynamic_slice_in_dim(jnp.pad(well_mask, ((0, 0), (8, 0))), 32 * u, 40, 1)
    mask = mask.astype(F32).reshape(128, 2, 8, 5).transpose(1, 3, 2, 0).reshape(2, 40, 128)
    cz = lax.dynamic_slice_in_dim(jnp.pad(conc_start, ((0, 0), (0, 0), (4, 0))), 32 * g, 36, 2)
    cz = cz.reshape(128, 2, 16, 36).transpose(1, 3, 2, 0)

    vmem = pl.BlockSpec(memory_space=pltpu.VMEM)
    smem = pl.BlockSpec(memory_space=pltpu.SMEM)
    dma = pltpu.SemaphoreType.DMA
    total = pl.pallas_call(
        kernel,
        out_shape=jax.ShapeDtypeStruct((2, 16, 40, 128), F32),
        in_specs=[smem, smem] + [vmem] * 7,
        out_specs=vmem,
        scratch_shapes=[
            pltpu.VMEM((40 * 128, 128), F32),
            pltpu.VMEM((NROUND, 4, 128, 128), F32),
            pltpu.VMEM((NROUND, 8, 40, 256), F32),
            pltpu.VMEM((NROUND, 2, 4, 40, 256), F32),
            pltpu.VMEM((2, 20, 40, 128), F32),
            pltpu.VMEM((2, 160, 256), F32),
            pltpu.VMEM((POINTS, STEPS, 5, 2, 8, 128), F32),
            pltpu.VMEM((2, 5, 2, 8, 128), F32),
            pltpu.VMEM((64, 256), F32),
            dma((NROUND, 4)),
            dma((NROUND, 4)),
            dma((NROUND,)),
            dma((NROUND, 8)),
            dma((NROUND, 8)),
            dma((NROUND,)),
            dma((4,)),
            dma((3,)),
        ],
        compiler_params=pltpu.CompilerParams(
            collective_id=0, has_side_effects=True, vmem_limit_bytes=60 * 2**20
        ),
    )(nodes, prof, xi_map, basis, tz, cy, cx, cz, mask)

    part = total[:, :, 8:].reshape(2, 16, 2, 16, 8, 16).transpose(4, 2, 5, 0, 3, 1)
    part = part.reshape(8, 1, 2, 32, 16, 16)
    part = jnp.where((jnp.arange(2) == c).reshape(1, 2, 1, 1, 1, 1), part, 0.0)
    part = part.reshape(32, 32, 16, 16)
    part = lax.all_to_all(part, ("pts", "pz"), split_axis=0, concat_axis=0, tiled=True)
    part = part.reshape(4, 2, 2, 2, 32, 16, 16)
    part = lax.dynamic_index_in_dim(part, h, 3, keepdims=False)
    part = jnp.stack([part[:, :, 0], part[:, ::-1, 1]], axis=2)
    return part.transpose(3, 4, 0, 1, 2, 5).reshape(32, 16, 256)


def solution(mesh):
    placed = (
        P("py", "pz", None),
        P(None, "py", "pz", None),
        P("pts", None),
        P(None, ("py", "pz"), None),
        P(),
        P(),
    )
    return jax.shard_map(
        local, mesh=mesh, in_specs=placed, out_specs=P("pts", ("py", "pz"), None), check_vma=False
    )
```

```python
import functools

import jax
import jax.numpy as jnp
import ml_dtypes
import numpy as np
from jax import lax
from jax.experimental import pallas as pl
from jax.experimental.pallas import tpu as pltpu
from jax.sharding import PartitionSpec as P

MESH = pl.DeviceIdType.MESH
STEPS = 4
POINTS = 16
G = 256
NROUND = 10
ROOT3 = 1.7320508075688772
F32 = jnp.float32
BF16 = jnp.bfloat16
NT = (((1,), (1,)), ((), ()))


def split_table(table):
    table = np.asarray(table, np.float64)
    high = table.astype(np.float32).astype(ml_dtypes.bfloat16)
    low = (table - high.astype(np.float64)).astype(np.float32).astype(ml_dtypes.bfloat16)
    return high, low


def tables():
    spots = np.arange(G, dtype=np.float64)
    full = np.sqrt(2.0 / G) * np.cos(np.pi * (spots[:, None] + 0.5) * spots[None, :] / G)
    full[:, 0] *= np.sqrt(0.5)
    tz = np.zeros((G + 64, G))
    tz[4 : 4 + G] = full
    cy = np.zeros((8, 5, 8, G))
    for u in range(8):
        for t in range(5):
            for q in range(8):
                y = 32 * u - 8 + 5 * q + t
                if y >= 0:
                    cy[u, t, q] = full[y]
    cx = 0.5 * np.concatenate([full[0::2], full[1::2]], axis=0).T
    return split_table(tz), split_table(cy.reshape(320, G)), split_table(cx)


def halves(value):
    high = value.astype(BF16)
    low = (value - high.astype(F32)).astype(BF16)
    return high, low


def kernel(
    nodes,
    prof,
    xi,
    basis,
    tz,
    cy,
    cx,
    cz,
    mask,
    out,
    share,
    got1,
    rows2,
    got2,
    conc0,
    fields,
    carry,
    plane,
    wave,
    s1,
    r1,
    own1,
    s2,
    r2,
    own2,
    sc,
    rc,
):
    pts = lax.axis_index("pts")
    i = lax.axis_index("py")
    pz = lax.axis_index("pz")
    yy, x_lo = pts // 2, pts % 2
    h, c = pz // 2, pz % 2
    xt = (x_lo + h) % 2
    u = 2 * i + c

    def at(i_, h_, c_):
        return {"pts": 2 * yy + (xt + h_) % 2, "py": i_, "pz": 2 * h_ + c_}

    barrier = pltpu.get_barrier_semaphore()
    for di in range(4):
        for dh in range(2):
            for dc in range(2):
                if di + dh + dc > 0:
                    pl.semaphore_signal(
                        barrier,
                        inc=1,
                        device_id=at((i + di) % 4, (h + dh) % 2, (c + dc) % 2),
                        device_id_type=MESH,
                    )
    pl.semaphore_wait(barrier, 15)

    def slab_copy(to_h):
        return pltpu.make_async_remote_copy(
            src_ref=cz.at[:, pl.ds(16 * to_h, 20)],
            dst_ref=conc0.at[:, :, pl.ds(pl.multiple_of(8 + 16 * c, 8), 16)],
            send_sem=sc.at[to_h],
            recv_sem=rc.at[c],
            device_id=at(i, to_h, h),
            device_id_type=MESH,
        )

    def slab_local(to_h):
        return pltpu.make_async_copy(
            cz.at[:, pl.ds(16 * to_h, 20)],
            conc0.at[:, :, pl.ds(pl.multiple_of(8 + 16 * c, 8), 16)],
            rc.at[c],
        )

    above = 2 * i + h + 1

    def halo_copy(to_h):
        return pltpu.make_async_remote_copy(
            src_ref=cz.at[:, pl.ds(16 * to_h, 20), pl.ds(8, 8)],
            dst_ref=conc0.at[:, :, pl.ds(0, 8)],
            send_sem=sc.at[2 + to_h],
            recv_sem=rc.at[2],
            device_id=at((above // 2) % 4, to_h, above % 2),
            device_id_type=MESH,
        )

    def halo_local(to_h):
        return pltpu.make_async_copy(
            cz.at[:, pl.ds(16 * to_h, 20), pl.ds(8, 8)], conc0.at[:, :, pl.ds(0, 8)], rc.at[2]
        )

    def slab_here(to_h):
        return jnp.logical_and(h == to_h, c == to_h)

    def halo_some():
        return jnp.logical_and(c == 1, above < 8)

    def halo_here(to_h):
        return (h == 0) if to_h == 0 else None

    for to_h in range(2):

        @pl.when(slab_here(to_h))
        def _():
            slab_local(to_h).start()

        @pl.when(jnp.logical_not(slab_here(to_h)))
        def _():
            slab_copy(to_h).start()

    @pl.when(jnp.logical_and(halo_some(), h == 0))
    def _():
        halo_local(0).start()

    @pl.when(jnp.logical_and(halo_some(), h == 1))
    def _():
        halo_copy(0).start()

    @pl.when(halo_some())
    def _():
        halo_copy(1).start()

    @pl.when(u == 0)
    def _():
        conc0[:, :, 0:8, :] = jnp.zeros((2, 20, 8, 128), F32)

    spot_b = (lax.broadcasted_iota(jnp.int32, (64, G), 0) + 64 * pz).astype(F32)
    spot_c = lax.broadcasted_iota(jnp.int32, (64, G), 1).astype(F32)
    wave[...] = 64.0 + spot_b * spot_b + spot_c * spot_c
    front = 64.0 * 0.9 * (32.0**1.5)

    def stage(step, _):
        amps = []
        for part in range(2):
            for half in range(2):
                a = (64 * i + 2 * step + part + 32 * half).astype(F32)
                amps.append(front / (wave[...] + a * a))
        for f in range(4):
            parts = []
            for part in range(2):
                for half in range(2):
                    row = 2 * step + part + 32 * half
                    value = xi[row] if f == 0 else basis[f - 1, row].astype(F32)
                    parts.append(value * amps[2 * part + half])
            high, low = halves(jnp.concatenate(parts, axis=0))
            both = lax.dot_general(tz[...], high, NT, preferred_element_type=F32)
            rest = lax.dot_general(tz[0:48], low, NT, preferred_element_type=F32)
            total = both[0:40] + both[48:88] + rest[0:40]
            for part in range(2):
                share[pl.ds(32 * f + 2 * step + part, 40, stride=128), :] = total[
                    :, 128 * part : 128 * part + 128
                ]
        return 0

    lax.fori_loop(0, 16, stage, 0)

    def first(k, d):
        to_h, to_c = (h + d // 2) % 2, (c + d % 2) % 2
        return pltpu.make_async_remote_copy(
            src_ref=share.at[pl.ds(pl.multiple_of((16 * to_h + 2 * k + to_c) * 128, 128), 128)],
            dst_ref=got1.at[k, pz],
            send_sem=s1.at[k, d],
            recv_sem=r1.at[k, d],
            device_id=at(i, to_h, to_c),
            device_id_type=MESH,
        )

    def first_own(k):
        return pltpu.make_async_copy(
            share.at[pl.ds(pl.multiple_of((16 * h + 2 * k + c) * 128, 128), 128)], got1.at[k, pz], own1.at[k]
        )

    def send_first(k, _):
        for d in (2, 3, 1):
            first(k, d).start()
        first_own(k).start()
        return 0

    lax.fori_loop(0, NROUND, send_first, 0)

    def second(k, d):
        to_i, to_c = (i + d // 2) % 4, (c + d % 2) % 2
        return pltpu.make_async_remote_copy(
            src_ref=rows2.at[k, 2 * to_i + to_c],
            dst_ref=got2.at[k, c, i],
            send_sem=s2.at[k, d],
            recv_sem=r2.at[k, d],
            device_id=at(to_i, h, to_c),
            device_id_type=MESH,
        )

    def second_own(k):
        return pltpu.make_async_copy(rows2.at[k, u], got2.at[k, c, i], own2.at[k])

    lane = lax.broadcasted_iota(jnp.int32, (128, 128), 1)
    lane_low = lane < 64
    lane8 = lax.broadcasted_iota(jnp.int32, (8, 128), 1)
    lane_some = lane8 > 0
    lane40 = lax.broadcasted_iota(jnp.int32, (40, 128), 1) < 64

    def b_contraction(k):
        for d in range(1, 4):
            first(k, d).wait_recv()
        first_own(k).wait()
        sides = [[], []]
        for pair in range(2):
            one, two = got1[k, 2 * pair], got1[k, 2 * pair + 1]
            sides[0].append(jnp.where(lane_low, one, pltpu.roll(two, 64, 1)))
            sides[1].append(jnp.where(lane_low, pltpu.roll(one, 64, 1), two))
        both = [jnp.concatenate(side, axis=1) for side in sides]
        rows = []
        for f in range(4):
            rows += [both[0][32 * f : 32 * f + 32], both[1][32 * f : 32 * f + 32]]
        high, low = halves(jnp.concatenate(rows, axis=0))
        for part in range(2):
            top = lax.dot_general(
                cy[160 * part : 160 * part + 160], high, NT, preferred_element_type=F32
            )
            top += lax.dot_general(
                cy[320 + 160 * part : 480 + 160 * part], high, NT, preferred_element_type=F32
            )
            top += lax.dot_general(
                cy[160 * part : 160 * part + 160], low, NT, preferred_element_type=F32
            )
            for slab in range(4):
                rows2[k, 4 * part + slab] = top[40 * slab : 40 * slab + 40]
        for d in (4, 5, 2, 6, 3, 7, 1):
            second(k, d).start()
        second_own(k).start()

    def a_contraction(k):
        for d in range(1, 8):
            second(k, d).wait_recv()
        second_own(k).wait()
        for core in range(2):
            rows = []
            for pair in range(2):
                cols = [[], []]
                for group in range(2):
                    one = got2[k, core, 2 * group, :, 128 * pair : 128 * pair + 128]
                    two = got2[k, core, 2 * group + 1, :, 128 * pair : 128 * pair + 128]
                    cols[0].append(jnp.where(lane40, one, pltpu.roll(two, 64, 1)))
                    cols[1].append(jnp.where(lane40, pltpu.roll(one, 64, 1), two))
                rows += [jnp.concatenate(col, axis=1) for col in cols]
            high, low = halves(jnp.concatenate(rows, axis=0))
            total = jnp.dot(high, cx[0:256], preferred_element_type=F32)
            total += jnp.dot(high, cx[256:512], preferred_element_type=F32)
            total += jnp.dot(low, cx[0:256], preferred_element_type=F32)
            fields[core] = total

    tiles = [(t, v) for t in range(5) for v in range(2)]

    def transport(k, core, halo):
        zz = 2 * k + core
        well = prof[zz]
        for t, v in tiles:
            plane[0, t, v] = conc0[v, zz, pl.ds(t, 8, stride=5), :]
            plane[1, t, v] = mask[v, 8 * t : 8 * t + 8, :] * well
            if not halo:
                plane[2, t, v] = jnp.zeros((8, 128), F32)
        steps = zz + 1 if halo else STEPS

        def one_point(n, _):
            node = [nodes[4 * n + r] for r in range(3)]
            weight = nodes[4 * n + 3]
            speed, keep, conc = {}, {}, {}
            for t, v in tiles:
                logs = [
                    fields[core, 40 * f + 8 * t : 40 * f + 8 * t + 8, 128 * v : 128 * v + 128]
                    for f in range(4)
                ]
                value = logs[0] + node[0] * logs[1] + node[1] * logs[2] + node[2] * logs[3]
                value = jnp.tanh(value)
                speed[t, v] = 0.125 + 0.125 * value
                keep[t, v] = 0.55 - 0.45 * value
                conc[t, v] = plane[0, t, v]
            for step in range(steps):
                last = halo and step == steps - 1
                flux = {tv: speed[tv] * conc[tv] for tv in tiles}
                for t, v in tiles:
                    if last:
                        carry[n, step, t, v] = flux[t, v]
                        continue
                    behind = carry[n, step, t, v]
                    carry[n, step, t, v] = flux[t, v]
                    prev_b = flux[t - 1, v] if t > 0 else pltpu.roll(flux[4, v], 1, 0)
                    prev_a = (
                        flux[t, 0]
                        if v == 1
                        else jnp.where(lane_some, pltpu.roll(flux[t, 1], 1, 1), 0.0)
                    )
                    conc[t, v] = (
                        keep[t, v] * conc[t, v]
                        + plane[1, t, v]
                        + behind
                        + prev_b
                        + 1.6 * prev_a
                    )
            if not halo:
                for t, v in tiles:
                    plane[2, t, v] += weight * conc[t, v]
            return 0

        lax.fori_loop(0, POINTS, one_point, 0)
        if not halo:
            for t, v in tiles:
                out[v, zz - 4, pl.ds(t, 8, stride=5), :] = plane[2, t, v]

    carry[...] = jnp.zeros(carry.shape, F32)
    lag = 2

    def wait_conc():
        for core in range(2):
            slab = pltpu.make_async_copy(
                cz.at[:, pl.ds(0, 20)], conc0.at[:, :, pl.ds(8 + 16 * core, 16)], rc.at[core]
            )
            slab.wait()

        @pl.when(u > 0)
        def _():
            pltpu.make_async_copy(
                cz.at[:, pl.ds(0, 20), pl.ds(8, 8)], conc0.at[:, :, pl.ds(0, 8)], rc.at[2]
            ).wait()

    def rounds(step, _):
        @pl.when(step < NROUND)
        def _():
            b_contraction(step)

        @pl.when(step >= lag)
        def _():
            a_contraction(step - lag)

        for early in range(2):

            @pl.when(step == lag + early)
            def _():
                for core in range(2):
                    transport(early, core, True)

        @pl.when(step >= lag + 2)
        def _():
            for core in range(2):
                transport(step - lag, core, False)

        return 0

    wait_conc()
    lax.fori_loop(0, NROUND + lag, rounds, 0)

    def drain(k, _):
        for d in range(1, 4):
            first(k, d).wait_send()
        for d in range(1, 8):
            second(k, d).wait_send()
        return 0

    lax.fori_loop(0, NROUND, drain, 0)
    for to_h in range(2):

        @pl.when(jnp.logical_not(slab_here(to_h)))
        def _():
            slab_copy(to_h).wait_send()

    @pl.when(jnp.logical_and(halo_some(), h == 1))
    def _():
        halo_copy(0).wait_send()

    @pl.when(halo_some())
    def _():
        halo_copy(1).wait_send()


def lookup(index, low, mid, high):
    return jnp.where(index == 0, low, jnp.where(index == 1, mid, high)).astype(F32)


def local(xi_map, basis, point_index, conc_start, well_mask, profile):
    (tz_hi, tz_lo), (cy_hi, cy_lo), (cx_hi, cx_lo) = tables()
    pts = lax.axis_index("pts")
    i = lax.axis_index("py")
    pz = lax.axis_index("pz")
    yy, x_lo = pts // 2, pts % 2
    h, c = pz // 2, pz % 2
    xt = (x_lo + h) % 2
    g = 2 * yy + xt
    u = 2 * i + c

    index = lax.all_gather(point_index, "pts", axis=0, tiled=True)
    nodes = lookup(index, -ROOT3, 0.0, ROOT3)
    weights = jnp.prod(lookup(index, 1.0 / 6.0, 2.0 / 3.0, 1.0 / 6.0), axis=1)
    nodes = jnp.concatenate([nodes, weights[:, None]], axis=1).reshape(-1)

    tz = jnp.concatenate(
        [lax.dynamic_slice_in_dim(jnp.asarray(part), 32 * g, 48, 0) for part in (tz_hi, tz_lo)], axis=0
    )
    cy = jnp.concatenate([cy_hi, cy_lo], axis=0)
    cx = jnp.concatenate([cx_hi, cx_lo], axis=0)

    prof = 0.5 * lax.dynamic_slice_in_dim(jnp.pad(profile, (4, 0)), 16 * (2 * g + h), 20, 0)
    mask = lax.dynamic_slice_in_dim(jnp.pad(well_mask, ((0, 0), (8, 0))), 32 * u, 40, 1)
    mask = mask.astype(F32).reshape(128, 2, 8, 5).transpose(1, 3, 2, 0).reshape(2, 40, 128)
    cz = lax.dynamic_slice_in_dim(jnp.pad(conc_start, ((0, 0), (0, 0), (4, 0))), 32 * g, 36, 2)
    cz = cz.reshape(128, 2, 16, 36).transpose(1, 3, 2, 0)

    vmem = pl.BlockSpec(memory_space=pltpu.VMEM)
    smem = pl.BlockSpec(memory_space=pltpu.SMEM)
    dma = pltpu.SemaphoreType.DMA
    total = pl.pallas_call(
        kernel,
        out_shape=jax.ShapeDtypeStruct((2, 16, 40, 128), F32),
        in_specs=[smem, smem] + [vmem] * 7,
        out_specs=vmem,
        scratch_shapes=[
            pltpu.VMEM((40 * 128, 128), F32),
            pltpu.VMEM((NROUND, 4, 128, 128), F32),
            pltpu.VMEM((NROUND, 8, 40, 256), F32),
            pltpu.VMEM((NROUND, 2, 4, 40, 256), F32),
            pltpu.VMEM((2, 20, 40, 128), F32),
            pltpu.VMEM((2, 160, 256), F32),
            pltpu.VMEM((POINTS, STEPS, 5, 2, 8, 128), F32),
            pltpu.VMEM((3, 5, 2, 8, 128), F32),
            pltpu.VMEM((64, 256), F32),
            dma((NROUND, 4)),
            dma((NROUND, 4)),
            dma((NROUND,)),
            dma((NROUND, 8)),
            dma((NROUND, 8)),
            dma((NROUND,)),
            dma((4,)),
            dma((3,)),
        ],
        compiler_params=pltpu.CompilerParams(
            collective_id=0, has_side_effects=True, vmem_limit_bytes=60 * 2**20
        ),
    )(nodes, prof, xi_map, basis, tz, cy, cx, cz, mask)

    part = total[:, :, 8:].reshape(2, 16, 2, 16, 8, 16).transpose(4, 2, 5, 0, 3, 1)
    part = part.reshape(8, 1, 2, 32, 16, 16)
    part = jnp.where((jnp.arange(2) == c).reshape(1, 2, 1, 1, 1, 1), part, 0.0)
    part = part.reshape(32, 32, 16, 16)
    part = lax.all_to_all(part, ("pts", "pz"), split_axis=0, concat_axis=0, tiled=True)
    part = part.reshape(4, 2, 2, 2, 32, 16, 16)
    part = lax.dynamic_index_in_dim(part, h, 3, keepdims=False)
    part = jnp.stack([part[:, :, 0], part[:, ::-1, 1]], axis=2)
    return part.transpose(3, 4, 0, 1, 2, 5).reshape(32, 16, 256)


def solution(mesh):
    placed = (
        P("py", "pz", None),
        P(None, "py", "pz", None),
        P("pts", None),
        P(None, ("py", "pz"), None),
        P(),
        P(),
    )
    return jax.shard_map(
        local, mesh=mesh, in_specs=placed, out_specs=P("pts", ("py", "pz"), None), check_vma=False
    )
```

```python
import functools

import jax
import jax.numpy as jnp
import ml_dtypes
import numpy as np
from jax import lax
from jax.experimental import pallas as pl
from jax.experimental.pallas import tpu as pltpu
from jax.sharding import PartitionSpec as P

MESH = pl.DeviceIdType.MESH
STEPS = 4
POINTS = 16
G = 256
NROUND = 10
ROOT3 = 1.7320508075688772
F32 = jnp.float32
BF16 = jnp.bfloat16
NT = (((1,), (1,)), ((), ()))


def split_table(table):
    table = np.asarray(table, np.float64)
    high = table.astype(np.float32).astype(ml_dtypes.bfloat16)
    low = (table - high.astype(np.float64)).astype(np.float32).astype(ml_dtypes.bfloat16)
    return high, low


def tables():
    spots = np.arange(G, dtype=np.float64)
    full = np.sqrt(2.0 / G) * np.cos(np.pi * (spots[:, None] + 0.5) * spots[None, :] / G)
    full[:, 0] *= np.sqrt(0.5)
    tz = np.zeros((G + 64, G))
    tz[4 : 4 + G] = full
    cy = np.zeros((8, 5, 8, G))
    for u in range(8):
        for t in range(5):
            for q in range(8):
                y = 32 * u - 8 + 5 * q + t
                if y >= 0:
                    cy[u, t, q] = full[y]
    cx = 0.5 * np.concatenate([full[0::2], full[1::2]], axis=0).T
    return split_table(tz), split_table(cy.reshape(320, G)), split_table(cx)


def halves(value):
    high = value.astype(BF16)
    low = (value - high.astype(F32)).astype(BF16)
    return high, low


def kernel(
    nodes,
    prof,
    xi,
    basis,
    tz,
    cy,
    cx,
    cz,
    mask,
    out,
    share,
    got1,
    rows2,
    got2,
    conc0,
    fields,
    carry,
    plane,
    wave,
    s1,
    r1,
    own1,
    s2,
    r2,
    own2,
    sc,
    rc,
):
    pts = lax.axis_index("pts")
    i = lax.axis_index("py")
    pz = lax.axis_index("pz")
    yy, x_lo = pts // 2, pts % 2
    h, c = pz // 2, pz % 2
    xt = (x_lo + h) % 2
    u = 2 * i + c

    def at(i_, h_, c_):
        return {"pts": 2 * yy + (xt + h_) % 2, "py": i_, "pz": 2 * h_ + c_}

    barrier = pltpu.get_barrier_semaphore()
    for di in range(4):
        for dh in range(2):
            for dc in range(2):
                if di + dh + dc > 0:
                    pl.semaphore_signal(
                        barrier,
                        inc=1,
                        device_id=at((i + di) % 4, (h + dh) % 2, (c + dc) % 2),
                        device_id_type=MESH,
                    )
    pl.semaphore_wait(barrier, 15)

    def slab_copy(to_h):
        return pltpu.make_async_remote_copy(
            src_ref=cz.at[:, pl.ds(16 * to_h, 20)],
            dst_ref=conc0.at[:, :, pl.ds(pl.multiple_of(8 + 16 * c, 8), 16)],
            send_sem=sc.at[to_h],
            recv_sem=rc.at[c],
            device_id=at(i, to_h, h),
            device_id_type=MESH,
        )

    def slab_local(to_h):
        return pltpu.make_async_copy(
            cz.at[:, pl.ds(16 * to_h, 20)],
            conc0.at[:, :, pl.ds(pl.multiple_of(8 + 16 * c, 8), 16)],
            rc.at[c],
        )

    above = 2 * i + h + 1

    def halo_copy(to_h):
        return pltpu.make_async_remote_copy(
            src_ref=cz.at[:, pl.ds(16 * to_h, 20), pl.ds(8, 8)],
            dst_ref=conc0.at[:, :, pl.ds(0, 8)],
            send_sem=sc.at[2 + to_h],
            recv_sem=rc.at[2],
            device_id=at((above // 2) % 4, to_h, above % 2),
            device_id_type=MESH,
        )

    def halo_local(to_h):
        return pltpu.make_async_copy(
            cz.at[:, pl.ds(16 * to_h, 20), pl.ds(8, 8)], conc0.at[:, :, pl.ds(0, 8)], rc.at[2]
        )

    def slab_here(to_h):
        return jnp.logical_and(h == to_h, c == to_h)

    def halo_some():
        return jnp.logical_and(c == 1, above < 8)

    def halo_here(to_h):
        return (h == 0) if to_h == 0 else None

    for to_h in range(2):

        @pl.when(slab_here(to_h))
        def _():
            slab_local(to_h).start()

        @pl.when(jnp.logical_not(slab_here(to_h)))
        def _():
            slab_copy(to_h).start()

    @pl.when(jnp.logical_and(halo_some(), h == 0))
    def _():
        halo_local(0).start()

    @pl.when(jnp.logical_and(halo_some(), h == 1))
    def _():
        halo_copy(0).start()

    @pl.when(halo_some())
    def _():
        halo_copy(1).start()

    @pl.when(u == 0)
    def _():
        conc0[:, :, 0:8, :] = jnp.zeros((2, 20, 8, 128), F32)

    spot_b = (lax.broadcasted_iota(jnp.int32, (64, G), 0) + 64 * pz).astype(F32)
    spot_c = lax.broadcasted_iota(jnp.int32, (64, G), 1).astype(F32)
    wave[...] = 64.0 + spot_b * spot_b + spot_c * spot_c
    front = 64.0 * 0.9 * (32.0**1.5)

    def stage(step, _):
        amps = []
        for part in range(2):
            for half in range(2):
                a = (64 * i + 2 * step + part + 32 * half).astype(F32)
                amps.append(front / (wave[...] + a * a))
        for f in range(4):
            parts = []
            for part in range(2):
                for half in range(2):
                    row = 2 * step + part + 32 * half
                    value = xi[row] if f == 0 else basis[f - 1, row].astype(F32)
                    parts.append(value * amps[2 * part + half])
            high, low = halves(jnp.concatenate(parts, axis=0))
            both = jnp.dot(high, tz[...], preferred_element_type=F32)
            both += jnp.dot(low, tz[...], preferred_element_type=F32)
            both = both.T
            total = both[0:40] + both[48:88]
            for part in range(2):
                share[pl.ds(32 * f + 2 * step + part, 40, stride=128), :] = total[
                    :, 128 * part : 128 * part + 128
                ]
        return 0

    lax.fori_loop(0, 16, stage, 0)

    def first(k, d):
        to_h, to_c = (h + d // 2) % 2, (c + d % 2) % 2
        return pltpu.make_async_remote_copy(
            src_ref=share.at[pl.ds(pl.multiple_of((16 * to_h + 2 * k + to_c) * 128, 128), 128)],
            dst_ref=got1.at[k, pz],
            send_sem=s1.at[k, d],
            recv_sem=r1.at[k, d],
            device_id=at(i, to_h, to_c),
            device_id_type=MESH,
        )

    def first_own(k):
        return pltpu.make_async_copy(
            share.at[pl.ds(pl.multiple_of((16 * h + 2 * k + c) * 128, 128), 128)], got1.at[k, pz], own1.at[k]
        )

    def send_first(k, _):
        for d in (2, 3, 1):
            first(k, d).start()
        first_own(k).start()
        return 0

    lax.fori_loop(0, NROUND, send_first, 0)

    def second(k, d):
        to_i, to_c = (i + d // 2) % 4, (c + d % 2) % 2
        return pltpu.make_async_remote_copy(
            src_ref=rows2.at[k, 2 * to_i + to_c],
            dst_ref=got2.at[k, c, i],
            send_sem=s2.at[k, d],
            recv_sem=r2.at[k, d],
            device_id=at(to_i, h, to_c),
            device_id_type=MESH,
        )

    def second_own(k):
        return pltpu.make_async_copy(rows2.at[k, u], got2.at[k, c, i], own2.at[k])

    lane = lax.broadcasted_iota(jnp.int32, (128, 128), 1)
    lane_low = lane < 64
    lane8 = lax.broadcasted_iota(jnp.int32, (8, 128), 1)
    lane_some = lane8 > 0
    lane40 = lax.broadcasted_iota(jnp.int32, (40, 128), 1) < 64

    def b_contraction(k):
        for d in range(1, 4):
            first(k, d).wait_recv()
        first_own(k).wait()
        sides = [[], []]
        for pair in range(2):
            one, two = got1[k, 2 * pair], got1[k, 2 * pair + 1]
            sides[0].append(jnp.where(lane_low, one, pltpu.roll(two, 64, 1)))
            sides[1].append(jnp.where(lane_low, pltpu.roll(one, 64, 1), two))
        both = [jnp.concatenate(side, axis=1) for side in sides]
        rows = []
        for f in range(4):
            rows += [both[0][32 * f : 32 * f + 32], both[1][32 * f : 32 * f + 32]]
        high, low = halves(jnp.concatenate(rows, axis=0))
        for part in range(2):
            top = lax.dot_general(
                cy[160 * part : 160 * part + 160], high, NT, preferred_element_type=F32
            )
            top += lax.dot_general(
                cy[320 + 160 * part : 480 + 160 * part], high, NT, preferred_element_type=F32
            )
            top += lax.dot_general(
                cy[160 * part : 160 * part + 160], low, NT, preferred_element_type=F32
            )
            for slab in range(4):
                rows2[k, 4 * part + slab] = top[40 * slab : 40 * slab + 40]
        for d in (4, 5, 2, 6, 3, 7, 1):
            second(k, d).start()
        second_own(k).start()

    def a_contraction(k):
        for d in range(1, 8):
            second(k, d).wait_recv()
        second_own(k).wait()
        for core in range(2):
            rows = []
            for pair in range(2):
                cols = [[], []]
                for group in range(2):
                    one = got2[k, core, 2 * group, :, 128 * pair : 128 * pair + 128]
                    two = got2[k, core, 2 * group + 1, :, 128 * pair : 128 * pair + 128]
                    cols[0].append(jnp.where(lane40, one, pltpu.roll(two, 64, 1)))
                    cols[1].append(jnp.where(lane40, pltpu.roll(one, 64, 1), two))
                rows += [jnp.concatenate(col, axis=1) for col in cols]
            high, low = halves(jnp.concatenate(rows, axis=0))
            total = jnp.dot(high, cx[0:256], preferred_element_type=F32)
            total += jnp.dot(high, cx[256:512], preferred_element_type=F32)
            total += jnp.dot(low, cx[0:256], preferred_element_type=F32)
            fields[core] = total

    tiles = [(t, v) for t in range(5) for v in range(2)]

    def transport(k, core, halo):
        zz = 2 * k + core
        well = prof[zz]
        for t, v in tiles:
            plane[0, t, v] = conc0[v, zz, pl.ds(t, 8, stride=5), :]
            plane[1, t, v] = mask[v, 8 * t : 8 * t + 8, :] * well
            if not halo:
                plane[2, t, v] = jnp.zeros((8, 128), F32)
        steps = zz + 1 if halo else STEPS

        def one_point(n, _):
            node = [nodes[4 * n + r] for r in range(3)]
            weight = nodes[4 * n + 3]
            speed, keep, conc = {}, {}, {}
            for t, v in tiles:
                logs = [
                    fields[core, 40 * f + 8 * t : 40 * f + 8 * t + 8, 128 * v : 128 * v + 128]
                    for f in range(4)
                ]
                value = logs[0] + node[0] * logs[1] + node[1] * logs[2] + node[2] * logs[3]
                value = jnp.tanh(value)
                speed[t, v] = 0.125 + 0.125 * value
                keep[t, v] = 0.55 - 0.45 * value
                conc[t, v] = plane[0, t, v]
            for step in range(steps):
                last = halo and step == steps - 1
                flux = {tv: speed[tv] * conc[tv] for tv in tiles}
                for t, v in tiles:
                    if last:
                        carry[n, step, t, v] = flux[t, v]
                        continue
                    behind = carry[n, step, t, v]
                    carry[n, step, t, v] = flux[t, v]
                    prev_b = flux[t - 1, v] if t > 0 else pltpu.roll(flux[4, v], 1, 0)
                    prev_a = (
                        flux[t, 0]
                        if v == 1
                        else jnp.where(lane_some, pltpu.roll(flux[t, 1], 1, 1), 0.0)
                    )
                    conc[t, v] = (
                        keep[t, v] * conc[t, v]
                        + plane[1, t, v]
                        + behind
                        + prev_b
                        + 1.6 * prev_a
                    )
            if not halo:
                for t, v in tiles:
                    plane[2, t, v] += weight * conc[t, v]
            return 0

        lax.fori_loop(0, POINTS, one_point, 0)
        if not halo:
            for t, v in tiles:
                out[v, zz - 4, pl.ds(t, 8, stride=5), :] = plane[2, t, v]

    carry[...] = jnp.zeros(carry.shape, F32)
    lag = 2

    def wait_conc():
        for core in range(2):
            slab = pltpu.make_async_copy(
                cz.at[:, pl.ds(0, 20)], conc0.at[:, :, pl.ds(8 + 16 * core, 16)], rc.at[core]
            )
            slab.wait()

        @pl.when(u > 0)
        def _():
            pltpu.make_async_copy(
                cz.at[:, pl.ds(0, 20), pl.ds(8, 8)], conc0.at[:, :, pl.ds(0, 8)], rc.at[2]
            ).wait()

    def rounds(step, _):
        @pl.when(step < NROUND)
        def _():
            b_contraction(step)

        @pl.when(step >= lag)
        def _():
            a_contraction(step - lag)

        for early in range(2):

            @pl.when(step == lag + early)
            def _():
                for core in range(2):
                    transport(early, core, True)

        @pl.when(step >= lag + 2)
        def _():
            for core in range(2):
                transport(step - lag, core, False)

        return 0

    wait_conc()
    lax.fori_loop(0, NROUND + lag, rounds, 0)

    def drain(k, _):
        for d in range(1, 4):
            first(k, d).wait_send()
        for d in range(1, 8):
            second(k, d).wait_send()
        return 0

    lax.fori_loop(0, NROUND, drain, 0)
    for to_h in range(2):

        @pl.when(jnp.logical_not(slab_here(to_h)))
        def _():
            slab_copy(to_h).wait_send()

    @pl.when(jnp.logical_and(halo_some(), h == 1))
    def _():
        halo_copy(0).wait_send()

    @pl.when(halo_some())
    def _():
        halo_copy(1).wait_send()


def lookup(index, low, mid, high):
    return jnp.where(index == 0, low, jnp.where(index == 1, mid, high)).astype(F32)


def local(xi_map, basis, point_index, conc_start, well_mask, profile):
    (tz_hi, tz_lo), (cy_hi, cy_lo), (cx_hi, cx_lo) = tables()
    pts = lax.axis_index("pts")
    i = lax.axis_index("py")
    pz = lax.axis_index("pz")
    yy, x_lo = pts // 2, pts % 2
    h, c = pz // 2, pz % 2
    xt = (x_lo + h) % 2
    g = 2 * yy + xt
    u = 2 * i + c

    index = lax.all_gather(point_index, "pts", axis=0, tiled=True)
    nodes = lookup(index, -ROOT3, 0.0, ROOT3)
    weights = jnp.prod(lookup(index, 1.0 / 6.0, 2.0 / 3.0, 1.0 / 6.0), axis=1)
    nodes = jnp.concatenate([nodes, weights[:, None]], axis=1).reshape(-1)

    tz = jnp.concatenate(
        [lax.dynamic_slice_in_dim(jnp.asarray(part), 32 * g, 48, 0) for part in (tz_hi, tz_lo)], axis=0
    )
    tz = jnp.pad(tz, ((0, 32), (0, 0))).T
    cy = jnp.concatenate([cy_hi, cy_lo], axis=0)
    cx = jnp.concatenate([cx_hi, cx_lo], axis=0)

    prof = 0.5 * lax.dynamic_slice_in_dim(jnp.pad(profile, (4, 0)), 16 * (2 * g + h), 20, 0)
    mask = lax.dynamic_slice_in_dim(jnp.pad(well_mask, ((0, 0), (8, 0))), 32 * u, 40, 1)
    mask = mask.astype(F32).reshape(128, 2, 8, 5).transpose(1, 3, 2, 0).reshape(2, 40, 128)
    cz = lax.dynamic_slice_in_dim(jnp.pad(conc_start, ((0, 0), (0, 0), (4, 0))), 32 * g, 36, 2)
    cz = cz.reshape(128, 2, 16, 36).transpose(1, 3, 2, 0)

    vmem = pl.BlockSpec(memory_space=pltpu.VMEM)
    smem = pl.BlockSpec(memory_space=pltpu.SMEM)
    dma = pltpu.SemaphoreType.DMA
    total = pl.pallas_call(
        kernel,
        out_shape=jax.ShapeDtypeStruct((2, 16, 40, 128), F32),
        in_specs=[smem, smem] + [vmem] * 7,
        out_specs=vmem,
        scratch_shapes=[
            pltpu.VMEM((40 * 128, 128), F32),
            pltpu.VMEM((NROUND, 4, 128, 128), F32),
            pltpu.VMEM((NROUND, 8, 40, 256), F32),
            pltpu.VMEM((NROUND, 2, 4, 40, 256), F32),
            pltpu.VMEM((2, 20, 40, 128), F32),
            pltpu.VMEM((2, 160, 256), F32),
            pltpu.VMEM((POINTS, STEPS, 5, 2, 8, 128), F32),
            pltpu.VMEM((3, 5, 2, 8, 128), F32),
            pltpu.VMEM((64, 256), F32),
            dma((NROUND, 4)),
            dma((NROUND, 4)),
            dma((NROUND,)),
            dma((NROUND, 8)),
            dma((NROUND, 8)),
            dma((NROUND,)),
            dma((4,)),
            dma((3,)),
        ],
        compiler_params=pltpu.CompilerParams(
            collective_id=0, has_side_effects=True, vmem_limit_bytes=60 * 2**20
        ),
    )(nodes, prof, xi_map, basis, tz, cy, cx, cz, mask)

    part = total[:, :, 8:].reshape(2, 16, 2, 16, 8, 16).transpose(4, 2, 5, 0, 3, 1)
    part = part.reshape(8, 1, 2, 32, 16, 16)
    part = jnp.where((jnp.arange(2) == c).reshape(1, 2, 1, 1, 1, 1), part, 0.0)
    part = part.reshape(32, 32, 16, 16)
    part = lax.all_to_all(part, ("pts", "pz"), split_axis=0, concat_axis=0, tiled=True)
    part = part.reshape(4, 2, 2, 2, 32, 16, 16)
    part = lax.dynamic_index_in_dim(part, h, 3, keepdims=False)
    part = jnp.stack([part[:, :, 0], part[:, ::-1, 1]], axis=2)
    return part.transpose(3, 4, 0, 1, 2, 5).reshape(32, 16, 256)


def solution(mesh):
    placed = (
        P("py", "pz", None),
        P(None, "py", "pz", None),
        P("pts", None),
        P(None, ("py", "pz"), None),
        P(),
        P(),
    )
    return jax.shard_map(
        local, mesh=mesh, in_specs=placed, out_specs=P("pts", ("py", "pz"), None), check_vma=False
    )
```

```python
import functools

import jax
import jax.numpy as jnp
import ml_dtypes
import numpy as np
from jax import lax
from jax.experimental import pallas as pl
from jax.experimental.pallas import tpu as pltpu
from jax.sharding import PartitionSpec as P

MESH = pl.DeviceIdType.MESH
STEPS = 4
POINTS = 16
G = 256
NROUND = 10
ROOT3 = 1.7320508075688772
F32 = jnp.float32
BF16 = jnp.bfloat16
NT = (((1,), (1,)), ((), ()))


def split_table(table):
    table = np.asarray(table, np.float64)
    high = table.astype(np.float32).astype(ml_dtypes.bfloat16)
    low = (table - high.astype(np.float64)).astype(np.float32).astype(ml_dtypes.bfloat16)
    return high, low


def tables():
    spots = np.arange(G, dtype=np.float64)
    full = np.sqrt(2.0 / G) * np.cos(np.pi * (spots[:, None] + 0.5) * spots[None, :] / G)
    full[:, 0] *= np.sqrt(0.5)
    tz = np.zeros((G + 64, G))
    tz[4 : 4 + G] = full
    cy = np.zeros((8, 5, 8, G))
    for u in range(8):
        for t in range(5):
            for q in range(8):
                y = 32 * u - 8 + 5 * q + t
                if y >= 0:
                    cy[u, t, q] = full[y]
    cx = 0.5 * np.concatenate([full[0::2], full[1::2]], axis=0).T
    return split_table(tz), split_table(cy.reshape(320, G)), split_table(cx)


def halves(value):
    high = value.astype(BF16)
    low = (value - high.astype(F32)).astype(BF16)
    return high, low


def kernel(
    point,
    prof,
    xi_far,
    basis_far,
    tz,
    cy,
    cx,
    cz,
    mask,
    out,
    xi,
    basis,
    share,
    got1,
    rows2,
    got2,
    conc0,
    fields,
    carry,
    plane,
    wave,
    mine,
    listed,
    nodes,
    sums,
    parcel,
    landed,
    final,
    s1,
    r1,
    own1,
    s2,
    r2,
    own2,
    sc,
    rc,
    load,
    sn,
    rn,
    so,
    ro,
):
    pts = lax.axis_index("pts")
    i = lax.axis_index("py")
    pz = lax.axis_index("pz")
    yy, x_lo = pts // 2, pts % 2
    h, c = pz // 2, pz % 2
    xt = (x_lo + h) % 2
    u = 2 * i + c

    def at(i_, h_, c_):
        return {"pts": 2 * yy + (xt + h_) % 2, "py": i_, "pz": 2 * h_ + c_}

    barrier = pltpu.get_barrier_semaphore()
    peers = []
    for dp in range(8):
        for dh in range(2):
            for dc in range(2):
                if dp + dh + dc > 0:
                    peers.append({"pts": (pts + dp) % 8, "py": i, "pz": 2 * ((h + dh) % 2) + (c + dc) % 2})
    for di in range(1, 4):
        for dh in range(2):
            for dc in range(2):
                peers.append(at((i + di) % 4, (h + dh) % 2, (c + dc) % 2))
    for peer in peers:
        pl.semaphore_signal(barrier, inc=1, device_id=peer, device_id_type=MESH)

    def loads(q):
        copies = []
        for half in range(2):
            rows = pl.ds(pl.multiple_of(8 * q + 32 * half, 8), 8)
            copies.append(pltpu.make_async_copy(xi_far.at[rows], xi.at[rows], load.at[q, 2 * half]))
            copies.append(
                pltpu.make_async_copy(basis_far.at[:, rows], basis.at[:, rows], load.at[q, 2 * half + 1])
            )
        return copies

    def start_loads(q, _):
        for copy in loads(q):
            copy.start()
        return 0

    lax.fori_loop(0, 4, start_loads, 0)

    def slab_copy(to_h):
        return pltpu.make_async_remote_copy(
            src_ref=cz.at[:, pl.ds(16 * to_h, 20)],
            dst_ref=conc0.at[:, :, pl.ds(pl.multiple_of(8 + 16 * c, 8), 16)],
            send_sem=sc.at[to_h],
            recv_sem=rc.at[c],
            device_id=at(i, to_h, h),
            device_id_type=MESH,
        )

    def slab_local(to_h):
        return pltpu.make_async_copy(
            cz.at[:, pl.ds(16 * to_h, 20)],
            conc0.at[:, :, pl.ds(pl.multiple_of(8 + 16 * c, 8), 16)],
            rc.at[c],
        )

    above = 2 * i + h + 1

    def halo_copy(to_h):
        return pltpu.make_async_remote_copy(
            src_ref=cz.at[:, pl.ds(16 * to_h, 20), pl.ds(8, 8)],
            dst_ref=conc0.at[:, :, pl.ds(0, 8)],
            send_sem=sc.at[2 + to_h],
            recv_sem=rc.at[2],
            device_id=at((above // 2) % 4, to_h, above % 2),
            device_id_type=MESH,
        )

    def halo_local(to_h):
        return pltpu.make_async_copy(
            cz.at[:, pl.ds(16 * to_h, 20), pl.ds(8, 8)], conc0.at[:, :, pl.ds(0, 8)], rc.at[2]
        )

    def slab_here(to_h):
        return jnp.logical_and(h == to_h, c == to_h)

    def halo_some():
        return jnp.logical_and(c == 1, above < 8)

    for m in range(2):
        weight = 1.0
        for r in range(3):
            index = point[m, r]
            value = jnp.where(index == 0, -ROOT3, jnp.where(index == 1, 0.0, ROOT3))
            weight = weight * jnp.where(index == 1, 2.0 / 3.0, 1.0 / 6.0)
            mine[4 * m + r : 4 * m + r + 1, :] = jnp.full((1, 128), value, F32)
        mine[4 * m + 3 : 4 * m + 4, :] = jnp.full((1, 128), weight, F32)

    def node_copy(dp):
        return pltpu.make_async_remote_copy(
            src_ref=mine,
            dst_ref=listed.at[pts],
            send_sem=sn.at[dp],
            recv_sem=rn.at[dp],
            device_id={"pts": (pts + dp) % 8, "py": i, "pz": pz},
            device_id_type=MESH,
        )

    def greet():
        pl.semaphore_wait(barrier, len(peers))
        for dp in range(1, 8):
            node_copy(dp).start()
        listed[pts] = mine[...]
        for to_h in range(2):

            @pl.when(slab_here(to_h))
            def _():
                slab_local(to_h).start()

            @pl.when(jnp.logical_not(slab_here(to_h)))
            def _():
                slab_copy(to_h).start()

        @pl.when(jnp.logical_and(halo_some(), h == 0))
        def _():
            halo_local(0).start()

        @pl.when(jnp.logical_and(halo_some(), h == 1))
        def _():
            halo_copy(0).start()

        @pl.when(halo_some())
        def _():
            halo_copy(1).start()

        @pl.when(u == 0)
        def _():
            conc0[:, :, 0:8, :] = jnp.zeros((2, 20, 8, 128), F32)

    spot_b = (lax.broadcasted_iota(jnp.int32, (64, G), 0) + 64 * pz).astype(F32)
    spot_c = lax.broadcasted_iota(jnp.int32, (64, G), 1).astype(F32)
    wave[...] = 64.0 + spot_b * spot_b + spot_c * spot_c
    front = 64.0 * 0.9 * (32.0**1.5)

    def stage(step, _):
        amps = []
        for part in range(2):
            for half in range(2):
                a = (64 * i + 2 * step + part + 32 * half).astype(F32)
                amps.append(front / (wave[...] + a * a))
        for f in range(4):
            parts = []
            for part in range(2):
                for half in range(2):
                    row = 2 * step + part + 32 * half
                    value = xi[row] if f == 0 else basis[f - 1, row].astype(F32)
                    parts.append(value * amps[2 * part + half])
            high, low = halves(jnp.concatenate(parts, axis=0))
            both = jnp.dot(high, tz[...], preferred_element_type=F32)
            both += jnp.dot(low, tz[...], preferred_element_type=F32)
            both = both.T
            total = both[0:40] + both[48:88]
            for part in range(2):
                share[pl.ds(32 * f + 2 * step + part, 40, stride=128), :] = total[
                    :, 128 * part : 128 * part + 128
                ]
        return 0

    def stages(q, _):
        for copy in loads(q):
            copy.wait()
        return lax.fori_loop(4 * q, 4 * q + 4, stage, 0)

    lax.fori_loop(0, 1, stages, 0)
    greet()
    lax.fori_loop(1, 4, stages, 0)

    def first(k, d):
        to_h, to_c = (h + d // 2) % 2, (c + d % 2) % 2
        return pltpu.make_async_remote_copy(
            src_ref=share.at[pl.ds(pl.multiple_of((16 * to_h + 2 * k + to_c) * 128, 128), 128)],
            dst_ref=got1.at[k, pz],
            send_sem=s1.at[k, d],
            recv_sem=r1.at[k, d],
            device_id=at(i, to_h, to_c),
            device_id_type=MESH,
        )

    def first_own(k):
        return pltpu.make_async_copy(
            share.at[pl.ds(pl.multiple_of((16 * h + 2 * k + c) * 128, 128), 128)], got1.at[k, pz], own1.at[k]
        )

    def send_first(k, _):
        for d in (2, 3, 1):
            first(k, d).start()
        first_own(k).start()
        return 0

    lax.fori_loop(0, NROUND, send_first, 0)

    def second(k, d):
        to_i, to_c = (i + d // 2) % 4, (c + d % 2) % 2
        return pltpu.make_async_remote_copy(
            src_ref=rows2.at[k, 2 * to_i + to_c],
            dst_ref=got2.at[k, c, i],
            send_sem=s2.at[k, d],
            recv_sem=r2.at[k, d],
            device_id=at(to_i, h, to_c),
            device_id_type=MESH,
        )

    def second_own(k):
        return pltpu.make_async_copy(rows2.at[k, u], got2.at[k, c, i], own2.at[k])

    lane = lax.broadcasted_iota(jnp.int32, (128, 128), 1)
    lane_low = lane < 64
    lane8 = lax.broadcasted_iota(jnp.int32, (8, 128), 1)
    lane_some = lane8 > 0
    lane40 = lax.broadcasted_iota(jnp.int32, (40, 128), 1) < 64

    def b_contraction(k):
        for d in range(1, 4):
            first(k, d).wait_recv()
        first_own(k).wait()
        sides = [[], []]
        for pair in range(2):
            one, two = got1[k, 2 * pair], got1[k, 2 * pair + 1]
            sides[0].append(jnp.where(lane_low, one, pltpu.roll(two, 64, 1)))
            sides[1].append(jnp.where(lane_low, pltpu.roll(one, 64, 1), two))
        both = [jnp.concatenate(side, axis=1) for side in sides]
        rows = []
        for f in range(4):
            rows += [both[0][32 * f : 32 * f + 32], both[1][32 * f : 32 * f + 32]]
        high, low = halves(jnp.concatenate(rows, axis=0))
        for part in range(2):
            top = lax.dot_general(
                cy[160 * part : 160 * part + 160], high, NT, preferred_element_type=F32
            )
            top += lax.dot_general(
                cy[320 + 160 * part : 480 + 160 * part], high, NT, preferred_element_type=F32
            )
            top += lax.dot_general(
                cy[160 * part : 160 * part + 160], low, NT, preferred_element_type=F32
            )
            for slab in range(4):
                rows2[k, 4 * part + slab] = top[40 * slab : 40 * slab + 40]
        for d in (4, 5, 2, 6, 3, 7, 1):
            second(k, d).start()
        second_own(k).start()

    def a_contraction(k):
        for d in range(1, 8):
            second(k, d).wait_recv()
        second_own(k).wait()
        for core in range(2):
            rows = []
            for pair in range(2):
                cols = [[], []]
                for group in range(2):
                    one = got2[k, core, 2 * group, :, 128 * pair : 128 * pair + 128]
                    two = got2[k, core, 2 * group + 1, :, 128 * pair : 128 * pair + 128]
                    cols[0].append(jnp.where(lane40, one, pltpu.roll(two, 64, 1)))
                    cols[1].append(jnp.where(lane40, pltpu.roll(one, 64, 1), two))
                rows += [jnp.concatenate(col, axis=1) for col in cols]
            high, low = halves(jnp.concatenate(rows, axis=0))
            total = jnp.dot(high, cx[0:256], preferred_element_type=F32)
            total += jnp.dot(high, cx[256:512], preferred_element_type=F32)
            total += jnp.dot(low, cx[0:256], preferred_element_type=F32)
            fields[core] = total

    tiles = [(t, v) for t in range(5) for v in range(2)]

    def transport(k, core, halo):
        zz = 2 * k + core
        well = prof[zz]
        for t, v in tiles:
            plane[0, t, v] = conc0[v, zz, pl.ds(t, 8, stride=5), :]
            plane[1, t, v] = mask[v, 8 * t : 8 * t + 8, :] * well
            if not halo:
                plane[2, t, v] = jnp.zeros((8, 128), F32)
        steps = zz + 1 if halo else STEPS

        def one_point(n, _):
            node = [nodes[n, r] for r in range(3)]
            weight = nodes[n, 3]
            speed, keep, conc = {}, {}, {}
            for t, v in tiles:
                logs = [
                    fields[core, 40 * f + 8 * t : 40 * f + 8 * t + 8, 128 * v : 128 * v + 128]
                    for f in range(4)
                ]
                value = logs[0] + node[0] * logs[1] + node[1] * logs[2] + node[2] * logs[3]
                value = jnp.tanh(value)
                speed[t, v] = 0.125 + 0.125 * value
                keep[t, v] = 0.55 - 0.45 * value
                conc[t, v] = plane[0, t, v]
            for step in range(steps):
                last = halo and step == steps - 1
                flux = {tv: speed[tv] * conc[tv] for tv in tiles}
                for t, v in tiles:
                    if last:
                        carry[n, step, t, v] = flux[t, v]
                        continue
                    behind = carry[n, step, t, v]
                    carry[n, step, t, v] = flux[t, v]
                    prev_b = flux[t - 1, v] if t > 0 else pltpu.roll(flux[4, v], 1, 0)
                    prev_a = (
                        flux[t, 0]
                        if v == 1
                        else jnp.where(lane_some, pltpu.roll(flux[t, 1], 1, 1), 0.0)
                    )
                    conc[t, v] = (
                        keep[t, v] * conc[t, v]
                        + plane[1, t, v]
                        + behind
                        + prev_b
                        + 1.6 * prev_a
                    )
            if not halo:
                for t, v in tiles:
                    plane[2, t, v] += weight * conc[t, v]
            return 0

        lax.fori_loop(0, POINTS, one_point, 0)
        if not halo:
            for t, v in tiles:
                sums[v, pl.ds(16 * t + zz - 4, 8, stride=80), :] = plane[2, t, v]

    carry[...] = jnp.zeros(carry.shape, F32)
    lag = 2

    def wait_conc():
        for core in range(2):
            slab = pltpu.make_async_copy(
                cz.at[:, pl.ds(0, 20)], conc0.at[:, :, pl.ds(8 + 16 * core, 16)], rc.at[core]
            )
            slab.wait()

        @pl.when(u > 0)
        def _():
            pltpu.make_async_copy(
                cz.at[:, pl.ds(0, 20), pl.ds(8, 8)], conc0.at[:, :, pl.ds(0, 8)], rc.at[2]
            ).wait()

    def rounds(step, _):
        @pl.when(step < NROUND)
        def _():
            b_contraction(step)

        @pl.when(step >= lag)
        def _():
            a_contraction(step - lag)

        for early in range(2):

            @pl.when(step == lag + early)
            def _():
                for core in range(2):
                    transport(early, core, True)

        @pl.when(step >= lag + 2)
        def _():
            for core in range(2):
                transport(step - lag, core, False)

        return 0

    wait_conc()
    for dp in range(1, 8):
        node_copy(dp).wait_recv()
    for n in range(POINTS):
        for r in range(4):
            row = 4 * (n % 2) + r
            nodes[n, r] = jnp.broadcast_to(listed[n // 2, row : row + 1, :], (8, 128))
    lax.fori_loop(0, NROUND + lag, rounds, 0)

    granule = lax.broadcasted_iota(jnp.int32, (16, 128), 1) // 16

    def regroup(which, _):
        half, yg = which // 4, which % 4
        arrays = []
        for yy in range(4):
            for v in range(2):
                row = pl.multiple_of(16 * (8 + 16 * half + 4 * yg + yy), 16)
                arrays.append(sums[v, pl.ds(row, 16), :])
        for bit in (4, 2, 1):
            clear = (granule // bit) % 2 == 0
            for m in range(8):
                if m // bit % 2 == 0:
                    one, two = arrays[m], arrays[m + bit]
                    arrays[m] = jnp.where(clear, one, pltpu.roll(two, 16 * bit, 1))
                    arrays[m + bit] = jnp.where(clear, pltpu.roll(one, 128 - 16 * bit, 1), two)
        for p in range(8):
            parcel[p, half, yg] = arrays[p]
        return 0

    zr = pl.multiple_of(16 * (4 * yy + 2 * xt + h), 16)

    def home(dp, half):
        to = (pts + dp) % 8
        return pltpu.make_async_remote_copy(
            src_ref=parcel.at[to, half],
            dst_ref=landed.at[:, pl.ds(zr, 16)],
            send_sem=so.at[dp, half],
            recv_sem=ro.at[dp, h],
            device_id={"pts": to, "py": i, "pz": 2 * c + half},
            device_id_type=MESH,
        )

    def home_own(half):
        return pltpu.make_async_copy(parcel.at[pts, half], landed.at[:, pl.ds(zr, 16)], ro.at[0, h])

    for half in range(2):
        lax.fori_loop(4 * half, 4 * half + 4, regroup, 0)
        here = jnp.logical_and(c == h, c == half)

        @pl.when(here)
        def _():
            home_own(half).start()

        @pl.when(jnp.logical_not(here))
        def _():
            home(0, half).start()

        for dp in range(1, 8):
            home(dp, half).start()

    for dp in range(8):
        for from_h in range(2):
            pltpu.make_async_copy(
                parcel.at[0, 0], landed.at[:, pl.ds(0, 16)], ro.at[dp, from_h]
            ).wait()

    for yg in range(4):
        for zh in range(2):
            turned = landed[yg, 128 * zh : 128 * zh + 128, :].T
            for y in range(4):
                for v in range(2):
                    e = 16 * (2 * y + v)
                    final[zh, pl.ds(16 * v + 4 * yg + y, 16, stride=32), :] = turned[e : e + 16]
    for zh in range(2):
        out[:, 128 * zh : 128 * zh + 128] = final[zh]

    def drain(k, _):
        for d in range(1, 4):
            first(k, d).wait_send()
        for d in range(1, 8):
            second(k, d).wait_send()
        return 0

    lax.fori_loop(0, NROUND, drain, 0)
    for dp in range(1, 8):
        node_copy(dp).wait_send()
        for half in range(2):
            home(dp, half).wait_send()
    for half in range(2):

        @pl.when(jnp.logical_not(jnp.logical_and(c == h, c == half)))
        def _():
            home(0, half).wait_send()

    for to_h in range(2):

        @pl.when(jnp.logical_not(slab_here(to_h)))
        def _():
            slab_copy(to_h).wait_send()

    @pl.when(jnp.logical_and(halo_some(), h == 1))
    def _():
        halo_copy(0).wait_send()

    @pl.when(halo_some())
    def _():
        halo_copy(1).wait_send()


def local(xi_map, basis, point_index, conc_start, well_mask, profile):
    (tz_hi, tz_lo), (cy_hi, cy_lo), (cx_hi, cx_lo) = tables()
    pts = lax.axis_index("pts")
    i = lax.axis_index("py")
    pz = lax.axis_index("pz")
    yy, x_lo = pts // 2, pts % 2
    h, c = pz // 2, pz % 2
    xt = (x_lo + h) % 2
    g = 2 * yy + xt
    u = 2 * i + c

    tz = jnp.concatenate(
        [lax.dynamic_slice_in_dim(jnp.asarray(part), 32 * g, 48, 0) for part in (tz_hi, tz_lo)], axis=0
    )
    tz = jnp.pad(tz, ((0, 32), (0, 0))).T
    cy = jnp.concatenate([cy_hi, cy_lo], axis=0)
    cx = jnp.concatenate([cx_hi, cx_lo], axis=0)

    prof = 0.5 * lax.dynamic_slice_in_dim(jnp.pad(profile, (4, 0)), 16 * (2 * g + h), 20, 0)
    mask = lax.dynamic_slice_in_dim(jnp.pad(well_mask, ((0, 0), (8, 0))), 32 * u, 40, 1)
    mask = mask.astype(F32).reshape(128, 2, 8, 5).transpose(1, 3, 2, 0).reshape(2, 40, 128)
    cz = lax.dynamic_slice_in_dim(jnp.pad(conc_start, ((0, 0), (0, 0), (4, 0))), 32 * g, 36, 2)
    cz = cz.reshape(128, 2, 16, 36).transpose(1, 3, 2, 0)

    vmem = pl.BlockSpec(memory_space=pltpu.VMEM)
    smem = pl.BlockSpec(memory_space=pltpu.SMEM)
    dma = pltpu.SemaphoreType.DMA
    far = pl.BlockSpec(memory_space=pl.ANY)
    total = pl.pallas_call(
        kernel,
        out_shape=jax.ShapeDtypeStruct((512, 256), F32),
        in_specs=[smem, smem, far, far] + [vmem] * 5,
        out_specs=vmem,
        scratch_shapes=[
            pltpu.VMEM((64, 64, 256), F32),
            pltpu.VMEM((3, 64, 64, 256), BF16),
            pltpu.VMEM((40 * 128, 128), F32),
            pltpu.VMEM((NROUND, 4, 128, 128), F32),
            pltpu.VMEM((NROUND, 8, 40, 256), F32),
            pltpu.VMEM((NROUND, 2, 4, 40, 256), F32),
            pltpu.VMEM((2, 20, 40, 128), F32),
            pltpu.VMEM((2, 160, 256), F32),
            pltpu.VMEM((POINTS, STEPS, 5, 2, 8, 128), F32),
            pltpu.VMEM((3, 5, 2, 8, 128), F32),
            pltpu.VMEM((64, 256), F32),
            pltpu.VMEM((8, 128), F32),
            pltpu.VMEM((8, 8, 128), F32),
            pltpu.VMEM((POINTS, 4, 8, 128), F32),
            pltpu.VMEM((2, 640, 128), F32),
            pltpu.VMEM((8, 2, 4, 16, 128), F32),
            pltpu.VMEM((4, 256, 128), F32),
            pltpu.VMEM((2, 512, 128), F32),
            dma((NROUND, 4)),
            dma((NROUND, 4)),
            dma((NROUND,)),
            dma((NROUND, 8)),
            dma((NROUND, 8)),
            dma((NROUND,)),
            dma((4,)),
            dma((3,)),
            dma((4, 4)),
            dma((8,)),
            dma((8,)),
            dma((8, 2)),
            dma((8, 2)),
        ],
        compiler_params=pltpu.CompilerParams(
            collective_id=0, has_side_effects=True, vmem_limit_bytes=60 * 2**20
        ),
    )(point_index, prof, xi_map, basis, tz, cy, cx, cz, mask)
    return total.reshape(32, 16, 256)


def solution(mesh):
    placed = (
        P("py", "pz", None),
        P(None, "py", "pz", None),
        P("pts", None),
        P(None, ("py", "pz"), None),
        P(),
        P(),
    )
    return jax.shard_map(
        local, mesh=mesh, in_specs=placed, out_specs=P("pts", ("py", "pz"), None), check_vma=False
    )
```

```python
import functools

import jax
import jax.numpy as jnp
import ml_dtypes
import numpy as np
from jax import lax
from jax.experimental import pallas as pl
from jax.experimental.pallas import tpu as pltpu
from jax.sharding import PartitionSpec as P

MESH = pl.DeviceIdType.MESH
STEPS = 4
POINTS = 16
BATCH = 2
G = 256
NROUND = 10
ROOT3 = 1.7320508075688772
F32 = jnp.float32
BF16 = jnp.bfloat16
NT = (((1,), (1,)), ((), ()))


def split_table(table):
    table = np.asarray(table, np.float64)
    high = table.astype(np.float32).astype(ml_dtypes.bfloat16)
    low = (table - high.astype(np.float64)).astype(np.float32).astype(ml_dtypes.bfloat16)
    return high, low


def tables():
    spots = np.arange(G, dtype=np.float64)
    full = np.sqrt(2.0 / G) * np.cos(np.pi * (spots[:, None] + 0.5) * spots[None, :] / G)
    full[:, 0] *= np.sqrt(0.5)
    tz = np.zeros((G + 64, G))
    tz[4 : 4 + G] = full
    cy = np.zeros((8, 5, 8, G))
    for u in range(8):
        for t in range(5):
            for q in range(8):
                y = 32 * u - 8 + 5 * q + t
                if y >= 0:
                    cy[u, t, q] = full[y]
    cx = 0.5 * np.concatenate([full[0::2], full[1::2]], axis=0).T
    return split_table(tz), split_table(cy.reshape(320, G)), split_table(cx)


def halves(value):
    high = value.astype(BF16)
    low = (value - high.astype(F32)).astype(BF16)
    return high, low


def kernel(
    point,
    prof,
    xi_far,
    basis_far,
    tz,
    cy,
    cx,
    cz,
    mask,
    out,
    xi,
    basis,
    share,
    got1,
    rows2,
    got2,
    conc0,
    fields,
    carry,
    plane,
    wave,
    mine,
    listed,
    nodes,
    sums,
    parcel,
    landed,
    final,
    s1,
    r1,
    own1,
    s2,
    r2,
    own2,
    sc,
    rc,
    load,
    sn,
    rn,
    so,
    ro,
):
    pts = lax.axis_index("pts")
    i = lax.axis_index("py")
    pz = lax.axis_index("pz")
    yy, x_lo = pts // 2, pts % 2
    h, c = pz // 2, pz % 2
    xt = (x_lo + h) % 2
    u = 2 * i + c

    def at(i_, h_, c_):
        return {"pts": 2 * yy + (xt + h_) % 2, "py": i_, "pz": 2 * h_ + c_}

    barrier = pltpu.get_barrier_semaphore()
    peers = []
    for dp in range(8):
        for dh in range(2):
            for dc in range(2):
                if dp + dh + dc > 0:
                    peers.append({"pts": (pts + dp) % 8, "py": i, "pz": 2 * ((h + dh) % 2) + (c + dc) % 2})
    for di in range(1, 4):
        for dh in range(2):
            for dc in range(2):
                peers.append(at((i + di) % 4, (h + dh) % 2, (c + dc) % 2))
    for peer in peers:
        pl.semaphore_signal(barrier, inc=1, device_id=peer, device_id_type=MESH)

    def loads(q):
        copies = []
        for half in range(2):
            rows = pl.ds(pl.multiple_of(8 * q + 32 * half, 8), 8)
            copies.append(pltpu.make_async_copy(xi_far.at[rows], xi.at[rows], load.at[q, 2 * half]))
            copies.append(
                pltpu.make_async_copy(basis_far.at[:, rows], basis.at[:, rows], load.at[q, 2 * half + 1])
            )
        return copies

    def start_loads(q, _):
        for copy in loads(q):
            copy.start()
        return 0

    lax.fori_loop(0, 4, start_loads, 0)

    def slab_copy(to_h):
        return pltpu.make_async_remote_copy(
            src_ref=cz.at[:, pl.ds(16 * to_h, 20)],
            dst_ref=conc0.at[:, :, pl.ds(pl.multiple_of(8 + 16 * c, 8), 16)],
            send_sem=sc.at[to_h],
            recv_sem=rc.at[c],
            device_id=at(i, to_h, h),
            device_id_type=MESH,
        )

    def slab_local(to_h):
        return pltpu.make_async_copy(
            cz.at[:, pl.ds(16 * to_h, 20)],
            conc0.at[:, :, pl.ds(pl.multiple_of(8 + 16 * c, 8), 16)],
            rc.at[c],
        )

    above = 2 * i + h + 1

    def halo_copy(to_h):
        return pltpu.make_async_remote_copy(
            src_ref=cz.at[:, pl.ds(16 * to_h, 20), pl.ds(8, 8)],
            dst_ref=conc0.at[:, :, pl.ds(0, 8)],
            send_sem=sc.at[2 + to_h],
            recv_sem=rc.at[2],
            device_id=at((above // 2) % 4, to_h, above % 2),
            device_id_type=MESH,
        )

    def halo_local(to_h):
        return pltpu.make_async_copy(
            cz.at[:, pl.ds(16 * to_h, 20), pl.ds(8, 8)], conc0.at[:, :, pl.ds(0, 8)], rc.at[2]
        )

    def slab_here(to_h):
        return jnp.logical_and(h == to_h, c == to_h)

    def halo_some():
        return jnp.logical_and(c == 1, above < 8)

    for m in range(2):
        weight = 1.0
        for r in range(3):
            index = point[m, r]
            value = jnp.where(index == 0, -ROOT3, jnp.where(index == 1, 0.0, ROOT3))
            weight = weight * jnp.where(index == 1, 2.0 / 3.0, 1.0 / 6.0)
            mine[4 * m + r : 4 * m + r + 1, :] = jnp.full((1, 128), value, F32)
        mine[4 * m + 3 : 4 * m + 4, :] = jnp.full((1, 128), weight, F32)

    def node_copy(dp):
        return pltpu.make_async_remote_copy(
            src_ref=mine,
            dst_ref=listed.at[pts],
            send_sem=sn.at[dp],
            recv_sem=rn.at[dp],
            device_id={"pts": (pts + dp) % 8, "py": i, "pz": pz},
            device_id_type=MESH,
        )

    def greet():
        pl.semaphore_wait(barrier, len(peers))
        for dp in range(1, 8):
            node_copy(dp).start()
        listed[pts] = mine[...]
        for to_h in range(2):

            @pl.when(slab_here(to_h))
            def _():
                slab_local(to_h).start()

            @pl.when(jnp.logical_not(slab_here(to_h)))
            def _():
                slab_copy(to_h).start()

        @pl.when(jnp.logical_and(halo_some(), h == 0))
        def _():
            halo_local(0).start()

        @pl.when(jnp.logical_and(halo_some(), h == 1))
        def _():
            halo_copy(0).start()

        @pl.when(halo_some())
        def _():
            halo_copy(1).start()

        @pl.when(u == 0)
        def _():
            conc0[:, :, 0:8, :] = jnp.zeros((2, 20, 8, 128), F32)

    spot_b = (lax.broadcasted_iota(jnp.int32, (64, G), 0) + 64 * pz).astype(F32)
    spot_c = lax.broadcasted_iota(jnp.int32, (64, G), 1).astype(F32)
    wave[...] = 64.0 + spot_b * spot_b + spot_c * spot_c
    front = 64.0 * 0.9 * (32.0**1.5)

    def stage(step, _):
        amps = []
        for part in range(2):
            for half in range(2):
                a = (64 * i + 2 * step + part + 32 * half).astype(F32)
                amps.append(front / (wave[...] + a * a))
        for f in range(4):
            parts = []
            for part in range(2):
                for half in range(2):
                    row = 2 * step + part + 32 * half
                    value = xi[row] if f == 0 else basis[f - 1, row].astype(F32)
                    parts.append(value * amps[2 * part + half])
            high, low = halves(jnp.concatenate(parts, axis=0))
            both = jnp.dot(high, tz[...], preferred_element_type=F32)
            both += jnp.dot(low, tz[...], preferred_element_type=F32)
            both = both.T
            total = both[0:40] + both[48:88]
            for part in range(2):
                share[pl.ds(32 * f + 2 * step + part, 40, stride=128), :] = total[
                    :, 128 * part : 128 * part + 128
                ]
        return 0

    def stages(q, _):
        for copy in loads(q):
            copy.wait()
        return lax.fori_loop(4 * q, 4 * q + 4, stage, 0)

    lax.fori_loop(0, 1, stages, 0)
    greet()
    lax.fori_loop(1, 4, stages, 0)

    def first(k, d):
        to_h, to_c = (h + d // 2) % 2, (c + d % 2) % 2
        return pltpu.make_async_remote_copy(
            src_ref=share.at[pl.ds(pl.multiple_of((16 * to_h + 2 * k + to_c) * 128, 128), 128)],
            dst_ref=got1.at[k, pz],
            send_sem=s1.at[k, d],
            recv_sem=r1.at[k, d],
            device_id=at(i, to_h, to_c),
            device_id_type=MESH,
        )

    def first_own(k):
        return pltpu.make_async_copy(
            share.at[pl.ds(pl.multiple_of((16 * h + 2 * k + c) * 128, 128), 128)], got1.at[k, pz], own1.at[k]
        )

    def send_first(k, _):
        for d in (2, 3, 1):
            first(k, d).start()
        first_own(k).start()
        return 0

    lax.fori_loop(0, NROUND, send_first, 0)

    def second(k, d):
        to_i, to_c = (i + d // 2) % 4, (c + d % 2) % 2
        return pltpu.make_async_remote_copy(
            src_ref=rows2.at[k, 2 * to_i + to_c],
            dst_ref=got2.at[k, c, i],
            send_sem=s2.at[k, d],
            recv_sem=r2.at[k, d],
            device_id=at(to_i, h, to_c),
            device_id_type=MESH,
        )

    def second_own(k):
        return pltpu.make_async_copy(rows2.at[k, u], got2.at[k, c, i], own2.at[k])

    lane = lax.broadcasted_iota(jnp.int32, (128, 128), 1)
    lane_low = lane < 64
    lane8 = lax.broadcasted_iota(jnp.int32, (8, 128), 1)
    lane_some = lane8 > 0
    lane40 = lax.broadcasted_iota(jnp.int32, (40, 128), 1) < 64

    def b_contraction(k):
        for d in range(1, 4):
            first(k, d).wait_recv()
        first_own(k).wait()
        sides = [[], []]
        for pair in range(2):
            one, two = got1[k, 2 * pair], got1[k, 2 * pair + 1]
            sides[0].append(jnp.where(lane_low, one, pltpu.roll(two, 64, 1)))
            sides[1].append(jnp.where(lane_low, pltpu.roll(one, 64, 1), two))
        both = [jnp.concatenate(side, axis=1) for side in sides]
        rows = []
        for f in range(4):
            rows += [both[0][32 * f : 32 * f + 32], both[1][32 * f : 32 * f + 32]]
        high, low = halves(jnp.concatenate(rows, axis=0))
        both = lax.dot_general(cy[...], high, NT, preferred_element_type=F32)
        rest = lax.dot_general(cy[0:320], low, NT, preferred_element_type=F32)
        total = both[0:320] + both[320:640] + rest
        for slab in range(8):
            rows2[k, slab] = total[40 * slab : 40 * slab + 40]
        for d in (4, 5, 2, 6, 3, 7, 1):
            second(k, d).start()
        second_own(k).start()

    def a_contraction(k):
        for d in range(1, 8):
            second(k, d).wait_recv()
        second_own(k).wait()
        rows = []
        for core in range(2):
            for pair in range(2):
                cols = [[], []]
                for group in range(2):
                    one = got2[k, core, 2 * group, :, 128 * pair : 128 * pair + 128]
                    two = got2[k, core, 2 * group + 1, :, 128 * pair : 128 * pair + 128]
                    cols[0].append(jnp.where(lane40, one, pltpu.roll(two, 64, 1)))
                    cols[1].append(jnp.where(lane40, pltpu.roll(one, 64, 1), two))
                rows += [jnp.concatenate(col, axis=1) for col in cols]
        high, low = halves(jnp.concatenate(rows, axis=0))
        total = jnp.dot(high, cx[0:256], preferred_element_type=F32)
        total += jnp.dot(low, cx[0:256], preferred_element_type=F32)
        total += jnp.dot(high, cx[256:512], preferred_element_type=F32)
        for core in range(2):
            for f in range(4):
                row = 160 * core + 40 * f
                fields[core, f] = total[row : row + 40]

    tiles = [(t, v) for t in range(5) for v in range(2)]

    def transport(k, core, halo):
        zz = 2 * k + core
        well = prof[zz]
        for t, v in tiles:
            plane[0, t, v] = conc0[v, zz, pl.ds(t, 8, stride=5), :]
            plane[1, t, v] = mask[v, 8 * t : 8 * t + 8, :] * well
            if not halo:
                plane[2, t, v] = jnp.zeros((8, 128), F32)
        steps = zz + 1 if halo else STEPS

        def some_points(group, _):
            each = range(BATCH)
            speed, conc = [{} for _ in each], [{} for _ in each]
            for m in each:
                n = BATCH * group + m
                node = [nodes[n, r] for r in range(3)]
                for t, v in tiles:
                    logs = [
                        fields[core, f, 8 * t : 8 * t + 8, 128 * v : 128 * v + 128] for f in range(4)
                    ]
                    value = logs[0] + node[0] * logs[1] + node[1] * logs[2] + node[2] * logs[3]
                    speed[m][t, v] = 0.125 + 0.125 * jnp.tanh(value)
                    conc[m][t, v] = plane[0, t, v]
            for step in range(steps):
                last = halo and step == steps - 1
                flux = [{tv: speed[m][tv] * conc[m][tv] for tv in tiles} for m in each]
                for t, v in tiles:
                    for m in each:
                        n = BATCH * group + m
                        here = flux[m][t, v]
                        if last:
                            carry[n, step, t, v] = here
                            continue
                        behind = carry[n, step, t, v]
                        carry[n, step, t, v] = here
                        prev_b = flux[m][t - 1, v] if t > 0 else pltpu.roll(flux[m][4, v], 1, 0)
                        prev_a = (
                            flux[m][t, 0]
                            if v == 1
                            else jnp.where(lane_some, pltpu.roll(flux[m][t, 1], 1, 1), 0.0)
                        )
                        conc[m][t, v] = (
                            (conc[m][t, v] - 3.6 * here)
                            + (plane[1, t, v] + behind)
                            + (prev_b + 1.6 * prev_a)
                        )
            if not halo:
                for t, v in tiles:
                    part = nodes[BATCH * group, 3] * conc[0][t, v]
                    for m in range(1, BATCH):
                        part += nodes[BATCH * group + m, 3] * conc[m][t, v]
                    plane[2, t, v] += part
            return 0

        lax.fori_loop(0, POINTS // BATCH, some_points, 0)
        if not halo:
            for t, v in tiles:
                sums[v, pl.ds(16 * t + zz - 4, 8, stride=80), :] = plane[2, t, v]

    carry[...] = jnp.zeros(carry.shape, F32)
    lag = 2

    def wait_conc():
        for core in range(2):
            slab = pltpu.make_async_copy(
                cz.at[:, pl.ds(0, 20)], conc0.at[:, :, pl.ds(8 + 16 * core, 16)], rc.at[core]
            )
            slab.wait()

        @pl.when(u > 0)
        def _():
            pltpu.make_async_copy(
                cz.at[:, pl.ds(0, 20), pl.ds(8, 8)], conc0.at[:, :, pl.ds(0, 8)], rc.at[2]
            ).wait()

    def rounds(step, _):
        @pl.when(step < NROUND)
        def _():
            b_contraction(step)

        @pl.when(step >= lag)
        def _():
            a_contraction(step - lag)

        for early in range(2):

            @pl.when(step == lag + early)
            def _():
                for core in range(2):
                    transport(early, core, True)

        @pl.when(step >= lag + 2)
        def _():
            for core in range(2):
                transport(step - lag, core, False)

        return 0

    wait_conc()
    for dp in range(1, 8):
        node_copy(dp).wait_recv()
    for n in range(POINTS):
        for r in range(4):
            row = 4 * (n % 2) + r
            nodes[n, r] = jnp.broadcast_to(listed[n // 2, row : row + 1, :], (8, 128))
    lax.fori_loop(0, NROUND + lag, rounds, 0)

    granule = lax.broadcasted_iota(jnp.int32, (16, 128), 1) // 16

    def regroup(which, _):
        half, yg = which // 4, which % 4
        arrays = []
        for yy in range(4):
            for v in range(2):
                row = pl.multiple_of(16 * (8 + 16 * half + 4 * yg + yy), 16)
                arrays.append(sums[v, pl.ds(row, 16), :])
        for bit in (4, 2, 1):
            clear = (granule // bit) % 2 == 0
            for m in range(8):
                if m // bit % 2 == 0:
                    one, two = arrays[m], arrays[m + bit]
                    arrays[m] = jnp.where(clear, one, pltpu.roll(two, 16 * bit, 1))
                    arrays[m + bit] = jnp.where(clear, pltpu.roll(one, 128 - 16 * bit, 1), two)
        for p in range(8):
            parcel[p, half, yg] = arrays[p]
        return 0

    zr = pl.multiple_of(16 * (4 * yy + 2 * xt + h), 16)

    def home(dp, half):
        to = (pts + dp) % 8
        return pltpu.make_async_remote_copy(
            src_ref=parcel.at[to, half],
            dst_ref=landed.at[:, pl.ds(zr, 16)],
            send_sem=so.at[dp, half],
            recv_sem=ro.at[dp, h],
            device_id={"pts": to, "py": i, "pz": 2 * c + half},
            device_id_type=MESH,
        )

    def home_own(half):
        return pltpu.make_async_copy(parcel.at[pts, half], landed.at[:, pl.ds(zr, 16)], ro.at[0, h])

    for half in range(2):
        lax.fori_loop(4 * half, 4 * half + 4, regroup, 0)
        here = jnp.logical_and(c == h, c == half)

        @pl.when(here)
        def _():
            home_own(half).start()

        @pl.when(jnp.logical_not(here))
        def _():
            home(0, half).start()

        for dp in range(1, 8):
            home(dp, half).start()

    for dp in range(8):
        for from_h in range(2):
            pltpu.make_async_copy(
                parcel.at[0, 0], landed.at[:, pl.ds(0, 16)], ro.at[dp, from_h]
            ).wait()

    for yg in range(4):
        for zh in range(2):
            turned = landed[yg, 128 * zh : 128 * zh + 128, :].T
            for y in range(4):
                for v in range(2):
                    e = 16 * (2 * y + v)
                    final[zh, pl.ds(16 * v + 4 * yg + y, 16, stride=32), :] = turned[e : e + 16]
    for zh in range(2):
        out[:, 128 * zh : 128 * zh + 128] = final[zh]

    def drain(k, _):
        for d in range(1, 4):
            first(k, d).wait_send()
        for d in range(1, 8):
            second(k, d).wait_send()
        return 0

    lax.fori_loop(0, NROUND, drain, 0)
    for dp in range(1, 8):
        node_copy(dp).wait_send()
        for half in range(2):
            home(dp, half).wait_send()
    for half in range(2):

        @pl.when(jnp.logical_not(jnp.logical_and(c == h, c == half)))
        def _():
            home(0, half).wait_send()

    for to_h in range(2):

        @pl.when(jnp.logical_not(slab_here(to_h)))
        def _():
            slab_copy(to_h).wait_send()

    @pl.when(jnp.logical_and(halo_some(), h == 1))
    def _():
        halo_copy(0).wait_send()

    @pl.when(halo_some())
    def _():
        halo_copy(1).wait_send()


def local(xi_map, basis, point_index, conc_start, well_mask, profile):
    (tz_hi, tz_lo), (cy_hi, cy_lo), (cx_hi, cx_lo) = tables()
    pts = lax.axis_index("pts")
    i = lax.axis_index("py")
    pz = lax.axis_index("pz")
    yy, x_lo = pts // 2, pts % 2
    h, c = pz // 2, pz % 2
    xt = (x_lo + h) % 2
    g = 2 * yy + xt
    u = 2 * i + c

    tz = jnp.concatenate(
        [lax.dynamic_slice_in_dim(jnp.asarray(part), 32 * g, 48, 0) for part in (tz_hi, tz_lo)], axis=0
    )
    tz = jnp.pad(tz, ((0, 32), (0, 0))).T
    cy = jnp.concatenate([cy_hi, cy_lo], axis=0)
    cx = jnp.concatenate([cx_hi, cx_lo], axis=0)

    prof = 0.5 * lax.dynamic_slice_in_dim(jnp.pad(profile, (4, 0)), 16 * (2 * g + h), 20, 0)
    mask = lax.dynamic_slice_in_dim(jnp.pad(well_mask, ((0, 0), (8, 0))), 32 * u, 40, 1)
    mask = mask.astype(F32).reshape(128, 2, 8, 5).transpose(1, 3, 2, 0).reshape(2, 40, 128)
    cz = lax.dynamic_slice_in_dim(jnp.pad(conc_start, ((0, 0), (0, 0), (4, 0))), 32 * g, 36, 2)
    cz = cz.reshape(128, 2, 16, 36).transpose(1, 3, 2, 0)

    vmem = pl.BlockSpec(memory_space=pltpu.VMEM)
    smem = pl.BlockSpec(memory_space=pltpu.SMEM)
    dma = pltpu.SemaphoreType.DMA
    far = pl.BlockSpec(memory_space=pl.ANY)
    total = pl.pallas_call(
        kernel,
        out_shape=jax.ShapeDtypeStruct((512, 256), F32),
        in_specs=[smem, smem, far, far] + [vmem] * 5,
        out_specs=vmem,
        scratch_shapes=[
            pltpu.VMEM((64, 64, 256), F32),
            pltpu.VMEM((3, 64, 64, 256), BF16),
            pltpu.VMEM((40 * 128, 128), F32),
            pltpu.VMEM((NROUND, 4, 128, 128), F32),
            pltpu.VMEM((NROUND, 8, 40, 256), F32),
            pltpu.VMEM((NROUND, 2, 4, 40, 256), F32),
            pltpu.VMEM((2, 20, 40, 128), F32),
            pltpu.VMEM((2, 4, 40, 256), F32),
            pltpu.VMEM((POINTS, STEPS, 5, 2, 8, 128), F32),
            pltpu.VMEM((3, 5, 2, 8, 128), F32),
            pltpu.VMEM((64, 256), F32),
            pltpu.VMEM((8, 128), F32),
            pltpu.VMEM((8, 8, 128), F32),
            pltpu.VMEM((POINTS, 4, 8, 128), F32),
            pltpu.VMEM((2, 640, 128), F32),
            pltpu.VMEM((8, 2, 4, 16, 128), F32),
            pltpu.VMEM((4, 256, 128), F32),
            pltpu.VMEM((2, 512, 128), F32),
            dma((NROUND, 4)),
            dma((NROUND, 4)),
            dma((NROUND,)),
            dma((NROUND, 8)),
            dma((NROUND, 8)),
            dma((NROUND,)),
            dma((4,)),
            dma((3,)),
            dma((4, 4)),
            dma((8,)),
            dma((8,)),
            dma((8, 2)),
            dma((8, 2)),
        ],
        compiler_params=pltpu.CompilerParams(
            collective_id=0, has_side_effects=True, vmem_limit_bytes=60 * 2**20
        ),
    )(point_index, prof, xi_map, basis, tz, cy, cx, cz, mask)
    return total.reshape(32, 16, 256)


def solution(mesh):
    placed = (
        P("py", "pz", None),
        P(None, "py", "pz", None),
        P("pts", None),
        P(None, ("py", "pz"), None),
        P(),
        P(),
    )
    return jax.shard_map(
        local, mesh=mesh, in_specs=placed, out_specs=P("pts", ("py", "pz"), None), check_vma=False
    )
```

```python
import functools

import jax
import jax.numpy as jnp
import ml_dtypes
import numpy as np
from jax import lax
from jax.experimental import pallas as pl
from jax.experimental.pallas import tpu as pltpu
from jax.sharding import PartitionSpec as P

MESH = pl.DeviceIdType.MESH
STEPS = 4
POINTS = 16
BATCH = 4
G = 256
NROUND = 10
ROOT3 = 1.7320508075688772
F32 = jnp.float32
BF16 = jnp.bfloat16
NT = (((1,), (1,)), ((), ()))


def split_table(table):
    table = np.asarray(table, np.float64)
    high = table.astype(np.float32).astype(ml_dtypes.bfloat16)
    low = (table - high.astype(np.float64)).astype(np.float32).astype(ml_dtypes.bfloat16)
    return high, low


def tables():
    spots = np.arange(G, dtype=np.float64)
    full = np.sqrt(2.0 / G) * np.cos(np.pi * (spots[:, None] + 0.5) * spots[None, :] / G)
    full[:, 0] *= np.sqrt(0.5)
    tz = np.zeros((G + 64, G))
    tz[4 : 4 + G] = full
    cy = np.zeros((8, 5, 8, G))
    for u in range(8):
        for t in range(5):
            for q in range(8):
                y = 32 * u - 8 + 5 * q + t
                if y >= 0:
                    cy[u, t, q] = full[y]
    cx = 0.5 * np.concatenate([full[0::2], full[1::2]], axis=0).T
    return split_table(tz), split_table(cy.reshape(320, G)), split_table(cx)


def halves(value):
    high = value.astype(BF16)
    low = (value - high.astype(F32)).astype(BF16)
    return high, low


def kernel(
    point,
    prof,
    xi_far,
    basis_far,
    tz,
    cy,
    cx,
    cz,
    mask,
    out,
    xi,
    basis,
    share,
    got1,
    rows2,
    got2,
    conc0,
    fields,
    carry,
    plane,
    wave,
    mine,
    listed,
    nodes,
    sums,
    parcel,
    landed,
    final,
    s1,
    r1,
    own1,
    s2,
    r2,
    own2,
    sc,
    rc,
    load,
    sn,
    rn,
    so,
    ro,
):
    pts = lax.axis_index("pts")
    i = lax.axis_index("py")
    pz = lax.axis_index("pz")
    yy, x_lo = pts // 2, pts % 2
    h, c = pz // 2, pz % 2
    xt = (x_lo + h) % 2
    u = 2 * i + c

    def at(i_, h_, c_):
        return {"pts": 2 * yy + (xt + h_) % 2, "py": i_, "pz": 2 * h_ + c_}

    barrier = pltpu.get_barrier_semaphore()
    peers = []
    for dp in range(8):
        for dh in range(2):
            for dc in range(2):
                if dp + dh + dc > 0:
                    peers.append({"pts": (pts + dp) % 8, "py": i, "pz": 2 * ((h + dh) % 2) + (c + dc) % 2})
    for di in range(1, 4):
        for dh in range(2):
            for dc in range(2):
                peers.append(at((i + di) % 4, (h + dh) % 2, (c + dc) % 2))
    for peer in peers:
        pl.semaphore_signal(barrier, inc=1, device_id=peer, device_id_type=MESH)

    def loads(q):
        copies = []
        for half in range(2):
            rows = pl.ds(pl.multiple_of(8 * q + 32 * half, 8), 8)
            copies.append(pltpu.make_async_copy(xi_far.at[rows], xi.at[rows], load.at[q, 2 * half]))
            copies.append(
                pltpu.make_async_copy(basis_far.at[:, rows], basis.at[:, rows], load.at[q, 2 * half + 1])
            )
        return copies

    def start_loads(q, _):
        for copy in loads(q):
            copy.start()
        return 0

    lax.fori_loop(0, 4, start_loads, 0)

    def slab_copy(to_h):
        return pltpu.make_async_remote_copy(
            src_ref=cz.at[:, pl.ds(16 * to_h, 20)],
            dst_ref=conc0.at[:, :, pl.ds(pl.multiple_of(8 + 16 * c, 8), 16)],
            send_sem=sc.at[to_h],
            recv_sem=rc.at[c],
            device_id=at(i, to_h, h),
            device_id_type=MESH,
        )

    def slab_local(to_h):
        return pltpu.make_async_copy(
            cz.at[:, pl.ds(16 * to_h, 20)],
            conc0.at[:, :, pl.ds(pl.multiple_of(8 + 16 * c, 8), 16)],
            rc.at[c],
        )

    above = 2 * i + h + 1

    def halo_copy(to_h):
        return pltpu.make_async_remote_copy(
            src_ref=cz.at[:, pl.ds(16 * to_h, 20), pl.ds(8, 8)],
            dst_ref=conc0.at[:, :, pl.ds(0, 8)],
            send_sem=sc.at[2 + to_h],
            recv_sem=rc.at[2],
            device_id=at((above // 2) % 4, to_h, above % 2),
            device_id_type=MESH,
        )

    def halo_local(to_h):
        return pltpu.make_async_copy(
            cz.at[:, pl.ds(16 * to_h, 20), pl.ds(8, 8)], conc0.at[:, :, pl.ds(0, 8)], rc.at[2]
        )

    def slab_here(to_h):
        return jnp.logical_and(h == to_h, c == to_h)

    def halo_some():
        return jnp.logical_and(c == 1, above < 8)

    for m in range(2):
        weight = 1.0
        for r in range(3):
            index = point[m, r]
            value = jnp.where(index == 0, -ROOT3, jnp.where(index == 1, 0.0, ROOT3))
            weight = weight * jnp.where(index == 1, 2.0 / 3.0, 1.0 / 6.0)
            mine[4 * m + r : 4 * m + r + 1, :] = jnp.full((1, 128), value, F32)
        mine[4 * m + 3 : 4 * m + 4, :] = jnp.full((1, 128), weight, F32)

    def node_copy(dp):
        return pltpu.make_async_remote_copy(
            src_ref=mine,
            dst_ref=listed.at[pts],
            send_sem=sn.at[dp],
            recv_sem=rn.at[dp],
            device_id={"pts": (pts + dp) % 8, "py": i, "pz": pz},
            device_id_type=MESH,
        )

    def greet():
        pl.semaphore_wait(barrier, len(peers))
        for dp in range(1, 8):
            node_copy(dp).start()
        listed[pts] = mine[...]
        for to_h in range(2):

            @pl.when(slab_here(to_h))
            def _():
                slab_local(to_h).start()

            @pl.when(jnp.logical_not(slab_here(to_h)))
            def _():
                slab_copy(to_h).start()

        @pl.when(jnp.logical_and(halo_some(), h == 0))
        def _():
            halo_local(0).start()

        @pl.when(jnp.logical_and(halo_some(), h == 1))
        def _():
            halo_copy(0).start()

        @pl.when(halo_some())
        def _():
            halo_copy(1).start()

        @pl.when(u == 0)
        def _():
            conc0[:, :, 0:8, :] = jnp.zeros((2, 20, 8, 128), F32)

    spot_b = (lax.broadcasted_iota(jnp.int32, (64, G), 0) + 64 * pz).astype(F32)
    spot_c = lax.broadcasted_iota(jnp.int32, (64, G), 1).astype(F32)
    wave[...] = 64.0 + spot_b * spot_b + spot_c * spot_c
    front = 64.0 * 0.9 * (32.0**1.5)

    def stage(step, _):
        amps = []
        for part in range(2):
            for half in range(2):
                a = (64 * i + 2 * step + part + 32 * half).astype(F32)
                amps.append(front / (wave[...] + a * a))
        for f in range(4):
            parts = []
            for part in range(2):
                for half in range(2):
                    row = 2 * step + part + 32 * half
                    value = xi[row] if f == 0 else basis[f - 1, row].astype(F32)
                    parts.append(value * amps[2 * part + half])
            high, low = halves(jnp.concatenate(parts, axis=0))
            both = jnp.dot(high, tz[...], preferred_element_type=F32)
            both += jnp.dot(low, tz[...], preferred_element_type=F32)
            both = both.T
            total = both[0:40] + both[48:88]
            for part in range(2):
                share[pl.ds(32 * f + 2 * step + part, 40, stride=128), :] = total[
                    :, 128 * part : 128 * part + 128
                ]
        return 0

    def stages(q, _):
        for copy in loads(q):
            copy.wait()
        return lax.fori_loop(4 * q, 4 * q + 4, stage, 0)

    lax.fori_loop(0, 1, stages, 0)
    greet()
    lax.fori_loop(1, 4, stages, 0)

    def first(k, d):
        to_h, to_c = (h + d // 2) % 2, (c + d % 2) % 2
        return pltpu.make_async_remote_copy(
            src_ref=share.at[pl.ds(pl.multiple_of((16 * to_h + 2 * k + to_c) * 128, 128), 128)],
            dst_ref=got1.at[k, pz],
            send_sem=s1.at[k, d],
            recv_sem=r1.at[k, d],
            device_id=at(i, to_h, to_c),
            device_id_type=MESH,
        )

    def first_own(k):
        return pltpu.make_async_copy(
            share.at[pl.ds(pl.multiple_of((16 * h + 2 * k + c) * 128, 128), 128)], got1.at[k, pz], own1.at[k]
        )

    def send_first(k, _):
        for d in (2, 3, 1):
            first(k, d).start()
        first_own(k).start()
        return 0

    lax.fori_loop(0, NROUND, send_first, 0)

    def second(k, d):
        to_i, to_c = (i + d // 2) % 4, (c + d % 2) % 2
        return pltpu.make_async_remote_copy(
            src_ref=rows2.at[k, 2 * to_i + to_c],
            dst_ref=got2.at[k, c, i],
            send_sem=s2.at[k, d],
            recv_sem=r2.at[k, d],
            device_id=at(to_i, h, to_c),
            device_id_type=MESH,
        )

    def second_own(k):
        return pltpu.make_async_copy(rows2.at[k, u], got2.at[k, c, i], own2.at[k])

    lane = lax.broadcasted_iota(jnp.int32, (128, 128), 1)
    lane_low = lane < 64
    lane8 = lax.broadcasted_iota(jnp.int32, (8, 128), 1)
    lane_some = lane8 > 0
    lane40 = lax.broadcasted_iota(jnp.int32, (40, 128), 1) < 64

    def b_contraction(k):
        for d in range(1, 4):
            first(k, d).wait_recv()
        first_own(k).wait()
        sides = [[], []]
        for pair in range(2):
            one, two = got1[k, 2 * pair], got1[k, 2 * pair + 1]
            sides[0].append(jnp.where(lane_low, one, pltpu.roll(two, 64, 1)))
            sides[1].append(jnp.where(lane_low, pltpu.roll(one, 64, 1), two))
        both = [jnp.concatenate(side, axis=1) for side in sides]
        rows = []
        for f in range(4):
            rows += [both[0][32 * f : 32 * f + 32], both[1][32 * f : 32 * f + 32]]
        high, low = halves(jnp.concatenate(rows, axis=0))
        both = lax.dot_general(cy[...], high, NT, preferred_element_type=F32)
        rest = lax.dot_general(cy[0:320], low, NT, preferred_element_type=F32)
        total = both[0:320] + both[320:640] + rest
        for slab in range(8):
            rows2[k, slab] = total[40 * slab : 40 * slab + 40]
        for d in (4, 5, 2, 6, 3, 7, 1):
            second(k, d).start()
        second_own(k).start()

    def a_contraction(k):
        for d in range(1, 8):
            second(k, d).wait_recv()
        second_own(k).wait()
        rows = []
        for core in range(2):
            for pair in range(2):
                cols = [[], []]
                for group in range(2):
                    one = got2[k, core, 2 * group, :, 128 * pair : 128 * pair + 128]
                    two = got2[k, core, 2 * group + 1, :, 128 * pair : 128 * pair + 128]
                    cols[0].append(jnp.where(lane40, one, pltpu.roll(two, 64, 1)))
                    cols[1].append(jnp.where(lane40, pltpu.roll(one, 64, 1), two))
                rows += [jnp.concatenate(col, axis=1) for col in cols]
        high, low = halves(jnp.concatenate(rows, axis=0))
        total = jnp.dot(high, cx[0:256], preferred_element_type=F32)
        total += jnp.dot(low, cx[0:256], preferred_element_type=F32)
        total += jnp.dot(high, cx[256:512], preferred_element_type=F32)
        for core in range(2):
            for f in range(4):
                row = 160 * core + 40 * f
                fields[core, f] = total[row : row + 40]

    tiles = [(t, v) for t in range(5) for v in range(2)]

    def transport(k, core, halo):
        zz = 2 * k + core
        well = prof[zz]
        for t, v in tiles:
            plane[0, t, v] = conc0[v, zz, pl.ds(t, 8, stride=5), :]
            plane[1, t, v] = mask[v, 8 * t : 8 * t + 8, :] * well
            if not halo:
                plane[2, t, v] = jnp.zeros((8, 128), F32)
        steps = zz + 1 if halo else STEPS

        def some_points(group, _):
            each = range(BATCH)
            speed, conc = [{} for _ in each], [{} for _ in each]
            for m in each:
                n = BATCH * group + m
                node = [nodes[n, r] for r in range(3)]
                for t, v in tiles:
                    logs = [
                        fields[core, f, 8 * t : 8 * t + 8, 128 * v : 128 * v + 128] for f in range(4)
                    ]
                    value = logs[0] + node[0] * logs[1] + node[1] * logs[2] + node[2] * logs[3]
                    speed[m][t, v] = 0.125 + 0.125 * jnp.tanh(value)
                    conc[m][t, v] = plane[0, t, v]
            for step in range(steps):
                last = halo and step == steps - 1
                flux = [{tv: speed[m][tv] * conc[m][tv] for tv in tiles} for m in each]
                for t, v in tiles:
                    for m in each:
                        n = BATCH * group + m
                        here = flux[m][t, v]
                        if last:
                            carry[n, step, t, v] = here
                            continue
                        behind = carry[n, step, t, v]
                        carry[n, step, t, v] = here
                        prev_b = flux[m][t - 1, v] if t > 0 else pltpu.roll(flux[m][4, v], 1, 0)
                        prev_a = (
                            flux[m][t, 0]
                            if v == 1
                            else jnp.where(lane_some, pltpu.roll(flux[m][t, 1], 1, 1), 0.0)
                        )
                        conc[m][t, v] = (
                            (conc[m][t, v] - 3.6 * here)
                            + (plane[1, t, v] + behind)
                            + (prev_b + 1.6 * prev_a)
                        )
            if not halo:
                for t, v in tiles:
                    part = nodes[BATCH * group, 3] * conc[0][t, v]
                    for m in range(1, BATCH):
                        part += nodes[BATCH * group + m, 3] * conc[m][t, v]
                    plane[2, t, v] += part
            return 0

        lax.fori_loop(0, POINTS // BATCH, some_points, 0)
        if not halo:
            for t, v in tiles:
                sums[v, pl.ds(16 * t + zz - 4, 8, stride=80), :] = plane[2, t, v]

    carry[...] = jnp.zeros(carry.shape, F32)
    lag = 2

    def wait_conc():
        for core in range(2):
            slab = pltpu.make_async_copy(
                cz.at[:, pl.ds(0, 20)], conc0.at[:, :, pl.ds(8 + 16 * core, 16)], rc.at[core]
            )
            slab.wait()

        @pl.when(u > 0)
        def _():
            pltpu.make_async_copy(
                cz.at[:, pl.ds(0, 20), pl.ds(8, 8)], conc0.at[:, :, pl.ds(0, 8)], rc.at[2]
            ).wait()

    def rounds(step, _):
        @pl.when(step < NROUND)
        def _():
            b_contraction(step)

        @pl.when(step >= lag)
        def _():
            a_contraction(step - lag)

        for early in range(2):

            @pl.when(step == lag + early)
            def _():
                for core in range(2):
                    transport(early, core, True)

        @pl.when(step >= lag + 2)
        def _():
            for core in range(2):
                transport(step - lag, core, False)

        return 0

    wait_conc()
    for dp in range(1, 8):
        node_copy(dp).wait_recv()
    for n in range(POINTS):
        for r in range(4):
            row = 4 * (n % 2) + r
            nodes[n, r] = jnp.broadcast_to(listed[n // 2, row : row + 1, :], (8, 128))
    lax.fori_loop(0, NROUND + lag, rounds, 0)

    granule = lax.broadcasted_iota(jnp.int32, (16, 128), 1) // 16

    def regroup(which, _):
        half, yg = which // 4, which % 4
        arrays = []
        for yy in range(4):
            for v in range(2):
                row = pl.multiple_of(16 * (8 + 16 * half + 4 * yg + yy), 16)
                arrays.append(sums[v, pl.ds(row, 16), :])
        for bit in (4, 2, 1):
            clear = (granule // bit) % 2 == 0
            for m in range(8):
                if m // bit % 2 == 0:
                    one, two = arrays[m], arrays[m + bit]
                    arrays[m] = jnp.where(clear, one, pltpu.roll(two, 16 * bit, 1))
                    arrays[m + bit] = jnp.where(clear, pltpu.roll(one, 128 - 16 * bit, 1), two)
        for p in range(8):
            parcel[p, half, yg] = arrays[p]
        return 0

    zr = pl.multiple_of(16 * (4 * yy + 2 * xt + h), 16)

    def home(dp, half):
        to = (pts + dp) % 8
        return pltpu.make_async_remote_copy(
            src_ref=parcel.at[to, half],
            dst_ref=landed.at[:, pl.ds(zr, 16)],
            send_sem=so.at[dp, half],
            recv_sem=ro.at[dp, h],
            device_id={"pts": to, "py": i, "pz": 2 * c + half},
            device_id_type=MESH,
        )

    def home_own(half):
        return pltpu.make_async_copy(parcel.at[pts, half], landed.at[:, pl.ds(zr, 16)], ro.at[0, h])

    for half in range(2):
        lax.fori_loop(4 * half, 4 * half + 4, regroup, 0)
        here = jnp.logical_and(c == h, c == half)

        @pl.when(here)
        def _():
            home_own(half).start()

        @pl.when(jnp.logical_not(here))
        def _():
            home(0, half).start()

        for dp in range(1, 8):
            home(dp, half).start()

    for dp in range(8):
        for from_h in range(2):
            pltpu.make_async_copy(
                parcel.at[0, 0], landed.at[:, pl.ds(0, 16)], ro.at[dp, from_h]
            ).wait()

    for yg in range(4):
        for zh in range(2):
            turned = landed[yg, 128 * zh : 128 * zh + 128, :].T
            for y in range(4):
                for v in range(2):
                    e = 16 * (2 * y + v)
                    final[zh, pl.ds(16 * v + 4 * yg + y, 16, stride=32), :] = turned[e : e + 16]
    for zh in range(2):
        out[:, 128 * zh : 128 * zh + 128] = final[zh]

    def drain(k, _):
        for d in range(1, 4):
            first(k, d).wait_send()
        for d in range(1, 8):
            second(k, d).wait_send()
        return 0

    lax.fori_loop(0, NROUND, drain, 0)
    for dp in range(1, 8):
        node_copy(dp).wait_send()
        for half in range(2):
            home(dp, half).wait_send()
    for half in range(2):

        @pl.when(jnp.logical_not(jnp.logical_and(c == h, c == half)))
        def _():
            home(0, half).wait_send()

    for to_h in range(2):

        @pl.when(jnp.logical_not(slab_here(to_h)))
        def _():
            slab_copy(to_h).wait_send()

    @pl.when(jnp.logical_and(halo_some(), h == 1))
    def _():
        halo_copy(0).wait_send()

    @pl.when(halo_some())
    def _():
        halo_copy(1).wait_send()


def local(xi_map, basis, point_index, conc_start, well_mask, profile):
    (tz_hi, tz_lo), (cy_hi, cy_lo), (cx_hi, cx_lo) = tables()
    pts = lax.axis_index("pts")
    i = lax.axis_index("py")
    pz = lax.axis_index("pz")
    yy, x_lo = pts // 2, pts % 2
    h, c = pz // 2, pz % 2
    xt = (x_lo + h) % 2
    g = 2 * yy + xt
    u = 2 * i + c

    tz = jnp.concatenate(
        [lax.dynamic_slice_in_dim(jnp.asarray(part), 32 * g, 48, 0) for part in (tz_hi, tz_lo)], axis=0
    )
    tz = jnp.pad(tz, ((0, 32), (0, 0))).T
    cy = jnp.concatenate([cy_hi, cy_lo], axis=0)
    cx = jnp.concatenate([cx_hi, cx_lo], axis=0)

    prof = 0.5 * lax.dynamic_slice_in_dim(jnp.pad(profile, (4, 0)), 16 * (2 * g + h), 20, 0)
    mask = lax.dynamic_slice_in_dim(jnp.pad(well_mask, ((0, 0), (8, 0))), 32 * u, 40, 1)
    mask = mask.astype(F32).reshape(128, 2, 8, 5).transpose(1, 3, 2, 0).reshape(2, 40, 128)
    cz = lax.dynamic_slice_in_dim(jnp.pad(conc_start, ((0, 0), (0, 0), (4, 0))), 32 * g, 36, 2)
    cz = cz.reshape(128, 2, 16, 36).transpose(1, 3, 2, 0)

    vmem = pl.BlockSpec(memory_space=pltpu.VMEM)
    smem = pl.BlockSpec(memory_space=pltpu.SMEM)
    dma = pltpu.SemaphoreType.DMA
    far = pl.BlockSpec(memory_space=pl.ANY)
    total = pl.pallas_call(
        kernel,
        out_shape=jax.ShapeDtypeStruct((512, 256), F32),
        in_specs=[smem, smem, far, far] + [vmem] * 5,
        out_specs=vmem,
        scratch_shapes=[
            pltpu.VMEM((64, 64, 256), F32),
            pltpu.VMEM((3, 64, 64, 256), BF16),
            pltpu.VMEM((40 * 128, 128), F32),
            pltpu.VMEM((NROUND, 4, 128, 128), F32),
            pltpu.VMEM((NROUND, 8, 40, 256), F32),
            pltpu.VMEM((NROUND, 2, 4, 40, 256), F32),
            pltpu.VMEM((2, 20, 40, 128), F32),
            pltpu.VMEM((2, 4, 40, 256), F32),
            pltpu.VMEM((POINTS, STEPS, 5, 2, 8, 128), F32),
            pltpu.VMEM((3, 5, 2, 8, 128), F32),
            pltpu.VMEM((64, 256), F32),
            pltpu.VMEM((8, 128), F32),
            pltpu.VMEM((8, 8, 128), F32),
            pltpu.VMEM((POINTS, 4, 8, 128), F32),
            pltpu.VMEM((2, 640, 128), F32),
            pltpu.VMEM((8, 2, 4, 16, 128), F32),
            pltpu.VMEM((4, 256, 128), F32),
            pltpu.VMEM((2, 512, 128), F32),
            dma((NROUND, 4)),
            dma((NROUND, 4)),
            dma((NROUND,)),
            dma((NROUND, 8)),
            dma((NROUND, 8)),
            dma((NROUND,)),
            dma((4,)),
            dma((3,)),
            dma((4, 4)),
            dma((8,)),
            dma((8,)),
            dma((8, 2)),
            dma((8, 2)),
        ],
        compiler_params=pltpu.CompilerParams(
            collective_id=0, has_side_effects=True, vmem_limit_bytes=60 * 2**20
        ),
    )(point_index, prof, xi_map, basis, tz, cy, cx, cz, mask)
    return total.reshape(32, 16, 256)


def solution(mesh):
    placed = (
        P("py", "pz", None),
        P(None, "py", "pz", None),
        P("pts", None),
        P(None, ("py", "pz"), None),
        P(),
        P(),
    )
    return jax.shard_map(
        local, mesh=mesh, in_specs=placed, out_specs=P("pts", ("py", "pz"), None), check_vma=False
    )
```

```python
import functools

import jax
import jax.numpy as jnp
import ml_dtypes
import numpy as np
from jax import lax
from jax.experimental import pallas as pl
from jax.experimental.pallas import tpu as pltpu
from jax.sharding import PartitionSpec as P

MESH = pl.DeviceIdType.MESH
STEPS = 4
POINTS = 16
BATCH = 4
G = 256
NROUND = 10
EARLY = 4
ROOT3 = 1.7320508075688772
F32 = jnp.float32
BF16 = jnp.bfloat16
NT = (((1,), (1,)), ((), ()))


def split_table(table):
    table = np.asarray(table, np.float64)
    high = table.astype(np.float32).astype(ml_dtypes.bfloat16)
    low = (table - high.astype(np.float64)).astype(np.float32).astype(ml_dtypes.bfloat16)
    return high, low


def tables():
    spots = np.arange(G, dtype=np.float64)
    full = np.sqrt(2.0 / G) * np.cos(np.pi * (spots[:, None] + 0.5) * spots[None, :] / G)
    full[:, 0] *= np.sqrt(0.5)
    tz = np.zeros((8, 40, G))
    for g in range(8):
        for par in range(2):
            for w in range(18):
                z = 32 * g - 4 + 2 * w + par
                if z >= 0:
                    tz[g, 20 * par + w] = full[z]
    tz = tz.transpose(0, 2, 1)
    cy = np.zeros((8, 5, 8, G))
    for u in range(8):
        for t in range(5):
            for q in range(8):
                y = 32 * u - 8 + 5 * q + t
                if y >= 0:
                    cy[u, t, q] = full[y]
    cx = 0.5 * np.concatenate([full[0::2], full[1::2]], axis=0).T
    return split_table(tz), split_table(cy.reshape(320, G)), split_table(cx)


def halves(value):
    high = value.astype(BF16)
    low = (value - high.astype(F32)).astype(BF16)
    return high, low


def kernel(
    point,
    prof,
    xi_far,
    basis_far,
    conc_far,
    mask_far,
    tz_far,
    cy,
    cx,
    out,
    xi,
    basis,
    share,
    got1,
    rows2,
    got2,
    conc0,
    fields,
    carry,
    plane,
    wave,
    mine,
    listed,
    nodes,
    sums,
    parcel,
    landed,
    final,
    tz,
    start,
    turned_z,
    cz_flat,
    wells,
    turned_y,
    mask,
    s0,
    r0,
    own0,
    s1,
    r1,
    own1,
    s2,
    r2,
    own2,
    sc,
    rc,
    load,
    prep,
    sn,
    rn,
    so,
    ro,
):
    pts = lax.axis_index("pts")
    i = lax.axis_index("py")
    pz = lax.axis_index("pz")
    yy, x_lo = pts // 2, pts % 2
    h, c = pz // 2, pz % 2
    xt = (x_lo + h) % 2
    u = 2 * i + c
    g = 2 * yy + xt
    cz = cz_flat.reshape(2, 40, 16, 128)

    def at(i_, h_, c_):
        return {"pts": 2 * yy + (xt + h_) % 2, "py": i_, "pz": 2 * h_ + c_}

    barrier = pltpu.get_barrier_semaphore()
    peers = []
    for dp in range(8):
        for dh in range(2):
            for dc in range(2):
                if dp + dh + dc > 0:
                    peers.append({"pts": (pts + dp) % 8, "py": i, "pz": 2 * ((h + dh) % 2) + (c + dc) % 2})
    for di in range(1, 4):
        for dh in range(2):
            for dc in range(2):
                peers.append(at((i + di) % 4, (h + dh) % 2, (c + dc) % 2))
    for peer in peers:
        pl.semaphore_signal(barrier, inc=1, device_id=peer, device_id_type=MESH)

    def loads(q):
        copies = []
        for half in range(2):
            rows = pl.ds(pl.multiple_of(8 * q + 32 * half, 8), 8)
            copies.append(pltpu.make_async_copy(xi_far.at[rows], xi.at[rows], load.at[q, 2 * half]))
            copies.append(
                pltpu.make_async_copy(basis_far.at[:, rows], basis.at[:, rows], load.at[q, 2 * half + 1])
            )
        return copies

    def start_loads(q, _):
        for copy in loads(q):
            copy.start()
        return 0

    def load_conc(zh):
        return pltpu.make_async_copy(
            conc_far.at[:, pl.ds(128 * zh, 128)], start.at[zh], prep.at[zh]
        )

    def load_mask(yh):
        return pltpu.make_async_copy(
            mask_far.at[:, pl.ds(128 * yh, 128)], wells.at[yh], prep.at[2 + yh]
        )

    load_tz = pltpu.make_async_copy(tz_far.at[g], tz, prep.at[4])
    some_z = [g <= 4, g >= 4]
    for zh in range(2):

        @pl.when(some_z[zh])
        def _():
            load_conc(zh).start()

    load_tz.start()
    lax.fori_loop(0, 4, start_loads, 0)
    for yh in range(2):
        load_mask(yh).start()

    def slab_copy(to_h):
        return pltpu.make_async_remote_copy(
            src_ref=cz.at[:, pl.ds(16 * to_h, 20)],
            dst_ref=conc0.at[:, :, pl.ds(pl.multiple_of(8 + 16 * c, 8), 16)],
            send_sem=sc.at[to_h],
            recv_sem=rc.at[c],
            device_id=at(i, to_h, h),
            device_id_type=MESH,
        )

    def slab_local(to_h):
        return pltpu.make_async_copy(
            cz.at[:, pl.ds(16 * to_h, 20)],
            conc0.at[:, :, pl.ds(pl.multiple_of(8 + 16 * c, 8), 16)],
            rc.at[c],
        )

    above = 2 * i + h + 1

    def halo_copy(to_h):
        return pltpu.make_async_remote_copy(
            src_ref=cz.at[:, pl.ds(16 * to_h, 20), pl.ds(8, 8)],
            dst_ref=conc0.at[:, :, pl.ds(0, 8)],
            send_sem=sc.at[2 + to_h],
            recv_sem=rc.at[2],
            device_id=at((above // 2) % 4, to_h, above % 2),
            device_id_type=MESH,
        )

    def halo_local(to_h):
        return pltpu.make_async_copy(
            cz.at[:, pl.ds(16 * to_h, 20), pl.ds(8, 8)], conc0.at[:, :, pl.ds(0, 8)], rc.at[2]
        )

    def slab_here(to_h):
        return jnp.logical_and(h == to_h, c == to_h)

    def halo_some():
        return jnp.logical_and(c == 1, above < 8)

    for m in range(2):
        weight = 1.0
        for r in range(3):
            index = point[m, r]
            value = jnp.where(index == 0, -ROOT3, jnp.where(index == 1, 0.0, ROOT3))
            weight = weight * jnp.where(index == 1, 2.0 / 3.0, 1.0 / 6.0)
            mine[4 * m + r : 4 * m + r + 1, :] = jnp.full((1, 128), value, F32)
        mine[4 * m + 3 : 4 * m + 4, :] = jnp.full((1, 128), weight, F32)

    def node_copy(dp):
        return pltpu.make_async_remote_copy(
            src_ref=mine,
            dst_ref=listed.at[pts],
            send_sem=sn.at[dp],
            recv_sem=rn.at[dp],
            device_id={"pts": (pts + dp) % 8, "py": i, "pz": pz},
            device_id_type=MESH,
        )

    turned_z[:, 0:8, :] = jnp.zeros((2, 8, 128), F32)
    for zh in range(2):

        @pl.when(some_z[zh])
        def _():
            load_conc(zh).wait()

    def turn_conc(y, _):
        for zh in range(2):

            @pl.when(some_z[zh])
            def _():
                for v in range(2):
                    turned_z[v, 4 + 128 * zh : 132 + 128 * zh, :] = start[
                        zh, pl.ds(16 * v + y, 128, stride=32), :
                    ].T

        for v in range(2):
            cz_flat[v, pl.ds(y, 40, stride=16), :] = turned_z[v, pl.ds(pl.multiple_of(32 * g, 32), 40), :]
        return 0

    lax.fori_loop(0, 16, turn_conc, 0)

    def turn_mask():
        turned_y[:, 0:8, :] = jnp.zeros((2, 8, 128), F32)
        for yh in range(2):
            load_mask(yh).wait()
            for v in range(2):
                block = wells[yh, pl.ds(v, 128, stride=2), :].astype(F32)
                turned_y[v, 8 + 128 * yh : 136 + 128 * yh, :] = 0.5 * block.T
        for v in range(2):
            for t in range(5):
                mask[v, 8 * t : 8 * t + 8, :] = turned_y[v, pl.ds(32 * u + t, 8, stride=5), :]

    def greet():
        pl.semaphore_wait(barrier, len(peers))
        for dp in range(1, 8):
            node_copy(dp).start()
        listed[pts] = mine[...]
        for to_h in range(2):

            @pl.when(slab_here(to_h))
            def _():
                slab_local(to_h).start()

            @pl.when(jnp.logical_not(slab_here(to_h)))
            def _():
                slab_copy(to_h).start()

        @pl.when(jnp.logical_and(halo_some(), h == 0))
        def _():
            halo_local(0).start()

        @pl.when(jnp.logical_and(halo_some(), h == 1))
        def _():
            halo_copy(0).start()

        @pl.when(halo_some())
        def _():
            halo_copy(1).start()

        @pl.when(u == 0)
        def _():
            conc0[:, :, 0:8, :] = jnp.zeros((2, 20, 8, 128), F32)

    spot_b = (lax.broadcasted_iota(jnp.int32, (64, G), 0) + 64 * pz).astype(F32)
    spot_c = lax.broadcasted_iota(jnp.int32, (64, G), 1).astype(F32)
    wave[...] = 64.0 + spot_b * spot_b + spot_c * spot_c
    front = 64.0 * 0.9 * (32.0**1.5)

    def stage(step, _):
        amps = []
        for part in range(2):
            for half in range(2):
                a = (64 * i + 2 * step + part + 32 * half).astype(F32)
                amps.append(front / (wave[...] + a * a))
        for f in range(4):
            parts = []
            for part in range(2):
                for half in range(2):
                    row = 2 * step + part + 32 * half
                    value = xi[row] if f == 0 else basis[f - 1, row].astype(F32)
                    parts.append(value * amps[2 * part + half])
            high, low = halves(jnp.concatenate(parts, axis=0))
            both = jnp.dot(high, tz[...], preferred_element_type=F32)
            both += jnp.dot(low, tz[...], preferred_element_type=F32)
            both = both.T
            total = both[0:40] + both[40:80]
            for part in range(2):
                share[pl.ds(32 * f + 2 * step + part, 40, stride=128), :] = total[
                    :, 128 * part : 128 * part + 128
                ]
        return 0

    def stages(q, _):
        for copy in loads(q):
            copy.wait()
        lax.fori_loop(4 * q, 4 * q + 4, stage, 0)
        for d in (2, 3, 1):
            early(q, d).start()
        early_own(q).start()
        return 0

    blocks = share.reshape(40, 4, 32, 128)

    def early_parts(q, to_h, to_c):
        rows = pl.ds(pl.multiple_of(8 * q, 8), 8)
        src = blocks.at[pl.ds(20 * to_c + 8 * to_h, EARLY), :, rows]
        return src, got1.at[pl.ds(0, EARLY), pz, :, rows]

    def early(q, d):
        to_h, to_c = (h + d // 2) % 2, (c + d % 2) % 2
        src, dst = early_parts(q, to_h, to_c)
        return pltpu.make_async_remote_copy(
            src_ref=src,
            dst_ref=dst,
            send_sem=s0.at[q, d],
            recv_sem=r0.at[q, d],
            device_id=at(i, to_h, to_c),
            device_id_type=MESH,
        )

    def early_own(q):
        return pltpu.make_async_copy(*early_parts(q, h, c), own0.at[q])

    greet()
    load_tz.wait()
    lax.fori_loop(0, 4, stages, 0)

    def first(k, d):
        to_h, to_c = (h + d // 2) % 2, (c + d % 2) % 2
        return pltpu.make_async_remote_copy(
            src_ref=blocks.at[20 * to_c + 8 * to_h + k],
            dst_ref=got1.at[k, pz],
            send_sem=s1.at[k, d],
            recv_sem=r1.at[k, d],
            device_id=at(i, to_h, to_c),
            device_id_type=MESH,
        )

    def first_own(k):
        return pltpu.make_async_copy(blocks.at[20 * c + 8 * h + k], got1.at[k, pz], own1.at[k])

    def send_first(k, _):
        for d in (2, 3, 1):
            first(k, d).start()
        first_own(k).start()
        return 0

    lax.fori_loop(EARLY, NROUND, send_first, 0)

    def second(k, d):
        to_i, to_c = (i + d // 2) % 4, (c + d % 2) % 2
        return pltpu.make_async_remote_copy(
            src_ref=rows2.at[k, 2 * to_i + to_c],
            dst_ref=got2.at[k, c, i],
            send_sem=s2.at[k, d],
            recv_sem=r2.at[k, d],
            device_id=at(to_i, h, to_c),
            device_id_type=MESH,
        )

    def second_own(k):
        return pltpu.make_async_copy(rows2.at[k, u], got2.at[k, c, i], own2.at[k])

    lane = lax.broadcasted_iota(jnp.int32, (128, 128), 1)
    lane_low = lane < 64
    lane8 = lax.broadcasted_iota(jnp.int32, (8, 128), 1)
    lane_some = lane8 > 0
    lane40 = lax.broadcasted_iota(jnp.int32, (40, 128), 1) < 64

    def b_contraction(k):
        @pl.when(k == 0)
        def _():
            for q in range(4):
                for d in range(1, 4):
                    early(q, d).wait_recv()
                early_own(q).wait()

        @pl.when(k >= EARLY)
        def _():
            for d in range(1, 4):
                first(k, d).wait_recv()
            first_own(k).wait()

        sides = [[], []]
        for pair in range(2):
            one, two = (got1[k, 2 * pair + m].reshape(128, 128) for m in range(2))
            sides[0].append(jnp.where(lane_low, one, pltpu.roll(two, 64, 1)))
            sides[1].append(jnp.where(lane_low, pltpu.roll(one, 64, 1), two))
        both = [jnp.concatenate(side, axis=1) for side in sides]
        rows = []
        for f in range(4):
            rows += [both[0][32 * f : 32 * f + 32], both[1][32 * f : 32 * f + 32]]
        high, low = halves(jnp.concatenate(rows, axis=0))
        both = lax.dot_general(cy[...], high, NT, preferred_element_type=F32)
        rest = lax.dot_general(cy[0:320], low, NT, preferred_element_type=F32)
        total = both[0:320] + both[320:640] + rest
        for slab in range(8):
            rows2[k, slab] = total[40 * slab : 40 * slab + 40]
        for d in (4, 5, 2, 6, 3, 7, 1):
            second(k, d).start()
        second_own(k).start()

    def a_contraction(k):
        for d in range(1, 8):
            second(k, d).wait_recv()
        second_own(k).wait()
        rows = []
        for core in range(2):
            for pair in range(2):
                cols = [[], []]
                for group in range(2):
                    one = got2[k, core, 2 * group, :, 128 * pair : 128 * pair + 128]
                    two = got2[k, core, 2 * group + 1, :, 128 * pair : 128 * pair + 128]
                    cols[0].append(jnp.where(lane40, one, pltpu.roll(two, 64, 1)))
                    cols[1].append(jnp.where(lane40, pltpu.roll(one, 64, 1), two))
                rows += [jnp.concatenate(col, axis=1) for col in cols]
        high, low = halves(jnp.concatenate(rows, axis=0))
        total = jnp.dot(high, cx[0:256], preferred_element_type=F32)
        total += jnp.dot(low, cx[0:256], preferred_element_type=F32)
        total += jnp.dot(high, cx[256:512], preferred_element_type=F32)
        for core in range(2):
            for f in range(4):
                row = 160 * core + 40 * f
                fields[core, f] = total[row : row + 40]

    tiles = [(t, v) for t in range(5) for v in range(2)]

    def transport(k, core, halo):
        zz = 2 * k + core
        spot_z = 16 * (2 * g + h) - 4 + zz
        well = jnp.where(spot_z >= 0, prof[jnp.maximum(spot_z, 0)], 0.0)
        for t, v in tiles:
            plane[0, t, v] = conc0[v, zz, pl.ds(t, 8, stride=5), :]
            plane[1, t, v] = mask[v, 8 * t : 8 * t + 8, :] * well
            if not halo:
                plane[2, t, v] = jnp.zeros((8, 128), F32)
        steps = zz + 1 if halo else STEPS

        def some_points(group, _):
            each = range(BATCH)
            speed, conc = [{} for _ in each], [{} for _ in each]
            for m in each:
                n = BATCH * group + m
                node = [nodes[n, r] for r in range(3)]
                for t, v in tiles:
                    logs = [
                        fields[core, f, 8 * t : 8 * t + 8, 128 * v : 128 * v + 128] for f in range(4)
                    ]
                    value = logs[0] + node[0] * logs[1] + node[1] * logs[2] + node[2] * logs[3]
                    speed[m][t, v] = 0.125 + 0.125 * jnp.tanh(value)
                    conc[m][t, v] = plane[0, t, v]
            for step in range(steps):
                last = halo and step == steps - 1
                flux = [{tv: speed[m][tv] * conc[m][tv] for tv in tiles} for m in each]
                for t, v in tiles:
                    for m in each:
                        n = BATCH * group + m
                        here = flux[m][t, v]
                        if last:
                            carry[n, step, t, v] = here
                            continue
                        behind = carry[n, step, t, v]
                        carry[n, step, t, v] = here
                        prev_b = flux[m][t - 1, v] if t > 0 else pltpu.roll(flux[m][4, v], 1, 0)
                        prev_a = (
                            flux[m][t, 0]
                            if v == 1
                            else jnp.where(lane_some, pltpu.roll(flux[m][t, 1], 1, 1), 0.0)
                        )
                        conc[m][t, v] = (
                            (conc[m][t, v] - 3.6 * here)
                            + (plane[1, t, v] + behind)
                            + (prev_b + 1.6 * prev_a)
                        )
            if not halo:
                for t, v in tiles:
                    part = nodes[BATCH * group, 3] * conc[0][t, v]
                    for m in range(1, BATCH):
                        part += nodes[BATCH * group + m, 3] * conc[m][t, v]
                    plane[2, t, v] += part
            return 0

        lax.fori_loop(0, POINTS // BATCH, some_points, 0)
        if not halo:
            for t, v in tiles:
                sums[v, pl.ds(16 * t + zz - 4, 8, stride=80), :] = plane[2, t, v]

    carry[...] = jnp.zeros(carry.shape, F32)
    lag = 2

    def wait_conc():
        for core in range(2):
            slab = pltpu.make_async_copy(
                cz.at[:, pl.ds(0, 20)], conc0.at[:, :, pl.ds(8 + 16 * core, 16)], rc.at[core]
            )
            slab.wait()

        @pl.when(u > 0)
        def _():
            pltpu.make_async_copy(
                cz.at[:, pl.ds(0, 20), pl.ds(8, 8)], conc0.at[:, :, pl.ds(0, 8)], rc.at[2]
            ).wait()

    def rounds(step, _):
        @pl.when(step < NROUND)
        def _():
            b_contraction(step)

        @pl.when(step >= lag)
        def _():
            a_contraction(step - lag)

        for early in range(2):

            @pl.when(step == lag + early)
            def _():
                for core in range(2):
                    transport(early, core, True)

        @pl.when(step >= lag + 2)
        def _():
            for core in range(2):
                transport(step - lag, core, False)

        return 0

    turn_mask()
    wait_conc()
    for dp in range(1, 8):
        node_copy(dp).wait_recv()
    for n in range(POINTS):
        for r in range(4):
            row = 4 * (n % 2) + r
            nodes[n, r] = jnp.broadcast_to(listed[n // 2, row : row + 1, :], (8, 128))
    lax.fori_loop(0, NROUND + lag, rounds, 0)

    granule = lax.broadcasted_iota(jnp.int32, (16, 128), 1) // 16

    def regroup(which, _):
        half, yg = which // 4, which % 4
        arrays = []
        for yy in range(4):
            for v in range(2):
                row = pl.multiple_of(16 * (8 + 16 * half + 4 * yg + yy), 16)
                arrays.append(sums[v, pl.ds(row, 16), :])
        for bit in (4, 2, 1):
            clear = (granule // bit) % 2 == 0
            for m in range(8):
                if m // bit % 2 == 0:
                    one, two = arrays[m], arrays[m + bit]
                    arrays[m] = jnp.where(clear, one, pltpu.roll(two, 16 * bit, 1))
                    arrays[m + bit] = jnp.where(clear, pltpu.roll(one, 128 - 16 * bit, 1), two)
        for p in range(8):
            parcel[p, half, yg] = arrays[p]
        return 0

    zr = pl.multiple_of(16 * (4 * yy + 2 * xt + h), 16)

    def home(dp, half):
        to = (pts + dp) % 8
        return pltpu.make_async_remote_copy(
            src_ref=parcel.at[to, half],
            dst_ref=landed.at[:, pl.ds(zr, 16)],
            send_sem=so.at[dp, half],
            recv_sem=ro.at[dp, h],
            device_id={"pts": to, "py": i, "pz": 2 * c + half},
            device_id_type=MESH,
        )

    def home_own(half):
        return pltpu.make_async_copy(parcel.at[pts, half], landed.at[:, pl.ds(zr, 16)], ro.at[0, h])

    for half in range(2):
        lax.fori_loop(4 * half, 4 * half + 4, regroup, 0)
        here = jnp.logical_and(c == h, c == half)

        @pl.when(here)
        def _():
            home_own(half).start()

        @pl.when(jnp.logical_not(here))
        def _():
            home(0, half).start()

        for dp in range(1, 8):
            home(dp, half).start()

    for dp in range(8):
        for from_h in range(2):
            pltpu.make_async_copy(
                parcel.at[0, 0], landed.at[:, pl.ds(0, 16)], ro.at[dp, from_h]
            ).wait()

    for yg in range(4):
        for zh in range(2):
            turned = landed[yg, 128 * zh : 128 * zh + 128, :].T
            for y in range(4):
                for v in range(2):
                    e = 16 * (2 * y + v)
                    final[zh, pl.ds(16 * v + 4 * yg + y, 16, stride=32), :] = turned[e : e + 16]
    for zh in range(2):
        out[:, 128 * zh : 128 * zh + 128] = final[zh]

    def drain(k, _):
        @pl.when(k >= EARLY)
        def _():
            for d in range(1, 4):
                first(k, d).wait_send()

        @pl.when(k < 4)
        def _():
            for d in range(1, 4):
                early(k, d).wait_send()

        for d in range(1, 8):
            second(k, d).wait_send()
        return 0

    lax.fori_loop(0, NROUND, drain, 0)
    for dp in range(1, 8):
        node_copy(dp).wait_send()
        for half in range(2):
            home(dp, half).wait_send()
    for half in range(2):

        @pl.when(jnp.logical_not(jnp.logical_and(c == h, c == half)))
        def _():
            home(0, half).wait_send()

    for to_h in range(2):

        @pl.when(jnp.logical_not(slab_here(to_h)))
        def _():
            slab_copy(to_h).wait_send()

    @pl.when(jnp.logical_and(halo_some(), h == 1))
    def _():
        halo_copy(0).wait_send()

    @pl.when(halo_some())
    def _():
        halo_copy(1).wait_send()


def local(xi_map, basis, point_index, conc_start, well_mask, profile):
    (tz_hi, tz_lo), (cy_hi, cy_lo), (cx_hi, cx_lo) = tables()
    tz = np.concatenate([tz_hi, tz_lo, np.zeros((8, G, 48), ml_dtypes.bfloat16)], axis=2)
    cy = np.concatenate([cy_hi, cy_lo], axis=0)
    cx = np.concatenate([cx_hi, cx_lo], axis=0)

    vmem = pl.BlockSpec(memory_space=pltpu.VMEM)
    smem = pl.BlockSpec(memory_space=pltpu.SMEM)
    dma = pltpu.SemaphoreType.DMA
    far = pl.BlockSpec(memory_space=pl.ANY)
    total = pl.pallas_call(
        kernel,
        out_shape=jax.ShapeDtypeStruct((512, 256), F32),
        in_specs=[smem, smem] + [far] * 5 + [vmem] * 2,
        out_specs=vmem,
        scratch_shapes=[
            pltpu.VMEM((64, 64, 256), F32),
            pltpu.VMEM((3, 64, 64, 256), BF16),
            pltpu.VMEM((40 * 128, 128), F32),
            pltpu.VMEM((NROUND, 4, 4, 32, 128), F32),
            pltpu.VMEM((NROUND, 8, 40, 256), F32),
            pltpu.VMEM((NROUND, 2, 4, 40, 256), F32),
            pltpu.VMEM((2, 20, 40, 128), F32),
            pltpu.VMEM((2, 4, 40, 256), F32),
            pltpu.VMEM((POINTS, STEPS, 5, 2, 8, 128), F32),
            pltpu.VMEM((3, 5, 2, 8, 128), F32),
            pltpu.VMEM((64, 256), F32),
            pltpu.VMEM((8, 128), F32),
            pltpu.VMEM((8, 8, 128), F32),
            pltpu.VMEM((POINTS, 4, 8, 128), F32),
            pltpu.VMEM((2, 640, 128), F32),
            pltpu.VMEM((8, 2, 4, 16, 128), F32),
            pltpu.VMEM((4, 256, 128), F32),
            pltpu.VMEM((2, 512, 128), F32),
            pltpu.VMEM((256, 128), BF16),
            pltpu.VMEM((2, 4096, 128), F32),
            pltpu.VMEM((2, 272, 128), F32),
            pltpu.VMEM((2, 640, 128), F32),
            pltpu.VMEM((2, 256, 128), jnp.int32),
            pltpu.VMEM((2, 264, 128), F32),
            pltpu.VMEM((2, 40, 128), F32),
            dma((4, 4)),
            dma((4, 4)),
            dma((4,)),
            dma((NROUND, 4)),
            dma((NROUND, 4)),
            dma((NROUND,)),
            dma((NROUND, 8)),
            dma((NROUND, 8)),
            dma((NROUND,)),
            dma((4,)),
            dma((3,)),
            dma((4, 4)),
            dma((5,)),
            dma((8,)),
            dma((8,)),
            dma((8, 2)),
            dma((8, 2)),
        ],
        compiler_params=pltpu.CompilerParams(
            collective_id=0, has_side_effects=True, vmem_limit_bytes=60 * 2**20
        ),
    )(point_index, profile, xi_map, basis, conc_start.reshape(4096, 256), well_mask, tz, cy, cx)
    return total.reshape(32, 16, 256)


def solution(mesh):
    placed = (
        P("py", "pz", None),
        P(None, "py", "pz", None),
        P("pts", None),
        P(None, ("py", "pz"), None),
        P(),
        P(),
    )
    return jax.shard_map(
        local, mesh=mesh, in_specs=placed, out_specs=P("pts", ("py", "pz"), None), check_vma=False
    )
```

```python
import functools

import jax
import jax.numpy as jnp
import ml_dtypes
import numpy as np
from jax import lax
from jax.experimental import pallas as pl
from jax.experimental.pallas import tpu as pltpu
from jax.sharding import PartitionSpec as P

MESH = pl.DeviceIdType.MESH
STEPS = 4
POINTS = 16
BATCH = 4
G = 256
NROUND = 10
EARLY = 4
ROOT3 = 1.7320508075688772
F32 = jnp.float32
BF16 = jnp.bfloat16
NT = (((1,), (1,)), ((), ()))


def split_table(table):
    table = np.asarray(table, np.float64)
    high = table.astype(np.float32).astype(ml_dtypes.bfloat16)
    low = (table - high.astype(np.float64)).astype(np.float32).astype(ml_dtypes.bfloat16)
    return high, low


def tables():
    spots = np.arange(G, dtype=np.float64)
    full = np.sqrt(2.0 / G) * np.cos(np.pi * (spots[:, None] + 0.5) * spots[None, :] / G)
    full[:, 0] *= np.sqrt(0.5)
    tz = np.zeros((8, 40, G))
    for g in range(8):
        for par in range(2):
            for w in range(18):
                z = 32 * g - 4 + 2 * w + par
                if z >= 0:
                    tz[g, 20 * par + w] = full[z]
    tz = tz.transpose(0, 2, 1)
    cy = np.zeros((8, 5, 8, G))
    for u in range(8):
        for t in range(5):
            for q in range(8):
                y = 32 * u - 8 + 5 * q + t
                if y >= 0:
                    cy[u, t, q] = full[y]
    cx = 0.5 * np.concatenate([full[0::2], full[1::2]], axis=0).T
    return split_table(tz), split_table(cy.reshape(320, G)), split_table(cx)


def halves(value):
    high = value.astype(BF16)
    low = (value - high.astype(F32)).astype(BF16)
    return high, low


def kernel(
    point,
    prof,
    xi_far,
    basis_far,
    conc_far,
    mask_far,
    tz_far,
    cy,
    cx,
    out,
    xi,
    basis,
    share,
    got1,
    rows2,
    got2,
    conc0,
    fields,
    carry,
    plane,
    wave,
    mine,
    listed,
    nodes,
    sums,
    parcel,
    landed,
    final,
    tz,
    start,
    turned_z,
    cz_flat,
    wells,
    turned_y,
    mask,
    s0,
    r0,
    own0,
    s1,
    r1,
    own1,
    s2,
    r2,
    own2,
    sc,
    rc,
    load,
    prep,
    sn,
    rn,
    so,
    ro,
):
    pts = lax.axis_index("pts")
    i = lax.axis_index("py")
    pz = lax.axis_index("pz")
    yy, x_lo = pts // 2, pts % 2
    h, c = pz // 2, pz % 2
    xt = (x_lo + h) % 2
    u = 2 * i + c
    g = 2 * yy + xt
    cz = cz_flat.reshape(2, 40, 16, 128)

    def at(i_, h_, c_):
        return {"pts": 2 * yy + (xt + h_) % 2, "py": i_, "pz": 2 * h_ + c_}

    barrier = pltpu.get_barrier_semaphore()
    peers = []
    for dp in range(8):
        for dh in range(2):
            for dc in range(2):
                if dp + dh + dc > 0:
                    peers.append({"pts": (pts + dp) % 8, "py": i, "pz": 2 * ((h + dh) % 2) + (c + dc) % 2})
    for di in range(1, 4):
        for dh in range(2):
            for dc in range(2):
                peers.append(at((i + di) % 4, (h + dh) % 2, (c + dc) % 2))
    for peer in peers:
        pl.semaphore_signal(barrier, inc=1, device_id=peer, device_id_type=MESH)

    def loads(q):
        copies = []
        for half in range(2):
            rows = pl.ds(pl.multiple_of(8 * q + 32 * half, 8), 8)
            copies.append(pltpu.make_async_copy(xi_far.at[rows], xi.at[rows], load.at[q, 2 * half]))
            copies.append(
                pltpu.make_async_copy(basis_far.at[:, rows], basis.at[:, rows], load.at[q, 2 * half + 1])
            )
        return copies

    def start_loads(q, _):
        for copy in loads(q):
            copy.start()
        return 0

    def load_conc(zh):
        return pltpu.make_async_copy(
            conc_far.at[:, pl.ds(128 * zh, 128)], start.at[zh], prep.at[zh]
        )

    def load_mask(yh):
        return pltpu.make_async_copy(
            mask_far.at[:, pl.ds(128 * yh, 128)], wells.at[yh], prep.at[2 + yh]
        )

    load_tz = pltpu.make_async_copy(tz_far.at[g], tz, prep.at[4])
    some_z = [g <= 4, g >= 4]
    for zh in range(2):

        @pl.when(some_z[zh])
        def _():
            load_conc(zh).start()

    load_tz.start()
    lax.fori_loop(0, 4, start_loads, 0)
    for yh in range(2):
        load_mask(yh).start()

    def slab_copy(to_h):
        return pltpu.make_async_remote_copy(
            src_ref=cz.at[:, pl.ds(16 * to_h, 20)],
            dst_ref=conc0.at[:, :, pl.ds(pl.multiple_of(8 + 16 * c, 8), 16)],
            send_sem=sc.at[to_h],
            recv_sem=rc.at[c],
            device_id=at(i, to_h, h),
            device_id_type=MESH,
        )

    def slab_local(to_h):
        return pltpu.make_async_copy(
            cz.at[:, pl.ds(16 * to_h, 20)],
            conc0.at[:, :, pl.ds(pl.multiple_of(8 + 16 * c, 8), 16)],
            rc.at[c],
        )

    above = 2 * i + h + 1

    def halo_copy(to_h):
        return pltpu.make_async_remote_copy(
            src_ref=cz.at[:, pl.ds(16 * to_h, 20), pl.ds(8, 8)],
            dst_ref=conc0.at[:, :, pl.ds(0, 8)],
            send_sem=sc.at[2 + to_h],
            recv_sem=rc.at[2],
            device_id=at((above // 2) % 4, to_h, above % 2),
            device_id_type=MESH,
        )

    def halo_local(to_h):
        return pltpu.make_async_copy(
            cz.at[:, pl.ds(16 * to_h, 20), pl.ds(8, 8)], conc0.at[:, :, pl.ds(0, 8)], rc.at[2]
        )

    def slab_here(to_h):
        return jnp.logical_and(h == to_h, c == to_h)

    def halo_some():
        return jnp.logical_and(c == 1, above < 8)

    for m in range(2):
        weight = 1.0
        for r in range(3):
            index = point[m, r]
            value = jnp.where(index == 0, -ROOT3, jnp.where(index == 1, 0.0, ROOT3))
            weight = weight * jnp.where(index == 1, 2.0 / 3.0, 1.0 / 6.0)
            mine[4 * m + r : 4 * m + r + 1, :] = jnp.full((1, 128), value, F32)
        mine[4 * m + 3 : 4 * m + 4, :] = jnp.full((1, 128), weight, F32)

    def node_copy(dp):
        return pltpu.make_async_remote_copy(
            src_ref=mine,
            dst_ref=listed.at[pts],
            send_sem=sn.at[dp],
            recv_sem=rn.at[dp],
            device_id={"pts": (pts + dp) % 8, "py": i, "pz": pz},
            device_id_type=MESH,
        )

    turned_z[:, 0:8, :] = jnp.zeros((8, 8, 128), F32)
    for zh in range(2):

        @pl.when(some_z[zh])
        def _():
            load_conc(zh).wait()

    def turn_conc(y4, _):
        rows = [(m, v) for m in range(4) for v in range(2)]
        for zh in range(2):

            @pl.when(some_z[zh])
            def _():
                for m, v in rows:
                    turned_z[2 * m + v, 4 + 128 * zh : 132 + 128 * zh, :] = start[
                        zh, pl.ds(16 * v + 4 * y4 + m, 128, stride=32), :
                    ].T

        for m, v in rows:
            cz_flat[v, pl.ds(4 * y4 + m, 40, stride=16), :] = turned_z[
                2 * m + v, pl.ds(pl.multiple_of(32 * g, 32), 40), :
            ]
        return 0

    lax.fori_loop(0, 4, turn_conc, 0)

    def turn_mask():
        turned_y[:, 0:8, :] = jnp.zeros((2, 8, 128), F32)
        for yh in range(2):
            load_mask(yh).wait()
            for v in range(2):
                block = wells[yh, pl.ds(v, 128, stride=2), :].astype(F32)
                turned_y[v, 8 + 128 * yh : 136 + 128 * yh, :] = 0.5 * block.T
        for v in range(2):
            for t in range(5):
                mask[v, 8 * t : 8 * t + 8, :] = turned_y[v, pl.ds(32 * u + t, 8, stride=5), :]

    def greet():
        pl.semaphore_wait(barrier, len(peers))
        for dp in range(1, 8):
            node_copy(dp).start()
        listed[pts] = mine[...]
        for to_h in range(2):

            @pl.when(slab_here(to_h))
            def _():
                slab_local(to_h).start()

            @pl.when(jnp.logical_not(slab_here(to_h)))
            def _():
                slab_copy(to_h).start()

        @pl.when(jnp.logical_and(halo_some(), h == 0))
        def _():
            halo_local(0).start()

        @pl.when(jnp.logical_and(halo_some(), h == 1))
        def _():
            halo_copy(0).start()

        @pl.when(halo_some())
        def _():
            halo_copy(1).start()

        @pl.when(u == 0)
        def _():
            conc0[:, :, 0:8, :] = jnp.zeros((2, 20, 8, 128), F32)

    spot_b = (lax.broadcasted_iota(jnp.int32, (64, G), 0) + 64 * pz).astype(F32)
    spot_c = lax.broadcasted_iota(jnp.int32, (64, G), 1).astype(F32)
    wave[...] = 64.0 + spot_b * spot_b + spot_c * spot_c
    front = 64.0 * 0.9 * (32.0**1.5)

    def stage(step, _):
        amps = []
        for part in range(2):
            for half in range(2):
                a = (64 * i + 2 * step + part + 32 * half).astype(F32)
                amps.append(front / (wave[...] + a * a))
        for f in range(4):
            parts = []
            for part in range(2):
                for half in range(2):
                    row = 2 * step + part + 32 * half
                    value = xi[row] if f == 0 else basis[f - 1, row].astype(F32)
                    parts.append(value * amps[2 * part + half])
            high, low = halves(jnp.concatenate(parts, axis=0))
            both = jnp.dot(high, tz[...], preferred_element_type=F32)
            both += jnp.dot(low, tz[...], preferred_element_type=F32)
            both = both.T
            total = both[0:40] + both[40:80]
            for part in range(2):
                share[pl.ds(32 * f + 2 * step + part, 40, stride=128), :] = total[
                    :, 128 * part : 128 * part + 128
                ]
        return 0

    def stages(q, _):
        for copy in loads(q):
            copy.wait()
        lax.fori_loop(4 * q, 4 * q + 4, stage, 0)
        for d in (2, 3, 1):
            early(q, d).start()
        early_own(q).start()
        return 0

    blocks = share.reshape(40, 4, 32, 128)

    def early_parts(q, to_h, to_c):
        rows = pl.ds(pl.multiple_of(8 * q, 8), 8)
        src = blocks.at[pl.ds(20 * to_c + 8 * to_h, EARLY), :, rows]
        return src, got1.at[pl.ds(0, EARLY), pz, :, rows]

    def early(q, d):
        to_h, to_c = (h + d // 2) % 2, (c + d % 2) % 2
        src, dst = early_parts(q, to_h, to_c)
        return pltpu.make_async_remote_copy(
            src_ref=src,
            dst_ref=dst,
            send_sem=s0.at[q, d],
            recv_sem=r0.at[q, d],
            device_id=at(i, to_h, to_c),
            device_id_type=MESH,
        )

    def early_own(q):
        return pltpu.make_async_copy(*early_parts(q, h, c), own0.at[q])

    greet()
    load_tz.wait()
    lax.fori_loop(0, 4, stages, 0)

    def first(k, d):
        to_h, to_c = (h + d // 2) % 2, (c + d % 2) % 2
        return pltpu.make_async_remote_copy(
            src_ref=blocks.at[20 * to_c + 8 * to_h + k],
            dst_ref=got1.at[k, pz],
            send_sem=s1.at[k, d],
            recv_sem=r1.at[k, d],
            device_id=at(i, to_h, to_c),
            device_id_type=MESH,
        )

    def first_own(k):
        return pltpu.make_async_copy(blocks.at[20 * c + 8 * h + k], got1.at[k, pz], own1.at[k])

    def send_first(k, _):
        for d in (2, 3, 1):
            first(k, d).start()
        first_own(k).start()
        return 0

    lax.fori_loop(EARLY, NROUND, send_first, 0)

    def second(k, d):
        to_i, to_c = (i + d // 2) % 4, (c + d % 2) % 2
        return pltpu.make_async_remote_copy(
            src_ref=rows2.at[k, 2 * to_i + to_c],
            dst_ref=got2.at[k, c, i],
            send_sem=s2.at[k, d],
            recv_sem=r2.at[k, d],
            device_id=at(to_i, h, to_c),
            device_id_type=MESH,
        )

    def second_own(k):
        return pltpu.make_async_copy(rows2.at[k, u], got2.at[k, c, i], own2.at[k])

    lane = lax.broadcasted_iota(jnp.int32, (128, 128), 1)
    lane_low = lane < 64
    lane8 = lax.broadcasted_iota(jnp.int32, (8, 128), 1)
    lane_some = lane8 > 0
    lane40 = lax.broadcasted_iota(jnp.int32, (40, 128), 1) < 64

    def b_contraction(k):
        @pl.when(k == 0)
        def _():
            for q in range(4):
                for d in range(1, 4):
                    early(q, d).wait_recv()
                early_own(q).wait()

        @pl.when(k >= EARLY)
        def _():
            for d in range(1, 4):
                first(k, d).wait_recv()
            first_own(k).wait()

        sides = [[], []]
        for pair in range(2):
            one, two = (got1[k, 2 * pair + m].reshape(128, 128) for m in range(2))
            sides[0].append(jnp.where(lane_low, one, pltpu.roll(two, 64, 1)))
            sides[1].append(jnp.where(lane_low, pltpu.roll(one, 64, 1), two))
        both = [jnp.concatenate(side, axis=1) for side in sides]
        rows = []
        for f in range(4):
            rows += [both[0][32 * f : 32 * f + 32], both[1][32 * f : 32 * f + 32]]
        high, low = halves(jnp.concatenate(rows, axis=0))
        both = lax.dot_general(cy[...], high, NT, preferred_element_type=F32)
        rest = lax.dot_general(cy[0:320], low, NT, preferred_element_type=F32)
        total = both[0:320] + both[320:640] + rest
        for slab in range(8):
            rows2[k, slab] = total[40 * slab : 40 * slab + 40]
        for d in (4, 5, 2, 6, 3, 7, 1):
            second(k, d).start()
        second_own(k).start()

    def a_contraction(k):
        for d in range(1, 8):
            second(k, d).wait_recv()
        second_own(k).wait()
        rows = []
        for core in range(2):
            for pair in range(2):
                cols = [[], []]
                for group in range(2):
                    one = got2[k, core, 2 * group, :, 128 * pair : 128 * pair + 128]
                    two = got2[k, core, 2 * group + 1, :, 128 * pair : 128 * pair + 128]
                    cols[0].append(jnp.where(lane40, one, pltpu.roll(two, 64, 1)))
                    cols[1].append(jnp.where(lane40, pltpu.roll(one, 64, 1), two))
                rows += [jnp.concatenate(col, axis=1) for col in cols]
        high, low = halves(jnp.concatenate(rows, axis=0))
        total = jnp.dot(high, cx[0:256], preferred_element_type=F32)
        total += jnp.dot(low, cx[0:256], preferred_element_type=F32)
        total += jnp.dot(high, cx[256:512], preferred_element_type=F32)
        for core in range(2):
            for f in range(4):
                row = 160 * core + 40 * f
                fields[core, f] = total[row : row + 40]

    tiles = [(t, v) for t in range(5) for v in range(2)]

    def transport(k, core, halo):
        zz = 2 * k + core
        spot_z = 16 * (2 * g + h) - 4 + zz
        well = jnp.where(spot_z >= 0, prof[jnp.maximum(spot_z, 0)], 0.0)
        for t, v in tiles:
            plane[0, t, v] = conc0[v, zz, pl.ds(t, 8, stride=5), :]
            plane[1, t, v] = mask[v, 8 * t : 8 * t + 8, :] * well
            if not halo:
                plane[2, t, v] = jnp.zeros((8, 128), F32)
        steps = zz + 1 if halo else STEPS

        def some_points(group, _):
            each = range(BATCH)
            speed, conc = [{} for _ in each], [{} for _ in each]
            for m in each:
                n = BATCH * group + m
                node = [nodes[n, r] for r in range(3)]
                for t, v in tiles:
                    logs = [
                        fields[core, f, 8 * t : 8 * t + 8, 128 * v : 128 * v + 128] for f in range(4)
                    ]
                    value = logs[0] + node[0] * logs[1] + node[1] * logs[2] + node[2] * logs[3]
                    speed[m][t, v] = 0.125 + 0.125 * jnp.tanh(value)
                    conc[m][t, v] = plane[0, t, v]
            for step in range(steps):
                last = halo and step == steps - 1
                flux = [{tv: speed[m][tv] * conc[m][tv] for tv in tiles} for m in each]
                for t, v in tiles:
                    for m in each:
                        n = BATCH * group + m
                        here = flux[m][t, v]
                        if last:
                            carry[n, step, t, v] = here
                            continue
                        behind = carry[n, step, t, v]
                        carry[n, step, t, v] = here
                        prev_b = flux[m][t - 1, v] if t > 0 else pltpu.roll(flux[m][4, v], 1, 0)
                        prev_a = (
                            flux[m][t, 0]
                            if v == 1
                            else jnp.where(lane_some, pltpu.roll(flux[m][t, 1], 1, 1), 0.0)
                        )
                        conc[m][t, v] = (
                            (conc[m][t, v] - 3.6 * here)
                            + (plane[1, t, v] + behind)
                            + (prev_b + 1.6 * prev_a)
                        )
            if not halo:
                for t, v in tiles:
                    part = nodes[BATCH * group, 3] * conc[0][t, v]
                    for m in range(1, BATCH):
                        part += nodes[BATCH * group + m, 3] * conc[m][t, v]
                    plane[2, t, v] += part
            return 0

        lax.fori_loop(0, POINTS // BATCH, some_points, 0)
        if not halo:
            for t, v in tiles:
                sums[v, pl.ds(16 * t + zz - 4, 8, stride=80), :] = plane[2, t, v]

    carry[...] = jnp.zeros(carry.shape, F32)
    lag = 3

    def wait_conc():
        for core in range(2):
            slab = pltpu.make_async_copy(
                cz.at[:, pl.ds(0, 20)], conc0.at[:, :, pl.ds(8 + 16 * core, 16)], rc.at[core]
            )
            slab.wait()

        @pl.when(u > 0)
        def _():
            pltpu.make_async_copy(
                cz.at[:, pl.ds(0, 20), pl.ds(8, 8)], conc0.at[:, :, pl.ds(0, 8)], rc.at[2]
            ).wait()

    def rounds(step, _):
        @pl.when(step < NROUND)
        def _():
            b_contraction(step)

        @pl.when(step >= lag)
        def _():
            a_contraction(step - lag)

        for early in range(2):

            @pl.when(step == lag + early)
            def _():
                for core in range(2):
                    transport(early, core, True)

        @pl.when(step >= lag + 2)
        def _():
            for core in range(2):
                transport(step - lag, core, False)

        return 0

    turn_mask()
    wait_conc()
    for dp in range(1, 8):
        node_copy(dp).wait_recv()
    for n in range(POINTS):
        for r in range(4):
            row = 4 * (n % 2) + r
            nodes[n, r] = jnp.broadcast_to(listed[n // 2, row : row + 1, :], (8, 128))
    lax.fori_loop(0, NROUND + lag, rounds, 0)

    granule = lax.broadcasted_iota(jnp.int32, (16, 128), 1) // 16

    def regroup(which, _):
        half, yg = which // 4, which % 4
        arrays = []
        for yy in range(4):
            for v in range(2):
                row = pl.multiple_of(16 * (8 + 16 * half + 4 * yg + yy), 16)
                arrays.append(sums[v, pl.ds(row, 16), :])
        for bit in (4, 2, 1):
            clear = (granule // bit) % 2 == 0
            for m in range(8):
                if m // bit % 2 == 0:
                    one, two = arrays[m], arrays[m + bit]
                    arrays[m] = jnp.where(clear, one, pltpu.roll(two, 16 * bit, 1))
                    arrays[m + bit] = jnp.where(clear, pltpu.roll(one, 128 - 16 * bit, 1), two)
        for p in range(8):
            parcel[p, half, yg] = arrays[p]
        return 0

    zr = pl.multiple_of(16 * (4 * yy + 2 * xt + h), 16)

    def home(dp, half):
        to = (pts + dp) % 8
        return pltpu.make_async_remote_copy(
            src_ref=parcel.at[to, half],
            dst_ref=landed.at[:, pl.ds(zr, 16)],
            send_sem=so.at[dp, half],
            recv_sem=ro.at[dp, h],
            device_id={"pts": to, "py": i, "pz": 2 * c + half},
            device_id_type=MESH,
        )

    def home_own(half):
        return pltpu.make_async_copy(parcel.at[pts, half], landed.at[:, pl.ds(zr, 16)], ro.at[0, h])

    for half in range(2):
        lax.fori_loop(4 * half, 4 * half + 4, regroup, 0)
        here = jnp.logical_and(c == h, c == half)

        @pl.when(here)
        def _():
            home_own(half).start()

        @pl.when(jnp.logical_not(here))
        def _():
            home(0, half).start()

        for dp in range(1, 8):
            home(dp, half).start()

    for dp in range(8):
        for from_h in range(2):
            pltpu.make_async_copy(
                parcel.at[0, 0], landed.at[:, pl.ds(0, 16)], ro.at[dp, from_h]
            ).wait()

    for yg in range(4):
        for zh in range(2):
            turned = landed[yg, 128 * zh : 128 * zh + 128, :].T
            for y in range(4):
                for v in range(2):
                    e = 16 * (2 * y + v)
                    final[zh, pl.ds(16 * v + 4 * yg + y, 16, stride=32), :] = turned[e : e + 16]
    for zh in range(2):
        out[:, 128 * zh : 128 * zh + 128] = final[zh]

    def drain(k, _):
        @pl.when(k >= EARLY)
        def _():
            for d in range(1, 4):
                first(k, d).wait_send()

        @pl.when(k < 4)
        def _():
            for d in range(1, 4):
                early(k, d).wait_send()

        for d in range(1, 8):
            second(k, d).wait_send()
        return 0

    lax.fori_loop(0, NROUND, drain, 0)
    for dp in range(1, 8):
        node_copy(dp).wait_send()
        for half in range(2):
            home(dp, half).wait_send()
    for half in range(2):

        @pl.when(jnp.logical_not(jnp.logical_and(c == h, c == half)))
        def _():
            home(0, half).wait_send()

    for to_h in range(2):

        @pl.when(jnp.logical_not(slab_here(to_h)))
        def _():
            slab_copy(to_h).wait_send()

    @pl.when(jnp.logical_and(halo_some(), h == 1))
    def _():
        halo_copy(0).wait_send()

    @pl.when(halo_some())
    def _():
        halo_copy(1).wait_send()


def local(xi_map, basis, point_index, conc_start, well_mask, profile):
    (tz_hi, tz_lo), (cy_hi, cy_lo), (cx_hi, cx_lo) = tables()
    tz = np.concatenate([tz_hi, tz_lo, np.zeros((8, G, 48), ml_dtypes.bfloat16)], axis=2)
    cy = np.concatenate([cy_hi, cy_lo], axis=0)
    cx = np.concatenate([cx_hi, cx_lo], axis=0)

    vmem = pl.BlockSpec(memory_space=pltpu.VMEM)
    smem = pl.BlockSpec(memory_space=pltpu.SMEM)
    dma = pltpu.SemaphoreType.DMA
    far = pl.BlockSpec(memory_space=pl.ANY)
    total = pl.pallas_call(
        kernel,
        out_shape=jax.ShapeDtypeStruct((512, 256), F32),
        in_specs=[smem, smem] + [far] * 5 + [vmem] * 2,
        out_specs=vmem,
        scratch_shapes=[
            pltpu.VMEM((64, 64, 256), F32),
            pltpu.VMEM((3, 64, 64, 256), BF16),
            pltpu.VMEM((40 * 128, 128), F32),
            pltpu.VMEM((NROUND, 4, 4, 32, 128), F32),
            pltpu.VMEM((NROUND, 8, 40, 256), F32),
            pltpu.VMEM((NROUND, 2, 4, 40, 256), F32),
            pltpu.VMEM((2, 20, 40, 128), F32),
            pltpu.VMEM((2, 4, 40, 256), F32),
            pltpu.VMEM((POINTS, STEPS, 5, 2, 8, 128), F32),
            pltpu.VMEM((3, 5, 2, 8, 128), F32),
            pltpu.VMEM((64, 256), F32),
            pltpu.VMEM((8, 128), F32),
            pltpu.VMEM((8, 8, 128), F32),
            pltpu.VMEM((POINTS, 4, 8, 128), F32),
            pltpu.VMEM((2, 640, 128), F32),
            pltpu.VMEM((8, 2, 4, 16, 128), F32),
            pltpu.VMEM((4, 256, 128), F32),
            pltpu.VMEM((2, 512, 128), F32),
            pltpu.VMEM((256, 128), BF16),
            pltpu.VMEM((2, 4096, 128), F32),
            pltpu.VMEM((8, 272, 128), F32),
            pltpu.VMEM((2, 640, 128), F32),
            pltpu.VMEM((2, 256, 128), jnp.int32),
            pltpu.VMEM((2, 264, 128), F32),
            pltpu.VMEM((2, 40, 128), F32),
            dma((4, 4)),
            dma((4, 4)),
            dma((4,)),
            dma((NROUND, 4)),
            dma((NROUND, 4)),
            dma((NROUND,)),
            dma((NROUND, 8)),
            dma((NROUND, 8)),
            dma((NROUND,)),
            dma((4,)),
            dma((3,)),
            dma((4, 4)),
            dma((5,)),
            dma((8,)),
            dma((8,)),
            dma((8, 2)),
            dma((8, 2)),
        ],
        compiler_params=pltpu.CompilerParams(
            collective_id=0, has_side_effects=True, vmem_limit_bytes=60 * 2**20
        ),
    )(point_index, profile, xi_map, basis, conc_start.reshape(4096, 256), well_mask, tz, cy, cx)
    return total.reshape(32, 16, 256)


def solution(mesh):
    placed = (
        P("py", "pz", None),
        P(None, "py", "pz", None),
        P("pts", None),
        P(None, ("py", "pz"), None),
        P(),
        P(),
    )
    return jax.shard_map(
        local, mesh=mesh, in_specs=placed, out_specs=P("pts", ("py", "pz"), None), check_vma=False
    )
```

```python
import functools

import jax
import jax.numpy as jnp
import ml_dtypes
import numpy as np
from jax import lax
from jax.experimental import pallas as pl
from jax.experimental.pallas import tpu as pltpu
from jax.sharding import PartitionSpec as P

MESH = pl.DeviceIdType.MESH
STEPS = 4
POINTS = 16
BATCH = 4
G = 256
NROUND = 10
EARLY = 4
ROOT3 = 1.7320508075688772
F32 = jnp.float32
BF16 = jnp.bfloat16
NT = (((1,), (1,)), ((), ()))


def split_table(table):
    table = np.asarray(table, np.float64)
    high = table.astype(np.float32).astype(ml_dtypes.bfloat16)
    low = (table - high.astype(np.float64)).astype(np.float32).astype(ml_dtypes.bfloat16)
    return high, low


def tables():
    spots = np.arange(G, dtype=np.float64)
    full = np.sqrt(2.0 / G) * np.cos(np.pi * (spots[:, None] + 0.5) * spots[None, :] / G)
    full[:, 0] *= np.sqrt(0.5)
    tz = np.zeros((8, 40, G))
    for g in range(8):
        for par in range(2):
            for w in range(18):
                z = 32 * g - 4 + 2 * w + par
                if z >= 0:
                    tz[g, 20 * par + w] = full[z]
    tz = tz.transpose(0, 2, 1)
    cy = np.zeros((8, 5, 8, G))
    for u in range(8):
        for t in range(5):
            for q in range(8):
                y = 32 * u - 8 + 5 * q + t
                if y >= 0:
                    cy[u, t, q] = full[y]
    cx = 0.5 * np.concatenate([full[0::2], full[1::2]], axis=0).T
    return split_table(tz), split_table(cy.reshape(320, G)), split_table(cx)


def halves(value):
    high = value.astype(BF16)
    low = (value - high.astype(F32)).astype(BF16)
    return high, low


def kernel(
    point,
    prof,
    xi_far,
    basis_far,
    conc_far,
    mask_far,
    tz_far,
    cy,
    cx,
    out,
    xi,
    basis,
    share,
    got1,
    rows2,
    got2,
    conc0,
    fields,
    across,
    along,
    carry,
    plane,
    wave,
    mine,
    listed,
    nodes,
    sums,
    parcel,
    landed,
    final,
    tz,
    start,
    turned_z,
    cz_flat,
    wells,
    turned_y,
    mask,
    s0,
    r0,
    own0,
    s1,
    r1,
    own1,
    s2,
    r2,
    own2,
    sc,
    rc,
    load,
    prep,
    sn,
    rn,
    so,
    ro,
):
    pts = lax.axis_index("pts")
    i = lax.axis_index("py")
    pz = lax.axis_index("pz")
    yy, x_lo = pts // 2, pts % 2
    h, c = pz // 2, pz % 2
    xt = (x_lo + h) % 2
    u = 2 * i + c
    g = 2 * yy + xt
    cz = cz_flat.reshape(2, 40, 16, 128)

    def at(i_, h_, c_):
        return {"pts": 2 * yy + (xt + h_) % 2, "py": i_, "pz": 2 * h_ + c_}

    barrier = pltpu.get_barrier_semaphore()
    peers = []
    for dp in range(8):
        for dh in range(2):
            for dc in range(2):
                if dp + dh + dc > 0:
                    peers.append({"pts": (pts + dp) % 8, "py": i, "pz": 2 * ((h + dh) % 2) + (c + dc) % 2})
    for di in range(1, 4):
        for dh in range(2):
            for dc in range(2):
                peers.append(at((i + di) % 4, (h + dh) % 2, (c + dc) % 2))
    for peer in peers:
        pl.semaphore_signal(barrier, inc=1, device_id=peer, device_id_type=MESH)

    def loads(q):
        copies = []
        for half in range(2):
            rows = pl.ds(pl.multiple_of(8 * q + 32 * half, 8), 8)
            copies.append(pltpu.make_async_copy(xi_far.at[rows], xi.at[rows], load.at[q, 2 * half]))
            copies.append(
                pltpu.make_async_copy(basis_far.at[:, rows], basis.at[:, rows], load.at[q, 2 * half + 1])
            )
        return copies

    def start_loads(q, _):
        for copy in loads(q):
            copy.start()
        return 0

    def load_conc(zh):
        return pltpu.make_async_copy(
            conc_far.at[:, pl.ds(128 * zh, 128)], start.at[zh], prep.at[zh]
        )

    def load_mask(yh):
        return pltpu.make_async_copy(
            mask_far.at[:, pl.ds(128 * yh, 128)], wells.at[yh], prep.at[2 + yh]
        )

    load_tz = pltpu.make_async_copy(tz_far.at[g], tz, prep.at[4])
    some_z = [g <= 4, g >= 4]
    for zh in range(2):

        @pl.when(some_z[zh])
        def _():
            load_conc(zh).start()

    load_tz.start()
    lax.fori_loop(0, 4, start_loads, 0)
    for yh in range(2):
        load_mask(yh).start()

    def slab_copy(to_h):
        return pltpu.make_async_remote_copy(
            src_ref=cz.at[:, pl.ds(16 * to_h, 20)],
            dst_ref=conc0.at[:, :, pl.ds(pl.multiple_of(8 + 16 * c, 8), 16)],
            send_sem=sc.at[to_h],
            recv_sem=rc.at[c],
            device_id=at(i, to_h, h),
            device_id_type=MESH,
        )

    def slab_local(to_h):
        return pltpu.make_async_copy(
            cz.at[:, pl.ds(16 * to_h, 20)],
            conc0.at[:, :, pl.ds(pl.multiple_of(8 + 16 * c, 8), 16)],
            rc.at[c],
        )

    above = 2 * i + h + 1

    def halo_copy(to_h):
        return pltpu.make_async_remote_copy(
            src_ref=cz.at[:, pl.ds(16 * to_h, 20), pl.ds(8, 8)],
            dst_ref=conc0.at[:, :, pl.ds(0, 8)],
            send_sem=sc.at[2 + to_h],
            recv_sem=rc.at[2],
            device_id=at((above // 2) % 4, to_h, above % 2),
            device_id_type=MESH,
        )

    def halo_local(to_h):
        return pltpu.make_async_copy(
            cz.at[:, pl.ds(16 * to_h, 20), pl.ds(8, 8)], conc0.at[:, :, pl.ds(0, 8)], rc.at[2]
        )

    def slab_here(to_h):
        return jnp.logical_and(h == to_h, c == to_h)

    def halo_some():
        return jnp.logical_and(c == 1, above < 8)

    for m in range(2):
        weight = 1.0
        for r in range(3):
            index = point[m, r]
            value = jnp.where(index == 0, -ROOT3, jnp.where(index == 1, 0.0, ROOT3))
            weight = weight * jnp.where(index == 1, 2.0 / 3.0, 1.0 / 6.0)
            mine[4 * m + r : 4 * m + r + 1, :] = jnp.full((1, 128), value, F32)
        mine[4 * m + 3 : 4 * m + 4, :] = jnp.full((1, 128), weight, F32)

    def node_copy(dp):
        return pltpu.make_async_remote_copy(
            src_ref=mine,
            dst_ref=listed.at[pts],
            send_sem=sn.at[dp],
            recv_sem=rn.at[dp],
            device_id={"pts": (pts + dp) % 8, "py": i, "pz": pz},
            device_id_type=MESH,
        )

    turned_z[:, 0:8, :] = jnp.zeros((8, 8, 128), F32)
    for zh in range(2):

        @pl.when(some_z[zh])
        def _():
            load_conc(zh).wait()

    def turn_conc(y4, _):
        rows = [(m, v) for m in range(4) for v in range(2)]
        for zh in range(2):

            @pl.when(some_z[zh])
            def _():
                for m, v in rows:
                    turned_z[2 * m + v, 4 + 128 * zh : 132 + 128 * zh, :] = start[
                        zh, pl.ds(16 * v + 4 * y4 + m, 128, stride=32), :
                    ].T

        for m, v in rows:
            cz_flat[v, pl.ds(4 * y4 + m, 40, stride=16), :] = turned_z[
                2 * m + v, pl.ds(pl.multiple_of(32 * g, 32), 40), :
            ]
        return 0

    lax.fori_loop(0, 4, turn_conc, 0)

    def turn_mask():
        turned_y[:, 0:8, :] = jnp.zeros((2, 8, 128), F32)
        for yh in range(2):
            load_mask(yh).wait()
            for v in range(2):
                block = wells[yh, pl.ds(v, 128, stride=2), :].astype(F32)
                turned_y[v, 8 + 128 * yh : 136 + 128 * yh, :] = 0.5 * block.T
        for v in range(2):
            for t in range(5):
                mask[v, 8 * t : 8 * t + 8, :] = turned_y[v, pl.ds(32 * u + t, 8, stride=5), :]

    def greet():
        pl.semaphore_wait(barrier, len(peers))
        for dp in range(1, 8):
            node_copy(dp).start()
        listed[pts] = mine[...]
        for to_h in range(2):

            @pl.when(slab_here(to_h))
            def _():
                slab_local(to_h).start()

            @pl.when(jnp.logical_not(slab_here(to_h)))
            def _():
                slab_copy(to_h).start()

        @pl.when(jnp.logical_and(halo_some(), h == 0))
        def _():
            halo_local(0).start()

        @pl.when(jnp.logical_and(halo_some(), h == 1))
        def _():
            halo_copy(0).start()

        @pl.when(halo_some())
        def _():
            halo_copy(1).start()

        @pl.when(u == 0)
        def _():
            conc0[:, :, 0:8, :] = jnp.zeros((2, 20, 8, 128), F32)

    spot_b = (lax.broadcasted_iota(jnp.int32, (64, G), 0) + 64 * pz).astype(F32)
    spot_c = lax.broadcasted_iota(jnp.int32, (64, G), 1).astype(F32)
    wave[...] = 64.0 + spot_b * spot_b + spot_c * spot_c
    front = 64.0 * 0.9 * (32.0**1.5)

    def stage(step, _):
        amps = []
        for part in range(2):
            for half in range(2):
                a = (64 * i + 2 * step + part + 32 * half).astype(F32)
                amps.append(front / (wave[...] + a * a))
        for f in range(4):
            parts = []
            for part in range(2):
                for half in range(2):
                    row = 2 * step + part + 32 * half
                    value = xi[row] if f == 0 else basis[f - 1, row].astype(F32)
                    parts.append(value * amps[2 * part + half])
            high, low = halves(jnp.concatenate(parts, axis=0))
            both = jnp.dot(high, tz[...], preferred_element_type=F32)
            both += jnp.dot(low, tz[...], preferred_element_type=F32)
            both = both.T
            total = both[0:40] + both[40:80]
            for part in range(2):
                share[pl.ds(32 * f + 2 * step + part, 40, stride=128), :] = total[
                    :, 128 * part : 128 * part + 128
                ]
        return 0

    def stages(q, _):
        for copy in loads(q):
            copy.wait()
        lax.fori_loop(4 * q, 4 * q + 4, stage, 0)
        for d in (2, 3, 1):
            early(q, d).start()
        early_own(q).start()
        return 0

    blocks = share.reshape(40, 4, 32, 128)

    def early_parts(q, to_h, to_c):
        rows = pl.ds(pl.multiple_of(8 * q, 8), 8)
        src = blocks.at[pl.ds(20 * to_c + 8 * to_h, EARLY), :, rows]
        return src, got1.at[pl.ds(0, EARLY), pz, :, rows]

    def early(q, d):
        to_h, to_c = (h + d // 2) % 2, (c + d % 2) % 2
        src, dst = early_parts(q, to_h, to_c)
        return pltpu.make_async_remote_copy(
            src_ref=src,
            dst_ref=dst,
            send_sem=s0.at[q, d],
            recv_sem=r0.at[q, d],
            device_id=at(i, to_h, to_c),
            device_id_type=MESH,
        )

    def early_own(q):
        return pltpu.make_async_copy(*early_parts(q, h, c), own0.at[q])

    greet()
    load_tz.wait()
    lax.fori_loop(0, 4, stages, 0)

    def first(k, d):
        to_h, to_c = (h + d // 2) % 2, (c + d % 2) % 2
        return pltpu.make_async_remote_copy(
            src_ref=blocks.at[20 * to_c + 8 * to_h + k],
            dst_ref=got1.at[k, pz],
            send_sem=s1.at[k, d],
            recv_sem=r1.at[k, d],
            device_id=at(i, to_h, to_c),
            device_id_type=MESH,
        )

    def first_own(k):
        return pltpu.make_async_copy(blocks.at[20 * c + 8 * h + k], got1.at[k, pz], own1.at[k])

    def send_first(k, _):
        for d in (2, 3, 1):
            first(k, d).start()
        first_own(k).start()
        return 0

    lax.fori_loop(EARLY, NROUND, send_first, 0)

    def second(k, d):
        to_i, to_c = (i + d // 2) % 4, (c + d % 2) % 2
        return pltpu.make_async_remote_copy(
            src_ref=rows2.at[k, 2 * to_i + to_c],
            dst_ref=got2.at[k, c, i],
            send_sem=s2.at[k, d],
            recv_sem=r2.at[k, d],
            device_id=at(to_i, h, to_c),
            device_id_type=MESH,
        )

    def second_own(k):
        return pltpu.make_async_copy(rows2.at[k, u], got2.at[k, c, i], own2.at[k])

    lane = lax.broadcasted_iota(jnp.int32, (128, 128), 1)
    lane_low = lane < 64
    lane8 = lax.broadcasted_iota(jnp.int32, (8, 128), 1)
    lane_some = lane8 > 0
    lane40 = lax.broadcasted_iota(jnp.int32, (40, 128), 1) < 64

    def b_ready(k):
        @pl.when(k == 0)
        def _():
            for q in range(4):
                for d in range(1, 4):
                    early(q, d).wait_recv()
                early_own(q).wait()

        @pl.when(k >= EARLY)
        def _():
            for d in range(1, 4):
                first(k, d).wait_recv()
            first_own(k).wait()

        sides = [[], []]
        for pair in range(2):
            one, two = (got1[k, 2 * pair + m].reshape(128, 128) for m in range(2))
            sides[0].append(jnp.where(lane_low, one, pltpu.roll(two, 64, 1)))
            sides[1].append(jnp.where(lane_low, pltpu.roll(one, 64, 1), two))
        both = [jnp.concatenate(side, axis=1) for side in sides]
        rows = []
        for f in range(4):
            rows += [both[0][32 * f : 32 * f + 32], both[1][32 * f : 32 * f + 32]]
        high, low = halves(jnp.concatenate(rows, axis=0))
        across[0], across[1] = high, low

    def b_piece(k, m):
        top = cy[pl.ds(pl.multiple_of(80 * m, 16), 80), :]
        rest = cy[pl.ds(pl.multiple_of(320 + 80 * m, 16), 80), :]
        both = lax.dot_general(
            jnp.concatenate([top, rest], axis=0), across[0], NT, preferred_element_type=F32
        )
        total = both[0:80] + both[80:160]
        total += lax.dot_general(top, across[1], NT, preferred_element_type=F32)
        for slab in range(2):
            rows2[k, 2 * m + slab] = total[40 * slab : 40 * slab + 40]

    def send_second(k):
        for d in (4, 5, 2, 6, 3, 7, 1):
            second(k, d).start()
        second_own(k).start()

    def a_ready(k):
        for d in range(1, 8):
            second(k, d).wait_recv()
        second_own(k).wait()
        rows = []
        for core in range(2):
            for pair in range(2):
                cols = [[], []]
                for group in range(2):
                    one = got2[k, core, 2 * group, :, 128 * pair : 128 * pair + 128]
                    two = got2[k, core, 2 * group + 1, :, 128 * pair : 128 * pair + 128]
                    cols[0].append(jnp.where(lane40, one, pltpu.roll(two, 64, 1)))
                    cols[1].append(jnp.where(lane40, pltpu.roll(one, 64, 1), two))
                rows += [jnp.concatenate(col, axis=1) for col in cols]
        high, low = halves(jnp.concatenate(rows, axis=0))
        along[0], along[1] = high, low

    def a_piece(k, m):
        rows = pl.ds(pl.multiple_of(80 * m, 16), 80)
        top, rest = along[0, rows, :], along[1, rows, :]
        both = jnp.dot(jnp.concatenate([top, rest], axis=0), cx[0:256], preferred_element_type=F32)
        total = both[0:80] + both[80:160]
        total += jnp.dot(top, cx[256:512], preferred_element_type=F32)
        fields[k % 2, pl.ds(pl.multiple_of(80 * m, 16), 80), :] = total

    tiles = [(t, v) for t in range(5) for v in range(2)]

    def transport(k, core, halo, beside):
        zz = 2 * k + core
        spot_z = 16 * (2 * g + h) - 4 + zz
        well = jnp.where(spot_z >= 0, prof[jnp.maximum(spot_z, 0)], 0.0)
        for t, v in tiles:
            plane[0, t, v] = conc0[v, zz, pl.ds(t, 8, stride=5), :]
            plane[1, t, v] = mask[v, 8 * t : 8 * t + 8, :] * well
            if not halo:
                plane[2, t, v] = jnp.zeros((8, 128), F32)
        steps = zz + 1 if halo else STEPS

        def some_points(group, _):
            beside(group)
            each = range(BATCH)
            speed, conc = [{} for _ in each], [{} for _ in each]
            for m in each:
                n = BATCH * group + m
                node = [nodes[n, r] for r in range(3)]
                for t, v in tiles:
                    logs = [
                        fields[k % 2, 160 * core + 40 * f + 8 * t : 160 * core + 40 * f + 8 * t + 8, 128 * v : 128 * v + 128]
                        for f in range(4)
                    ]
                    value = logs[0] + node[0] * logs[1] + node[1] * logs[2] + node[2] * logs[3]
                    speed[m][t, v] = 0.125 + 0.125 * jnp.tanh(value)
                    conc[m][t, v] = plane[0, t, v]
            for step in range(steps):
                last = halo and step == steps - 1
                flux = [{tv: speed[m][tv] * conc[m][tv] for tv in tiles} for m in each]
                for t, v in tiles:
                    for m in each:
                        n = BATCH * group + m
                        here = flux[m][t, v]
                        if last:
                            carry[n, step, t, v] = here
                            continue
                        behind = carry[n, step, t, v]
                        carry[n, step, t, v] = here
                        prev_b = flux[m][t - 1, v] if t > 0 else pltpu.roll(flux[m][4, v], 1, 0)
                        prev_a = (
                            flux[m][t, 0]
                            if v == 1
                            else jnp.where(lane_some, pltpu.roll(flux[m][t, 1], 1, 1), 0.0)
                        )
                        conc[m][t, v] = (
                            (conc[m][t, v] - 3.6 * here)
                            + (plane[1, t, v] + behind)
                            + (prev_b + 1.6 * prev_a)
                        )
            if not halo:
                for t, v in tiles:
                    part = nodes[BATCH * group, 3] * conc[0][t, v]
                    for m in range(1, BATCH):
                        part += nodes[BATCH * group + m, 3] * conc[m][t, v]
                    plane[2, t, v] += part
            return 0

        lax.fori_loop(0, POINTS // BATCH, some_points, 0)
        if not halo:
            for t, v in tiles:
                sums[v, pl.ds(16 * t + zz - 4, 8, stride=80), :] = plane[2, t, v]

    carry[...] = jnp.zeros(carry.shape, F32)
    lag = 3

    def wait_conc():
        for core in range(2):
            slab = pltpu.make_async_copy(
                cz.at[:, pl.ds(0, 20)], conc0.at[:, :, pl.ds(8 + 16 * core, 16)], rc.at[core]
            )
            slab.wait()

        @pl.when(u > 0)
        def _():
            pltpu.make_async_copy(
                cz.at[:, pl.ds(0, 20), pl.ds(8, 8)], conc0.at[:, :, pl.ds(0, 8)], rc.at[2]
            ).wait()

    def rounds(step, _):
        @pl.when(step < NROUND)
        def _():
            b_ready(step)

        @pl.when(jnp.logical_and(step >= 2, step < NROUND + 2))
        def _():
            a_ready(step - 2)

        def piece_b(m):
            b_piece(step, m)

        def piece_a(m):
            a_piece(step - 2, m)

        def alone(piece):
            def one(m, _):
                piece(m)
                return 0

            lax.fori_loop(0, 4, one, 0)

        @pl.when(step < lag)
        def _():
            alone(piece_b)

        for early_round in range(2):

            @pl.when(step == lag + early_round)
            def _():
                transport(early_round, 0, True, piece_b)

        @pl.when(step >= lag + 2)
        def _():
            transport(step - lag, 0, False, piece_b)

        @pl.when(step < NROUND)
        def _():
            send_second(step)

        @pl.when(step == 2)
        def _():
            alone(piece_a)

        for early_round in range(2):

            @pl.when(step == lag + early_round)
            def _():
                transport(early_round, 1, True, piece_a)

        @pl.when(step >= lag + 2)
        def _():
            transport(step - lag, 1, False, piece_a)

        return 0

    turn_mask()
    wait_conc()
    for dp in range(1, 8):
        node_copy(dp).wait_recv()
    for n in range(POINTS):
        for r in range(4):
            row = 4 * (n % 2) + r
            nodes[n, r] = jnp.broadcast_to(listed[n // 2, row : row + 1, :], (8, 128))
    lax.fori_loop(0, NROUND + lag, rounds, 0)

    granule = lax.broadcasted_iota(jnp.int32, (16, 128), 1) // 16

    def regroup(which, _):
        half, yg = which // 4, which % 4
        arrays = []
        for yy in range(4):
            for v in range(2):
                row = pl.multiple_of(16 * (8 + 16 * half + 4 * yg + yy), 16)
                arrays.append(sums[v, pl.ds(row, 16), :])
        for bit in (4, 2, 1):
            clear = (granule // bit) % 2 == 0
            for m in range(8):
                if m // bit % 2 == 0:
                    one, two = arrays[m], arrays[m + bit]
                    arrays[m] = jnp.where(clear, one, pltpu.roll(two, 16 * bit, 1))
                    arrays[m + bit] = jnp.where(clear, pltpu.roll(one, 128 - 16 * bit, 1), two)
        for p in range(8):
            parcel[p, half, yg] = arrays[p]
        return 0

    zr = pl.multiple_of(16 * (4 * yy + 2 * xt + h), 16)

    def home(dp, half):
        to = (pts + dp) % 8
        return pltpu.make_async_remote_copy(
            src_ref=parcel.at[to, half],
            dst_ref=landed.at[:, pl.ds(zr, 16)],
            send_sem=so.at[dp, half],
            recv_sem=ro.at[dp, h],
            device_id={"pts": to, "py": i, "pz": 2 * c + half},
            device_id_type=MESH,
        )

    def home_own(half):
        return pltpu.make_async_copy(parcel.at[pts, half], landed.at[:, pl.ds(zr, 16)], ro.at[0, h])

    for half in range(2):
        lax.fori_loop(4 * half, 4 * half + 4, regroup, 0)
        here = jnp.logical_and(c == h, c == half)

        @pl.when(here)
        def _():
            home_own(half).start()

        @pl.when(jnp.logical_not(here))
        def _():
            home(0, half).start()

        for dp in range(1, 8):
            home(dp, half).start()

    for dp in range(8):
        for from_h in range(2):
            pltpu.make_async_copy(
                parcel.at[0, 0], landed.at[:, pl.ds(0, 16)], ro.at[dp, from_h]
            ).wait()

    for yg in range(4):
        for zh in range(2):
            turned = landed[yg, 128 * zh : 128 * zh + 128, :].T
            for y in range(4):
                for v in range(2):
                    e = 16 * (2 * y + v)
                    final[zh, pl.ds(16 * v + 4 * yg + y, 16, stride=32), :] = turned[e : e + 16]
    for zh in range(2):
        out[:, 128 * zh : 128 * zh + 128] = final[zh]

    def drain(k, _):
        @pl.when(k >= EARLY)
        def _():
            for d in range(1, 4):
                first(k, d).wait_send()

        @pl.when(k < 4)
        def _():
            for d in range(1, 4):
                early(k, d).wait_send()

        for d in range(1, 8):
            second(k, d).wait_send()
        return 0

    lax.fori_loop(0, NROUND, drain, 0)
    for dp in range(1, 8):
        node_copy(dp).wait_send()
        for half in range(2):
            home(dp, half).wait_send()
    for half in range(2):

        @pl.when(jnp.logical_not(jnp.logical_and(c == h, c == half)))
        def _():
            home(0, half).wait_send()

    for to_h in range(2):

        @pl.when(jnp.logical_not(slab_here(to_h)))
        def _():
            slab_copy(to_h).wait_send()

    @pl.when(jnp.logical_and(halo_some(), h == 1))
    def _():
        halo_copy(0).wait_send()

    @pl.when(halo_some())
    def _():
        halo_copy(1).wait_send()


def local(xi_map, basis, point_index, conc_start, well_mask, profile):
    (tz_hi, tz_lo), (cy_hi, cy_lo), (cx_hi, cx_lo) = tables()
    tz = np.concatenate([tz_hi, tz_lo, np.zeros((8, G, 48), ml_dtypes.bfloat16)], axis=2)
    cy = np.concatenate([cy_hi, cy_lo], axis=0)
    cx = np.concatenate([cx_hi, cx_lo], axis=0)

    vmem = pl.BlockSpec(memory_space=pltpu.VMEM)
    smem = pl.BlockSpec(memory_space=pltpu.SMEM)
    dma = pltpu.SemaphoreType.DMA
    far = pl.BlockSpec(memory_space=pl.ANY)
    total = pl.pallas_call(
        kernel,
        out_shape=jax.ShapeDtypeStruct((512, 256), F32),
        in_specs=[smem, smem] + [far] * 5 + [vmem] * 2,
        out_specs=vmem,
        scratch_shapes=[
            pltpu.VMEM((64, 64, 256), F32),
            pltpu.VMEM((3, 64, 64, 256), BF16),
            pltpu.VMEM((40 * 128, 128), F32),
            pltpu.VMEM((NROUND, 4, 4, 32, 128), F32),
            pltpu.VMEM((NROUND + 3, 8, 40, 256), F32),
            pltpu.VMEM((NROUND, 2, 4, 40, 256), F32),
            pltpu.VMEM((2, 20, 40, 128), F32),
            pltpu.VMEM((2, 320, 256), F32),
            pltpu.VMEM((2, 256, 256), BF16),
            pltpu.VMEM((2, 320, 256), BF16),
            pltpu.VMEM((POINTS, STEPS, 5, 2, 8, 128), F32),
            pltpu.VMEM((3, 5, 2, 8, 128), F32),
            pltpu.VMEM((64, 256), F32),
            pltpu.VMEM((8, 128), F32),
            pltpu.VMEM((8, 8, 128), F32),
            pltpu.VMEM((POINTS, 4, 8, 128), F32),
            pltpu.VMEM((2, 640, 128), F32),
            pltpu.VMEM((8, 2, 4, 16, 128), F32),
            pltpu.VMEM((4, 256, 128), F32),
            pltpu.VMEM((2, 512, 128), F32),
            pltpu.VMEM((256, 128), BF16),
            pltpu.VMEM((2, 4096, 128), F32),
            pltpu.VMEM((8, 272, 128), F32),
            pltpu.VMEM((2, 640, 128), F32),
            pltpu.VMEM((2, 256, 128), jnp.int32),
            pltpu.VMEM((2, 264, 128), F32),
            pltpu.VMEM((2, 40, 128), F32),
            dma((4, 4)),
            dma((4, 4)),
            dma((4,)),
            dma((NROUND, 4)),
            dma((NROUND, 4)),
            dma((NROUND,)),
            dma((NROUND, 8)),
            dma((NROUND, 8)),
            dma((NROUND,)),
            dma((4,)),
            dma((3,)),
            dma((4, 4)),
            dma((5,)),
            dma((8,)),
            dma((8,)),
            dma((8, 2)),
            dma((8, 2)),
        ],
        compiler_params=pltpu.CompilerParams(
            collective_id=0, has_side_effects=True, vmem_limit_bytes=60 * 2**20
        ),
    )(point_index, profile, xi_map, basis, conc_start.reshape(4096, 256), well_mask, tz, cy, cx)
    return total.reshape(32, 16, 256)


def solution(mesh):
    placed = (
        P("py", "pz", None),
        P(None, "py", "pz", None),
        P("pts", None),
        P(None, ("py", "pz"), None),
        P(),
        P(),
    )
    return jax.shard_map(
        local, mesh=mesh, in_specs=placed, out_specs=P("pts", ("py", "pz"), None), check_vma=False
    )
```

```python
import functools

import jax
import jax.numpy as jnp
import ml_dtypes
import numpy as np
from jax import lax
from jax.experimental import pallas as pl
from jax.experimental.pallas import tpu as pltpu
from jax.sharding import PartitionSpec as P

MESH = pl.DeviceIdType.MESH
STEPS = 4
POINTS = 16
BATCH = 4
G = 256
NROUND = 10
EARLY = 2
ROOT3 = 1.7320508075688772
F32 = jnp.float32
BF16 = jnp.bfloat16
NT = (((1,), (1,)), ((), ()))


def split_table(table):
    table = np.asarray(table, np.float64)
    high = table.astype(np.float32).astype(ml_dtypes.bfloat16)
    low = (table - high.astype(np.float64)).astype(np.float32).astype(ml_dtypes.bfloat16)
    return high, low


def tables():
    spots = np.arange(G, dtype=np.float64)
    full = np.sqrt(2.0 / G) * np.cos(np.pi * (spots[:, None] + 0.5) * spots[None, :] / G)
    full[:, 0] *= np.sqrt(0.5)
    tz = np.zeros((8, 40, G))
    for g in range(8):
        for par in range(2):
            for w in range(18):
                z = 32 * g - 4 + 2 * w + par
                if z >= 0:
                    tz[g, 20 * par + w] = full[z]
    tz = tz.transpose(0, 2, 1)
    cy = np.zeros((8, 5, 8, G))
    for u in range(8):
        for t in range(5):
            for q in range(8):
                y = 32 * u - 8 + 5 * q + t
                if y >= 0:
                    cy[u, t, q] = full[y]
    cx = 0.5 * np.concatenate([full[0::2], full[1::2]], axis=0).T
    return split_table(tz), split_table(cy.reshape(320, G)), split_table(cx)


def halves(value):
    high = value.astype(BF16)
    low = (value - high.astype(F32)).astype(BF16)
    return high, low


def kernel(
    point,
    prof,
    xi_far,
    basis_far,
    conc_far,
    mask_far,
    tz_far,
    cy,
    cx,
    out,
    xi,
    basis,
    share,
    got1,
    rows2,
    got2,
    passing,
    conc0,
    fields,
    carry,
    plane,
    wave,
    mine,
    listed,
    nodes,
    sums,
    parcel,
    landed,
    final,
    tz,
    start,
    turned_z,
    cz_flat,
    wells,
    turned_y,
    mask,
    s0,
    r0,
    own0,
    s1,
    r1,
    own1,
    s2,
    r2,
    own2,
    s3,
    r3,
    sc,
    rc,
    load,
    prep,
    sn,
    rn,
    so,
    ro,
):
    pts = lax.axis_index("pts")
    i = lax.axis_index("py")
    pz = lax.axis_index("pz")
    yy, x_lo = pts // 2, pts % 2
    h, c = pz // 2, pz % 2
    xt = (x_lo + h) % 2
    u = 2 * i + c
    g = 2 * yy + xt
    cz = cz_flat.reshape(2, 40, 16, 128)

    def at(i_, h_, c_):
        return {"pts": 2 * yy + (xt + h_) % 2, "py": i_, "pz": 2 * h_ + c_}

    barrier = pltpu.get_barrier_semaphore()
    peers = []
    for dp in range(8):
        for dh in range(2):
            for dc in range(2):
                if dp + dh + dc > 0:
                    peers.append({"pts": (pts + dp) % 8, "py": i, "pz": 2 * ((h + dh) % 2) + (c + dc) % 2})
    for di in range(1, 4):
        for dh in range(2):
            for dc in range(2):
                peers.append(at((i + di) % 4, (h + dh) % 2, (c + dc) % 2))
    for peer in peers:
        pl.semaphore_signal(barrier, inc=1, device_id=peer, device_id_type=MESH)

    def loads(q):
        copies = []
        for half in range(2):
            rows = pl.ds(pl.multiple_of(8 * q + 32 * half, 8), 8)
            copies.append(pltpu.make_async_copy(xi_far.at[rows], xi.at[rows], load.at[q, 2 * half]))
            copies.append(
                pltpu.make_async_copy(basis_far.at[:, rows], basis.at[:, rows], load.at[q, 2 * half + 1])
            )
        return copies

    def start_loads(q, _):
        for copy in loads(q):
            copy.start()
        return 0

    def load_conc(zh):
        return pltpu.make_async_copy(
            conc_far.at[:, pl.ds(128 * zh, 128)], start.at[zh], prep.at[zh]
        )

    def load_mask(yh):
        return pltpu.make_async_copy(
            mask_far.at[:, pl.ds(128 * yh, 128)], wells.at[yh], prep.at[2 + yh]
        )

    load_tz = pltpu.make_async_copy(tz_far.at[g], tz, prep.at[4])
    some_z = [g <= 4, g >= 4]
    for zh in range(2):

        @pl.when(some_z[zh])
        def _():
            load_conc(zh).start()

    load_tz.start()
    lax.fori_loop(0, 4, start_loads, 0)
    for yh in range(2):
        load_mask(yh).start()

    def slab_copy(to_h):
        return pltpu.make_async_remote_copy(
            src_ref=cz.at[:, pl.ds(16 * to_h, 20)],
            dst_ref=conc0.at[:, :, pl.ds(pl.multiple_of(8 + 16 * c, 8), 16)],
            send_sem=sc.at[to_h],
            recv_sem=rc.at[c],
            device_id=at(i, to_h, h),
            device_id_type=MESH,
        )

    def slab_local(to_h):
        return pltpu.make_async_copy(
            cz.at[:, pl.ds(16 * to_h, 20)],
            conc0.at[:, :, pl.ds(pl.multiple_of(8 + 16 * c, 8), 16)],
            rc.at[c],
        )

    above = 2 * i + h + 1

    def halo_copy(to_h):
        return pltpu.make_async_remote_copy(
            src_ref=cz.at[:, pl.ds(16 * to_h, 20), pl.ds(8, 8)],
            dst_ref=conc0.at[:, :, pl.ds(0, 8)],
            send_sem=sc.at[2 + to_h],
            recv_sem=rc.at[2],
            device_id=at((above // 2) % 4, to_h, above % 2),
            device_id_type=MESH,
        )

    def halo_local(to_h):
        return pltpu.make_async_copy(
            cz.at[:, pl.ds(16 * to_h, 20), pl.ds(8, 8)], conc0.at[:, :, pl.ds(0, 8)], rc.at[2]
        )

    def slab_here(to_h):
        return jnp.logical_and(h == to_h, c == to_h)

    def halo_some():
        return jnp.logical_and(c == 1, above < 8)

    for m in range(2):
        weight = 1.0
        for r in range(3):
            index = point[m, r]
            value = jnp.where(index == 0, -ROOT3, jnp.where(index == 1, 0.0, ROOT3))
            weight = weight * jnp.where(index == 1, 2.0 / 3.0, 1.0 / 6.0)
            mine[4 * m + r : 4 * m + r + 1, :] = jnp.full((1, 128), value, F32)
        mine[4 * m + 3 : 4 * m + 4, :] = jnp.full((1, 128), weight, F32)

    def node_copy(dp):
        return pltpu.make_async_remote_copy(
            src_ref=mine,
            dst_ref=listed.at[pts],
            send_sem=sn.at[dp],
            recv_sem=rn.at[dp],
            device_id={"pts": (pts + dp) % 8, "py": i, "pz": pz},
            device_id_type=MESH,
        )

    turned_z[:, 0:8, :] = jnp.zeros((8, 8, 128), F32)
    for zh in range(2):

        @pl.when(some_z[zh])
        def _():
            load_conc(zh).wait()

    def turn_conc(y4, _):
        rows = [(m, v) for m in range(4) for v in range(2)]
        for zh in range(2):

            @pl.when(some_z[zh])
            def _():
                for m, v in rows:
                    turned_z[2 * m + v, 4 + 128 * zh : 132 + 128 * zh, :] = start[
                        zh, pl.ds(16 * v + 4 * y4 + m, 128, stride=32), :
                    ].T

        for m, v in rows:
            cz_flat[v, pl.ds(4 * y4 + m, 40, stride=16), :] = turned_z[
                2 * m + v, pl.ds(pl.multiple_of(32 * g, 32), 40), :
            ]
        return 0

    lax.fori_loop(0, 4, turn_conc, 0)

    def turn_mask():
        turned_y[:, 0:8, :] = jnp.zeros((2, 8, 128), F32)
        for yh in range(2):
            load_mask(yh).wait()
            for v in range(2):
                block = wells[yh, pl.ds(v, 128, stride=2), :].astype(F32)
                turned_y[v, 8 + 128 * yh : 136 + 128 * yh, :] = 0.5 * block.T
        for v in range(2):
            for t in range(5):
                mask[v, 8 * t : 8 * t + 8, :] = turned_y[v, pl.ds(32 * u + t, 8, stride=5), :]

    def greet():
        pl.semaphore_wait(barrier, len(peers))
        for dp in range(1, 8):
            node_copy(dp).start()
        listed[pts] = mine[...]
        for to_h in range(2):

            @pl.when(slab_here(to_h))
            def _():
                slab_local(to_h).start()

            @pl.when(jnp.logical_not(slab_here(to_h)))
            def _():
                slab_copy(to_h).start()

        @pl.when(jnp.logical_and(halo_some(), h == 0))
        def _():
            halo_local(0).start()

        @pl.when(jnp.logical_and(halo_some(), h == 1))
        def _():
            halo_copy(0).start()

        @pl.when(halo_some())
        def _():
            halo_copy(1).start()

        @pl.when(u == 0)
        def _():
            conc0[:, :, 0:8, :] = jnp.zeros((2, 20, 8, 128), F32)

    spot_b = (lax.broadcasted_iota(jnp.int32, (64, G), 0) + 64 * pz).astype(F32)
    spot_c = lax.broadcasted_iota(jnp.int32, (64, G), 1).astype(F32)
    wave[...] = 64.0 + spot_b * spot_b + spot_c * spot_c
    front = 64.0 * 0.9 * (32.0**1.5)

    def stage(step, _):
        amps = []
        for part in range(2):
            for half in range(2):
                a = (64 * i + 2 * step + part + 32 * half).astype(F32)
                amps.append(front / (wave[...] + a * a))
        for f in range(4):
            parts = []
            for part in range(2):
                for half in range(2):
                    row = 2 * step + part + 32 * half
                    value = xi[row] if f == 0 else basis[f - 1, row].astype(F32)
                    parts.append(value * amps[2 * part + half])
            high, low = halves(jnp.concatenate(parts, axis=0))
            both = jnp.dot(jnp.concatenate([high, low], axis=0), tz[...], preferred_element_type=F32)
            both = (both[0:256] + both[256:512]).T
            total = both[0:40] + both[40:80]
            for part in range(2):
                share[pl.ds(32 * f + 2 * step + part, 40, stride=128), :] = total[
                    :, 128 * part : 128 * part + 128
                ]
        return 0

    def stages(q, _):
        for copy in loads(q):
            copy.wait()
        lax.fori_loop(4 * q, 4 * q + 4, stage, 0)
        for d in (2, 3, 1):
            early(q, d).start()
        early_own(q).start()
        return 0

    blocks = share.reshape(40, 4, 32, 128)

    def early_parts(q, to_h, to_c):
        rows = pl.ds(pl.multiple_of(8 * q, 8), 8)
        src = blocks.at[pl.ds(20 * to_c + 8 * to_h, EARLY), :, rows]
        return src, got1.at[pl.ds(0, EARLY), pz, :, rows]

    def early(q, d):
        to_h, to_c = (h + d // 2) % 2, (c + d % 2) % 2
        src, dst = early_parts(q, to_h, to_c)
        return pltpu.make_async_remote_copy(
            src_ref=src,
            dst_ref=dst,
            send_sem=s0.at[q, d],
            recv_sem=r0.at[q, d],
            device_id=at(i, to_h, to_c),
            device_id_type=MESH,
        )

    def early_own(q):
        return pltpu.make_async_copy(*early_parts(q, h, c), own0.at[q])

    greet()
    load_tz.wait()
    lax.fori_loop(0, 4, stages, 0)

    def first(k, d):
        to_h, to_c = (h + d // 2) % 2, (c + d % 2) % 2
        return pltpu.make_async_remote_copy(
            src_ref=blocks.at[20 * to_c + 8 * to_h + k],
            dst_ref=got1.at[k, pz],
            send_sem=s1.at[k, d],
            recv_sem=r1.at[k, d],
            device_id=at(i, to_h, to_c),
            device_id_type=MESH,
        )

    def first_own(k):
        return pltpu.make_async_copy(blocks.at[20 * c + 8 * h + k], got1.at[k, pz], own1.at[k])

    def send_first(k, _):
        for d in (2, 3, 1):
            first(k, d).start()
        first_own(k).start()
        return 0

    lax.fori_loop(EARLY, NROUND, send_first, 0)

    def second(k, d):
        to_i, to_c = (i + d // 2) % 4, (c + d % 2) % 2
        return pltpu.make_async_remote_copy(
            src_ref=rows2.at[k, 2 * to_i + to_c],
            dst_ref=got2.at[k, c, i],
            send_sem=s2.at[k, d],
            recv_sem=r2.at[k, d],
            device_id=at(to_i, h, to_c),
            device_id_type=MESH,
        )

    def hop(k, way):
        return pltpu.make_async_remote_copy(
            src_ref=rows2.at[k, 2 * ((i + 2) % 4) + way],
            dst_ref=passing.at[k, way],
            send_sem=s3.at[k, way],
            recv_sem=r3.at[k, way],
            device_id=at((i + 1 + 2 * way) % 4, h, c),
            device_id_type=MESH,
        )

    def forward(k, way):
        return pltpu.make_async_remote_copy(
            src_ref=passing.at[k, way],
            dst_ref=got2.at[k, c, (i + 3 + 2 * way) % 4],
            send_sem=s2.at[k, 4 + (c + way) % 2],
            recv_sem=r2.at[k, 4 + (c + way) % 2],
            device_id=at((i + 1 + 2 * way) % 4, h, way),
            device_id_type=MESH,
        )

    def send_on(k):
        for way in range(2):
            hop(k, way).wait_recv()
            forward(k, way).start()

    def second_own(k):
        return pltpu.make_async_copy(rows2.at[k, u], got2.at[k, c, i], own2.at[k])

    lane = lax.broadcasted_iota(jnp.int32, (128, 128), 1)
    lane_low = lane < 64
    lane8 = lax.broadcasted_iota(jnp.int32, (8, 128), 1)
    lane_some = lane8 > 0
    lane40 = lax.broadcasted_iota(jnp.int32, (40, 128), 1) < 64

    def b_contraction(k):
        @pl.when(k == 0)
        def _():
            for q in range(4):
                for d in range(1, 4):
                    early(q, d).wait_recv()
                early_own(q).wait()

        @pl.when(k >= EARLY)
        def _():
            for d in range(1, 4):
                first(k, d).wait_recv()
            first_own(k).wait()

        sides = [[], []]
        for pair in range(2):
            one, two = (got1[k, 2 * pair + m].reshape(128, 128) for m in range(2))
            sides[0].append(jnp.where(lane_low, one, pltpu.roll(two, 64, 1)))
            sides[1].append(jnp.where(lane_low, pltpu.roll(one, 64, 1), two))
        both = [jnp.concatenate(side, axis=1) for side in sides]
        rows = []
        for f in range(4):
            rows += [both[0][32 * f : 32 * f + 32], both[1][32 * f : 32 * f + 32]]
        high, low = halves(jnp.concatenate(rows, axis=0))
        both = lax.dot_general(cy[...], high, NT, preferred_element_type=F32)
        rest = lax.dot_general(cy[0:320], low, NT, preferred_element_type=F32)
        total = both[0:320] + both[320:640] + rest
        for slab in range(8):
            rows2[k, slab] = total[40 * slab : 40 * slab + 40]
        for way in range(2):
            hop(k, way).start()
        for d in (2, 6, 3, 7, 1):
            second(k, d).start()
        second_own(k).start()

    def a_contraction(k):
        for d in range(1, 8):
            second(k, d).wait_recv()
        second_own(k).wait()
        rows = []
        for core in range(2):
            for pair in range(2):
                cols = [[], []]
                for group in range(2):
                    one = got2[k, core, 2 * group, :, 128 * pair : 128 * pair + 128]
                    two = got2[k, core, 2 * group + 1, :, 128 * pair : 128 * pair + 128]
                    cols[0].append(jnp.where(lane40, one, pltpu.roll(two, 64, 1)))
                    cols[1].append(jnp.where(lane40, pltpu.roll(one, 64, 1), two))
                rows += [jnp.concatenate(col, axis=1) for col in cols]
        high, low = halves(jnp.concatenate(rows, axis=0))
        both = jnp.dot(jnp.concatenate([high, low], axis=0), cx[0:256], preferred_element_type=F32)
        total = both[0:320] + both[320:640]
        total += jnp.dot(high, cx[256:512], preferred_element_type=F32)
        for core in range(2):
            for f in range(4):
                row = 160 * core + 40 * f
                fields[core, f] = total[row : row + 40]

    tiles = [(t, v) for t in range(5) for v in range(2)]

    def transport(k, core, halo):
        zz = 2 * k + core
        spot_z = 16 * (2 * g + h) - 4 + zz
        well = jnp.where(spot_z >= 0, prof[jnp.maximum(spot_z, 0)], 0.0)
        for t, v in tiles:
            plane[0, t, v] = conc0[v, zz, pl.ds(t, 8, stride=5), :]
            plane[1, t, v] = mask[v, 8 * t : 8 * t + 8, :] * well
            if not halo:
                plane[2, t, v] = jnp.zeros((8, 128), F32)
        steps = zz + 1 if halo else STEPS

        def some_points(group, _):
            each = range(BATCH)
            speed, conc = [{} for _ in each], [{} for _ in each]
            for m in each:
                n = BATCH * group + m
                node = [nodes[n, r] for r in range(3)]
                for t, v in tiles:
                    logs = [
                        fields[core, f, 8 * t : 8 * t + 8, 128 * v : 128 * v + 128] for f in range(4)
                    ]
                    value = logs[0] + node[0] * logs[1] + node[1] * logs[2] + node[2] * logs[3]
                    speed[m][t, v] = 0.125 + 0.125 * jnp.tanh(value)
                    conc[m][t, v] = plane[0, t, v]
            for step in range(steps):
                last = halo and step == steps - 1
                flux = [{tv: speed[m][tv] * conc[m][tv] for tv in tiles} for m in each]
                for t, v in tiles:
                    for m in each:
                        n = BATCH * group + m
                        here = flux[m][t, v]
                        if last:
                            carry[n, step, t, v] = here
                            continue
                        behind = carry[n, step, t, v]
                        carry[n, step, t, v] = here
                        prev_b = flux[m][t - 1, v] if t > 0 else pltpu.roll(flux[m][4, v], 1, 0)
                        prev_a = (
                            flux[m][t, 0]
                            if v == 1
                            else jnp.where(lane_some, pltpu.roll(flux[m][t, 1], 1, 1), 0.0)
                        )
                        conc[m][t, v] = (
                            (conc[m][t, v] - 3.6 * here)
                            + (plane[1, t, v] + behind)
                            + (prev_b + 1.6 * prev_a)
                        )
            if not halo:
                for t, v in tiles:
                    part = nodes[BATCH * group, 3] * conc[0][t, v]
                    for m in range(1, BATCH):
                        part += nodes[BATCH * group + m, 3] * conc[m][t, v]
                    plane[2, t, v] += part
            return 0

        lax.fori_loop(0, POINTS // BATCH, some_points, 0)
        if not halo:
            for t, v in tiles:
                sums[v, pl.ds(16 * t + zz - 4, 8, stride=80), :] = plane[2, t, v]

    carry[...] = jnp.zeros(carry.shape, F32)
    lag = 3

    def wait_conc():
        for core in range(2):
            slab = pltpu.make_async_copy(
                cz.at[:, pl.ds(0, 20)], conc0.at[:, :, pl.ds(8 + 16 * core, 16)], rc.at[core]
            )
            slab.wait()

        @pl.when(u > 0)
        def _():
            pltpu.make_async_copy(
                cz.at[:, pl.ds(0, 20), pl.ds(8, 8)], conc0.at[:, :, pl.ds(0, 8)], rc.at[2]
            ).wait()

    def rounds(step, _):
        @pl.when(jnp.logical_and(step >= 1, step < NROUND + 1))
        def _():
            send_on(step - 1)

        @pl.when(step < NROUND)
        def _():
            b_contraction(step)

        @pl.when(step >= lag)
        def _():
            a_contraction(step - lag)

        for early in range(2):

            @pl.when(step == lag + early)
            def _():
                for core in range(2):
                    transport(early, core, True)

        @pl.when(step >= lag + 2)
        def _():
            for core in range(2):
                transport(step - lag, core, False)

        return 0

    turn_mask()
    wait_conc()
    for dp in range(1, 8):
        node_copy(dp).wait_recv()
    for n in range(POINTS):
        for r in range(4):
            row = 4 * (n % 2) + r
            nodes[n, r] = jnp.broadcast_to(listed[n // 2, row : row + 1, :], (8, 128))
    lax.fori_loop(0, NROUND + lag, rounds, 0)

    granule = lax.broadcasted_iota(jnp.int32, (16, 128), 1) // 16

    def regroup(which, _):
        half, yg = which // 4, which % 4
        arrays = []
        for yy in range(4):
            for v in range(2):
                row = pl.multiple_of(16 * (8 + 16 * half + 4 * yg + yy), 16)
                arrays.append(sums[v, pl.ds(row, 16), :])
        for bit in (4, 2, 1):
            clear = (granule // bit) % 2 == 0
            for m in range(8):
                if m // bit % 2 == 0:
                    one, two = arrays[m], arrays[m + bit]
                    arrays[m] = jnp.where(clear, one, pltpu.roll(two, 16 * bit, 1))
                    arrays[m + bit] = jnp.where(clear, pltpu.roll(one, 128 - 16 * bit, 1), two)
        for p in range(8):
            parcel[p, half, yg] = arrays[p]
        return 0

    zr = pl.multiple_of(16 * (4 * yy + 2 * xt + h), 16)

    def home(dp, half):
        to = (pts + dp) % 8
        return pltpu.make_async_remote_copy(
            src_ref=parcel.at[to, half],
            dst_ref=landed.at[:, pl.ds(zr, 16)],
            send_sem=so.at[dp, half],
            recv_sem=ro.at[dp, h],
            device_id={"pts": to, "py": i, "pz": 2 * c + half},
            device_id_type=MESH,
        )

    def home_own(half):
        return pltpu.make_async_copy(parcel.at[pts, half], landed.at[:, pl.ds(zr, 16)], ro.at[0, h])

    for half in range(2):
        lax.fori_loop(4 * half, 4 * half + 4, regroup, 0)
        here = jnp.logical_and(c == h, c == half)

        @pl.when(here)
        def _():
            home_own(half).start()

        @pl.when(jnp.logical_not(here))
        def _():
            home(0, half).start()

        for dp in range(1, 8):
            home(dp, half).start()

    for dp in range(8):
        for from_h in range(2):
            pltpu.make_async_copy(
                parcel.at[0, 0], landed.at[:, pl.ds(0, 16)], ro.at[dp, from_h]
            ).wait()

    for yg in range(4):
        for zh in range(2):
            turned = landed[yg, 128 * zh : 128 * zh + 128, :].T
            for y in range(4):
                for v in range(2):
                    e = 16 * (2 * y + v)
                    final[zh, pl.ds(16 * v + 4 * yg + y, 16, stride=32), :] = turned[e : e + 16]
    for zh in range(2):
        out[:, 128 * zh : 128 * zh + 128] = final[zh]

    def drain(k, _):
        @pl.when(k >= EARLY)
        def _():
            for d in range(1, 4):
                first(k, d).wait_send()

        @pl.when(k < 4)
        def _():
            for d in range(1, 4):
                early(k, d).wait_send()

        for d in (1, 2, 3, 6, 7):
            second(k, d).wait_send()
        for way in range(2):
            hop(k, way).wait_send()
            forward(k, way).wait_send()
        return 0

    lax.fori_loop(0, NROUND, drain, 0)
    for dp in range(1, 8):
        node_copy(dp).wait_send()
        for half in range(2):
            home(dp, half).wait_send()
    for half in range(2):

        @pl.when(jnp.logical_not(jnp.logical_and(c == h, c == half)))
        def _():
            home(0, half).wait_send()

    for to_h in range(2):

        @pl.when(jnp.logical_not(slab_here(to_h)))
        def _():
            slab_copy(to_h).wait_send()

    @pl.when(jnp.logical_and(halo_some(), h == 1))
    def _():
        halo_copy(0).wait_send()

    @pl.when(halo_some())
    def _():
        halo_copy(1).wait_send()


def local(xi_map, basis, point_index, conc_start, well_mask, profile):
    (tz_hi, tz_lo), (cy_hi, cy_lo), (cx_hi, cx_lo) = tables()
    tz = np.concatenate([tz_hi, tz_lo, np.zeros((8, G, 48), ml_dtypes.bfloat16)], axis=2)
    cy = np.concatenate([cy_hi, cy_lo], axis=0)
    cx = np.concatenate([cx_hi, cx_lo], axis=0)

    vmem = pl.BlockSpec(memory_space=pltpu.VMEM)
    smem = pl.BlockSpec(memory_space=pltpu.SMEM)
    dma = pltpu.SemaphoreType.DMA
    far = pl.BlockSpec(memory_space=pl.ANY)
    total = pl.pallas_call(
        kernel,
        out_shape=jax.ShapeDtypeStruct((512, 256), F32),
        in_specs=[smem, smem] + [far] * 5 + [vmem] * 2,
        out_specs=vmem,
        scratch_shapes=[
            pltpu.VMEM((64, 64, 256), F32),
            pltpu.VMEM((3, 64, 64, 256), BF16),
            pltpu.VMEM((40 * 128, 128), F32),
            pltpu.VMEM((NROUND, 4, 4, 32, 128), F32),
            pltpu.VMEM((NROUND, 8, 40, 256), F32),
            pltpu.VMEM((NROUND, 2, 4, 40, 256), F32),
            pltpu.VMEM((NROUND, 2, 40, 256), F32),
            pltpu.VMEM((2, 20, 40, 128), F32),
            pltpu.VMEM((2, 4, 40, 256), F32),
            pltpu.VMEM((POINTS, STEPS, 5, 2, 8, 128), F32),
            pltpu.VMEM((3, 5, 2, 8, 128), F32),
            pltpu.VMEM((64, 256), F32),
            pltpu.VMEM((8, 128), F32),
            pltpu.VMEM((8, 8, 128), F32),
            pltpu.VMEM((POINTS, 4, 8, 128), F32),
            pltpu.VMEM((2, 640, 128), F32),
            pltpu.VMEM((8, 2, 4, 16, 128), F32),
            pltpu.VMEM((4, 256, 128), F32),
            pltpu.VMEM((2, 512, 128), F32),
            pltpu.VMEM((256, 128), BF16),
            pltpu.VMEM((2, 4096, 128), F32),
            pltpu.VMEM((8, 272, 128), F32),
            pltpu.VMEM((2, 640, 128), F32),
            pltpu.VMEM((2, 256, 128), jnp.int32),
            pltpu.VMEM((2, 264, 128), F32),
            pltpu.VMEM((2, 40, 128), F32),
            dma((4, 4)),
            dma((4, 4)),
            dma((4,)),
            dma((NROUND, 4)),
            dma((NROUND, 4)),
            dma((NROUND,)),
            dma((NROUND, 8)),
            dma((NROUND, 8)),
            dma((NROUND,)),
            dma((NROUND, 2)),
            dma((NROUND, 2)),
            dma((4,)),
            dma((3,)),
            dma((4, 4)),
            dma((5,)),
            dma((8,)),
            dma((8,)),
            dma((8, 2)),
            dma((8, 2)),
        ],
        compiler_params=pltpu.CompilerParams(
            collective_id=0, has_side_effects=True, vmem_limit_bytes=60 * 2**20
        ),
    )(point_index, profile, xi_map, basis, conc_start.reshape(4096, 256), well_mask, tz, cy, cx)
    return total.reshape(32, 16, 256)


def solution(mesh):
    placed = (
        P("py", "pz", None),
        P(None, "py", "pz", None),
        P("pts", None),
        P(None, ("py", "pz"), None),
        P(),
        P(),
    )
    return jax.shard_map(
        local, mesh=mesh, in_specs=placed, out_specs=P("pts", ("py", "pz"), None), check_vma=False
    )
```

```python
import functools

import jax
import jax.numpy as jnp
import ml_dtypes
import numpy as np
from jax import lax
from jax.experimental import pallas as pl
from jax.experimental.pallas import tpu as pltpu
from jax.sharding import PartitionSpec as P

MESH = pl.DeviceIdType.MESH
STEPS = 4
POINTS = 16
BATCH = 4
G = 256
NROUND = 10
PAIRS = 5
ROOT3 = 1.7320508075688772
F32 = jnp.float32
BF16 = jnp.bfloat16
NT = (((1,), (1,)), ((), ()))


def split_table(table):
    table = np.asarray(table, np.float64)
    high = table.astype(np.float32).astype(ml_dtypes.bfloat16)
    low = (table - high.astype(np.float64)).astype(np.float32).astype(ml_dtypes.bfloat16)
    return high, low


def tables():
    spots = np.arange(G, dtype=np.float64)
    full = np.sqrt(2.0 / G) * np.cos(np.pi * (spots[:, None] + 0.5) * spots[None, :] / G)
    full[:, 0] *= np.sqrt(0.5)
    tz = np.zeros((8, 40, G))
    for g in range(8):
        for par in range(2):
            for w in range(18):
                z = 32 * g - 4 + 2 * w + par
                if z >= 0:
                    tz[g, 20 * par + w] = full[z]
    tz = tz.transpose(0, 2, 1)
    cy = np.zeros((8, 5, 8, G))
    for u in range(8):
        for t in range(5):
            for q in range(8):
                y = 32 * u - 8 + 5 * q + t
                if y >= 0:
                    cy[u, t, q] = full[y]
    cx = 0.5 * np.concatenate([full[0::2], full[1::2]], axis=0).T
    return split_table(tz), split_table(cy.reshape(320, G)), split_table(cx)


def halves(value):
    high = value.astype(BF16)
    low = (value - high.astype(F32)).astype(BF16)
    return high, low


def kernel(
    point,
    prof,
    xi_far,
    basis_far,
    conc_far,
    mask_far,
    tz_far,
    cy,
    cx,
    out,
    xi,
    basis,
    share,
    got1,
    rows2,
    got2,
    conc0,
    fields,
    carry,
    plane,
    wave,
    mine,
    listed,
    nodes,
    sums,
    parcel,
    landed,
    final,
    tz,
    start,
    turned_z,
    cz_flat,
    wells,
    turned_y,
    mask,
    s0,
    r0,
    s1,
    r1,
    s2,
    r2,
    sc,
    rc,
    load,
    prep,
    sn,
    rn,
    so,
    ro,
):
    pts = lax.axis_index("pts")
    i = lax.axis_index("py")
    pz = lax.axis_index("pz")
    yy, x_lo = pts // 2, pts % 2
    h, c = pz // 2, pz % 2
    xt = (x_lo + h) % 2
    u = 2 * i + c
    g = 2 * yy + xt
    cz = cz_flat.reshape(2, 40, 16, 128)

    def at(i_, h_, c_):
        return {"pts": 2 * yy + (xt + h_) % 2, "py": i_, "pz": 2 * h_ + c_}

    barrier = pltpu.get_barrier_semaphore()
    peers = []
    for dp in range(8):
        for dh in range(2):
            for dc in range(2):
                if dp + dh + dc > 0:
                    peers.append({"pts": (pts + dp) % 8, "py": i, "pz": 2 * ((h + dh) % 2) + (c + dc) % 2})
    for di in range(1, 4):
        for dh in range(2):
            for dc in range(2):
                peers.append(at((i + di) % 4, (h + dh) % 2, (c + dc) % 2))
    for peer in peers:
        pl.semaphore_signal(barrier, inc=1, device_id=peer, device_id_type=MESH)

    def loads(q):
        copies = []
        for half in range(2):
            rows = pl.ds(pl.multiple_of(8 * q + 32 * half, 8), 8)
            copies.append(pltpu.make_async_copy(xi_far.at[rows], xi.at[rows], load.at[q, 2 * half]))
            copies.append(
                pltpu.make_async_copy(basis_far.at[:, rows], basis.at[:, rows], load.at[q, 2 * half + 1])
            )
        return copies

    def start_loads(q, _):
        for copy in loads(q):
            copy.start()
        return 0

    def load_conc(zh):
        return pltpu.make_async_copy(
            conc_far.at[:, pl.ds(128 * zh, 128)], start.at[zh], prep.at[zh]
        )

    def load_mask(yh):
        return pltpu.make_async_copy(
            mask_far.at[:, pl.ds(128 * yh, 128)], wells.at[yh], prep.at[2 + yh]
        )

    load_tz = pltpu.make_async_copy(tz_far.at[g], tz, prep.at[4])
    some_z = [g <= 4, g >= 4]
    for zh in range(2):

        @pl.when(some_z[zh])
        def _():
            load_conc(zh).start()

    load_tz.start()
    lax.fori_loop(0, 4, start_loads, 0)
    for yh in range(2):
        load_mask(yh).start()

    def slab_copy(to_h):
        return pltpu.make_async_remote_copy(
            src_ref=cz.at[:, pl.ds(16 * to_h, 20)],
            dst_ref=conc0.at[:, :, pl.ds(pl.multiple_of(8 + 16 * c, 8), 16)],
            send_sem=sc.at[to_h],
            recv_sem=rc.at[c],
            device_id=at(i, to_h, h),
            device_id_type=MESH,
        )

    def slab_local(to_h):
        return pltpu.make_async_copy(
            cz.at[:, pl.ds(16 * to_h, 20)],
            conc0.at[:, :, pl.ds(pl.multiple_of(8 + 16 * c, 8), 16)],
            rc.at[c],
        )

    above = 2 * i + h + 1

    def halo_copy(to_h):
        return pltpu.make_async_remote_copy(
            src_ref=cz.at[:, pl.ds(16 * to_h, 20), pl.ds(8, 8)],
            dst_ref=conc0.at[:, :, pl.ds(0, 8)],
            send_sem=sc.at[2 + to_h],
            recv_sem=rc.at[2],
            device_id=at((above // 2) % 4, to_h, above % 2),
            device_id_type=MESH,
        )

    def halo_local(to_h):
        return pltpu.make_async_copy(
            cz.at[:, pl.ds(16 * to_h, 20), pl.ds(8, 8)], conc0.at[:, :, pl.ds(0, 8)], rc.at[2]
        )

    def slab_here(to_h):
        return jnp.logical_and(h == to_h, c == to_h)

    def halo_some():
        return jnp.logical_and(c == 1, above < 8)

    for m in range(2):
        weight = 1.0
        for r in range(3):
            index = point[m, r]
            value = jnp.where(index == 0, -ROOT3, jnp.where(index == 1, 0.0, ROOT3))
            weight = weight * jnp.where(index == 1, 2.0 / 3.0, 1.0 / 6.0)
            mine[4 * m + r : 4 * m + r + 1, :] = jnp.full((1, 128), value, F32)
        mine[4 * m + 3 : 4 * m + 4, :] = jnp.full((1, 128), weight, F32)

    def node_copy(dp):
        return pltpu.make_async_remote_copy(
            src_ref=mine,
            dst_ref=listed.at[pts],
            send_sem=sn.at[dp],
            recv_sem=rn.at[dp],
            device_id={"pts": (pts + dp) % 8, "py": i, "pz": pz},
            device_id_type=MESH,
        )

    turned_z[:, 0:8, :] = jnp.zeros((8, 8, 128), F32)
    for zh in range(2):

        @pl.when(some_z[zh])
        def _():
            load_conc(zh).wait()

    def turn_conc(y4, _):
        rows = [(m, v) for m in range(4) for v in range(2)]
        for zh in range(2):

            @pl.when(some_z[zh])
            def _():
                for m, v in rows:
                    turned_z[2 * m + v, 4 + 128 * zh : 132 + 128 * zh, :] = start[
                        zh, pl.ds(16 * v + 4 * y4 + m, 128, stride=32), :
                    ].T

        for m, v in rows:
            cz_flat[v, pl.ds(4 * y4 + m, 40, stride=16), :] = turned_z[
                2 * m + v, pl.ds(pl.multiple_of(32 * g, 32), 40), :
            ]
        return 0

    lax.fori_loop(0, 4, turn_conc, 0)

    def turn_mask():
        turned_y[:, 0:8, :] = jnp.zeros((2, 8, 128), F32)
        for yh in range(2):
            load_mask(yh).wait()
            for v in range(2):
                block = wells[yh, pl.ds(v, 128, stride=2), :].astype(F32)
                turned_y[v, 8 + 128 * yh : 136 + 128 * yh, :] = 0.5 * block.T
        for v in range(2):
            for t in range(5):
                mask[v, 8 * t : 8 * t + 8, :] = turned_y[v, pl.ds(32 * u + t, 8, stride=5), :]

    def greet():
        pl.semaphore_wait(barrier, len(peers))
        for dp in range(1, 8):
            node_copy(dp).start()
        listed[pts] = mine[...]
        for to_h in range(2):

            @pl.when(slab_here(to_h))
            def _():
                slab_local(to_h).start()

            @pl.when(jnp.logical_not(slab_here(to_h)))
            def _():
                slab_copy(to_h).start()

        @pl.when(jnp.logical_and(halo_some(), h == 0))
        def _():
            halo_local(0).start()

        @pl.when(jnp.logical_and(halo_some(), h == 1))
        def _():
            halo_copy(0).start()

        @pl.when(halo_some())
        def _():
            halo_copy(1).start()

        @pl.when(u == 0)
        def _():
            conc0[:, :, 0:8, :] = jnp.zeros((2, 20, 8, 128), F32)

    spot_b = (lax.broadcasted_iota(jnp.int32, (64, G), 0) + 64 * pz).astype(F32)
    spot_c = lax.broadcasted_iota(jnp.int32, (64, G), 1).astype(F32)
    wave[...] = 64.0 + spot_b * spot_b + spot_c * spot_c
    front = 64.0 * 0.9 * (32.0**1.5)

    def stage(step, _):
        amps = []
        for part in range(2):
            for half in range(2):
                a = (64 * i + 2 * step + part + 32 * half).astype(F32)
                amps.append(front / (wave[...] + a * a))
        for f in range(4):
            parts = []
            for part in range(2):
                for half in range(2):
                    row = 2 * step + part + 32 * half
                    value = xi[row] if f == 0 else basis[f - 1, row].astype(F32)
                    parts.append(value * amps[2 * part + half])
            high, low = halves(jnp.concatenate(parts, axis=0))
            both = jnp.dot(jnp.concatenate([high, low], axis=0), tz[...], preferred_element_type=F32)
            both = (both[0:256] + both[256:512]).T
            total = both[0:40] + both[40:80]
            for part in range(2):
                share[pl.ds(32 * f + 2 * step + part, 40, stride=128), :] = total[
                    :, 128 * part : 128 * part + 128
                ]
        return 0

    def stages(part, _):
        for q in range(2):
            for copy in loads(2 * part + q):
                copy.wait()
            lax.fori_loop(8 * part + 4 * q, 8 * part + 4 * q + 4, stage, 0)
        for d in (2, 3, 1):
            early(part, d).start()
        return 0

    blocks = share.reshape(40, 4, 32, 128)

    def early(part, d):
        to_h, to_c = (h + d // 2) % 2, (c + d % 2) % 2
        rows = pl.ds(pl.multiple_of(16 * part, 16), 16)
        return pltpu.make_async_remote_copy(
            src_ref=blocks.at[pl.ds(20 * to_c + 8 * to_h, 2), :, rows],
            dst_ref=got1.at[pl.ds(0, 2), pz, :, rows],
            send_sem=s0.at[part, d],
            recv_sem=r0.at[part, d],
            device_id=at(i, to_h, to_c),
            device_id_type=MESH,
        )

    greet()
    load_tz.wait()
    lax.fori_loop(0, 2, stages, 0)

    def first(pair, d):
        to_h, to_c = (h + d // 2) % 2, (c + d % 2) % 2
        return pltpu.make_async_remote_copy(
            src_ref=blocks.at[pl.ds(20 * to_c + 8 * to_h + 2 * pair, 2)],
            dst_ref=got1.at[pl.ds(2 * pair, 2), pz],
            send_sem=s1.at[pair, d],
            recv_sem=r1.at[pair, d],
            device_id=at(i, to_h, to_c),
            device_id_type=MESH,
        )

    def send_first(pair, _):
        for d in (2, 3, 1):
            first(pair, d).start()
        return 0

    lax.fori_loop(1, PAIRS, send_first, 0)

    def second(pair, d):
        to_i, to_c = (i + d // 2) % 4, (c + d % 2) % 2
        return pltpu.make_async_remote_copy(
            src_ref=rows2.at[pl.ds(2 * pair, 2), 2 * to_i + to_c],
            dst_ref=got2.at[pl.ds(2 * pair, 2), c, i],
            send_sem=s2.at[pair, d],
            recv_sem=r2.at[pair, d],
            device_id=at(to_i, h, to_c),
            device_id_type=MESH,
        )

    lane = lax.broadcasted_iota(jnp.int32, (128, 128), 1)
    lane_low = lane < 64
    lane8 = lax.broadcasted_iota(jnp.int32, (8, 128), 1)
    lane_some = lane8 > 0
    lane40 = lax.broadcasted_iota(jnp.int32, (40, 128), 1) < 64

    def b_contraction(k):
        own = share[pl.ds(pl.multiple_of((20 * c + 8 * h + k) * 128, 128), 128), :]
        got1[k, pz] = own.reshape(4, 32, 128)
        sides = [[], []]
        for pair in range(2):
            one, two = (got1[k, 2 * pair + m].reshape(128, 128) for m in range(2))
            sides[0].append(jnp.where(lane_low, one, pltpu.roll(two, 64, 1)))
            sides[1].append(jnp.where(lane_low, pltpu.roll(one, 64, 1), two))
        both = [jnp.concatenate(side, axis=1) for side in sides]
        rows = []
        for f in range(4):
            rows += [both[0][32 * f : 32 * f + 32], both[1][32 * f : 32 * f + 32]]
        high, low = halves(jnp.concatenate(rows, axis=0))
        both = lax.dot_general(cy[...], high, NT, preferred_element_type=F32)
        rest = lax.dot_general(cy[0:320], low, NT, preferred_element_type=F32)
        total = both[0:320] + both[320:640] + rest
        for slab in range(8):
            rows2[k, slab] = total[40 * slab : 40 * slab + 40]
        got2[k, c, i] = rows2[k, u]

    def a_contraction(k):
        rows = []
        for core in range(2):
            for pair in range(2):
                cols = [[], []]
                for group in range(2):
                    one = got2[k, core, 2 * group, :, 128 * pair : 128 * pair + 128]
                    two = got2[k, core, 2 * group + 1, :, 128 * pair : 128 * pair + 128]
                    cols[0].append(jnp.where(lane40, one, pltpu.roll(two, 64, 1)))
                    cols[1].append(jnp.where(lane40, pltpu.roll(one, 64, 1), two))
                rows += [jnp.concatenate(col, axis=1) for col in cols]
        high, low = halves(jnp.concatenate(rows, axis=0))
        both = jnp.dot(jnp.concatenate([high, low], axis=0), cx[0:256], preferred_element_type=F32)
        total = both[0:320] + both[320:640]
        total += jnp.dot(high, cx[256:512], preferred_element_type=F32)
        for core in range(2):
            for f in range(4):
                row = 160 * core + 40 * f
                fields[core, f] = total[row : row + 40]

    tiles = [(t, v) for t in range(5) for v in range(2)]

    def transport(k, core, halo):
        zz = 2 * k + core
        spot_z = 16 * (2 * g + h) - 4 + zz
        well = jnp.where(spot_z >= 0, prof[jnp.maximum(spot_z, 0)], 0.0)
        for t, v in tiles:
            plane[0, t, v] = conc0[v, zz, pl.ds(t, 8, stride=5), :]
            plane[1, t, v] = mask[v, 8 * t : 8 * t + 8, :] * well
            if not halo:
                plane[2, t, v] = jnp.zeros((8, 128), F32)
        steps = zz + 1 if halo else STEPS

        def some_points(group, _):
            each = range(BATCH)
            speed, conc = [{} for _ in each], [{} for _ in each]
            for m in each:
                n = BATCH * group + m
                node = [nodes[n, r] for r in range(3)]
                for t, v in tiles:
                    logs = [
                        fields[core, f, 8 * t : 8 * t + 8, 128 * v : 128 * v + 128] for f in range(4)
                    ]
                    value = logs[0] + node[0] * logs[1] + node[1] * logs[2] + node[2] * logs[3]
                    speed[m][t, v] = 0.125 + 0.125 * jnp.tanh(value)
                    conc[m][t, v] = plane[0, t, v]
            for step in range(steps):
                last = halo and step == steps - 1
                flux = [{tv: speed[m][tv] * conc[m][tv] for tv in tiles} for m in each]
                for t, v in tiles:
                    for m in each:
                        n = BATCH * group + m
                        here = flux[m][t, v]
                        if last:
                            carry[n, step, t, v] = here
                            continue
                        behind = carry[n, step, t, v]
                        carry[n, step, t, v] = here
                        prev_b = flux[m][t - 1, v] if t > 0 else pltpu.roll(flux[m][4, v], 1, 0)
                        prev_a = (
                            flux[m][t, 0]
                            if v == 1
                            else jnp.where(lane_some, pltpu.roll(flux[m][t, 1], 1, 1), 0.0)
                        )
                        conc[m][t, v] = (
                            (conc[m][t, v] - 3.6 * here)
                            + (plane[1, t, v] + behind)
                            + (prev_b + 1.6 * prev_a)
                        )
            if not halo:
                for t, v in tiles:
                    part = nodes[BATCH * group, 3] * conc[0][t, v]
                    for m in range(1, BATCH):
                        part += nodes[BATCH * group + m, 3] * conc[m][t, v]
                    plane[2, t, v] += part
            return 0

        lax.fori_loop(0, POINTS // BATCH, some_points, 0)
        if not halo:
            for t, v in tiles:
                sums[v, pl.ds(16 * t + zz - 4, 8, stride=80), :] = plane[2, t, v]

    carry[...] = jnp.zeros(carry.shape, F32)

    def wait_conc():
        for core in range(2):
            slab = pltpu.make_async_copy(
                cz.at[:, pl.ds(0, 20)], conc0.at[:, :, pl.ds(8 + 16 * core, 16)], rc.at[core]
            )
            slab.wait()

        @pl.when(u > 0)
        def _():
            pltpu.make_async_copy(
                cz.at[:, pl.ds(0, 20), pl.ds(8, 8)], conc0.at[:, :, pl.ds(0, 8)], rc.at[2]
            ).wait()

    def each_round(pair, work):
        def one(sub, _):
            work(2 * pair + sub)
            return 0

        lax.fori_loop(0, 2, one, 0)

    def whole_round(k):
        a_contraction(k)
        for core in range(2):
            transport(k, core, False)

    def rounds(step, _):
        @pl.when(step == 0)
        def _():
            for part in range(2):
                for d in range(1, 4):
                    early(part, d).wait_recv()

        @pl.when(jnp.logical_and(step > 0, step < PAIRS))
        def _():
            for d in range(1, 4):
                first(step, d).wait_recv()

        @pl.when(step < PAIRS)
        def _():
            each_round(step, b_contraction)
            for d in (4, 5, 2, 6, 3, 7, 1):
                second(step, d).start()

        @pl.when(step > 0)
        def _():
            for d in range(1, 8):
                second(step - 1, d).wait_recv()

        @pl.when(step == 1)
        def _():
            for k in range(2):
                a_contraction(k)
                for core in range(2):
                    transport(k, core, True)

        @pl.when(step > 1)
        def _():
            each_round(step - 1, whole_round)

        return 0

    turn_mask()
    wait_conc()
    for dp in range(1, 8):
        node_copy(dp).wait_recv()
    for n in range(POINTS):
        for r in range(4):
            row = 4 * (n % 2) + r
            nodes[n, r] = jnp.broadcast_to(listed[n // 2, row : row + 1, :], (8, 128))
    lax.fori_loop(0, PAIRS + 1, rounds, 0)

    granule = lax.broadcasted_iota(jnp.int32, (16, 128), 1) // 16

    def regroup(which, _):
        half, yg = which // 4, which % 4
        arrays = []
        for yy in range(4):
            for v in range(2):
                row = pl.multiple_of(16 * (8 + 16 * half + 4 * yg + yy), 16)
                arrays.append(sums[v, pl.ds(row, 16), :])
        for bit in (4, 2, 1):
            clear = (granule // bit) % 2 == 0
            for m in range(8):
                if m // bit % 2 == 0:
                    one, two = arrays[m], arrays[m + bit]
                    arrays[m] = jnp.where(clear, one, pltpu.roll(two, 16 * bit, 1))
                    arrays[m + bit] = jnp.where(clear, pltpu.roll(one, 128 - 16 * bit, 1), two)
        for p in range(8):
            parcel[p, half, yg] = arrays[p]
        return 0

    zr = pl.multiple_of(16 * (4 * yy + 2 * xt + h), 16)

    def home(dp, half):
        to = (pts + dp) % 8
        return pltpu.make_async_remote_copy(
            src_ref=parcel.at[to, half],
            dst_ref=landed.at[:, pl.ds(zr, 16)],
            send_sem=so.at[dp, half],
            recv_sem=ro.at[dp, h],
            device_id={"pts": to, "py": i, "pz": 2 * c + half},
            device_id_type=MESH,
        )

    def home_own(half):
        return pltpu.make_async_copy(parcel.at[pts, half], landed.at[:, pl.ds(zr, 16)], ro.at[0, h])

    for half in range(2):
        lax.fori_loop(4 * half, 4 * half + 4, regroup, 0)
        here = jnp.logical_and(c == h, c == half)

        @pl.when(here)
        def _():
            home_own(half).start()

        @pl.when(jnp.logical_not(here))
        def _():
            home(0, half).start()

        for dp in range(1, 8):
            home(dp, half).start()

    for dp in range(8):
        for from_h in range(2):
            pltpu.make_async_copy(
                parcel.at[0, 0], landed.at[:, pl.ds(0, 16)], ro.at[dp, from_h]
            ).wait()

    for yg in range(4):
        for zh in range(2):
            turned = landed[yg, 128 * zh : 128 * zh + 128, :].T
            for y in range(4):
                for v in range(2):
                    e = 16 * (2 * y + v)
                    final[zh, pl.ds(16 * v + 4 * yg + y, 16, stride=32), :] = turned[e : e + 16]
    for zh in range(2):
        out[:, 128 * zh : 128 * zh + 128] = final[zh]

    for part in range(2):
        for d in range(1, 4):
            early(part, d).wait_send()

    def drain(pair, _):
        @pl.when(pair > 0)
        def _():
            for d in range(1, 4):
                first(pair, d).wait_send()

        for d in range(1, 8):
            second(pair, d).wait_send()
        return 0

    lax.fori_loop(0, PAIRS, drain, 0)
    for dp in range(1, 8):
        node_copy(dp).wait_send()
        for half in range(2):
            home(dp, half).wait_send()
    for half in range(2):

        @pl.when(jnp.logical_not(jnp.logical_and(c == h, c == half)))
        def _():
            home(0, half).wait_send()

    for to_h in range(2):

        @pl.when(jnp.logical_not(slab_here(to_h)))
        def _():
            slab_copy(to_h).wait_send()

    @pl.when(jnp.logical_and(halo_some(), h == 1))
    def _():
        halo_copy(0).wait_send()

    @pl.when(halo_some())
    def _():
        halo_copy(1).wait_send()


def local(xi_map, basis, point_index, conc_start, well_mask, profile):
    (tz_hi, tz_lo), (cy_hi, cy_lo), (cx_hi, cx_lo) = tables()
    tz = np.concatenate([tz_hi, tz_lo, np.zeros((8, G, 48), ml_dtypes.bfloat16)], axis=2)
    cy = np.concatenate([cy_hi, cy_lo], axis=0)
    cx = np.concatenate([cx_hi, cx_lo], axis=0)

    vmem = pl.BlockSpec(memory_space=pltpu.VMEM)
    smem = pl.BlockSpec(memory_space=pltpu.SMEM)
    dma = pltpu.SemaphoreType.DMA
    far = pl.BlockSpec(memory_space=pl.ANY)
    total = pl.pallas_call(
        kernel,
        out_shape=jax.ShapeDtypeStruct((512, 256), F32),
        in_specs=[smem, smem] + [far] * 5 + [vmem] * 2,
        out_specs=vmem,
        scratch_shapes=[
            pltpu.VMEM((64, 64, 256), F32),
            pltpu.VMEM((3, 64, 64, 256), BF16),
            pltpu.VMEM((40 * 128, 128), F32),
            pltpu.VMEM((NROUND, 4, 4, 32, 128), F32),
            pltpu.VMEM((NROUND, 8, 40, 256), F32),
            pltpu.VMEM((NROUND, 2, 4, 40, 256), F32),
            pltpu.VMEM((2, 20, 40, 128), F32),
            pltpu.VMEM((2, 4, 40, 256), F32),
            pltpu.VMEM((POINTS, STEPS, 5, 2, 8, 128), F32),
            pltpu.VMEM((3, 5, 2, 8, 128), F32),
            pltpu.VMEM((64, 256), F32),
            pltpu.VMEM((8, 128), F32),
            pltpu.VMEM((8, 8, 128), F32),
            pltpu.VMEM((POINTS, 4, 8, 128), F32),
            pltpu.VMEM((2, 640, 128), F32),
            pltpu.VMEM((8, 2, 4, 16, 128), F32),
            pltpu.VMEM((4, 256, 128), F32),
            pltpu.VMEM((2, 512, 128), F32),
            pltpu.VMEM((256, 128), BF16),
            pltpu.VMEM((2, 4096, 128), F32),
            pltpu.VMEM((8, 272, 128), F32),
            pltpu.VMEM((2, 640, 128), F32),
            pltpu.VMEM((2, 256, 128), jnp.int32),
            pltpu.VMEM((2, 264, 128), F32),
            pltpu.VMEM((2, 40, 128), F32),
            dma((2, 4)),
            dma((2, 4)),
            dma((PAIRS, 4)),
            dma((PAIRS, 4)),
            dma((PAIRS, 8)),
            dma((PAIRS, 8)),
            dma((4,)),
            dma((3,)),
            dma((4, 4)),
            dma((5,)),
            dma((8,)),
            dma((8,)),
            dma((8, 2)),
            dma((8, 2)),
        ],
        compiler_params=pltpu.CompilerParams(
            collective_id=0, has_side_effects=True, vmem_limit_bytes=60 * 2**20
        ),
    )(point_index, profile, xi_map, basis, conc_start.reshape(4096, 256), well_mask, tz, cy, cx)
    return total.reshape(32, 16, 256)


def solution(mesh):
    placed = (
        P("py", "pz", None),
        P(None, "py", "pz", None),
        P("pts", None),
        P(None, ("py", "pz"), None),
        P(),
        P(),
    )
    return jax.shard_map(
        local, mesh=mesh, in_specs=placed, out_specs=P("pts", ("py", "pz"), None), check_vma=False
    )
```

```python
import functools

import jax
import jax.numpy as jnp
import ml_dtypes
import numpy as np
from jax import lax
from jax.experimental import pallas as pl
from jax.experimental.pallas import tpu as pltpu
from jax.sharding import PartitionSpec as P

MESH = pl.DeviceIdType.MESH
STEPS = 4
POINTS = 16
BATCH = 2
G = 256
NROUND = 10
PAIRS = 5
ROOT3 = 1.7320508075688772
F32 = jnp.float32
BF16 = jnp.bfloat16
NT = (((1,), (1,)), ((), ()))


def split_table(table):
    table = np.asarray(table, np.float64)
    high = table.astype(np.float32).astype(ml_dtypes.bfloat16)
    low = (table - high.astype(np.float64)).astype(np.float32).astype(ml_dtypes.bfloat16)
    return high, low


def tables():
    spots = np.arange(G, dtype=np.float64)
    full = np.sqrt(2.0 / G) * np.cos(np.pi * (spots[:, None] + 0.5) * spots[None, :] / G)
    full[:, 0] *= np.sqrt(0.5)
    tz = np.zeros((8, 40, G))
    for g in range(8):
        for par in range(2):
            for w in range(18):
                z = 32 * g - 4 + 2 * w + par
                if z >= 0:
                    tz[g, 20 * par + w] = full[z]
    tz = tz.transpose(0, 2, 1)
    cy = np.zeros((8, 5, 8, G))
    for u in range(8):
        for t in range(5):
            for q in range(8):
                y = 32 * u - 8 + 5 * q + t
                if y >= 0:
                    cy[u, t, q] = full[y]
    cx = 0.5 * np.concatenate([full[0::2], full[1::2]], axis=0).T
    return split_table(tz), split_table(cy.reshape(320, G)), split_table(cx)


def halves(value):
    high = value.astype(BF16)
    low = (value - high.astype(F32)).astype(BF16)
    return high, low


def kernel(
    point,
    prof,
    xi_far,
    basis_far,
    conc_far,
    mask_far,
    tz_far,
    cy,
    cx,
    out,
    xi,
    basis,
    share,
    got1,
    rows2,
    got2,
    conc0,
    fields,
    carry,
    plane,
    wave,
    mine,
    listed,
    nodes,
    sums,
    parcel,
    landed,
    final,
    tz,
    start,
    turned_z,
    cz_flat,
    wells,
    turned_y,
    mask,
    s0,
    r0,
    s1,
    r1,
    s2,
    r2,
    sc,
    rc,
    load,
    prep,
    sn,
    rn,
    so,
    ro,
):
    pts = lax.axis_index("pts")
    i = lax.axis_index("py")
    pz = lax.axis_index("pz")
    yy, x_lo = pts // 2, pts % 2
    h, c = pz // 2, pz % 2
    xt = (x_lo + h) % 2
    u = 2 * i + c
    g = 2 * yy + xt
    cz = cz_flat.reshape(2, 40, 16, 128)

    def at(i_, h_, c_):
        return {"pts": 2 * yy + (xt + h_) % 2, "py": i_, "pz": 2 * h_ + c_}

    barrier = pltpu.get_barrier_semaphore()
    peers = []
    for dp in range(8):
        for dh in range(2):
            for dc in range(2):
                if dp + dh + dc > 0:
                    peers.append({"pts": (pts + dp) % 8, "py": i, "pz": 2 * ((h + dh) % 2) + (c + dc) % 2})
    for di in range(1, 4):
        for dh in range(2):
            for dc in range(2):
                peers.append(at((i + di) % 4, (h + dh) % 2, (c + dc) % 2))
    for peer in peers:
        pl.semaphore_signal(barrier, inc=1, device_id=peer, device_id_type=MESH)

    def loads(q):
        copies = []
        for half in range(2):
            rows = pl.ds(pl.multiple_of(8 * q + 32 * half, 8), 8)
            copies.append(pltpu.make_async_copy(xi_far.at[rows], xi.at[rows], load.at[q, 2 * half]))
            copies.append(
                pltpu.make_async_copy(basis_far.at[:, rows], basis.at[:, rows], load.at[q, 2 * half + 1])
            )
        return copies

    def start_loads(q, _):
        for copy in loads(q):
            copy.start()
        return 0

    def load_conc(zh):
        return pltpu.make_async_copy(
            conc_far.at[:, pl.ds(128 * zh, 128)], start.at[zh], prep.at[zh]
        )

    def load_mask(yh):
        return pltpu.make_async_copy(
            mask_far.at[:, pl.ds(128 * yh, 128)], wells.at[yh], prep.at[2 + yh]
        )

    load_tz = pltpu.make_async_copy(tz_far.at[g], tz, prep.at[4])
    some_z = [g <= 4, g >= 4]
    for zh in range(2):

        @pl.when(some_z[zh])
        def _():
            load_conc(zh).start()

    load_tz.start()
    lax.fori_loop(0, 4, start_loads, 0)
    for yh in range(2):
        load_mask(yh).start()

    def slab_copy(to_h):
        return pltpu.make_async_remote_copy(
            src_ref=cz.at[:, pl.ds(16 * to_h, 20)],
            dst_ref=conc0.at[:, :, pl.ds(pl.multiple_of(8 + 16 * c, 8), 16)],
            send_sem=sc.at[to_h],
            recv_sem=rc.at[c],
            device_id=at(i, to_h, h),
            device_id_type=MESH,
        )

    def slab_local(to_h):
        return pltpu.make_async_copy(
            cz.at[:, pl.ds(16 * to_h, 20)],
            conc0.at[:, :, pl.ds(pl.multiple_of(8 + 16 * c, 8), 16)],
            rc.at[c],
        )

    above = 2 * i + h + 1

    def halo_copy(to_h):
        return pltpu.make_async_remote_copy(
            src_ref=cz.at[:, pl.ds(16 * to_h, 20), pl.ds(8, 8)],
            dst_ref=conc0.at[:, :, pl.ds(0, 8)],
            send_sem=sc.at[2 + to_h],
            recv_sem=rc.at[2],
            device_id=at((above // 2) % 4, to_h, above % 2),
            device_id_type=MESH,
        )

    def halo_local(to_h):
        return pltpu.make_async_copy(
            cz.at[:, pl.ds(16 * to_h, 20), pl.ds(8, 8)], conc0.at[:, :, pl.ds(0, 8)], rc.at[2]
        )

    def slab_here(to_h):
        return jnp.logical_and(h == to_h, c == to_h)

    def halo_some():
        return jnp.logical_and(c == 1, above < 8)

    for m in range(2):
        weight = 1.0
        for r in range(3):
            index = point[m, r]
            value = jnp.where(index == 0, -ROOT3, jnp.where(index == 1, 0.0, ROOT3))
            weight = weight * jnp.where(index == 1, 2.0 / 3.0, 1.0 / 6.0)
            mine[4 * m + r : 4 * m + r + 1, :] = jnp.full((1, 128), value, F32)
        mine[4 * m + 3 : 4 * m + 4, :] = jnp.full((1, 128), weight, F32)

    def node_copy(dp):
        return pltpu.make_async_remote_copy(
            src_ref=mine,
            dst_ref=listed.at[pts],
            send_sem=sn.at[dp],
            recv_sem=rn.at[dp],
            device_id={"pts": (pts + dp) % 8, "py": i, "pz": pz},
            device_id_type=MESH,
        )

    turned_z[:, 0:8, :] = jnp.zeros((8, 8, 128), F32)
    for zh in range(2):

        @pl.when(some_z[zh])
        def _():
            load_conc(zh).wait()

    def turn_conc(y4, _):
        rows = [(m, v) for m in range(4) for v in range(2)]
        for zh in range(2):

            @pl.when(some_z[zh])
            def _():
                for m, v in rows:
                    turned_z[2 * m + v, 4 + 128 * zh : 132 + 128 * zh, :] = start[
                        zh, pl.ds(16 * v + 4 * y4 + m, 128, stride=32), :
                    ].T

        for m, v in rows:
            cz_flat[v, pl.ds(4 * y4 + m, 40, stride=16), :] = turned_z[
                2 * m + v, pl.ds(pl.multiple_of(32 * g, 32), 40), :
            ]
        return 0

    lax.fori_loop(0, 4, turn_conc, 0)

    def turn_mask():
        turned_y[:, 0:8, :] = jnp.zeros((2, 8, 128), F32)
        for yh in range(2):
            load_mask(yh).wait()
            for v in range(2):
                block = wells[yh, pl.ds(v, 128, stride=2), :].astype(F32)
                turned_y[v, 8 + 128 * yh : 136 + 128 * yh, :] = 0.5 * block.T
        for v in range(2):
            for t in range(5):
                mask[v, 8 * t : 8 * t + 8, :] = turned_y[v, pl.ds(32 * u + t, 8, stride=5), :]

    def greet():
        pl.semaphore_wait(barrier, len(peers))
        for dp in range(1, 8):
            node_copy(dp).start()
        listed[pts] = mine[...]
        for to_h in range(2):

            @pl.when(slab_here(to_h))
            def _():
                slab_local(to_h).start()

            @pl.when(jnp.logical_not(slab_here(to_h)))
            def _():
                slab_copy(to_h).start()

        @pl.when(jnp.logical_and(halo_some(), h == 0))
        def _():
            halo_local(0).start()

        @pl.when(jnp.logical_and(halo_some(), h == 1))
        def _():
            halo_copy(0).start()

        @pl.when(halo_some())
        def _():
            halo_copy(1).start()

        @pl.when(u == 0)
        def _():
            conc0[:, :, 0:8, :] = jnp.zeros((2, 20, 8, 128), F32)

    spot_b = (lax.broadcasted_iota(jnp.int32, (64, G), 0) + 64 * pz).astype(F32)
    spot_c = lax.broadcasted_iota(jnp.int32, (64, G), 1).astype(F32)
    wave[...] = 64.0 + spot_b * spot_b + spot_c * spot_c
    front = 64.0 * 0.9 * (32.0**1.5)

    def stage(step, _):
        amps = []
        for part in range(2):
            for half in range(2):
                a = (64 * i + 2 * step + part + 32 * half).astype(F32)
                amps.append(front / (wave[...] + a * a))
        for f in range(4):
            parts = []
            for part in range(2):
                for half in range(2):
                    row = 2 * step + part + 32 * half
                    value = xi[row] if f == 0 else basis[f - 1, row].astype(F32)
                    parts.append(value * amps[2 * part + half])
            high, low = halves(jnp.concatenate(parts, axis=0))
            both = jnp.dot(jnp.concatenate([high, low], axis=0), tz[...], preferred_element_type=F32)
            both = (both[0:256] + both[256:512]).T
            total = both[0:40] + both[40:80]
            for part in range(2):
                share[pl.ds(32 * f + 2 * step + part, 40, stride=128), :] = total[
                    :, 128 * part : 128 * part + 128
                ]
        return 0

    def stages(part, _):
        for q in range(2):
            for copy in loads(2 * part + q):
                copy.wait()
            lax.fori_loop(8 * part + 4 * q, 8 * part + 4 * q + 4, stage, 0)
        for d in (2, 3, 1):
            early(part, d).start()
        return 0

    blocks = share.reshape(40, 4, 32, 128)

    def early(part, d):
        to_h, to_c = (h + d // 2) % 2, (c + d % 2) % 2
        rows = pl.ds(pl.multiple_of(16 * part, 16), 16)
        return pltpu.make_async_remote_copy(
            src_ref=blocks.at[pl.ds(20 * to_c + 8 * to_h, 2), :, rows],
            dst_ref=got1.at[pl.ds(0, 2), pz, :, rows],
            send_sem=s0.at[part, d],
            recv_sem=r0.at[part, d],
            device_id=at(i, to_h, to_c),
            device_id_type=MESH,
        )

    greet()
    load_tz.wait()
    lax.fori_loop(0, 2, stages, 0)

    def first(pair, d):
        to_h, to_c = (h + d // 2) % 2, (c + d % 2) % 2
        return pltpu.make_async_remote_copy(
            src_ref=blocks.at[pl.ds(20 * to_c + 8 * to_h + 2 * pair, 2)],
            dst_ref=got1.at[pl.ds(2 * pair, 2), pz],
            send_sem=s1.at[pair, d],
            recv_sem=r1.at[pair, d],
            device_id=at(i, to_h, to_c),
            device_id_type=MESH,
        )

    def send_first(pair, _):
        for d in (2, 3, 1):
            first(pair, d).start()
        return 0

    lax.fori_loop(1, PAIRS, send_first, 0)

    def second(pair, d):
        to_i, to_c = (i + d // 2) % 4, (c + d % 2) % 2
        return pltpu.make_async_remote_copy(
            src_ref=rows2.at[pl.ds(2 * pair, 2), 2 * to_i + to_c],
            dst_ref=got2.at[pl.ds(2 * pair, 2), c, i],
            send_sem=s2.at[pair, d],
            recv_sem=r2.at[pair, d],
            device_id=at(to_i, h, to_c),
            device_id_type=MESH,
        )

    lane = lax.broadcasted_iota(jnp.int32, (128, 128), 1)
    lane_low = lane < 64
    lane8 = lax.broadcasted_iota(jnp.int32, (8, 128), 1)
    lane_some = lane8 > 0
    lane40 = lax.broadcasted_iota(jnp.int32, (40, 128), 1) < 64

    def b_contraction(k):
        own = share[pl.ds(pl.multiple_of((20 * c + 8 * h + k) * 128, 128), 128), :]
        got1[k, pz] = own.reshape(4, 32, 128)
        sides = [[], []]
        for pair in range(2):
            one, two = (got1[k, 2 * pair + m].reshape(128, 128) for m in range(2))
            sides[0].append(jnp.where(lane_low, one, pltpu.roll(two, 64, 1)))
            sides[1].append(jnp.where(lane_low, pltpu.roll(one, 64, 1), two))
        both = [jnp.concatenate(side, axis=1) for side in sides]
        rows = []
        for f in range(4):
            rows += [both[0][32 * f : 32 * f + 32], both[1][32 * f : 32 * f + 32]]
        high, low = halves(jnp.concatenate(rows, axis=0))
        both = lax.dot_general(cy[...], high, NT, preferred_element_type=F32)
        rest = lax.dot_general(cy[0:320], low, NT, preferred_element_type=F32)
        total = both[0:320] + both[320:640] + rest
        for slab in range(8):
            rows2[k, slab] = total[40 * slab : 40 * slab + 40]
        got2[k, c, i] = rows2[k, u]

    def a_contraction(k):
        rows = []
        for core in range(2):
            for pair in range(2):
                cols = [[], []]
                for group in range(2):
                    one = got2[k, core, 2 * group, :, 128 * pair : 128 * pair + 128]
                    two = got2[k, core, 2 * group + 1, :, 128 * pair : 128 * pair + 128]
                    cols[0].append(jnp.where(lane40, one, pltpu.roll(two, 64, 1)))
                    cols[1].append(jnp.where(lane40, pltpu.roll(one, 64, 1), two))
                rows += [jnp.concatenate(col, axis=1) for col in cols]
        high, low = halves(jnp.concatenate(rows, axis=0))
        both = jnp.dot(jnp.concatenate([high, low], axis=0), cx[0:256], preferred_element_type=F32)
        total = both[0:320] + both[320:640]
        total += jnp.dot(high, cx[256:512], preferred_element_type=F32)
        for core in range(2):
            for f in range(4):
                row = 160 * core + 40 * f
                fields[k % 2, core, f] = total[row : row + 40]

    tiles = [(t, v) for t in range(5) for v in range(2)]

    def transport(k, halo):
        sub = k % 2
        levels = range(2)
        for p in levels:
            zz = 2 * k + p
            spot_z = 16 * (2 * g + h) - 4 + zz
            well = jnp.where(spot_z >= 0, prof[jnp.maximum(spot_z, 0)], 0.0)
            for t, v in tiles:
                plane[p, 0, t, v] = conc0[v, zz, pl.ds(t, 8, stride=5), :]
                plane[p, 1, t, v] = mask[v, 8 * t : 8 * t + 8, :] * well
                if not halo:
                    plane[p, 2, t, v] = jnp.zeros((8, 128), F32)

        def some_points(group, _):
            each = [(m, p) for m in range(BATCH) for p in levels]
            speed, conc = {e: {} for e in each}, {e: {} for e in each}
            for m, p in each:
                n = BATCH * group + m
                node = [nodes[n, r] for r in range(3)]
                for t, v in tiles:
                    logs = [
                        fields[sub, p, f, 8 * t : 8 * t + 8, 128 * v : 128 * v + 128] for f in range(4)
                    ]
                    value = logs[0] + node[0] * logs[1] + node[1] * logs[2] + node[2] * logs[3]
                    speed[m, p][t, v] = 0.125 + 0.125 * jnp.tanh(value)
                    conc[m, p][t, v] = plane[p, 0, t, v]
            for step in range(STEPS):
                flux = {
                    (m, p): {tv: speed[m, p][tv] * conc[m, p][tv] for tv in tiles}
                    for m, p in each
                    if not halo or step <= 2 * k + p
                }
                for t, v in tiles:
                    for m, p in each:
                        if (m, p) not in flux:
                            continue
                        n = BATCH * group + m
                        here = flux[m, p]
                        more = not halo or step < 2 * k + p
                        if more:
                            behind = carry[n, step, t, v] if p == 0 else flux[m, 0][t, v]
                        if p == 1:
                            carry[n, step, t, v] = here[t, v]
                        if not more:
                            continue
                        prev_b = here[t - 1, v] if t > 0 else pltpu.roll(here[4, v], 1, 0)
                        prev_a = (
                            here[t, 0]
                            if v == 1
                            else jnp.where(lane_some, pltpu.roll(here[t, 1], 1, 1), 0.0)
                        )
                        conc[m, p][t, v] = (
                            (conc[m, p][t, v] - 3.6 * here[t, v])
                            + (plane[p, 1, t, v] + behind)
                            + (prev_b + 1.6 * prev_a)
                        )
            if not halo:
                for p in levels:
                    for t, v in tiles:
                        part = nodes[BATCH * group, 3] * conc[0, p][t, v]
                        for m in range(1, BATCH):
                            part += nodes[BATCH * group + m, 3] * conc[m, p][t, v]
                        plane[p, 2, t, v] += part
            return 0

        lax.fori_loop(0, POINTS // BATCH, some_points, 0)
        if not halo:
            for p in levels:
                for t, v in tiles:
                    sums[v, pl.ds(16 * t + 2 * k + p - 4, 8, stride=80), :] = plane[p, 2, t, v]

    def wait_conc():
        for core in range(2):
            slab = pltpu.make_async_copy(
                cz.at[:, pl.ds(0, 20)], conc0.at[:, :, pl.ds(8 + 16 * core, 16)], rc.at[core]
            )
            slab.wait()

        @pl.when(u > 0)
        def _():
            pltpu.make_async_copy(
                cz.at[:, pl.ds(0, 20), pl.ds(8, 8)], conc0.at[:, :, pl.ds(0, 8)], rc.at[2]
            ).wait()

    def rounds(step, _):
        @pl.when(step == 0)
        def _():
            for part in range(2):
                for d in range(1, 4):
                    early(part, d).wait_recv()

        @pl.when(jnp.logical_and(step > 0, step < PAIRS))
        def _():
            for d in range(1, 4):
                first(step, d).wait_recv()

        @pl.when(step < PAIRS)
        def _():
            for sub in range(2):
                b_contraction(2 * step + sub)
            for d in (4, 5, 2, 6, 3, 7, 1):
                second(step, d).start()

        @pl.when(step > 0)
        def _():
            for d in range(1, 8):
                second(step - 1, d).wait_recv()
            for sub in range(2):
                a_contraction(2 * step - 2 + sub)

        @pl.when(step == 1)
        def _():
            for k in range(2):
                transport(k, True)

        @pl.when(step > 1)
        def _():
            def one(sub, _):
                transport(2 * step - 2 + sub, False)
                return 0

            lax.fori_loop(0, 2, one, 0)

        return 0

    turn_mask()
    wait_conc()
    for dp in range(1, 8):
        node_copy(dp).wait_recv()
    for n in range(POINTS):
        for r in range(4):
            row = 4 * (n % 2) + r
            nodes[n, r] = jnp.broadcast_to(listed[n // 2, row : row + 1, :], (8, 128))
    lax.fori_loop(0, PAIRS + 1, rounds, 0)

    granule = lax.broadcasted_iota(jnp.int32, (16, 128), 1) // 16

    def regroup(which, _):
        half, yg = which // 4, which % 4
        arrays = []
        for yy in range(4):
            for v in range(2):
                row = pl.multiple_of(16 * (8 + 16 * half + 4 * yg + yy), 16)
                arrays.append(sums[v, pl.ds(row, 16), :])
        for bit in (4, 2, 1):
            clear = (granule // bit) % 2 == 0
            for m in range(8):
                if m // bit % 2 == 0:
                    one, two = arrays[m], arrays[m + bit]
                    arrays[m] = jnp.where(clear, one, pltpu.roll(two, 16 * bit, 1))
                    arrays[m + bit] = jnp.where(clear, pltpu.roll(one, 128 - 16 * bit, 1), two)
        for p in range(8):
            parcel[p, half, yg] = arrays[p]
        return 0

    zr = pl.multiple_of(16 * (4 * yy + 2 * xt + h), 16)

    def home(dp, half):
        to = (pts + dp) % 8
        return pltpu.make_async_remote_copy(
            src_ref=parcel.at[to, half],
            dst_ref=landed.at[:, pl.ds(zr, 16)],
            send_sem=so.at[dp, half],
            recv_sem=ro.at[dp, h],
            device_id={"pts": to, "py": i, "pz": 2 * c + half},
            device_id_type=MESH,
        )

    def home_own(half):
        return pltpu.make_async_copy(parcel.at[pts, half], landed.at[:, pl.ds(zr, 16)], ro.at[0, h])

    for half in range(2):
        lax.fori_loop(4 * half, 4 * half + 4, regroup, 0)
        here = jnp.logical_and(c == h, c == half)

        @pl.when(here)
        def _():
            home_own(half).start()

        @pl.when(jnp.logical_not(here))
        def _():
            home(0, half).start()

        for dp in range(1, 8):
            home(dp, half).start()

    for dp in range(8):
        for from_h in range(2):
            pltpu.make_async_copy(
                parcel.at[0, 0], landed.at[:, pl.ds(0, 16)], ro.at[dp, from_h]
            ).wait()

    for yg in range(4):
        for zh in range(2):
            turned = landed[yg, 128 * zh : 128 * zh + 128, :].T
            for y in range(4):
                for v in range(2):
                    e = 16 * (2 * y + v)
                    final[zh, pl.ds(16 * v + 4 * yg + y, 16, stride=32), :] = turned[e : e + 16]
    for zh in range(2):
        out[:, 128 * zh : 128 * zh + 128] = final[zh]

    for part in range(2):
        for d in range(1, 4):
            early(part, d).wait_send()

    def drain(pair, _):
        @pl.when(pair > 0)
        def _():
            for d in range(1, 4):
                first(pair, d).wait_send()

        for d in range(1, 8):
            second(pair, d).wait_send()
        return 0

    lax.fori_loop(0, PAIRS, drain, 0)
    for dp in range(1, 8):
        node_copy(dp).wait_send()
        for half in range(2):
            home(dp, half).wait_send()
    for half in range(2):

        @pl.when(jnp.logical_not(jnp.logical_and(c == h, c == half)))
        def _():
            home(0, half).wait_send()

    for to_h in range(2):

        @pl.when(jnp.logical_not(slab_here(to_h)))
        def _():
            slab_copy(to_h).wait_send()

    @pl.when(jnp.logical_and(halo_some(), h == 1))
    def _():
        halo_copy(0).wait_send()

    @pl.when(halo_some())
    def _():
        halo_copy(1).wait_send()


def local(xi_map, basis, point_index, conc_start, well_mask, profile):
    (tz_hi, tz_lo), (cy_hi, cy_lo), (cx_hi, cx_lo) = tables()
    tz = np.concatenate([tz_hi, tz_lo, np.zeros((8, G, 48), ml_dtypes.bfloat16)], axis=2)
    cy = np.concatenate([cy_hi, cy_lo], axis=0)
    cx = np.concatenate([cx_hi, cx_lo], axis=0)

    vmem = pl.BlockSpec(memory_space=pltpu.VMEM)
    smem = pl.BlockSpec(memory_space=pltpu.SMEM)
    dma = pltpu.SemaphoreType.DMA
    far = pl.BlockSpec(memory_space=pl.ANY)
    total = pl.pallas_call(
        kernel,
        out_shape=jax.ShapeDtypeStruct((512, 256), F32),
        in_specs=[smem, smem] + [far] * 5 + [vmem] * 2,
        out_specs=vmem,
        scratch_shapes=[
            pltpu.VMEM((64, 64, 256), F32),
            pltpu.VMEM((3, 64, 64, 256), BF16),
            pltpu.VMEM((40 * 128, 128), F32),
            pltpu.VMEM((NROUND, 4, 4, 32, 128), F32),
            pltpu.VMEM((NROUND, 8, 40, 256), F32),
            pltpu.VMEM((NROUND, 2, 4, 40, 256), F32),
            pltpu.VMEM((2, 20, 40, 128), F32),
            pltpu.VMEM((2, 2, 4, 40, 256), F32),
            pltpu.VMEM((POINTS, STEPS, 5, 2, 8, 128), F32),
            pltpu.VMEM((2, 3, 5, 2, 8, 128), F32),
            pltpu.VMEM((64, 256), F32),
            pltpu.VMEM((8, 128), F32),
            pltpu.VMEM((8, 8, 128), F32),
            pltpu.VMEM((POINTS, 4, 8, 128), F32),
            pltpu.VMEM((2, 640, 128), F32),
            pltpu.VMEM((8, 2, 4, 16, 128), F32),
            pltpu.VMEM((4, 256, 128), F32),
            pltpu.VMEM((2, 512, 128), F32),
            pltpu.VMEM((256, 128), BF16),
            pltpu.VMEM((2, 4096, 128), F32),
            pltpu.VMEM((8, 272, 128), F32),
            pltpu.VMEM((2, 640, 128), F32),
            pltpu.VMEM((2, 256, 128), jnp.int32),
            pltpu.VMEM((2, 264, 128), F32),
            pltpu.VMEM((2, 40, 128), F32),
            dma((2, 4)),
            dma((2, 4)),
            dma((PAIRS, 4)),
            dma((PAIRS, 4)),
            dma((PAIRS, 8)),
            dma((PAIRS, 8)),
            dma((4,)),
            dma((3,)),
            dma((4, 4)),
            dma((5,)),
            dma((8,)),
            dma((8,)),
            dma((8, 2)),
            dma((8, 2)),
        ],
        compiler_params=pltpu.CompilerParams(
            collective_id=0, has_side_effects=True, vmem_limit_bytes=60 * 2**20
        ),
    )(point_index, profile, xi_map, basis, conc_start.reshape(4096, 256), well_mask, tz, cy, cx)
    return total.reshape(32, 16, 256)


def solution(mesh):
    placed = (
        P("py", "pz", None),
        P(None, "py", "pz", None),
        P("pts", None),
        P(None, ("py", "pz"), None),
        P(),
        P(),
    )
    return jax.shard_map(
        local, mesh=mesh, in_specs=placed, out_specs=P("pts", ("py", "pz"), None), check_vma=False
    )
```

```python
import functools

import jax
import jax.numpy as jnp
import ml_dtypes
import numpy as np
from jax import lax
from jax.experimental import pallas as pl
from jax.experimental.pallas import tpu as pltpu
from jax.sharding import PartitionSpec as P

MESH = pl.DeviceIdType.MESH
STEPS = 4
POINTS = 16
BATCH = 2
G = 256
NROUND = 10
PAIRS = 5
ROOT3 = 1.7320508075688772
F32 = jnp.float32
BF16 = jnp.bfloat16
NT = (((1,), (1,)), ((), ()))


def split_table(table):
    table = np.asarray(table, np.float64)
    high = table.astype(np.float32).astype(ml_dtypes.bfloat16)
    low = (table - high.astype(np.float64)).astype(np.float32).astype(ml_dtypes.bfloat16)
    return high, low


def tables():
    spots = np.arange(G, dtype=np.float64)
    full = np.sqrt(2.0 / G) * np.cos(np.pi * (spots[:, None] + 0.5) * spots[None, :] / G)
    full[:, 0] *= np.sqrt(0.5)
    tz = np.zeros((8, 40, G))
    for g in range(8):
        for par in range(2):
            for w in range(18):
                z = 32 * g - 4 + 2 * w + par
                if z >= 0:
                    tz[g, 20 * par + w] = full[z]
    tz = tz.transpose(0, 2, 1)
    cy = np.zeros((8, 5, 8, G))
    for u in range(8):
        for t in range(5):
            for q in range(8):
                y = 32 * u - 8 + 5 * q + t
                if y >= 0:
                    cy[u, t, q] = full[y]
    cx = 0.5 * np.concatenate([full[0::2], full[1::2]], axis=0).T
    return split_table(tz), split_table(cy.reshape(320, G)), split_table(cx)


def halves(value):
    high = value.astype(BF16)
    low = (value - high.astype(F32)).astype(BF16)
    return high, low


def kernel(
    point,
    prof,
    xi_far,
    basis_far,
    conc_far,
    mask_far,
    tz_far,
    cy,
    cx,
    out,
    xi,
    basis,
    share,
    got1,
    rows2,
    got2,
    conc0,
    fields,
    carry,
    plane,
    wave,
    mine,
    listed,
    nodes,
    sums,
    parcel,
    landed,
    final,
    tz,
    start,
    turned_z,
    cz_flat,
    wells,
    turned_y,
    mask,
    s0,
    r0,
    s1,
    r1,
    s2,
    r2,
    s3,
    r3,
    sc,
    rc,
    load,
    prep,
    sn,
    rn,
    so,
    ro,
):
    pts = lax.axis_index("pts")
    i = lax.axis_index("py")
    pz = lax.axis_index("pz")
    yy, x_lo = pts // 2, pts % 2
    h, c = pz // 2, pz % 2
    xt = (x_lo + h) % 2
    u = 2 * i + c
    g = 2 * yy + xt
    cz = cz_flat.reshape(2, 40, 16, 128)

    def at(i_, h_, c_):
        return {"pts": 2 * yy + (xt + h_) % 2, "py": i_, "pz": 2 * h_ + c_}

    barrier = pltpu.get_barrier_semaphore()
    peers = []
    for dp in range(8):
        for dh in range(2):
            for dc in range(2):
                if dp + dh + dc > 0:
                    peers.append({"pts": (pts + dp) % 8, "py": i, "pz": 2 * ((h + dh) % 2) + (c + dc) % 2})
    for di in range(1, 4):
        for dh in range(2):
            for dc in range(2):
                peers.append(at((i + di) % 4, (h + dh) % 2, (c + dc) % 2))
    for peer in peers:
        pl.semaphore_signal(barrier, inc=1, device_id=peer, device_id_type=MESH)

    def loads(q):
        copies = []
        for half in range(2):
            rows = pl.ds(pl.multiple_of(8 * q + 32 * half, 8), 8)
            copies.append(pltpu.make_async_copy(xi_far.at[rows], xi.at[rows], load.at[q, 2 * half]))
            copies.append(
                pltpu.make_async_copy(basis_far.at[:, rows], basis.at[:, rows], load.at[q, 2 * half + 1])
            )
        return copies

    def start_loads(q, _):
        for copy in loads(q):
            copy.start()
        return 0

    def load_conc(zh):
        return pltpu.make_async_copy(
            conc_far.at[:, pl.ds(128 * zh, 128)], start.at[zh], prep.at[zh]
        )

    def load_mask(yh):
        return pltpu.make_async_copy(
            mask_far.at[:, pl.ds(128 * yh, 128)], wells.at[yh], prep.at[2 + yh]
        )

    load_tz = pltpu.make_async_copy(tz_far.at[g], tz, prep.at[4])
    some_z = [g <= 4, g >= 4]
    for zh in range(2):

        @pl.when(some_z[zh])
        def _():
            load_conc(zh).start()

    load_tz.start()
    lax.fori_loop(0, 4, start_loads, 0)
    for yh in range(2):
        load_mask(yh).start()

    def slab_copy(to_h):
        return pltpu.make_async_remote_copy(
            src_ref=cz.at[:, pl.ds(16 * to_h, 20)],
            dst_ref=conc0.at[:, :, pl.ds(pl.multiple_of(8 + 16 * c, 8), 16)],
            send_sem=sc.at[to_h],
            recv_sem=rc.at[c],
            device_id=at(i, to_h, h),
            device_id_type=MESH,
        )

    def slab_local(to_h):
        return pltpu.make_async_copy(
            cz.at[:, pl.ds(16 * to_h, 20)],
            conc0.at[:, :, pl.ds(pl.multiple_of(8 + 16 * c, 8), 16)],
            rc.at[c],
        )

    above = 2 * i + h + 1

    def halo_copy(to_h):
        return pltpu.make_async_remote_copy(
            src_ref=cz.at[:, pl.ds(16 * to_h, 20), pl.ds(8, 8)],
            dst_ref=conc0.at[:, :, pl.ds(0, 8)],
            send_sem=sc.at[2 + to_h],
            recv_sem=rc.at[2],
            device_id=at((above // 2) % 4, to_h, above % 2),
            device_id_type=MESH,
        )

    def halo_local(to_h):
        return pltpu.make_async_copy(
            cz.at[:, pl.ds(16 * to_h, 20), pl.ds(8, 8)], conc0.at[:, :, pl.ds(0, 8)], rc.at[2]
        )

    def slab_here(to_h):
        return jnp.logical_and(h == to_h, c == to_h)

    def halo_some():
        return jnp.logical_and(c == 1, above < 8)

    for m in range(2):
        weight = 1.0
        for r in range(3):
            index = point[m, r]
            value = jnp.where(index == 0, -ROOT3, jnp.where(index == 1, 0.0, ROOT3))
            weight = weight * jnp.where(index == 1, 2.0 / 3.0, 1.0 / 6.0)
            mine[4 * m + r : 4 * m + r + 1, :] = jnp.full((1, 128), value, F32)
        mine[4 * m + 3 : 4 * m + 4, :] = jnp.full((1, 128), weight, F32)

    def node_copy(dp):
        return pltpu.make_async_remote_copy(
            src_ref=mine,
            dst_ref=listed.at[pts],
            send_sem=sn.at[dp],
            recv_sem=rn.at[dp],
            device_id={"pts": (pts + dp) % 8, "py": i, "pz": pz},
            device_id_type=MESH,
        )

    def turn_conc(y4, _):
        rows = [(m, v) for m in range(4) for v in range(2)]
        for zh in range(2):

            @pl.when(some_z[zh])
            def _():
                for m, v in rows:
                    turned_z[2 * m + v, 4 + 128 * zh : 132 + 128 * zh, :] = start[
                        zh, pl.ds(16 * v + 4 * y4 + m, 128, stride=32), :
                    ].T

        for m, v in rows:
            cz_flat[v, pl.ds(4 * y4 + m, 40, stride=16), :] = turned_z[
                2 * m + v, pl.ds(pl.multiple_of(32 * g, 32), 40), :
            ]
        return 0

    def prepare_conc():
        turned_z[:, 0:8, :] = jnp.zeros((8, 8, 128), F32)
        for zh in range(2):

            @pl.when(some_z[zh])
            def _():
                load_conc(zh).wait()

        lax.fori_loop(0, 4, turn_conc, 0)

    def turn_mask():
        turned_y[:, 0:8, :] = jnp.zeros((2, 8, 128), F32)
        for yh in range(2):
            load_mask(yh).wait()
            for v in range(2):
                block = wells[yh, pl.ds(v, 128, stride=2), :].astype(F32)
                turned_y[v, 8 + 128 * yh : 136 + 128 * yh, :] = 0.5 * block.T
        for v in range(2):
            for t in range(5):
                mask[v, 8 * t : 8 * t + 8, :] = turned_y[v, pl.ds(32 * u + t, 8, stride=5), :]

    def greet():
        pl.semaphore_wait(barrier, len(peers))
        for dp in range(1, 8):
            node_copy(dp).start()
        listed[pts] = mine[...]

    def send_conc():
        for to_h in range(2):

            @pl.when(slab_here(to_h))
            def _():
                slab_local(to_h).start()

            @pl.when(jnp.logical_not(slab_here(to_h)))
            def _():
                slab_copy(to_h).start()

        @pl.when(jnp.logical_and(halo_some(), h == 0))
        def _():
            halo_local(0).start()

        @pl.when(jnp.logical_and(halo_some(), h == 1))
        def _():
            halo_copy(0).start()

        @pl.when(halo_some())
        def _():
            halo_copy(1).start()

        @pl.when(u == 0)
        def _():
            conc0[:, :, 0:8, :] = jnp.zeros((2, 20, 8, 128), F32)

    spot_b = (lax.broadcasted_iota(jnp.int32, (64, G), 0) + 64 * pz).astype(F32)
    spot_c = lax.broadcasted_iota(jnp.int32, (64, G), 1).astype(F32)
    wave[...] = 64.0 + spot_b * spot_b + spot_c * spot_c
    front = 64.0 * 0.9 * (32.0**1.5)

    def stage(step, _):
        amps = []
        for part in range(2):
            for half in range(2):
                a = (64 * i + 2 * step + part + 32 * half).astype(F32)
                amps.append(front / (wave[...] + a * a))
        for f in range(4):
            parts = []
            for part in range(2):
                for half in range(2):
                    row = 2 * step + part + 32 * half
                    value = xi[row] if f == 0 else basis[f - 1, row].astype(F32)
                    parts.append(value * amps[2 * part + half])
            high, low = halves(jnp.concatenate(parts, axis=0))
            both = jnp.dot(jnp.concatenate([high, low], axis=0), tz[...], preferred_element_type=F32)
            both = (both[0:256] + both[256:512]).T
            total = both[0:40] + both[40:80]
            for part in range(2):
                share[pl.ds(32 * f + 2 * step + part, 40, stride=128), :] = total[
                    :, 128 * part : 128 * part + 128
                ]
        return 0

    def stages(part, _):
        for q in range(2):
            for copy in loads(2 * part + q):
                copy.wait()
            lax.fori_loop(8 * part + 4 * q, 8 * part + 4 * q + 4, stage, 0)
        for d in (2, 3, 1):
            early(part, d).start()
        return 0

    blocks = share.reshape(40, 4, 32, 128)

    def early(part, d):
        to_h, to_c = (h + d // 2) % 2, (c + d % 2) % 2
        rows = pl.ds(pl.multiple_of(16 * part, 16), 16)
        return pltpu.make_async_remote_copy(
            src_ref=blocks.at[pl.ds(20 * to_c + 8 * to_h, 2), :, rows],
            dst_ref=got1.at[pl.ds(0, 2), pz, :, rows],
            send_sem=s0.at[part, d],
            recv_sem=r0.at[part, d],
            device_id=at(i, to_h, to_c),
            device_id_type=MESH,
        )

    greet()
    load_tz.wait()
    lax.fori_loop(0, 2, stages, 0)

    def first(pair, d):
        to_h, to_c = (h + d // 2) % 2, (c + d % 2) % 2
        return pltpu.make_async_remote_copy(
            src_ref=blocks.at[pl.ds(20 * to_c + 8 * to_h + 2 * pair, 2)],
            dst_ref=got1.at[pl.ds(2 * pair, 2), pz],
            send_sem=s1.at[pair, d],
            recv_sem=r1.at[pair, d],
            device_id=at(i, to_h, to_c),
            device_id_type=MESH,
        )

    def send_first(pair, _):
        for d in (2, 3, 1):
            first(pair, d).start()
        return 0

    lax.fori_loop(1, 2, send_first, 0)
    prepare_conc()
    send_conc()
    lax.fori_loop(2, PAIRS, send_first, 0)

    def second(pair, d):
        to_i, to_c = (i + d // 2) % 4, (c + d % 2) % 2
        return pltpu.make_async_remote_copy(
            src_ref=rows2.at[pl.ds(2 * pair, 2), 2 * to_i + to_c],
            dst_ref=got2.at[pl.ds(2 * pair, 2), c, i],
            send_sem=s2.at[pair, d],
            recv_sem=r2.at[pair, d],
            device_id=at(to_i, h, to_c),
            device_id_type=MESH,
        )

    def single(k, d):
        to_i, to_c = (i + d // 2) % 4, (c + d % 2) % 2
        slot = k % 2 + 2 * (k // 8)
        return pltpu.make_async_remote_copy(
            src_ref=rows2.at[k, 2 * to_i + to_c],
            dst_ref=got2.at[k, c, i],
            send_sem=s3.at[slot, d],
            recv_sem=r3.at[slot, d],
            device_id=at(to_i, h, to_c),
            device_id_type=MESH,
        )

    lane = lax.broadcasted_iota(jnp.int32, (128, 128), 1)
    lane_low = lane < 64
    lane8 = lax.broadcasted_iota(jnp.int32, (8, 128), 1)
    lane_some = lane8 > 0
    lane40 = lax.broadcasted_iota(jnp.int32, (40, 128), 1) < 64

    def b_contraction(k):
        own = share[pl.ds(pl.multiple_of((20 * c + 8 * h + k) * 128, 128), 128), :]
        got1[k, pz] = own.reshape(4, 32, 128)
        sides = [[], []]
        for pair in range(2):
            one, two = (got1[k, 2 * pair + m].reshape(128, 128) for m in range(2))
            sides[0].append(jnp.where(lane_low, one, pltpu.roll(two, 64, 1)))
            sides[1].append(jnp.where(lane_low, pltpu.roll(one, 64, 1), two))
        both = [jnp.concatenate(side, axis=1) for side in sides]
        rows = []
        for f in range(4):
            rows += [both[0][32 * f : 32 * f + 32], both[1][32 * f : 32 * f + 32]]
        high, low = halves(jnp.concatenate(rows, axis=0))
        both = lax.dot_general(cy[...], high, NT, preferred_element_type=F32)
        rest = lax.dot_general(cy[0:320], low, NT, preferred_element_type=F32)
        total = both[0:320] + both[320:640] + rest
        for slab in range(8):
            rows2[k, slab] = total[40 * slab : 40 * slab + 40]
        got2[k, c, i] = rows2[k, u]

    def a_contraction(k):
        rows = []
        for core in range(2):
            for pair in range(2):
                cols = [[], []]
                for group in range(2):
                    one = got2[k, core, 2 * group, :, 128 * pair : 128 * pair + 128]
                    two = got2[k, core, 2 * group + 1, :, 128 * pair : 128 * pair + 128]
                    cols[0].append(jnp.where(lane40, one, pltpu.roll(two, 64, 1)))
                    cols[1].append(jnp.where(lane40, pltpu.roll(one, 64, 1), two))
                rows += [jnp.concatenate(col, axis=1) for col in cols]
        high, low = halves(jnp.concatenate(rows, axis=0))
        both = jnp.dot(jnp.concatenate([high, low], axis=0), cx[0:256], preferred_element_type=F32)
        total = both[0:320] + both[320:640]
        total += jnp.dot(high, cx[256:512], preferred_element_type=F32)
        for core in range(2):
            for f in range(4):
                row = 160 * core + 40 * f
                fields[k % 2, core, f] = total[row : row + 40]

    tiles = [(t, v) for t in range(5) for v in range(2)]

    def transport(k, halo):
        sub = k % 2
        levels = range(2)
        for p in levels:
            zz = 2 * k + p
            spot_z = 16 * (2 * g + h) - 4 + zz
            well = jnp.where(spot_z >= 0, prof[jnp.maximum(spot_z, 0)], 0.0)
            for t, v in tiles:
                plane[p, 0, t, v] = conc0[v, zz, pl.ds(t, 8, stride=5), :]
                plane[p, 1, t, v] = mask[v, 8 * t : 8 * t + 8, :] * well
                if not halo:
                    plane[p, 2, t, v] = jnp.zeros((8, 128), F32)

        def some_points(group, _):
            each = [(m, p) for m in range(BATCH) for p in levels]
            speed, conc = {e: {} for e in each}, {e: {} for e in each}
            for m, p in each:
                n = BATCH * group + m
                node = [nodes[n, r] for r in range(3)]
                for t, v in tiles:
                    logs = [
                        fields[sub, p, f, 8 * t : 8 * t + 8, 128 * v : 128 * v + 128] for f in range(4)
                    ]
                    value = logs[0] + node[0] * logs[1] + node[1] * logs[2] + node[2] * logs[3]
                    speed[m, p][t, v] = 0.125 + 0.125 * jnp.tanh(value)
                    conc[m, p][t, v] = plane[p, 0, t, v]
            for step in range(STEPS):
                flux = {
                    (m, p): {tv: speed[m, p][tv] * conc[m, p][tv] for tv in tiles}
                    for m, p in each
                    if not halo or step <= 2 * k + p
                }
                for t, v in tiles:
                    for m, p in each:
                        if (m, p) not in flux:
                            continue
                        n = BATCH * group + m
                        here = flux[m, p]
                        more = not halo or step < 2 * k + p
                        if more:
                            behind = carry[n, step, t, v] if p == 0 else flux[m, 0][t, v]
                        if p == 1:
                            carry[n, step, t, v] = here[t, v]
                        if not more:
                            continue
                        prev_b = here[t - 1, v] if t > 0 else pltpu.roll(here[4, v], 1, 0)
                        prev_a = (
                            here[t, 0]
                            if v == 1
                            else jnp.where(lane_some, pltpu.roll(here[t, 1], 1, 1), 0.0)
                        )
                        conc[m, p][t, v] = (
                            (conc[m, p][t, v] - 3.6 * here[t, v])
                            + (plane[p, 1, t, v] + behind)
                            + (prev_b + 1.6 * prev_a)
                        )
            if not halo:
                for p in levels:
                    for t, v in tiles:
                        part = nodes[BATCH * group, 3] * conc[0, p][t, v]
                        for m in range(1, BATCH):
                            part += nodes[BATCH * group + m, 3] * conc[m, p][t, v]
                        plane[p, 2, t, v] += part
            return 0

        lax.fori_loop(0, POINTS // BATCH, some_points, 0)
        if not halo:
            for p in levels:
                for t, v in tiles:
                    sums[v, pl.ds(16 * t + 2 * k + p - 4, 8, stride=80), :] = plane[p, 2, t, v]

    def wait_conc():
        for core in range(2):
            slab = pltpu.make_async_copy(
                cz.at[:, pl.ds(0, 20)], conc0.at[:, :, pl.ds(8 + 16 * core, 16)], rc.at[core]
            )
            slab.wait()

        @pl.when(u > 0)
        def _():
            pltpu.make_async_copy(
                cz.at[:, pl.ds(0, 20), pl.ds(8, 8)], conc0.at[:, :, pl.ds(0, 8)], rc.at[2]
            ).wait()

    granule = lax.broadcasted_iota(jnp.int32, (8, 128), 1) // 16
    zr = 16 * (4 * yy + 2 * xt + h)

    def home(zp, dp, half):
        to = (pts + dp) % 8
        return pltpu.make_async_remote_copy(
            src_ref=parcel.at[zp, to, half],
            dst_ref=landed.at[:, pl.ds(pl.multiple_of(zr + 8 * zp, 8), 8)],
            send_sem=so.at[zp, dp, half],
            recv_sem=ro.at[zp, dp, h],
            device_id={"pts": to, "py": i, "pz": 2 * c + half},
            device_id_type=MESH,
        )

    def home_own(zp, half):
        return pltpu.make_async_copy(
            parcel.at[zp, pts, half],
            landed.at[:, pl.ds(pl.multiple_of(zr + 8 * zp, 8), 8)],
            ro.at[zp, 0, h],
        )

    def go_home(zp):
        def regroup(which, _):
            half, yg = which // 4, which % 4
            arrays = []
            for y in range(4):
                for v in range(2):
                    row = pl.multiple_of(16 * (8 + 16 * half + 4 * yg + y) + 8 * zp, 8)
                    arrays.append(sums[v, pl.ds(row, 8), :])
            for bit in (4, 2, 1):
                clear = (granule // bit) % 2 == 0
                for m in range(8):
                    if m // bit % 2 == 0:
                        one, two = arrays[m], arrays[m + bit]
                        arrays[m] = jnp.where(clear, one, pltpu.roll(two, 16 * bit, 1))
                        arrays[m + bit] = jnp.where(clear, pltpu.roll(one, 128 - 16 * bit, 1), two)
            for p in range(8):
                parcel[zp, p, half, yg] = arrays[p]
            return 0

        for half in range(2):
            lax.fori_loop(4 * half, 4 * half + 4, regroup, 0)
            here = jnp.logical_and(c == h, c == half)

            @pl.when(here)
            def _():
                home_own(zp, half).start()

            @pl.when(jnp.logical_not(here))
            def _():
                home(zp, 0, half).start()

            for dp in range(1, 8):
                home(zp, dp, half).start()

    def prepare_rest():
        turn_mask()
        for dp in range(1, 8):
            node_copy(dp).wait_recv()
        for n in range(POINTS):
            for r in range(4):
                row = 4 * (n % 2) + r
                nodes[n, r] = jnp.broadcast_to(listed[n // 2, row : row + 1, :], (8, 128))

    def rounds(step, _):
        @pl.when(step == 0)
        def _():
            for part in range(2):
                for d in range(1, 4):
                    early(part, d).wait_recv()

        @pl.when(jnp.logical_and(step > 0, step < PAIRS))
        def _():
            for d in range(1, 4):
                first(step, d).wait_recv()

        @pl.when(jnp.logical_or(step == 0, step == PAIRS - 1))
        def _():
            def one(k, _):
                b_contraction(k)
                for d in (4, 5, 2, 6, 3, 7, 1):
                    single(k, d).start()
                return 0

            lax.fori_loop(2 * step, 2 * step + 2, one, 0)

        @pl.when(step == 0)
        def _():
            prepare_rest()

        @pl.when(jnp.logical_and(step > 0, step < PAIRS - 1))
        def _():
            for sub in range(2):
                b_contraction(2 * step + sub)
            for d in (4, 5, 2, 6, 3, 7, 1):
                second(step, d).start()

        @pl.when(step == 1)
        def _():
            wait_conc()
            for k in range(2):
                for d in range(1, 8):
                    single(k, d).wait_recv()
                a_contraction(k)
                transport(k, True)

        @pl.when(jnp.logical_and(step > 1, step < PAIRS))
        def _():
            for d in range(1, 8):
                second(step - 1, d).wait_recv()
            for sub in range(2):
                a_contraction(2 * step - 2 + sub)

            def one(sub, _):
                transport(2 * step - 2 + sub, False)
                return 0

            lax.fori_loop(0, 2, one, 0)

        @pl.when(step == 3)
        def _():
            go_home(0)

        @pl.when(step == PAIRS)
        def _():
            def one(k, _):
                for d in range(1, 8):
                    single(k, d).wait_recv()
                a_contraction(k)
                transport(k, False)
                return 0

            lax.fori_loop(2 * PAIRS - 2, 2 * PAIRS, one, 0)

        return 0

    lax.fori_loop(0, PAIRS + 1, rounds, 0)

    go_home(1)
    for zp in range(2):
        for dp in range(8):
            for from_h in range(2):
                pltpu.make_async_copy(
                    parcel.at[0, 0, 0], landed.at[:, pl.ds(0, 8)], ro.at[zp, dp, from_h]
                ).wait()

    for yg in range(4):
        for zh in range(2):
            turned = landed[yg, 128 * zh : 128 * zh + 128, :].T
            for y in range(4):
                for v in range(2):
                    e = 16 * (2 * y + v)
                    final[zh, pl.ds(16 * v + 4 * yg + y, 16, stride=32), :] = turned[e : e + 16]
    for zh in range(2):
        out[:, 128 * zh : 128 * zh + 128] = final[zh]

    for part in range(2):
        for d in range(1, 4):
            early(part, d).wait_send()

    def drain(pair, _):
        for d in range(1, 4):
            first(pair, d).wait_send()
        return 0

    lax.fori_loop(1, PAIRS, drain, 0)

    def drain_pairs(pair, _):
        for d in range(1, 8):
            second(pair, d).wait_send()
        return 0

    lax.fori_loop(1, PAIRS - 1, drain_pairs, 0)
    for k in (0, 1, 8, 9):
        for d in range(1, 8):
            single(k, d).wait_send()
    for dp in range(1, 8):
        node_copy(dp).wait_send()
        for zp in range(2):
            for half in range(2):
                home(zp, dp, half).wait_send()
    for half in range(2):

        @pl.when(jnp.logical_not(jnp.logical_and(c == h, c == half)))
        def _():
            for zp in range(2):
                home(zp, 0, half).wait_send()

    for to_h in range(2):

        @pl.when(jnp.logical_not(slab_here(to_h)))
        def _():
            slab_copy(to_h).wait_send()

    @pl.when(jnp.logical_and(halo_some(), h == 1))
    def _():
        halo_copy(0).wait_send()

    @pl.when(halo_some())
    def _():
        halo_copy(1).wait_send()


def local(xi_map, basis, point_index, conc_start, well_mask, profile):
    (tz_hi, tz_lo), (cy_hi, cy_lo), (cx_hi, cx_lo) = tables()
    tz = np.concatenate([tz_hi, tz_lo, np.zeros((8, G, 48), ml_dtypes.bfloat16)], axis=2)
    cy = np.concatenate([cy_hi, cy_lo], axis=0)
    cx = np.concatenate([cx_hi, cx_lo], axis=0)

    vmem = pl.BlockSpec(memory_space=pltpu.VMEM)
    smem = pl.BlockSpec(memory_space=pltpu.SMEM)
    dma = pltpu.SemaphoreType.DMA
    far = pl.BlockSpec(memory_space=pl.ANY)
    total = pl.pallas_call(
        kernel,
        out_shape=jax.ShapeDtypeStruct((512, 256), F32),
        in_specs=[smem, smem] + [far] * 5 + [vmem] * 2,
        out_specs=vmem,
        scratch_shapes=[
            pltpu.VMEM((64, 64, 256), F32),
            pltpu.VMEM((3, 64, 64, 256), BF16),
            pltpu.VMEM((40 * 128, 128), F32),
            pltpu.VMEM((NROUND, 4, 4, 32, 128), F32),
            pltpu.VMEM((NROUND, 8, 40, 256), F32),
            pltpu.VMEM((NROUND, 2, 4, 40, 256), F32),
            pltpu.VMEM((2, 20, 40, 128), F32),
            pltpu.VMEM((2, 2, 4, 40, 256), F32),
            pltpu.VMEM((POINTS, STEPS, 5, 2, 8, 128), F32),
            pltpu.VMEM((2, 3, 5, 2, 8, 128), F32),
            pltpu.VMEM((64, 256), F32),
            pltpu.VMEM((8, 128), F32),
            pltpu.VMEM((8, 8, 128), F32),
            pltpu.VMEM((POINTS, 4, 8, 128), F32),
            pltpu.VMEM((2, 640, 128), F32),
            pltpu.VMEM((2, 8, 2, 4, 8, 128), F32),
            pltpu.VMEM((4, 256, 128), F32),
            pltpu.VMEM((2, 512, 128), F32),
            pltpu.VMEM((256, 128), BF16),
            pltpu.VMEM((2, 4096, 128), F32),
            pltpu.VMEM((8, 272, 128), F32),
            pltpu.VMEM((2, 640, 128), F32),
            pltpu.VMEM((2, 256, 128), jnp.int32),
            pltpu.VMEM((2, 264, 128), F32),
            pltpu.VMEM((2, 40, 128), F32),
            dma((2, 4)),
            dma((2, 4)),
            dma((PAIRS, 4)),
            dma((PAIRS, 4)),
            dma((PAIRS, 8)),
            dma((PAIRS, 8)),
            dma((4, 8)),
            dma((4, 8)),
            dma((4,)),
            dma((3,)),
            dma((4, 4)),
            dma((5,)),
            dma((8,)),
            dma((8,)),
            dma((2, 8, 2)),
            dma((2, 8, 2)),
        ],
        compiler_params=pltpu.CompilerParams(
            collective_id=0, has_side_effects=True, vmem_limit_bytes=60 * 2**20
        ),
    )(point_index, profile, xi_map, basis, conc_start.reshape(4096, 256), well_mask, tz, cy, cx)
    return total.reshape(32, 16, 256)


def solution(mesh):
    placed = (
        P("py", "pz", None),
        P(None, "py", "pz", None),
        P("pts", None),
        P(None, ("py", "pz"), None),
        P(),
        P(),
    )
    return jax.shard_map(
        local, mesh=mesh, in_specs=placed, out_specs=P("pts", ("py", "pz"), None), check_vma=False
    )
```

```python
import functools

import jax
import jax.numpy as jnp
import ml_dtypes
import numpy as np
from jax import lax
from jax.experimental import pallas as pl
from jax.experimental.pallas import tpu as pltpu
from jax.sharding import PartitionSpec as P

MESH = pl.DeviceIdType.MESH
STEPS = 4
POINTS = 16
BATCH = 2
G = 256
NROUND = 10
PAIRS = 5
ROOT3 = 1.7320508075688772
F32 = jnp.float32
BF16 = jnp.bfloat16
NT = (((1,), (1,)), ((), ()))


def split_table(table):
    table = np.asarray(table, np.float64)
    high = table.astype(np.float32).astype(ml_dtypes.bfloat16)
    low = (table - high.astype(np.float64)).astype(np.float32).astype(ml_dtypes.bfloat16)
    return high, low


def tables():
    spots = np.arange(G, dtype=np.float64)
    full = np.sqrt(2.0 / G) * np.cos(np.pi * (spots[:, None] + 0.5) * spots[None, :] / G)
    full[:, 0] *= np.sqrt(0.5)
    tz = np.zeros((8, 40, G))
    for g in range(8):
        for par in range(2):
            for w in range(18):
                z = 32 * g - 4 + 2 * w + par
                if z >= 0:
                    tz[g, 20 * par + w] = full[z]
    tz = tz.transpose(0, 2, 1)
    cy = np.zeros((8, 5, 8, G))
    for u in range(8):
        for t in range(5):
            for q in range(8):
                y = 32 * u - 8 + 5 * q + t
                if y >= 0:
                    cy[u, t, q] = full[y]
    cx = 0.5 * np.concatenate([full[0::2], full[1::2]], axis=0).T
    return split_table(tz), split_table(cy.reshape(320, G)), split_table(cx)


def halves(value):
    high = value.astype(BF16)
    low = (value - high.astype(F32)).astype(BF16)
    return high, low


def kernel(
    point,
    prof,
    xi_far,
    basis_far,
    conc_far,
    mask_far,
    tz_far,
    cy,
    cx,
    out,
    xi,
    basis,
    share,
    got1,
    rows2,
    got2,
    conc0,
    fields,
    carry,
    plane,
    wave,
    mine,
    listed,
    nodes,
    sums,
    parcel,
    landed,
    final,
    tz,
    start,
    turned_z,
    cz_flat,
    wells,
    turned_y,
    mask,
    s0,
    r0,
    s1,
    r1,
    s2,
    r2,
    sc,
    rc,
    load,
    prep,
    sn,
    rn,
    so,
    ro,
):
    pts = lax.axis_index("pts")
    i = lax.axis_index("py")
    pz = lax.axis_index("pz")
    yy, x_lo = pts // 2, pts % 2
    h, c = pz // 2, pz % 2
    xt = (x_lo + h) % 2
    u = 2 * i + c
    g = 2 * yy + xt
    cz = cz_flat.reshape(2, 40, 16, 128)

    def at(i_, h_, c_):
        return {"pts": 2 * yy + (xt + h_) % 2, "py": i_, "pz": 2 * h_ + c_}

    barrier = pltpu.get_barrier_semaphore()
    peers = []
    for dp in range(8):
        for dh in range(2):
            for dc in range(2):
                if dp + dh + dc > 0:
                    peers.append({"pts": (pts + dp) % 8, "py": i, "pz": 2 * ((h + dh) % 2) + (c + dc) % 2})
    for di in range(1, 4):
        for dh in range(2):
            for dc in range(2):
                peers.append(at((i + di) % 4, (h + dh) % 2, (c + dc) % 2))
    for peer in peers:
        pl.semaphore_signal(barrier, inc=1, device_id=peer, device_id_type=MESH)

    def loads(q):
        copies = []
        for half in range(2):
            rows = pl.ds(pl.multiple_of(16 * q + 32 * half, 16), 16)
            copies.append(pltpu.make_async_copy(xi_far.at[rows], xi.at[rows], load.at[q, 2 * half]))
            copies.append(
                pltpu.make_async_copy(basis_far.at[:, rows], basis.at[:, rows], load.at[q, 2 * half + 1])
            )
        return copies

    def start_loads(q, _):
        for copy in loads(q):
            copy.start()
        return 0

    def load_conc(zh):
        return pltpu.make_async_copy(
            conc_far.at[:, pl.ds(128 * zh, 128)], start.at[zh], prep.at[zh]
        )

    def load_mask(yh):
        return pltpu.make_async_copy(
            mask_far.at[:, pl.ds(128 * yh, 128)], wells.at[yh], prep.at[2 + yh]
        )

    load_tz = pltpu.make_async_copy(tz_far.at[g], tz, prep.at[4])
    some_z = [g <= 4, g >= 4]
    for zh in range(2):

        @pl.when(some_z[zh])
        def _():
            load_conc(zh).start()

    load_tz.start()
    lax.fori_loop(0, 2, start_loads, 0)
    for yh in range(2):
        load_mask(yh).start()

    def slab_copy(to_h):
        return pltpu.make_async_remote_copy(
            src_ref=cz.at[:, pl.ds(16 * to_h, 20)],
            dst_ref=conc0.at[:, :, pl.ds(pl.multiple_of(8 + 16 * c, 8), 16)],
            send_sem=sc.at[to_h],
            recv_sem=rc.at[c],
            device_id=at(i, to_h, h),
            device_id_type=MESH,
        )

    def slab_local(to_h):
        return pltpu.make_async_copy(
            cz.at[:, pl.ds(16 * to_h, 20)],
            conc0.at[:, :, pl.ds(pl.multiple_of(8 + 16 * c, 8), 16)],
            rc.at[c],
        )

    above = 2 * i + h + 1

    def halo_copy(to_h):
        return pltpu.make_async_remote_copy(
            src_ref=cz.at[:, pl.ds(16 * to_h, 20), pl.ds(8, 8)],
            dst_ref=conc0.at[:, :, pl.ds(0, 8)],
            send_sem=sc.at[2 + to_h],
            recv_sem=rc.at[2],
            device_id=at((above // 2) % 4, to_h, above % 2),
            device_id_type=MESH,
        )

    def halo_local(to_h):
        return pltpu.make_async_copy(
            cz.at[:, pl.ds(16 * to_h, 20), pl.ds(8, 8)], conc0.at[:, :, pl.ds(0, 8)], rc.at[2]
        )

    def slab_here(to_h):
        return jnp.logical_and(h == to_h, c == to_h)

    def halo_some():
        return jnp.logical_and(c == 1, above < 8)

    for m in range(2):
        weight = 1.0
        for r in range(3):
            index = point[m, r]
            value = jnp.where(index == 0, -ROOT3, jnp.where(index == 1, 0.0, ROOT3))
            weight = weight * jnp.where(index == 1, 2.0 / 3.0, 1.0 / 6.0)
            mine[4 * m + r : 4 * m + r + 1, :] = jnp.full((1, 128), value, F32)
        mine[4 * m + 3 : 4 * m + 4, :] = jnp.full((1, 128), weight, F32)

    def node_copy(dp):
        return pltpu.make_async_remote_copy(
            src_ref=mine,
            dst_ref=listed.at[pts],
            send_sem=sn.at[dp],
            recv_sem=rn.at[dp],
            device_id={"pts": (pts + dp) % 8, "py": i, "pz": pz},
            device_id_type=MESH,
        )

    turned_z[:, 0:8, :] = jnp.zeros((8, 8, 128), F32)
    for zh in range(2):

        @pl.when(some_z[zh])
        def _():
            load_conc(zh).wait()

    def turn_conc(y4, _):
        rows = [(m, v) for m in range(4) for v in range(2)]
        for zh in range(2):

            @pl.when(some_z[zh])
            def _():
                for m, v in rows:
                    turned_z[2 * m + v, 4 + 128 * zh : 132 + 128 * zh, :] = start[
                        zh, pl.ds(16 * v + 4 * y4 + m, 128, stride=32), :
                    ].T

        for m, v in rows:
            cz_flat[v, pl.ds(4 * y4 + m, 40, stride=16), :] = turned_z[
                2 * m + v, pl.ds(pl.multiple_of(32 * g, 32), 40), :
            ]
        return 0

    lax.fori_loop(0, 4, turn_conc, 0)

    def turn_mask():
        turned_y[:, 0:8, :] = jnp.zeros((2, 8, 128), F32)
        for yh in range(2):
            load_mask(yh).wait()
            for v in range(2):
                block = wells[yh, pl.ds(v, 128, stride=2), :].astype(F32)
                turned_y[v, 8 + 128 * yh : 136 + 128 * yh, :] = 0.5 * block.T
        for v in range(2):
            for t in range(5):
                mask[v, 8 * t : 8 * t + 8, :] = turned_y[v, pl.ds(32 * u + t, 8, stride=5), :]

    def greet():
        pl.semaphore_wait(barrier, len(peers))
        for dp in range(1, 8):
            node_copy(dp).start()
        listed[pts] = mine[...]
        for to_h in range(2):

            @pl.when(slab_here(to_h))
            def _():
                slab_local(to_h).start()

            @pl.when(jnp.logical_not(slab_here(to_h)))
            def _():
                slab_copy(to_h).start()

        @pl.when(jnp.logical_and(halo_some(), h == 0))
        def _():
            halo_local(0).start()

        @pl.when(jnp.logical_and(halo_some(), h == 1))
        def _():
            halo_copy(0).start()

        @pl.when(halo_some())
        def _():
            halo_copy(1).start()

        @pl.when(u == 0)
        def _():
            conc0[:, :, 0:8, :] = jnp.zeros((2, 20, 8, 128), F32)

    spot_b = (lax.broadcasted_iota(jnp.int32, (64, G), 0) + 64 * pz).astype(F32)
    spot_c = lax.broadcasted_iota(jnp.int32, (64, G), 1).astype(F32)
    wave[...] = 64.0 + spot_b * spot_b + spot_c * spot_c
    front = 64.0 * 0.9 * (32.0**1.5)

    def stage(step, _):
        amps = []
        for part in range(2):
            for half in range(2):
                a = (64 * i + 2 * step + part + 32 * half).astype(F32)
                amps.append(front / (wave[...] + a * a))
        for f in range(4):
            parts = []
            for part in range(2):
                for half in range(2):
                    row = 2 * step + part + 32 * half
                    value = xi[row] if f == 0 else basis[f - 1, row].astype(F32)
                    parts.append(value * amps[2 * part + half])
            high, low = halves(jnp.concatenate(parts, axis=0))
            both = jnp.dot(jnp.concatenate([high, low], axis=0), tz[...], preferred_element_type=F32)
            both = (both[0:256] + both[256:512]).T
            total = both[0:40] + both[40:80]
            for part in range(2):
                share[pl.ds(32 * f + 2 * step + part, 40, stride=128), :] = total[
                    :, 128 * part : 128 * part + 128
                ]
        return 0

    def stages(part, _):
        for copy in loads(part):
            copy.wait()
        lax.fori_loop(8 * part, 8 * part + 8, stage, 0)
        for d in (2, 3, 1):
            early(part, d).start()
        return 0

    blocks = share.reshape(40, 4, 32, 128)

    def early(part, d):
        to_h, to_c = (h + d // 2) % 2, (c + d % 2) % 2
        rows = pl.ds(pl.multiple_of(16 * part, 16), 16)
        return pltpu.make_async_remote_copy(
            src_ref=blocks.at[pl.ds(20 * to_c + 8 * to_h, 2), :, rows],
            dst_ref=got1.at[pl.ds(0, 2), pz, :, rows],
            send_sem=s0.at[part, d],
            recv_sem=r0.at[part, d],
            device_id=at(i, to_h, to_c),
            device_id_type=MESH,
        )

    greet()
    load_tz.wait()
    lax.fori_loop(0, 2, stages, 0)

    def first(pair, d):
        to_h, to_c = (h + d // 2) % 2, (c + d % 2) % 2
        return pltpu.make_async_remote_copy(
            src_ref=blocks.at[pl.ds(20 * to_c + 8 * to_h + 4 * pair - 2, 4)],
            dst_ref=got1.at[pl.ds(4 * pair - 2, 4), pz],
            send_sem=s1.at[pair, d],
            recv_sem=r1.at[pair, d],
            device_id=at(i, to_h, to_c),
            device_id_type=MESH,
        )

    def send_first(pair, _):
        for d in (2, 3, 1):
            first(pair, d).start()
        return 0

    lax.fori_loop(1, 3, send_first, 0)

    def second(pair, d):
        to_i, to_c = (i + d // 2) % 4, (c + d % 2) % 2
        return pltpu.make_async_remote_copy(
            src_ref=rows2.at[pl.ds(2 * pair, 2), 2 * to_i + to_c],
            dst_ref=got2.at[pl.ds(2 * pair, 2), c, i],
            send_sem=s2.at[pair, d],
            recv_sem=r2.at[pair, d],
            device_id=at(to_i, h, to_c),
            device_id_type=MESH,
        )

    lane = lax.broadcasted_iota(jnp.int32, (128, 128), 1)
    lane_low = lane < 64
    lane8 = lax.broadcasted_iota(jnp.int32, (8, 128), 1)
    edge = jnp.where(lane8 > 0, 1.6 * 1.6, 0.0).astype(F32)
    lane40 = lax.broadcasted_iota(jnp.int32, (40, 128), 1) < 64

    def b_contraction(k):
        own = share[pl.ds(pl.multiple_of((20 * c + 8 * h + k) * 128, 128), 128), :]
        got1[k, pz] = own.reshape(4, 32, 128)
        sides = [[], []]
        for pair in range(2):
            one, two = (got1[k, 2 * pair + m].reshape(128, 128) for m in range(2))
            sides[0].append(jnp.where(lane_low, one, pltpu.roll(two, 64, 1)))
            sides[1].append(jnp.where(lane_low, pltpu.roll(one, 64, 1), two))
        both = [jnp.concatenate(side, axis=1) for side in sides]
        rows = []
        for f in range(4):
            rows += [both[0][32 * f : 32 * f + 32], both[1][32 * f : 32 * f + 32]]
        high, low = halves(jnp.concatenate(rows, axis=0))
        both = lax.dot_general(cy[...], high, NT, preferred_element_type=F32)
        rest = lax.dot_general(cy[0:320], low, NT, preferred_element_type=F32)
        total = both[0:320] + both[320:640] + rest
        for slab in range(8):
            rows2[k, slab] = total[40 * slab : 40 * slab + 40]
        got2[k, c, i] = rows2[k, u]

    def a_contraction(k):
        rows = []
        for core in range(2):
            for pair in range(2):
                cols = [[], []]
                for group in range(2):
                    one = got2[k, core, 2 * group, :, 128 * pair : 128 * pair + 128]
                    two = got2[k, core, 2 * group + 1, :, 128 * pair : 128 * pair + 128]
                    cols[0].append(jnp.where(lane40, one, pltpu.roll(two, 64, 1)))
                    cols[1].append(jnp.where(lane40, pltpu.roll(one, 64, 1), two))
                rows += [jnp.concatenate(col, axis=1) for col in cols]
        high, low = halves(jnp.concatenate(rows, axis=0))
        both = jnp.dot(jnp.concatenate([high, low], axis=0), cx[0:256], preferred_element_type=F32)
        total = both[0:320] + both[320:640]
        total += jnp.dot(high, cx[256:512], preferred_element_type=F32)
        for core in range(2):
            for f in range(4):
                row = 160 * core + 40 * f
                fields[k % 2, core, f] = total[row : row + 40]

    tiles = [(t, v) for t in range(5) for v in range(2)]

    def transport(k, halo):
        sub = k % 2
        levels = range(2)
        for p in levels:
            zz = 2 * k + p
            spot_z = 16 * (2 * g + h) - 4 + zz
            well = jnp.where(spot_z >= 0, prof[jnp.maximum(spot_z, 0)], 0.0)
            for t, v in tiles:
                share_v = 1.0 if v == 0 else 1.0 / 1.6
                plane[p, 0, t, v] = conc0[v, zz, pl.ds(t, 8, stride=5), :] * share_v
                plane[p, 1, t, v] = mask[v, 8 * t : 8 * t + 8, :] * (well * share_v)
                if not halo:
                    plane[p, 2, t, v] = jnp.zeros((8, 128), F32)

        def some_points(group, _):
            each = [(m, p) for m in range(BATCH) for p in levels]
            speed, conc = {e: {} for e in each}, {e: {} for e in each}
            for m, p in each:
                n = BATCH * group + m
                node = [nodes[n, r] for r in range(3)]
                for t, v in tiles:
                    logs = [
                        fields[sub, p, f, 8 * t : 8 * t + 8, 128 * v : 128 * v + 128] for f in range(4)
                    ]
                    value = logs[0] + node[0] * logs[1] + node[1] * logs[2] + node[2] * logs[3]
                    speed[m, p][t, v] = 0.125 + 0.125 * jnp.tanh(value)
                    conc[m, p][t, v] = plane[p, 0, t, v]
            for step in range(STEPS):
                flux = {
                    (m, p): {tv: speed[m, p][tv] * conc[m, p][tv] for tv in tiles}
                    for m, p in each
                    if not halo or step <= 2 * k + p
                }
                for t, v in tiles:
                    for m, p in each:
                        if (m, p) not in flux:
                            continue
                        n = BATCH * group + m
                        here = flux[m, p]
                        more = not halo or step < 2 * k + p
                        if more:
                            behind = carry[n, step, t, v] if p == 0 else flux[m, 0][t, v]
                        if p == 1:
                            carry[n, step, t, v] = here[t, v]
                        if not more:
                            continue
                        prev_b = here[t - 1, v] if t > 0 else pltpu.roll(here[4, v], 1, 0)
                        prev_a = here[t, 0] if v == 1 else edge * pltpu.roll(here[t, 1], 1, 1)
                        conc[m, p][t, v] = (
                            (conc[m, p][t, v] - 3.6 * here[t, v])
                            + (plane[p, 1, t, v] + behind)
                            + (prev_b + prev_a)
                        )
            if not halo:
                for p in levels:
                    for t, v in tiles:
                        part = nodes[BATCH * group, 3] * conc[0, p][t, v]
                        for m in range(1, BATCH):
                            part += nodes[BATCH * group + m, 3] * conc[m, p][t, v]
                        plane[p, 2, t, v] += part
            return 0

        lax.fori_loop(0, POINTS // BATCH, some_points, 0)
        if not halo:
            for p in levels:
                for t, v in tiles:
                    sums[v, pl.ds(16 * t + 2 * k + p - 4, 8, stride=80), :] = (
                        plane[p, 2, t, v] * (1.0 if v == 0 else 1.6)
                    )

    def wait_conc():
        for core in range(2):
            slab = pltpu.make_async_copy(
                cz.at[:, pl.ds(0, 20)], conc0.at[:, :, pl.ds(8 + 16 * core, 16)], rc.at[core]
            )
            slab.wait()

        @pl.when(u > 0)
        def _():
            pltpu.make_async_copy(
                cz.at[:, pl.ds(0, 20), pl.ds(8, 8)], conc0.at[:, :, pl.ds(0, 8)], rc.at[2]
            ).wait()

    def rounds(step, _):
        @pl.when(step == 0)
        def _():
            for part in range(2):
                for d in range(1, 4):
                    early(part, d).wait_recv()

        @pl.when(jnp.logical_or(step == 1, step == 3))
        def _():
            for d in range(1, 4):
                first((step + 1) // 2, d).wait_recv()

        @pl.when(step < PAIRS)
        def _():
            for sub in range(2):
                b_contraction(2 * step + sub)
            for d in (4, 5, 2, 6, 3, 7, 1):
                second(step, d).start()

        @pl.when(step > 0)
        def _():
            for d in range(1, 8):
                second(step - 1, d).wait_recv()
            for sub in range(2):
                a_contraction(2 * step - 2 + sub)

        @pl.when(step == 1)
        def _():
            for k in range(2):
                transport(k, True)

        @pl.when(step > 1)
        def _():
            def one(sub, _):
                transport(2 * step - 2 + sub, False)
                return 0

            lax.fori_loop(0, 2, one, 0)

        return 0

    turn_mask()
    wait_conc()
    for dp in range(1, 8):
        node_copy(dp).wait_recv()
    for n in range(POINTS):
        for r in range(4):
            row = 4 * (n % 2) + r
            nodes[n, r] = jnp.broadcast_to(listed[n // 2, row : row + 1, :], (8, 128))
    lax.fori_loop(0, PAIRS + 1, rounds, 0)

    granule = lax.broadcasted_iota(jnp.int32, (16, 128), 1) // 16

    def regroup(which, _):
        half, yg = which // 4, which % 4
        arrays = []
        for yy in range(4):
            for v in range(2):
                row = pl.multiple_of(16 * (8 + 16 * half + 4 * yg + yy), 16)
                arrays.append(sums[v, pl.ds(row, 16), :])
        for bit in (4, 2, 1):
            clear = (granule // bit) % 2 == 0
            for m in range(8):
                if m // bit % 2 == 0:
                    one, two = arrays[m], arrays[m + bit]
                    arrays[m] = jnp.where(clear, one, pltpu.roll(two, 16 * bit, 1))
                    arrays[m + bit] = jnp.where(clear, pltpu.roll(one, 128 - 16 * bit, 1), two)
        for p in range(8):
            parcel[p, half, yg] = arrays[p]
        return 0

    zr = pl.multiple_of(16 * (4 * yy + 2 * xt + h), 16)

    def home(dp, half):
        to = (pts + dp) % 8
        return pltpu.make_async_remote_copy(
            src_ref=parcel.at[to, half],
            dst_ref=landed.at[:, pl.ds(zr, 16)],
            send_sem=so.at[dp, half],
            recv_sem=ro.at[dp, h],
            device_id={"pts": to, "py": i, "pz": 2 * c + half},
            device_id_type=MESH,
        )

    def home_own(half):
        return pltpu.make_async_copy(parcel.at[pts, half], landed.at[:, pl.ds(zr, 16)], ro.at[0, h])

    for half in range(2):
        lax.fori_loop(4 * half, 4 * half + 4, regroup, 0)
        here = jnp.logical_and(c == h, c == half)

        @pl.when(here)
        def _():
            home_own(half).start()

        @pl.when(jnp.logical_not(here))
        def _():
            home(0, half).start()

        for dp in range(1, 8):
            home(dp, half).start()

    for dp in range(8):
        for from_h in range(2):
            pltpu.make_async_copy(
                parcel.at[0, 0], landed.at[:, pl.ds(0, 16)], ro.at[dp, from_h]
            ).wait()

    for yg in range(4):
        for zh in range(2):
            turned = landed[yg, 128 * zh : 128 * zh + 128, :].T
            for y in range(4):
                for v in range(2):
                    e = 16 * (2 * y + v)
                    final[zh, pl.ds(16 * v + 4 * yg + y, 16, stride=32), :] = turned[e : e + 16]
    for zh in range(2):
        out[:, 128 * zh : 128 * zh + 128] = final[zh]

    for part in range(2):
        for d in range(1, 4):
            early(part, d).wait_send()

    def drain(pair, _):
        @pl.when(jnp.logical_and(pair > 0, pair < 3))
        def _():
            for d in range(1, 4):
                first(pair, d).wait_send()

        for d in range(1, 8):
            second(pair, d).wait_send()
        return 0

    lax.fori_loop(0, PAIRS, drain, 0)
    for dp in range(1, 8):
        node_copy(dp).wait_send()
        for half in range(2):
            home(dp, half).wait_send()
    for half in range(2):

        @pl.when(jnp.logical_not(jnp.logical_and(c == h, c == half)))
        def _():
            home(0, half).wait_send()

    for to_h in range(2):

        @pl.when(jnp.logical_not(slab_here(to_h)))
        def _():
            slab_copy(to_h).wait_send()

    @pl.when(jnp.logical_and(halo_some(), h == 1))
    def _():
        halo_copy(0).wait_send()

    @pl.when(halo_some())
    def _():
        halo_copy(1).wait_send()


def local(xi_map, basis, point_index, conc_start, well_mask, profile):
    (tz_hi, tz_lo), (cy_hi, cy_lo), (cx_hi, cx_lo) = tables()
    tz = np.concatenate([tz_hi, tz_lo, np.zeros((8, G, 48), ml_dtypes.bfloat16)], axis=2)
    cy = np.concatenate([cy_hi, cy_lo], axis=0)
    cx = np.concatenate([cx_hi, cx_lo], axis=0)

    vmem = pl.BlockSpec(memory_space=pltpu.VMEM)
    smem = pl.BlockSpec(memory_space=pltpu.SMEM)
    dma = pltpu.SemaphoreType.DMA
    far = pl.BlockSpec(memory_space=pl.ANY)
    total = pl.pallas_call(
        kernel,
        out_shape=jax.ShapeDtypeStruct((512, 256), F32),
        in_specs=[smem, smem] + [far] * 5 + [vmem] * 2,
        out_specs=vmem,
        scratch_shapes=[
            pltpu.VMEM((64, 64, 256), F32),
            pltpu.VMEM((3, 64, 64, 256), BF16),
            pltpu.VMEM((40 * 128, 128), F32),
            pltpu.VMEM((NROUND, 4, 4, 32, 128), F32),
            pltpu.VMEM((NROUND, 8, 40, 256), F32),
            pltpu.VMEM((NROUND, 2, 4, 40, 256), F32),
            pltpu.VMEM((2, 20, 40, 128), F32),
            pltpu.VMEM((2, 2, 4, 40, 256), F32),
            pltpu.VMEM((POINTS, STEPS, 5, 2, 8, 128), F32),
            pltpu.VMEM((2, 3, 5, 2, 8, 128), F32),
            pltpu.VMEM((64, 256), F32),
            pltpu.VMEM((8, 128), F32),
            pltpu.VMEM((8, 8, 128), F32),
            pltpu.VMEM((POINTS, 4, 8, 128), F32),
            pltpu.VMEM((2, 640, 128), F32),
            pltpu.VMEM((8, 2, 4, 16, 128), F32),
            pltpu.VMEM((4, 256, 128), F32),
            pltpu.VMEM((2, 512, 128), F32),
            pltpu.VMEM((256, 128), BF16),
            pltpu.VMEM((2, 4096, 128), F32),
            pltpu.VMEM((8, 272, 128), F32),
            pltpu.VMEM((2, 640, 128), F32),
            pltpu.VMEM((2, 256, 128), jnp.int32),
            pltpu.VMEM((2, 264, 128), F32),
            pltpu.VMEM((2, 40, 128), F32),
            dma((2, 4)),
            dma((2, 4)),
            dma((PAIRS, 4)),
            dma((PAIRS, 4)),
            dma((PAIRS, 8)),
            dma((PAIRS, 8)),
            dma((4,)),
            dma((3,)),
            dma((4, 4)),
            dma((5,)),
            dma((8,)),
            dma((8,)),
            dma((8, 2)),
            dma((8, 2)),
        ],
        compiler_params=pltpu.CompilerParams(
            collective_id=0, has_side_effects=True, vmem_limit_bytes=60 * 2**20
        ),
    )(point_index, profile, xi_map, basis, conc_start.reshape(4096, 256), well_mask, tz, cy, cx)
    return total.reshape(32, 16, 256)


def solution(mesh):
    placed = (
        P("py", "pz", None),
        P(None, "py", "pz", None),
        P("pts", None),
        P(None, ("py", "pz"), None),
        P(),
        P(),
    )
    return jax.shard_map(
        local, mesh=mesh, in_specs=placed, out_specs=P("pts", ("py", "pz"), None), check_vma=False
    )
```

```python
import functools

import jax
import jax.numpy as jnp
import ml_dtypes
import numpy as np
from jax import lax
from jax.experimental import pallas as pl
from jax.experimental.pallas import tpu as pltpu
from jax.sharding import PartitionSpec as P

MESH = pl.DeviceIdType.MESH
STEPS = 4
POINTS = 16
BATCH = 2
G = 256
NROUND = 10
PAIRS = 5
ROOT3 = 1.7320508075688772
F32 = jnp.float32
BF16 = jnp.bfloat16
NT = (((1,), (1,)), ((), ()))


def split_table(table):
    table = np.asarray(table, np.float64)
    high = table.astype(np.float32).astype(ml_dtypes.bfloat16)
    low = (table - high.astype(np.float64)).astype(np.float32).astype(ml_dtypes.bfloat16)
    return high, low


def tables():
    spots = np.arange(G, dtype=np.float64)
    full = np.sqrt(2.0 / G) * np.cos(np.pi * (spots[:, None] + 0.5) * spots[None, :] / G)
    full[:, 0] *= np.sqrt(0.5)
    tz = np.zeros((8, 40, G))
    for g in range(8):
        for par in range(2):
            for w in range(18):
                z = 32 * g - 4 + 2 * w + par
                if z >= 0:
                    tz[g, 20 * par + w] = full[z]
    tz = tz.transpose(0, 2, 1)
    cy = np.zeros((8, 5, 8, G))
    for u in range(8):
        for t in range(5):
            for q in range(8):
                y = 32 * u - 8 + 5 * q + t
                if y >= 0:
                    cy[u, t, q] = full[y]
    cx = 0.5 * np.concatenate([full[0::2], full[1::2]], axis=0).T
    return split_table(tz), split_table(cy.reshape(320, G)), split_table(cx)


def halves(value):
    high = value.astype(BF16)
    low = (value - high.astype(F32)).astype(BF16)
    return high, low


def kernel(
    point,
    prof,
    xi_far,
    basis_far,
    conc_far,
    mask_far,
    tz_far,
    cy,
    cx,
    out,
    xi,
    basis,
    share,
    got1,
    rows2,
    got2,
    conc0,
    fields,
    carry,
    plane,
    wave,
    mine,
    listed,
    nodes,
    sums,
    parcel,
    landed,
    final,
    tz,
    start,
    turned_z,
    cz_flat,
    wells,
    turned_y,
    mask,
    r0,
    s1,
    r1,
    s2,
    r2,
    sc,
    rc,
    load,
    prep,
    sn,
    so,
    ro,
):
    pts = lax.axis_index("pts")
    i = lax.axis_index("py")
    pz = lax.axis_index("pz")
    yy, x_lo = pts // 2, pts % 2
    h, c = pz // 2, pz % 2
    xt = (x_lo + h) % 2
    u = 2 * i + c
    g = 2 * yy + xt
    cz = cz_flat.reshape(2, 40, 16, 128)

    def at(i_, h_, c_):
        return {"pts": 2 * yy + (xt + h_) % 2, "py": i_, "pz": 2 * h_ + c_}

    def await_bytes(view, sem):
        pltpu.make_async_copy(view, view, sem).wait()

    barrier = pltpu.get_barrier_semaphore()
    peers = []
    for dp in range(8):
        for dh in range(2):
            for dc in range(2):
                if dp + dh + dc > 0:
                    peers.append({"pts": (pts + dp) % 8, "py": i, "pz": 2 * ((h + dh) % 2) + (c + dc) % 2})
    for di in range(1, 4):
        for dh in range(2):
            for dc in range(2):
                peers.append(at((i + di) % 4, (h + dh) % 2, (c + dc) % 2))
    for peer in peers:
        pl.semaphore_signal(barrier, inc=1, device_id=peer, device_id_type=MESH)

    def loads(q):
        copies = []
        for half in range(2):
            rows = pl.ds(pl.multiple_of(8 * q + 32 * half, 8), 8)
            copies.append(pltpu.make_async_copy(xi_far.at[rows], xi.at[rows], load.at[q, 0]))
            copies.append(
                pltpu.make_async_copy(basis_far.at[:, rows], basis.at[:, rows], load.at[q, 1])
            )
        return copies

    def start_loads(q, _):
        for copy in loads(q):
            copy.start()
        return 0

    def load_conc(zh):
        return pltpu.make_async_copy(
            conc_far.at[:, pl.ds(128 * zh, 128)], start.at[zh], prep.at[zh]
        )

    def load_mask(yh):
        return pltpu.make_async_copy(
            mask_far.at[:, pl.ds(128 * yh, 128)], wells.at[yh], prep.at[2 + yh]
        )

    load_tz = pltpu.make_async_copy(tz_far.at[g], tz, prep.at[4])
    some_z = [g <= 4, g >= 4]
    for zh in range(2):

        @pl.when(some_z[zh])
        def _():
            load_conc(zh).start()

    load_tz.start()
    lax.fori_loop(0, 4, start_loads, 0)
    for yh in range(2):
        load_mask(yh).start()

    def slab_copy(to_h):
        return pltpu.make_async_remote_copy(
            src_ref=cz.at[:, pl.ds(16 * to_h, 20)],
            dst_ref=conc0.at[:, :, pl.ds(pl.multiple_of(8 + 16 * c, 8), 16)],
            send_sem=sc.at[to_h],
            recv_sem=rc.at[c],
            device_id=at(i, to_h, h),
            device_id_type=MESH,
        )

    def slab_local(to_h):
        return pltpu.make_async_copy(
            cz.at[:, pl.ds(16 * to_h, 20)],
            conc0.at[:, :, pl.ds(pl.multiple_of(8 + 16 * c, 8), 16)],
            rc.at[c],
        )

    above = 2 * i + h + 1

    def halo_copy(to_h):
        return pltpu.make_async_remote_copy(
            src_ref=cz.at[:, pl.ds(16 * to_h, 20), pl.ds(8, 8)],
            dst_ref=conc0.at[:, :, pl.ds(0, 8)],
            send_sem=sc.at[2 + to_h],
            recv_sem=rc.at[2],
            device_id=at((above // 2) % 4, to_h, above % 2),
            device_id_type=MESH,
        )

    def halo_local(to_h):
        return pltpu.make_async_copy(
            cz.at[:, pl.ds(16 * to_h, 20), pl.ds(8, 8)], conc0.at[:, :, pl.ds(0, 8)], rc.at[2]
        )

    def slab_here(to_h):
        return jnp.logical_and(h == to_h, c == to_h)

    def halo_some():
        return jnp.logical_and(c == 1, above < 8)

    for m in range(2):
        weight = 1.0
        for r in range(3):
            index = point[m, r]
            value = jnp.where(index == 0, -ROOT3, jnp.where(index == 1, 0.0, ROOT3))
            weight = weight * jnp.where(index == 1, 2.0 / 3.0, 1.0 / 6.0)
            mine[4 * m + r : 4 * m + r + 1, :] = jnp.full((1, 128), value, F32)
        mine[4 * m + 3 : 4 * m + 4, :] = jnp.full((1, 128), weight, F32)

    def node_copy(dp):
        return pltpu.make_async_remote_copy(
            src_ref=mine,
            dst_ref=listed.at[pts],
            send_sem=sn.at[0],
            recv_sem=sn.at[1],
            device_id={"pts": (pts + dp) % 8, "py": i, "pz": pz},
            device_id_type=MESH,
        )

    turned_z[:, 0:8, :] = jnp.zeros((8, 8, 128), F32)
    for zh in range(2):

        @pl.when(some_z[zh])
        def _():
            load_conc(zh).wait()

    def turn_conc(y4, _):
        rows = [(m, v) for m in range(4) for v in range(2)]
        for zh in range(2):

            @pl.when(some_z[zh])
            def _():
                for m, v in rows:
                    turned_z[2 * m + v, 4 + 128 * zh : 132 + 128 * zh, :] = start[
                        zh, pl.ds(16 * v + 4 * y4 + m, 128, stride=32), :
                    ].T

        for m, v in rows:
            cz_flat[v, pl.ds(4 * y4 + m, 40, stride=16), :] = turned_z[
                2 * m + v, pl.ds(pl.multiple_of(32 * g, 32), 40), :
            ]
        return 0

    lax.fori_loop(0, 4, turn_conc, 0)

    def turn_mask():
        turned_y[:, 0:8, :] = jnp.zeros((2, 8, 128), F32)
        for yh in range(2):
            load_mask(yh).wait()
            for v in range(2):
                block = wells[yh, pl.ds(v, 128, stride=2), :].astype(F32)
                turned_y[v, 8 + 128 * yh : 136 + 128 * yh, :] = 0.5 * block.T
        for v in range(2):
            for t in range(5):
                mask[v, 8 * t : 8 * t + 8, :] = turned_y[v, pl.ds(32 * u + t, 8, stride=5), :]

    def greet():
        pl.semaphore_wait(barrier, len(peers))
        for dp in range(1, 8):
            node_copy(dp).start()
        listed[pts] = mine[...]
        for to_h in range(2):

            @pl.when(slab_here(to_h))
            def _():
                slab_local(to_h).start()

            @pl.when(jnp.logical_not(slab_here(to_h)))
            def _():
                slab_copy(to_h).start()

        @pl.when(jnp.logical_and(halo_some(), h == 0))
        def _():
            halo_local(0).start()

        @pl.when(jnp.logical_and(halo_some(), h == 1))
        def _():
            halo_copy(0).start()

        @pl.when(halo_some())
        def _():
            halo_copy(1).start()

        @pl.when(u == 0)
        def _():
            conc0[:, :, 0:8, :] = jnp.zeros((2, 20, 8, 128), F32)

    spot_b = (lax.broadcasted_iota(jnp.int32, (64, G), 0) + 64 * pz).astype(F32)
    spot_c = lax.broadcasted_iota(jnp.int32, (64, G), 1).astype(F32)
    wave[...] = 64.0 + spot_b * spot_b + spot_c * spot_c
    front = 64.0 * 0.9 * (32.0**1.5)

    def stage(step, _):
        amps = []
        for part in range(2):
            for half in range(2):
                a = (64 * i + 2 * step + part + 32 * half).astype(F32)
                amps.append(front / (wave[...] + a * a))
        for f in range(4):
            parts = []
            for part in range(2):
                for half in range(2):
                    row = 2 * step + part + 32 * half
                    value = xi[row] if f == 0 else basis[f - 1, row].astype(F32)
                    parts.append(value * amps[2 * part + half])
            high, low = halves(jnp.concatenate(parts, axis=0))
            both = jnp.dot(jnp.concatenate([high, low], axis=0), tz[...], preferred_element_type=F32)
            both = (both[0:256] + both[256:512]).T
            total = both[0:40] + both[40:80]
            for part in range(2):
                share[pl.ds(32 * f + 2 * step + part, 40, stride=128), :] = total[
                    :, 128 * part : 128 * part + 128
                ]
        return 0

    def stages(part, _):
        for q in range(2):
            await_bytes(xi.at[pl.ds(0, 16)], load.at[2 * part + q, 0])
            await_bytes(basis.at[:, pl.ds(0, 16)], load.at[2 * part + q, 1])
            lax.fori_loop(8 * part + 4 * q, 8 * part + 4 * q + 4, stage, 0)

        @pl.when(part == 0)
        def _():
            for d in (2, 3, 1):
                early(0, 0, 4, d).start()

        @pl.when(part == 1)
        def _():
            for begin in (0, 2):
                for d in (2, 3, 1):
                    early(1, begin, 2, d).start()

        return 0

    blocks = share.reshape(40, 4, 32, 128)

    def early(part, begin, count, d):
        to_h, to_c = (h + d // 2) % 2, (c + d % 2) % 2
        rows = pl.ds(16 * part, 16)
        return pltpu.make_async_remote_copy(
            src_ref=blocks.at[pl.ds(20 * to_c + 8 * to_h + begin, count), :, rows],
            dst_ref=got1.at[pl.ds(begin, count), pz, :, rows],
            send_sem=s1.at[0],
            recv_sem=r0.at[part + begin // 2],
            device_id=at(i, to_h, to_c),
            device_id_type=MESH,
        )

    def early_come(part, begin, count):
        await_bytes(
            got1.at[pl.ds(begin, count), pl.ds(0, 3), :, pl.ds(16 * part, 16)], r0.at[part + begin // 2]
        )

    greet()
    load_tz.wait()
    lax.fori_loop(0, 2, stages, 0)

    def first(pair, d):
        to_h, to_c = (h + d // 2) % 2, (c + d % 2) % 2
        return pltpu.make_async_remote_copy(
            src_ref=blocks.at[pl.ds(20 * to_c + 8 * to_h + 2 * pair, 2)],
            dst_ref=got1.at[pl.ds(2 * pair, 2), pz],
            send_sem=s1.at[0],
            recv_sem=r1.at[pair],
            device_id=at(i, to_h, to_c),
            device_id_type=MESH,
        )

    def send_first(pair, _):
        for d in (2, 3, 1):
            first(pair, d).start()
        return 0

    lax.fori_loop(2, PAIRS, send_first, 0)

    def second(pair, d):
        to_i, to_c = (i + d // 2) % 4, (c + d % 2) % 2
        return pltpu.make_async_remote_copy(
            src_ref=rows2.at[pl.ds(2 * pair, 2), 2 * to_i + to_c],
            dst_ref=got2.at[pl.ds(2 * pair, 2), 4 * c + i],
            send_sem=s2.at[0],
            recv_sem=r2.at[pair],
            device_id=at(to_i, h, to_c),
            device_id_type=MESH,
        )

    lane = lax.broadcasted_iota(jnp.int32, (128, 128), 1)
    lane_low = lane < 64
    lane8 = lax.broadcasted_iota(jnp.int32, (8, 128), 1)
    edge = jnp.where(lane8 > 0, 1.6 * 1.6, 0.0).astype(F32)
    lane40 = lax.broadcasted_iota(jnp.int32, (40, 128), 1) < 64

    def b_contraction(k):
        own = share[pl.ds(pl.multiple_of((20 * c + 8 * h + k) * 128, 128), 128), :]
        got1[k, pz] = own.reshape(4, 32, 128)
        sides = [[], []]
        for pair in range(2):
            one, two = (got1[k, 2 * pair + m].reshape(128, 128) for m in range(2))
            sides[0].append(jnp.where(lane_low, one, pltpu.roll(two, 64, 1)))
            sides[1].append(jnp.where(lane_low, pltpu.roll(one, 64, 1), two))
        both = [jnp.concatenate(side, axis=1) for side in sides]
        rows = []
        for f in range(4):
            rows += [both[0][32 * f : 32 * f + 32], both[1][32 * f : 32 * f + 32]]
        high, low = halves(jnp.concatenate(rows, axis=0))
        both = lax.dot_general(cy[...], high, NT, preferred_element_type=F32)
        rest = lax.dot_general(cy[0:320], low, NT, preferred_element_type=F32)
        total = both[0:320] + both[320:640] + rest
        for slab in range(8):
            rows2[k, slab] = total[40 * slab : 40 * slab + 40]
        got2[k, 4 * c + i] = rows2[k, u]

    def a_contraction(k):
        rows = []
        for core in range(2):
            for pair in range(2):
                cols = [[], []]
                for group in range(2):
                    one = got2[k, 4 * core + 2 * group, :, 128 * pair : 128 * pair + 128]
                    two = got2[k, 4 * core + 2 * group + 1, :, 128 * pair : 128 * pair + 128]
                    cols[0].append(jnp.where(lane40, one, pltpu.roll(two, 64, 1)))
                    cols[1].append(jnp.where(lane40, pltpu.roll(one, 64, 1), two))
                rows += [jnp.concatenate(col, axis=1) for col in cols]
        high, low = halves(jnp.concatenate(rows, axis=0))
        both = jnp.dot(jnp.concatenate([high, low], axis=0), cx[0:256], preferred_element_type=F32)
        total = both[0:320] + both[320:640]
        total += jnp.dot(high, cx[256:512], preferred_element_type=F32)
        for core in range(2):
            for f in range(4):
                row = 160 * core + 40 * f
                fields[k % 2, core, f] = total[row : row + 40]

    tiles = [(t, v) for t in range(5) for v in range(2)]

    def transport(k, halo):
        sub = k % 2
        levels = range(2)
        for p in levels:
            zz = 2 * k + p
            spot_z = 16 * (2 * g + h) - 4 + zz
            well = jnp.where(spot_z >= 0, prof[jnp.maximum(spot_z, 0)], 0.0)
            for t, v in tiles:
                share_v = 1.0 if v == 0 else 1.0 / 1.6
                plane[p, 0, t, v] = conc0[v, zz, pl.ds(t, 8, stride=5), :] * share_v
                plane[p, 1, t, v] = mask[v, 8 * t : 8 * t + 8, :] * (well * share_v)
                if not halo:
                    plane[p, 2, t, v] = jnp.zeros((8, 128), F32)

        def some_points(group, _):
            each = [(m, p) for m in range(BATCH) for p in levels]
            speed, conc = {e: {} for e in each}, {e: {} for e in each}
            for m, p in each:
                n = BATCH * group + m
                node = [nodes[n, r] for r in range(3)]
                for t, v in tiles:
                    logs = [
                        fields[sub, p, f, 8 * t : 8 * t + 8, 128 * v : 128 * v + 128] for f in range(4)
                    ]
                    value = logs[0] + node[0] * logs[1] + node[1] * logs[2] + node[2] * logs[3]
                    speed[m, p][t, v] = 0.125 + 0.125 * jnp.tanh(value)
                    conc[m, p][t, v] = plane[p, 0, t, v]
            for step in range(STEPS):
                flux = {
                    (m, p): {tv: speed[m, p][tv] * conc[m, p][tv] for tv in tiles}
                    for m, p in each
                    if not halo or step <= 2 * k + p
                }
                for t, v in tiles:
                    for m, p in each:
                        if (m, p) not in flux:
                            continue
                        n = BATCH * group + m
                        here = flux[m, p]
                        more = not halo or step < 2 * k + p
                        if more:
                            behind = carry[n, step, t, v] if p == 0 else flux[m, 0][t, v]
                        if p == 1:
                            carry[n, step, t, v] = here[t, v]
                        if not more:
                            continue
                        prev_b = here[t - 1, v] if t > 0 else pltpu.roll(here[4, v], 1, 0)
                        prev_a = here[t, 0] if v == 1 else edge * pltpu.roll(here[t, 1], 1, 1)
                        conc[m, p][t, v] = (
                            (conc[m, p][t, v] - 3.6 * here[t, v])
                            + (plane[p, 1, t, v] + behind)
                            + (prev_b + prev_a)
                        )
            if not halo:
                for p in levels:
                    for t, v in tiles:
                        part = nodes[BATCH * group, 3] * conc[0, p][t, v]
                        for m in range(1, BATCH):
                            part += nodes[BATCH * group + m, 3] * conc[m, p][t, v]
                        plane[p, 2, t, v] += part
            return 0

        lax.fori_loop(0, POINTS // BATCH, some_points, 0)
        if not halo:
            for p in levels:
                for t, v in tiles:
                    sums[v, pl.ds(16 * t + 2 * k + p - 4, 8, stride=80), :] = (
                        plane[p, 2, t, v] * (1.0 if v == 0 else 1.6)
                    )

    def wait_conc():
        for core in range(2):
            slab = pltpu.make_async_copy(
                cz.at[:, pl.ds(0, 20)], conc0.at[:, :, pl.ds(8 + 16 * core, 16)], rc.at[core]
            )
            slab.wait()

        @pl.when(u > 0)
        def _():
            pltpu.make_async_copy(
                cz.at[:, pl.ds(0, 20), pl.ds(8, 8)], conc0.at[:, :, pl.ds(0, 8)], rc.at[2]
            ).wait()

    def rounds(step, _):
        @pl.when(step == 0)
        def _():
            early_come(0, 0, 4)
            early_come(1, 0, 2)

        @pl.when(step == 1)
        def _():
            early_come(1, 2, 2)

        @pl.when(jnp.logical_and(step > 1, step < PAIRS))
        def _():
            await_bytes(got1.at[pl.ds(2 * step, 2), pl.ds(0, 3)], r1.at[step])

        @pl.when(step < PAIRS)
        def _():
            for sub in range(2):
                b_contraction(2 * step + sub)
            for d in (4, 5, 2, 6, 3, 7, 1):
                second(step, d).start()

        @pl.when(step > 0)
        def _():
            await_bytes(got2.at[pl.ds(2 * step - 2, 2), pl.ds(0, 7)], r2.at[step - 1])
            for sub in range(2):
                a_contraction(2 * step - 2 + sub)

        @pl.when(step == 1)
        def _():
            for k in range(2):
                transport(k, True)

        @pl.when(step > 1)
        def _():
            def one(sub, _):
                transport(2 * step - 2 + sub, False)
                return 0

            lax.fori_loop(0, 2, one, 0)

        return 0

    turn_mask()
    wait_conc()
    await_bytes(listed.at[pl.ds(0, 7)], sn.at[1])
    for n in range(POINTS):
        for r in range(4):
            row = 4 * (n % 2) + r
            nodes[n, r] = jnp.broadcast_to(listed[n // 2, row : row + 1, :], (8, 128))
    lax.fori_loop(0, PAIRS + 1, rounds, 0)

    granule = lax.broadcasted_iota(jnp.int32, (16, 128), 1) // 16

    def regroup(which, _):
        half, yg = which // 4, which % 4
        arrays = []
        for yy in range(4):
            for v in range(2):
                row = pl.multiple_of(16 * (8 + 16 * half + 4 * yg + yy), 16)
                arrays.append(sums[v, pl.ds(row, 16), :])
        for bit in (4, 2, 1):
            clear = (granule // bit) % 2 == 0
            for m in range(8):
                if m // bit % 2 == 0:
                    one, two = arrays[m], arrays[m + bit]
                    arrays[m] = jnp.where(clear, one, pltpu.roll(two, 16 * bit, 1))
                    arrays[m + bit] = jnp.where(clear, pltpu.roll(one, 128 - 16 * bit, 1), two)
        for p in range(8):
            parcel[p, half, yg] = arrays[p]
        return 0

    zr = pl.multiple_of(16 * (4 * yy + 2 * xt + h), 16)

    def home(dp, half):
        to = (pts + dp) % 8
        return pltpu.make_async_remote_copy(
            src_ref=parcel.at[to, half],
            dst_ref=landed.at[:, pl.ds(zr, 16)],
            send_sem=so.at[0 if dp else 1 + half],
            recv_sem=ro.at[0],
            device_id={"pts": to, "py": i, "pz": 2 * c + half},
            device_id_type=MESH,
        )

    def home_own(half):
        return pltpu.make_async_copy(parcel.at[pts, half], landed.at[:, pl.ds(zr, 16)], ro.at[0])

    for half in range(2):
        lax.fori_loop(4 * half, 4 * half + 4, regroup, 0)
        here = jnp.logical_and(c == h, c == half)

        @pl.when(here)
        def _():
            home_own(half).start()

        @pl.when(jnp.logical_not(here))
        def _():
            home(0, half).start()

        for dp in range(1, 8):
            home(dp, half).start()

    await_bytes(landed, ro.at[0])

    for yg in range(4):
        for zh in range(2):
            turned = landed[yg, 128 * zh : 128 * zh + 128, :].T
            for y in range(4):
                for v in range(2):
                    e = 16 * (2 * y + v)
                    final[zh, pl.ds(16 * v + 4 * yg + y, 16, stride=32), :] = turned[e : e + 16]
    for zh in range(2):
        out[:, 128 * zh : 128 * zh + 128] = final[zh]

    await_bytes(share.at[pl.ds(0, 3 * 128 * NROUND)], s1.at[0])
    await_bytes(rows2.at[:, pl.ds(0, 7)], s2.at[0])
    await_bytes(listed.at[pl.ds(0, 7)], sn.at[0])
    await_bytes(parcel.at[pl.ds(0, 7)], so.at[0])
    for half in range(2):

        @pl.when(jnp.logical_not(jnp.logical_and(c == h, c == half)))
        def _():
            home(0, half).wait_send()

    for to_h in range(2):

        @pl.when(jnp.logical_not(slab_here(to_h)))
        def _():
            slab_copy(to_h).wait_send()

    @pl.when(jnp.logical_and(halo_some(), h == 1))
    def _():
        halo_copy(0).wait_send()

    @pl.when(halo_some())
    def _():
        halo_copy(1).wait_send()


def local(xi_map, basis, point_index, conc_start, well_mask, profile):
    (tz_hi, tz_lo), (cy_hi, cy_lo), (cx_hi, cx_lo) = tables()
    tz = np.concatenate([tz_hi, tz_lo, np.zeros((8, G, 48), ml_dtypes.bfloat16)], axis=2)
    cy = np.concatenate([cy_hi, cy_lo], axis=0)
    cx = np.concatenate([cx_hi, cx_lo], axis=0)

    vmem = pl.BlockSpec(memory_space=pltpu.VMEM)
    smem = pl.BlockSpec(memory_space=pltpu.SMEM)
    dma = pltpu.SemaphoreType.DMA
    far = pl.BlockSpec(memory_space=pl.ANY)
    total = pl.pallas_call(
        kernel,
        out_shape=jax.ShapeDtypeStruct((512, 256), F32),
        in_specs=[smem, smem] + [far] * 5 + [vmem] * 2,
        out_specs=vmem,
        scratch_shapes=[
            pltpu.VMEM((64, 64, 256), F32),
            pltpu.VMEM((3, 64, 64, 256), BF16),
            pltpu.VMEM((40 * 128, 128), F32),
            pltpu.VMEM((NROUND, 4, 4, 32, 128), F32),
            pltpu.VMEM((NROUND, 8, 40, 256), F32),
            pltpu.VMEM((NROUND, 8, 40, 256), F32),
            pltpu.VMEM((2, 20, 40, 128), F32),
            pltpu.VMEM((2, 2, 4, 40, 256), F32),
            pltpu.VMEM((POINTS, STEPS, 5, 2, 8, 128), F32),
            pltpu.VMEM((2, 3, 5, 2, 8, 128), F32),
            pltpu.VMEM((64, 256), F32),
            pltpu.VMEM((8, 128), F32),
            pltpu.VMEM((8, 8, 128), F32),
            pltpu.VMEM((POINTS, 4, 8, 128), F32),
            pltpu.VMEM((2, 640, 128), F32),
            pltpu.VMEM((8, 2, 4, 16, 128), F32),
            pltpu.VMEM((4, 256, 128), F32),
            pltpu.VMEM((2, 512, 128), F32),
            pltpu.VMEM((256, 128), BF16),
            pltpu.VMEM((2, 4096, 128), F32),
            pltpu.VMEM((8, 272, 128), F32),
            pltpu.VMEM((2, 640, 128), F32),
            pltpu.VMEM((2, 256, 128), jnp.int32),
            pltpu.VMEM((2, 264, 128), F32),
            pltpu.VMEM((2, 40, 128), F32),
            dma((3,)),
            dma((1,)),
            dma((PAIRS,)),
            dma((1,)),
            dma((PAIRS,)),
            dma((4,)),
            dma((3,)),
            dma((4, 2)),
            dma((5,)),
            dma((2,)),
            dma((3,)),
            dma((1,)),
        ],
        compiler_params=pltpu.CompilerParams(
            collective_id=0, has_side_effects=True, vmem_limit_bytes=60 * 2**20
        ),
    )(point_index, profile, xi_map, basis, conc_start.reshape(4096, 256), well_mask, tz, cy, cx)
    return total.reshape(32, 16, 256)


def solution(mesh):
    placed = (
        P("py", "pz", None),
        P(None, "py", "pz", None),
        P("pts", None),
        P(None, ("py", "pz"), None),
        P(),
        P(),
    )
    return jax.shard_map(
        local, mesh=mesh, in_specs=placed, out_specs=P("pts", ("py", "pz"), None), check_vma=False
    )
```

```python
import functools

import jax
import jax.numpy as jnp
import ml_dtypes
import numpy as np
from jax import lax
from jax.experimental import pallas as pl
from jax.experimental.pallas import tpu as pltpu
from jax.sharding import PartitionSpec as P

MESH = pl.DeviceIdType.MESH
STEPS = 4
POINTS = 16
BATCH = 2
G = 256
NROUND = 10
PAIRS = 5
ROOT3 = 1.7320508075688772
F32 = jnp.float32
BF16 = jnp.bfloat16
NT = (((1,), (1,)), ((), ()))


def split_table(table):
    table = np.asarray(table, np.float64)
    high = table.astype(np.float32).astype(ml_dtypes.bfloat16)
    low = (table - high.astype(np.float64)).astype(np.float32).astype(ml_dtypes.bfloat16)
    return high, low


def tables():
    spots = np.arange(G, dtype=np.float64)
    full = np.sqrt(2.0 / G) * np.cos(np.pi * (spots[:, None] + 0.5) * spots[None, :] / G)
    full[:, 0] *= np.sqrt(0.5)
    tz = np.zeros((8, 40, G))
    for g in range(8):
        for par in range(2):
            for w in range(18):
                z = 32 * g - 4 + 2 * w + par
                if z >= 0:
                    tz[g, 20 * par + w] = full[z]
    tz = tz.transpose(0, 2, 1)
    cy = np.zeros((8, 5, 8, G))
    for u in range(8):
        for t in range(5):
            for q in range(8):
                y = 32 * u - 8 + 5 * q + t
                if y >= 0:
                    cy[u, t, q] = full[y]
    cx = 0.5 * np.concatenate([full[0::2], full[1::2]], axis=0).T
    return split_table(tz), split_table(cy.reshape(320, G)), split_table(cx)


def halves(value):
    high = value.astype(BF16)
    low = (value - high.astype(F32)).astype(BF16)
    return high, low


def kernel(
    point,
    prof,
    xi_far,
    basis_far,
    conc_far,
    mask_far,
    tz_far,
    cy,
    cx,
    out,
    xi,
    basis,
    share,
    got1,
    rows2,
    got2,
    conc0,
    fields,
    carry,
    plane,
    wave,
    mine,
    listed,
    nodes,
    sums,
    parcel,
    landed,
    final,
    tz,
    start,
    turned_z,
    cz_flat,
    wells,
    turned_y,
    mask,
    r0,
    s1,
    r1,
    s2,
    r2,
    r3,
    sc,
    rc,
    load,
    prep,
    sn,
    so,
    ro,
):
    pts = lax.axis_index("pts")
    i = lax.axis_index("py")
    pz = lax.axis_index("pz")
    yy, x_lo = pts // 2, pts % 2
    h, c = pz // 2, pz % 2
    xt = (x_lo + h) % 2
    u = 2 * i + c
    g = 2 * yy + xt
    cz = cz_flat.reshape(2, 40, 16, 128)

    def at(i_, h_, c_):
        return {"pts": 2 * yy + (xt + h_) % 2, "py": i_, "pz": 2 * h_ + c_}

    def await_bytes(view, sem):
        pltpu.make_async_copy(view, view, sem).wait()

    barrier = pltpu.get_barrier_semaphore()
    peers = []
    for dp in range(8):
        for dh in range(2):
            for dc in range(2):
                if dp + dh + dc > 0:
                    peers.append({"pts": (pts + dp) % 8, "py": i, "pz": 2 * ((h + dh) % 2) + (c + dc) % 2})
    for di in range(1, 4):
        for dh in range(2):
            for dc in range(2):
                peers.append(at((i + di) % 4, (h + dh) % 2, (c + dc) % 2))
    for peer in peers:
        pl.semaphore_signal(barrier, inc=1, device_id=peer, device_id_type=MESH)

    def loads(q):
        copies = []
        for half in range(2):
            rows = pl.ds(pl.multiple_of(8 * q + 32 * half, 8), 8)
            copies.append(pltpu.make_async_copy(xi_far.at[rows], xi.at[rows], load.at[q, 0]))
            copies.append(
                pltpu.make_async_copy(basis_far.at[:, rows], basis.at[:, rows], load.at[q, 1])
            )
        return copies

    def start_loads(q, _):
        for copy in loads(q):
            copy.start()
        return 0

    def load_conc(zh):
        return pltpu.make_async_copy(
            conc_far.at[:, pl.ds(128 * zh, 128)], start.at[zh], prep.at[zh]
        )

    def load_mask(yh):
        return pltpu.make_async_copy(
            mask_far.at[:, pl.ds(128 * yh, 128)], wells.at[yh], prep.at[2 + yh]
        )

    load_tz = pltpu.make_async_copy(tz_far.at[g], tz, prep.at[4])
    some_z = [g <= 4, g >= 4]
    for zh in range(2):

        @pl.when(some_z[zh])
        def _():
            load_conc(zh).start()

    load_tz.start()
    lax.fori_loop(0, 4, start_loads, 0)
    for yh in range(2):
        load_mask(yh).start()

    def slab_copy(to_h):
        return pltpu.make_async_remote_copy(
            src_ref=cz.at[:, pl.ds(16 * to_h, 20)],
            dst_ref=conc0.at[:, :, pl.ds(pl.multiple_of(8 + 16 * c, 8), 16)],
            send_sem=sc.at[to_h],
            recv_sem=rc.at[c],
            device_id=at(i, to_h, h),
            device_id_type=MESH,
        )

    def slab_local(to_h):
        return pltpu.make_async_copy(
            cz.at[:, pl.ds(16 * to_h, 20)],
            conc0.at[:, :, pl.ds(pl.multiple_of(8 + 16 * c, 8), 16)],
            rc.at[c],
        )

    above = 2 * i + h + 1

    def halo_copy(to_h):
        return pltpu.make_async_remote_copy(
            src_ref=cz.at[:, pl.ds(16 * to_h, 20), pl.ds(8, 8)],
            dst_ref=conc0.at[:, :, pl.ds(0, 8)],
            send_sem=sc.at[2 + to_h],
            recv_sem=rc.at[2],
            device_id=at((above // 2) % 4, to_h, above % 2),
            device_id_type=MESH,
        )

    def halo_local(to_h):
        return pltpu.make_async_copy(
            cz.at[:, pl.ds(16 * to_h, 20), pl.ds(8, 8)], conc0.at[:, :, pl.ds(0, 8)], rc.at[2]
        )

    def slab_here(to_h):
        return jnp.logical_and(h == to_h, c == to_h)

    def halo_some():
        return jnp.logical_and(c == 1, above < 8)

    for m in range(2):
        weight = 1.0
        for r in range(3):
            index = point[m, r]
            value = jnp.where(index == 0, -ROOT3, jnp.where(index == 1, 0.0, ROOT3))
            weight = weight * jnp.where(index == 1, 2.0 / 3.0, 1.0 / 6.0)
            mine[4 * m + r : 4 * m + r + 1, :] = jnp.full((1, 128), value, F32)
        mine[4 * m + 3 : 4 * m + 4, :] = jnp.full((1, 128), weight, F32)

    def node_copy(dp):
        return pltpu.make_async_remote_copy(
            src_ref=mine,
            dst_ref=listed.at[pts],
            send_sem=sn.at[0],
            recv_sem=sn.at[1],
            device_id={"pts": (pts + dp) % 8, "py": i, "pz": pz},
            device_id_type=MESH,
        )

    turned_z[:, 0:8, :] = jnp.zeros((8, 8, 128), F32)
    for zh in range(2):

        @pl.when(some_z[zh])
        def _():
            load_conc(zh).wait()

    def turn_conc(y4, _):
        rows = [(m, v) for m in range(4) for v in range(2)]
        for zh in range(2):

            @pl.when(some_z[zh])
            def _():
                for m, v in rows:
                    turned_z[2 * m + v, 4 + 128 * zh : 132 + 128 * zh, :] = start[
                        zh, pl.ds(16 * v + 4 * y4 + m, 128, stride=32), :
                    ].T

        for m, v in rows:
            cz_flat[v, pl.ds(4 * y4 + m, 40, stride=16), :] = turned_z[
                2 * m + v, pl.ds(pl.multiple_of(32 * g, 32), 40), :
            ]
        return 0

    lax.fori_loop(0, 4, turn_conc, 0)

    def turn_mask():
        turned_y[:, 0:8, :] = jnp.zeros((2, 8, 128), F32)
        for yh in range(2):
            load_mask(yh).wait()
            for v in range(2):
                block = wells[yh, pl.ds(v, 128, stride=2), :].astype(F32)
                turned_y[v, 8 + 128 * yh : 136 + 128 * yh, :] = 0.5 * block.T
        for v in range(2):
            for t in range(5):
                mask[v, 8 * t : 8 * t + 8, :] = turned_y[v, pl.ds(32 * u + t, 8, stride=5), :]

    def greet():
        pl.semaphore_wait(barrier, len(peers))
        for dp in range(1, 8):
            node_copy(dp).start()
        listed[pts] = mine[...]
        for to_h in range(2):

            @pl.when(slab_here(to_h))
            def _():
                slab_local(to_h).start()

            @pl.when(jnp.logical_not(slab_here(to_h)))
            def _():
                slab_copy(to_h).start()

        @pl.when(jnp.logical_and(halo_some(), h == 0))
        def _():
            halo_local(0).start()

        @pl.when(jnp.logical_and(halo_some(), h == 1))
        def _():
            halo_copy(0).start()

        @pl.when(halo_some())
        def _():
            halo_copy(1).start()

        @pl.when(u == 0)
        def _():
            conc0[:, :, 0:8, :] = jnp.zeros((2, 20, 8, 128), F32)

    spot_b = (lax.broadcasted_iota(jnp.int32, (64, G), 0) + 64 * pz).astype(F32)
    spot_c = lax.broadcasted_iota(jnp.int32, (64, G), 1).astype(F32)
    wave[...] = 64.0 + spot_b * spot_b + spot_c * spot_c
    front = 64.0 * 0.9 * (32.0**1.5)

    def stage(step, _):
        amps = []
        for part in range(2):
            for half in range(2):
                a = (64 * i + 2 * step + part + 32 * half).astype(F32)
                amps.append(front / (wave[...] + a * a))
        for f in range(4):
            parts = []
            for part in range(2):
                for half in range(2):
                    row = 2 * step + part + 32 * half
                    value = xi[row] if f == 0 else basis[f - 1, row].astype(F32)
                    parts.append(value * amps[2 * part + half])
            high, low = halves(jnp.concatenate(parts, axis=0))
            both = jnp.dot(jnp.concatenate([high, low], axis=0), tz[...], preferred_element_type=F32)
            both = (both[0:256] + both[256:512]).T
            total = both[0:40] + both[40:80]
            for part in range(2):
                share[pl.ds(32 * f + 2 * step + part, 40, stride=128), :] = total[
                    :, 128 * part : 128 * part + 128
                ]
        return 0

    def stages(part, _):
        for q in range(2):
            await_bytes(xi.at[pl.ds(0, 16)], load.at[2 * part + q, 0])
            await_bytes(basis.at[:, pl.ds(0, 16)], load.at[2 * part + q, 1])
            lax.fori_loop(8 * part + 4 * q, 8 * part + 4 * q + 4, stage, 0)

        @pl.when(part == 0)
        def _():
            for d in (2, 3, 1):
                early(0, 0, 2, d).start()

        @pl.when(part == 1)
        def _():
            for begin in (0, 1):
                for d in (2, 3, 1):
                    early(1, begin, 1, d).start()

        return 0

    blocks = share.reshape(40, 4, 32, 128)

    def early(part, begin, count, d):
        to_h, to_c = (h + d // 2) % 2, (c + d % 2) % 2
        rows = pl.ds(16 * part, 16)
        return pltpu.make_async_remote_copy(
            src_ref=blocks.at[pl.ds(20 * to_c + 8 * to_h + begin, count), :, rows],
            dst_ref=got1.at[pl.ds(begin, count), pz, :, rows],
            send_sem=s1.at[0],
            recv_sem=r0.at[part + begin],
            device_id=at(i, to_h, to_c),
            device_id_type=MESH,
        )

    def early_come(part, begin, count):
        await_bytes(
            got1.at[pl.ds(begin, count), pl.ds(0, 3), :, pl.ds(16 * part, 16)], r0.at[part + begin]
        )

    greet()
    load_tz.wait()
    lax.fori_loop(0, 2, stages, 0)

    def first(pair, d):
        to_h, to_c = (h + d // 2) % 2, (c + d % 2) % 2
        return pltpu.make_async_remote_copy(
            src_ref=blocks.at[pl.ds(20 * to_c + 8 * to_h + 2 * pair, 2)],
            dst_ref=got1.at[pl.ds(2 * pair, 2), pz],
            send_sem=s1.at[0],
            recv_sem=r1.at[pair],
            device_id=at(i, to_h, to_c),
            device_id_type=MESH,
        )

    def send_first(pair, _):
        for d in (2, 3, 1):
            first(pair, d).start()
        return 0

    lax.fori_loop(1, PAIRS, send_first, 0)

    def second(pair, d):
        to_i, to_c = (i + d // 2) % 4, (c + d % 2) % 2
        return pltpu.make_async_remote_copy(
            src_ref=rows2.at[pl.ds(2 * pair, 2), 2 * to_i + to_c],
            dst_ref=got2.at[pl.ds(2 * pair, 2), 4 * c + i],
            send_sem=s2.at[0],
            recv_sem=r2.at[pair],
            device_id=at(to_i, h, to_c),
            device_id_type=MESH,
        )

    def single(k, d):
        to_i, to_c = (i + d // 2) % 4, (c + d % 2) % 2
        return pltpu.make_async_remote_copy(
            src_ref=rows2.at[k, 2 * to_i + to_c],
            dst_ref=got2.at[k, 4 * c + i],
            send_sem=s2.at[0],
            recv_sem=r3.at[k % 2 + 2 * (k // 8)],
            device_id=at(to_i, h, to_c),
            device_id_type=MESH,
        )

    def single_come(k):
        await_bytes(got2.at[k, pl.ds(0, 7)], r3.at[k % 2 + 2 * (k // 8)])

    lane = lax.broadcasted_iota(jnp.int32, (128, 128), 1)
    lane_low = lane < 64
    lane8 = lax.broadcasted_iota(jnp.int32, (8, 128), 1)
    edge = jnp.where(lane8 > 0, 1.6 * 1.6, 0.0).astype(F32)
    lane40 = lax.broadcasted_iota(jnp.int32, (40, 128), 1) < 64

    def b_contraction(k):
        own = share[pl.ds(pl.multiple_of((20 * c + 8 * h + k) * 128, 128), 128), :]
        got1[k, pz] = own.reshape(4, 32, 128)
        sides = [[], []]
        for pair in range(2):
            one, two = (got1[k, 2 * pair + m].reshape(128, 128) for m in range(2))
            sides[0].append(jnp.where(lane_low, one, pltpu.roll(two, 64, 1)))
            sides[1].append(jnp.where(lane_low, pltpu.roll(one, 64, 1), two))
        both = [jnp.concatenate(side, axis=1) for side in sides]
        rows = []
        for f in range(4):
            rows += [both[0][32 * f : 32 * f + 32], both[1][32 * f : 32 * f + 32]]
        high, low = halves(jnp.concatenate(rows, axis=0))
        both = lax.dot_general(cy[...], high, NT, preferred_element_type=F32)
        rest = lax.dot_general(cy[0:320], low, NT, preferred_element_type=F32)
        total = both[0:320] + both[320:640] + rest
        for slab in range(8):
            rows2[k, slab] = total[40 * slab : 40 * slab + 40]
        got2[k, 4 * c + i] = rows2[k, u]

    def a_contraction(k):
        rows = []
        for core in range(2):
            for pair in range(2):
                cols = [[], []]
                for group in range(2):
                    one = got2[k, 4 * core + 2 * group, :, 128 * pair : 128 * pair + 128]
                    two = got2[k, 4 * core + 2 * group + 1, :, 128 * pair : 128 * pair + 128]
                    cols[0].append(jnp.where(lane40, one, pltpu.roll(two, 64, 1)))
                    cols[1].append(jnp.where(lane40, pltpu.roll(one, 64, 1), two))
                rows += [jnp.concatenate(col, axis=1) for col in cols]
        high, low = halves(jnp.concatenate(rows, axis=0))
        both = jnp.dot(jnp.concatenate([high, low], axis=0), cx[0:256], preferred_element_type=F32)
        total = both[0:320] + both[320:640]
        total += jnp.dot(high, cx[256:512], preferred_element_type=F32)
        for core in range(2):
            for f in range(4):
                row = 160 * core + 40 * f
                fields[k % 2, core, f] = total[row : row + 40]

    tiles = [(t, v) for t in range(5) for v in range(2)]

    def transport(k, halo):
        sub = k % 2
        levels = range(2)
        for p in levels:
            zz = 2 * k + p
            spot_z = 16 * (2 * g + h) - 4 + zz
            well = jnp.where(spot_z >= 0, prof[jnp.maximum(spot_z, 0)], 0.0)
            for t, v in tiles:
                share_v = 1.0 if v == 0 else 1.0 / 1.6
                plane[p, 0, t, v] = conc0[v, zz, pl.ds(t, 8, stride=5), :] * share_v
                plane[p, 1, t, v] = mask[v, 8 * t : 8 * t + 8, :] * (well * share_v)
                if not halo:
                    plane[p, 2, t, v] = jnp.zeros((8, 128), F32)

        def some_points(group, _):
            each = [(m, p) for m in range(BATCH) for p in levels]
            speed, conc = {e: {} for e in each}, {e: {} for e in each}
            for m, p in each:
                n = BATCH * group + m
                node = [nodes[n, r] for r in range(3)]
                for t, v in tiles:
                    logs = [
                        fields[sub, p, f, 8 * t : 8 * t + 8, 128 * v : 128 * v + 128] for f in range(4)
                    ]
                    value = logs[0] + node[0] * logs[1] + node[1] * logs[2] + node[2] * logs[3]
                    speed[m, p][t, v] = 0.125 + 0.125 * jnp.tanh(value)
                    conc[m, p][t, v] = plane[p, 0, t, v]
            for step in range(STEPS):
                flux = {
                    (m, p): {tv: speed[m, p][tv] * conc[m, p][tv] for tv in tiles}
                    for m, p in each
                    if not halo or step <= 2 * k + p
                }
                for t, v in tiles:
                    for m, p in each:
                        if (m, p) not in flux:
                            continue
                        n = BATCH * group + m
                        here = flux[m, p]
                        more = not halo or step < 2 * k + p
                        if more:
                            behind = carry[n, step, t, v] if p == 0 else flux[m, 0][t, v]
                        if p == 1:
                            carry[n, step, t, v] = here[t, v]
                        if not more:
                            continue
                        prev_b = here[t - 1, v] if t > 0 else pltpu.roll(here[4, v], 1, 0)
                        prev_a = here[t, 0] if v == 1 else edge * pltpu.roll(here[t, 1], 1, 1)
                        conc[m, p][t, v] = (
                            (conc[m, p][t, v] - 3.6 * here[t, v])
                            + (plane[p, 1, t, v] + behind)
                            + (prev_b + prev_a)
                        )
            if not halo:
                for p in levels:
                    for t, v in tiles:
                        part = nodes[BATCH * group, 3] * conc[0, p][t, v]
                        for m in range(1, BATCH):
                            part += nodes[BATCH * group + m, 3] * conc[m, p][t, v]
                        plane[p, 2, t, v] += part
            return 0

        lax.fori_loop(0, POINTS // BATCH, some_points, 0)
        if not halo:
            for p in levels:
                for t, v in tiles:
                    sums[v, pl.ds(16 * t + 2 * k + p - 4, 8, stride=80), :] = (
                        plane[p, 2, t, v] * (1.0 if v == 0 else 1.6)
                    )

    def wait_conc():
        for core in range(2):
            slab = pltpu.make_async_copy(
                cz.at[:, pl.ds(0, 20)], conc0.at[:, :, pl.ds(8 + 16 * core, 16)], rc.at[core]
            )
            slab.wait()

        @pl.when(u > 0)
        def _():
            pltpu.make_async_copy(
                cz.at[:, pl.ds(0, 20), pl.ds(8, 8)], conc0.at[:, :, pl.ds(0, 8)], rc.at[2]
            ).wait()

    def rounds(step, _):
        @pl.when(step == 0)
        def _():
            early_come(0, 0, 2)

        @pl.when(step > 0)
        def _():
            @pl.when(step < PAIRS)
            def _():
                await_bytes(got1.at[pl.ds(2 * step, 2), pl.ds(0, 3)], r1.at[step])

        @pl.when(jnp.logical_or(step == 0, step == PAIRS - 1))
        def _():
            def one(k, _):
                for begin in (0, 1):

                    @pl.when(k == begin)
                    def _():
                        early_come(1, begin, 1)

                b_contraction(k)
                for d in (4, 5, 2, 6, 3, 7, 1):
                    single(k, d).start()
                return 0

            lax.fori_loop(2 * step, 2 * step + 2, one, 0)

        @pl.when(jnp.logical_and(step > 0, step < PAIRS - 1))
        def _():
            for sub in range(2):
                b_contraction(2 * step + sub)
            for d in (4, 5, 2, 6, 3, 7, 1):
                second(step, d).start()

        @pl.when(step == 1)
        def _():
            for k in range(2):
                single_come(k)
                a_contraction(k)
                transport(k, True)

        @pl.when(jnp.logical_and(step > 1, step < PAIRS))
        def _():
            await_bytes(got2.at[pl.ds(2 * step - 2, 2), pl.ds(0, 7)], r2.at[step - 1])
            for sub in range(2):
                a_contraction(2 * step - 2 + sub)

            def one(sub, _):
                transport(2 * step - 2 + sub, False)
                return 0

            lax.fori_loop(0, 2, one, 0)

        @pl.when(step == PAIRS)
        def _():
            def one(k, _):
                single_come(k)
                a_contraction(k)
                transport(k, False)
                return 0

            lax.fori_loop(2 * PAIRS - 2, 2 * PAIRS, one, 0)

        return 0

    turn_mask()
    wait_conc()
    await_bytes(listed.at[pl.ds(0, 7)], sn.at[1])
    for n in range(POINTS):
        for r in range(4):
            row = 4 * (n % 2) + r
            nodes[n, r] = jnp.broadcast_to(listed[n // 2, row : row + 1, :], (8, 128))
    lax.fori_loop(0, PAIRS + 1, rounds, 0)

    granule = lax.broadcasted_iota(jnp.int32, (16, 128), 1) // 16

    def regroup(which, _):
        half, yg = which // 4, which % 4
        arrays = []
        for yy in range(4):
            for v in range(2):
                row = pl.multiple_of(16 * (8 + 16 * half + 4 * yg + yy), 16)
                arrays.append(sums[v, pl.ds(row, 16), :])
        for bit in (4, 2, 1):
            clear = (granule // bit) % 2 == 0
            for m in range(8):
                if m // bit % 2 == 0:
                    one, two = arrays[m], arrays[m + bit]
                    arrays[m] = jnp.where(clear, one, pltpu.roll(two, 16 * bit, 1))
                    arrays[m + bit] = jnp.where(clear, pltpu.roll(one, 128 - 16 * bit, 1), two)
        for p in range(8):
            parcel[p, half, yg] = arrays[p]
        return 0

    zr = pl.multiple_of(16 * (4 * yy + 2 * xt + h), 16)

    def home(dp, half):
        to = (pts + dp) % 8
        return pltpu.make_async_remote_copy(
            src_ref=parcel.at[to, half],
            dst_ref=landed.at[:, pl.ds(zr, 16)],
            send_sem=so.at[0 if dp else 1 + half],
            recv_sem=ro.at[0],
            device_id={"pts": to, "py": i, "pz": 2 * c + half},
            device_id_type=MESH,
        )

    def home_own(half):
        return pltpu.make_async_copy(parcel.at[pts, half], landed.at[:, pl.ds(zr, 16)], ro.at[0])

    for half in range(2):
        lax.fori_loop(4 * half, 4 * half + 4, regroup, 0)
        here = jnp.logical_and(c == h, c == half)

        @pl.when(here)
        def _():
            home_own(half).start()

        @pl.when(jnp.logical_not(here))
        def _():
            home(0, half).start()

        for dp in range(1, 8):
            home(dp, half).start()

    await_bytes(landed, ro.at[0])

    for yg in range(4):
        for zh in range(2):
            turned = landed[yg, 128 * zh : 128 * zh + 128, :].T
            for y in range(4):
                for v in range(2):
                    e = 16 * (2 * y + v)
                    final[zh, pl.ds(16 * v + 4 * yg + y, 16, stride=32), :] = turned[e : e + 16]
    for zh in range(2):
        out[:, 128 * zh : 128 * zh + 128] = final[zh]

    await_bytes(share.at[pl.ds(0, 3 * 128 * NROUND)], s1.at[0])
    await_bytes(rows2.at[:, pl.ds(0, 7)], s2.at[0])
    await_bytes(listed.at[pl.ds(0, 7)], sn.at[0])
    await_bytes(parcel.at[pl.ds(0, 7)], so.at[0])
    for half in range(2):

        @pl.when(jnp.logical_not(jnp.logical_and(c == h, c == half)))
        def _():
            home(0, half).wait_send()

    for to_h in range(2):

        @pl.when(jnp.logical_not(slab_here(to_h)))
        def _():
            slab_copy(to_h).wait_send()

    @pl.when(jnp.logical_and(halo_some(), h == 1))
    def _():
        halo_copy(0).wait_send()

    @pl.when(halo_some())
    def _():
        halo_copy(1).wait_send()


def local(xi_map, basis, point_index, conc_start, well_mask, profile):
    (tz_hi, tz_lo), (cy_hi, cy_lo), (cx_hi, cx_lo) = tables()
    tz = np.concatenate([tz_hi, tz_lo, np.zeros((8, G, 48), ml_dtypes.bfloat16)], axis=2)
    cy = np.concatenate([cy_hi, cy_lo], axis=0)
    cx = np.concatenate([cx_hi, cx_lo], axis=0)

    vmem = pl.BlockSpec(memory_space=pltpu.VMEM)
    smem = pl.BlockSpec(memory_space=pltpu.SMEM)
    dma = pltpu.SemaphoreType.DMA
    far = pl.BlockSpec(memory_space=pl.ANY)
    total = pl.pallas_call(
        kernel,
        out_shape=jax.ShapeDtypeStruct((512, 256), F32),
        in_specs=[smem, smem] + [far] * 5 + [vmem] * 2,
        out_specs=vmem,
        scratch_shapes=[
            pltpu.VMEM((64, 64, 256), F32),
            pltpu.VMEM((3, 64, 64, 256), BF16),
            pltpu.VMEM((40 * 128, 128), F32),
            pltpu.VMEM((NROUND, 4, 4, 32, 128), F32),
            pltpu.VMEM((NROUND, 8, 40, 256), F32),
            pltpu.VMEM((NROUND, 8, 40, 256), F32),
            pltpu.VMEM((2, 20, 40, 128), F32),
            pltpu.VMEM((2, 2, 4, 40, 256), F32),
            pltpu.VMEM((POINTS, STEPS, 5, 2, 8, 128), F32),
            pltpu.VMEM((2, 3, 5, 2, 8, 128), F32),
            pltpu.VMEM((64, 256), F32),
            pltpu.VMEM((8, 128), F32),
            pltpu.VMEM((8, 8, 128), F32),
            pltpu.VMEM((POINTS, 4, 8, 128), F32),
            pltpu.VMEM((2, 640, 128), F32),
            pltpu.VMEM((8, 2, 4, 16, 128), F32),
            pltpu.VMEM((4, 256, 128), F32),
            pltpu.VMEM((2, 512, 128), F32),
            pltpu.VMEM((256, 128), BF16),
            pltpu.VMEM((2, 4096, 128), F32),
            pltpu.VMEM((8, 272, 128), F32),
            pltpu.VMEM((2, 640, 128), F32),
            pltpu.VMEM((2, 256, 128), jnp.int32),
            pltpu.VMEM((2, 264, 128), F32),
            pltpu.VMEM((2, 40, 128), F32),
            dma((3,)),
            dma((1,)),
            dma((PAIRS,)),
            dma((1,)),
            dma((PAIRS,)),
            dma((4,)),
            dma((4,)),
            dma((3,)),
            dma((4, 2)),
            dma((5,)),
            dma((2,)),
            dma((3,)),
            dma((1,)),
        ],
        compiler_params=pltpu.CompilerParams(
            collective_id=0, has_side_effects=True, vmem_limit_bytes=60 * 2**20
        ),
    )(point_index, profile, xi_map, basis, conc_start.reshape(4096, 256), well_mask, tz, cy, cx)
    return total.reshape(32, 16, 256)


def solution(mesh):
    placed = (
        P("py", "pz", None),
        P(None, "py", "pz", None),
        P("pts", None),
        P(None, ("py", "pz"), None),
        P(),
        P(),
    )
    return jax.shard_map(
        local, mesh=mesh, in_specs=placed, out_specs=P("pts", ("py", "pz"), None), check_vma=False
    )
```

```python
import functools

import jax
import jax.numpy as jnp
import ml_dtypes
import numpy as np
from jax import lax
from jax.experimental import pallas as pl
from jax.experimental.pallas import tpu as pltpu
from jax.sharding import PartitionSpec as P

MESH = pl.DeviceIdType.MESH
STEPS = 4
POINTS = 16
BATCH = 2
G = 256
NROUND = 10
PAIRS = 5
ROOT3 = 1.7320508075688772
F32 = jnp.float32
BF16 = jnp.bfloat16
NT = (((1,), (1,)), ((), ()))


def split_table(table):
    table = np.asarray(table, np.float64)
    high = table.astype(np.float32).astype(ml_dtypes.bfloat16)
    low = (table - high.astype(np.float64)).astype(np.float32).astype(ml_dtypes.bfloat16)
    return high, low


def tables():
    spots = np.arange(G, dtype=np.float64)
    full = np.sqrt(2.0 / G) * np.cos(np.pi * (spots[:, None] + 0.5) * spots[None, :] / G)
    full[:, 0] *= np.sqrt(0.5)
    tz = np.zeros((8, 40, G))
    for g in range(8):
        for par in range(2):
            for w in range(18):
                z = 32 * g - 4 + 2 * w + par
                if z >= 0:
                    tz[g, 20 * par + w] = full[z]
    tz = tz.transpose(0, 2, 1)
    cy = np.zeros((8, 40, G))
    for u in range(8):
        for t in range(5):
            for q in range(8):
                y = 32 * u - 8 + 5 * q + t
                if y >= 0 and (t == 4 or q > 0):
                    cy[u, q if t == 4 else 7 + 7 * t + q] = full[y]
    cx = 0.5 * np.concatenate([full[0::2], full[1::2]], axis=0).T
    return split_table(tz), split_table(cy.reshape(320, G)), split_table(cx)


def halves(value):
    high = value.astype(BF16)
    low = (value - high.astype(F32)).astype(BF16)
    return high, low


def kernel(
    point,
    prof,
    xi_far,
    basis_far,
    conc_far,
    mask_far,
    tz_far,
    cy,
    cx,
    out,
    xi,
    basis,
    share,
    got1,
    rows2,
    got2,
    conc0,
    fields,
    carry,
    plane,
    wave,
    mine,
    listed,
    nodes,
    sums,
    parcel,
    landed,
    final,
    tz,
    start,
    turned_z,
    cz_flat,
    wells,
    turned_y,
    mask,
    r0,
    s1,
    r1,
    s2,
    r2,
    r3,
    sc,
    rc,
    load,
    prep,
    sn,
    so,
    ro,
):
    pts = lax.axis_index("pts")
    i = lax.axis_index("py")
    pz = lax.axis_index("pz")
    yy, x_lo = pts // 2, pts % 2
    h, c = pz // 2, pz % 2
    xt = (x_lo + h) % 2
    u = 2 * i + c
    g = 2 * yy + xt
    cz = cz_flat.reshape(2, 40, 16, 128)

    def at(i_, h_, c_):
        return {"pts": 2 * yy + (xt + h_) % 2, "py": i_, "pz": 2 * h_ + c_}

    def await_bytes(view, sem):
        pltpu.make_async_copy(view, view, sem).wait()

    barrier = pltpu.get_barrier_semaphore()
    peers = []
    for dp in range(8):
        for dh in range(2):
            for dc in range(2):
                if dp + dh + dc > 0:
                    peers.append({"pts": (pts + dp) % 8, "py": i, "pz": 2 * ((h + dh) % 2) + (c + dc) % 2})
    for di in range(1, 4):
        for dh in range(2):
            for dc in range(2):
                peers.append(at((i + di) % 4, (h + dh) % 2, (c + dc) % 2))
    for peer in peers:
        pl.semaphore_signal(barrier, inc=1, device_id=peer, device_id_type=MESH)

    def loads(q):
        copies = []
        for half in range(2):
            rows = pl.ds(pl.multiple_of(8 * q + 32 * half, 8), 8)
            copies.append(pltpu.make_async_copy(xi_far.at[rows], xi.at[rows], load.at[q, 0]))
            copies.append(
                pltpu.make_async_copy(basis_far.at[:, rows], basis.at[:, rows], load.at[q, 1])
            )
        return copies

    def start_loads(q, _):
        for copy in loads(q):
            copy.start()
        return 0

    def load_conc(zh):
        return pltpu.make_async_copy(
            conc_far.at[:, pl.ds(128 * zh, 128)], start.at[zh], prep.at[zh]
        )

    def load_mask(yh):
        return pltpu.make_async_copy(
            mask_far.at[:, pl.ds(128 * yh, 128)], wells.at[yh], prep.at[2 + yh]
        )

    load_tz = pltpu.make_async_copy(tz_far.at[g], tz, prep.at[4])
    some_z = [g <= 4, g >= 4]
    for zh in range(2):

        @pl.when(some_z[zh])
        def _():
            load_conc(zh).start()

    load_tz.start()
    lax.fori_loop(0, 4, start_loads, 0)
    for yh in range(2):
        load_mask(yh).start()

    def slab_copy(to_h):
        return pltpu.make_async_remote_copy(
            src_ref=cz.at[:, pl.ds(16 * to_h, 20)],
            dst_ref=conc0.at[:, :, pl.ds(pl.multiple_of(8 + 16 * c, 8), 16)],
            send_sem=sc.at[to_h],
            recv_sem=rc.at[c],
            device_id=at(i, to_h, h),
            device_id_type=MESH,
        )

    def slab_local(to_h):
        return pltpu.make_async_copy(
            cz.at[:, pl.ds(16 * to_h, 20)],
            conc0.at[:, :, pl.ds(pl.multiple_of(8 + 16 * c, 8), 16)],
            rc.at[c],
        )

    above = 2 * i + h + 1

    def halo_copy(to_h):
        return pltpu.make_async_remote_copy(
            src_ref=cz.at[:, pl.ds(16 * to_h, 20), pl.ds(8, 8)],
            dst_ref=conc0.at[:, :, pl.ds(0, 8)],
            send_sem=sc.at[2 + to_h],
            recv_sem=rc.at[2],
            device_id=at((above // 2) % 4, to_h, above % 2),
            device_id_type=MESH,
        )

    def halo_local(to_h):
        return pltpu.make_async_copy(
            cz.at[:, pl.ds(16 * to_h, 20), pl.ds(8, 8)], conc0.at[:, :, pl.ds(0, 8)], rc.at[2]
        )

    def slab_here(to_h):
        return jnp.logical_and(h == to_h, c == to_h)

    def halo_some():
        return jnp.logical_and(c == 1, above < 8)

    for m in range(2):
        weight = 1.0
        for r in range(3):
            index = point[m, r]
            value = jnp.where(index == 0, -ROOT3, jnp.where(index == 1, 0.0, ROOT3))
            weight = weight * jnp.where(index == 1, 2.0 / 3.0, 1.0 / 6.0)
            mine[4 * m + r : 4 * m + r + 1, :] = jnp.full((1, 128), value, F32)
        mine[4 * m + 3 : 4 * m + 4, :] = jnp.full((1, 128), weight, F32)

    def node_copy(dp):
        return pltpu.make_async_remote_copy(
            src_ref=mine,
            dst_ref=listed.at[pts],
            send_sem=sn.at[0],
            recv_sem=sn.at[1],
            device_id={"pts": (pts + dp) % 8, "py": i, "pz": pz},
            device_id_type=MESH,
        )

    turned_z[:, 0:8, :] = jnp.zeros((8, 8, 128), F32)
    for zh in range(2):

        @pl.when(some_z[zh])
        def _():
            load_conc(zh).wait()

    def turn_conc(y4, _):
        rows = [(m, v) for m in range(4) for v in range(2)]
        for zh in range(2):

            @pl.when(some_z[zh])
            def _():
                for m, v in rows:
                    turned_z[2 * m + v, 4 + 128 * zh : 132 + 128 * zh, :] = start[
                        zh, pl.ds(16 * v + 4 * y4 + m, 128, stride=32), :
                    ].T

        for m, v in rows:
            cz_flat[v, pl.ds(4 * y4 + m, 40, stride=16), :] = turned_z[
                2 * m + v, pl.ds(pl.multiple_of(32 * g, 32), 40), :
            ]
        return 0

    lax.fori_loop(0, 4, turn_conc, 0)

    def turn_mask():
        turned_y[:, 0:8, :] = jnp.zeros((2, 8, 128), F32)
        for yh in range(2):
            load_mask(yh).wait()
            for v in range(2):
                block = wells[yh, pl.ds(v, 128, stride=2), :].astype(F32)
                turned_y[v, 8 + 128 * yh : 136 + 128 * yh, :] = 0.5 * block.T
        for v in range(2):
            for t in range(5):
                mask[v, 8 * t : 8 * t + 8, :] = turned_y[v, pl.ds(32 * u + t, 8, stride=5), :]

    def greet():
        pl.semaphore_wait(barrier, len(peers))
        for dp in range(1, 8):
            node_copy(dp).start()
        listed[pts] = mine[...]
        for to_h in range(2):

            @pl.when(slab_here(to_h))
            def _():
                slab_local(to_h).start()

            @pl.when(jnp.logical_not(slab_here(to_h)))
            def _():
                slab_copy(to_h).start()

        @pl.when(jnp.logical_and(halo_some(), h == 0))
        def _():
            halo_local(0).start()

        @pl.when(jnp.logical_and(halo_some(), h == 1))
        def _():
            halo_copy(0).start()

        @pl.when(halo_some())
        def _():
            halo_copy(1).start()

        @pl.when(u == 0)
        def _():
            conc0[:, :, 0:8, :] = jnp.zeros((2, 20, 8, 128), F32)

    spot_b = (lax.broadcasted_iota(jnp.int32, (64, G), 0) + 64 * pz).astype(F32)
    spot_c = lax.broadcasted_iota(jnp.int32, (64, G), 1).astype(F32)
    wave[...] = 64.0 + spot_b * spot_b + spot_c * spot_c
    front = 64.0 * 0.9 * (32.0**1.5)

    def stage(step, _):
        amps = []
        for part in range(2):
            for half in range(2):
                a = (64 * i + 2 * step + part + 32 * half).astype(F32)
                amps.append(front / (wave[...] + a * a))
        for f in range(4):
            parts = []
            for part in range(2):
                for half in range(2):
                    row = 2 * step + part + 32 * half
                    value = xi[row] if f == 0 else basis[f - 1, row].astype(F32)
                    parts.append(value * amps[2 * part + half])
            high, low = halves(jnp.concatenate(parts, axis=0))
            both = jnp.dot(jnp.concatenate([high, low], axis=0), tz[...], preferred_element_type=F32)
            both = (both[0:256] + both[256:512]).T
            total = both[0:40] + both[40:80]
            for part in range(2):
                share[pl.ds(32 * f + 2 * step + part, 40, stride=128), :] = total[
                    :, 128 * part : 128 * part + 128
                ]
        return 0

    def stages(part, _):
        for q in range(2):
            await_bytes(xi.at[pl.ds(0, 16)], load.at[2 * part + q, 0])
            await_bytes(basis.at[:, pl.ds(0, 16)], load.at[2 * part + q, 1])
            lax.fori_loop(8 * part + 4 * q, 8 * part + 4 * q + 4, stage, 0)

        @pl.when(part == 0)
        def _():
            for d in (2, 3, 1):
                early(0, 0, 2, d).start()

        @pl.when(part == 1)
        def _():
            for begin in (0, 1):
                for d in (2, 3, 1):
                    early(1, begin, 1, d).start()

        return 0

    blocks = share.reshape(40, 4, 32, 128)

    def early(part, begin, count, d):
        to_h, to_c = (h + d // 2) % 2, (c + d % 2) % 2
        rows = pl.ds(16 * part, 16)
        return pltpu.make_async_remote_copy(
            src_ref=blocks.at[pl.ds(20 * to_c + 8 * to_h + begin, count), :, rows],
            dst_ref=got1.at[pl.ds(begin, count), pz, :, rows],
            send_sem=s1.at[0],
            recv_sem=r0.at[part + begin],
            device_id=at(i, to_h, to_c),
            device_id_type=MESH,
        )

    def early_come(part, begin, count):
        await_bytes(
            got1.at[pl.ds(begin, count), pl.ds(0, 3), :, pl.ds(16 * part, 16)], r0.at[part + begin]
        )

    greet()
    load_tz.wait()
    lax.fori_loop(0, 2, stages, 0)

    def first(pair, d):
        to_h, to_c = (h + d // 2) % 2, (c + d % 2) % 2
        return pltpu.make_async_remote_copy(
            src_ref=blocks.at[pl.ds(20 * to_c + 8 * to_h + 2 * pair, 2)],
            dst_ref=got1.at[pl.ds(2 * pair, 2), pz],
            send_sem=s1.at[0],
            recv_sem=r1.at[pair],
            device_id=at(i, to_h, to_c),
            device_id_type=MESH,
        )

    def send_first(pair, _):
        for d in (2, 3, 1):
            first(pair, d).start()
        return 0

    lax.fori_loop(1, PAIRS, send_first, 0)

    def second(pair, d):
        to_i, to_c = (i + d // 2) % 4, (c + d % 2) % 2
        return pltpu.make_async_remote_copy(
            src_ref=rows2.at[pl.ds(2 * pair, 2), 2 * to_i + to_c],
            dst_ref=got2.at[pl.ds(2 * pair, 2), 4 * c + i],
            send_sem=s2.at[0],
            recv_sem=r2.at[pair],
            device_id=at(to_i, h, to_c),
            device_id_type=MESH,
        )

    def single(k, d):
        to_i, to_c = (i + d // 2) % 4, (c + d % 2) % 2
        return pltpu.make_async_remote_copy(
            src_ref=rows2.at[k, 2 * to_i + to_c],
            dst_ref=got2.at[k, 4 * c + i],
            send_sem=s2.at[0],
            recv_sem=r3.at[k % 2 + 2 * (k // 8)],
            device_id=at(to_i, h, to_c),
            device_id_type=MESH,
        )

    def single_come(k):
        await_bytes(got2.at[k, pl.ds(0, 7)], r3.at[k % 2 + 2 * (k // 8)])

    lane = lax.broadcasted_iota(jnp.int32, (128, 128), 1)
    lane_low = lane < 64
    lane8 = lax.broadcasted_iota(jnp.int32, (8, 128), 1)
    edge = jnp.where(lane8 > 0, 1.6 * 1.6, 0.0).astype(F32)
    lane40 = lax.broadcasted_iota(jnp.int32, (40, 128), 1) < 64

    def b_contraction(k):
        own = share[pl.ds(pl.multiple_of((20 * c + 8 * h + k) * 128, 128), 128), :]
        got1[k, pz] = own.reshape(4, 32, 128)
        sides = [[], []]
        for pair in range(2):
            one, two = (got1[k, 2 * pair + m].reshape(128, 128) for m in range(2))
            sides[0].append(jnp.where(lane_low, one, pltpu.roll(two, 64, 1)))
            sides[1].append(jnp.where(lane_low, pltpu.roll(one, 64, 1), two))
        both = [jnp.concatenate(side, axis=1) for side in sides]
        rows = []
        for f in range(4):
            rows += [both[0][32 * f : 32 * f + 32], both[1][32 * f : 32 * f + 32]]
        high, low = halves(jnp.concatenate(rows, axis=0))
        both = lax.dot_general(cy[...], high, NT, preferred_element_type=F32)
        rest = lax.dot_general(cy[0:320], low, NT, preferred_element_type=F32)
        total = both[0:320] + both[320:640] + rest
        for slab in range(8):
            rows2[k, slab] = total[40 * slab : 40 * slab + 36]
        got2[k, 4 * c + i] = rows2[k, u]

    def a_contraction(k):
        rows = []
        for core in range(2):
            for pair in range(2):
                cols = [[], []]
                for group in range(2):
                    one, two = (
                        jnp.concatenate(
                            [
                                got2[k, 4 * core + 2 * group + m, first_row : first_row + 8, 128 * pair : 128 * pair + 128]
                                for first_row in (7, 14, 21, 28, 0)
                            ],
                            axis=0,
                        )
                        for m in range(2)
                    )
                    cols[0].append(jnp.where(lane40, one, pltpu.roll(two, 64, 1)))
                    cols[1].append(jnp.where(lane40, pltpu.roll(one, 64, 1), two))
                rows += [jnp.concatenate(col, axis=1) for col in cols]
        high, low = halves(jnp.concatenate(rows, axis=0))
        both = jnp.dot(jnp.concatenate([high, low], axis=0), cx[0:256], preferred_element_type=F32)
        total = both[0:320] + both[320:640]
        total += jnp.dot(high, cx[256:512], preferred_element_type=F32)
        for core in range(2):
            for f in range(4):
                row = 160 * core + 40 * f
                fields[k % 2, core, f] = total[row : row + 40]

    tiles = [(t, v) for t in range(5) for v in range(2)]

    def transport(k, halo):
        sub = k % 2
        levels = range(2)
        for p in levels:
            zz = 2 * k + p
            spot_z = 16 * (2 * g + h) - 4 + zz
            well = jnp.where(spot_z >= 0, prof[jnp.maximum(spot_z, 0)], 0.0)
            for t, v in tiles:
                share_v = 1.0 if v == 0 else 1.0 / 1.6
                plane[p, 0, t, v] = conc0[v, zz, pl.ds(t, 8, stride=5), :] * share_v
                plane[p, 1, t, v] = mask[v, 8 * t : 8 * t + 8, :] * (well * share_v)
                if not halo:
                    plane[p, 2, t, v] = jnp.zeros((8, 128), F32)

        def some_points(group, _):
            each = [(m, p) for m in range(BATCH) for p in levels]
            speed, conc = {e: {} for e in each}, {e: {} for e in each}
            for m, p in each:
                n = BATCH * group + m
                node = [nodes[n, r] for r in range(3)]
                for t, v in tiles:
                    logs = [
                        fields[sub, p, f, 8 * t : 8 * t + 8, 128 * v : 128 * v + 128] for f in range(4)
                    ]
                    value = logs[0] + node[0] * logs[1] + node[1] * logs[2] + node[2] * logs[3]
                    speed[m, p][t, v] = 0.125 + 0.125 * jnp.tanh(value)
                    conc[m, p][t, v] = plane[p, 0, t, v]
            for step in range(STEPS):
                flux = {
                    (m, p): {tv: speed[m, p][tv] * conc[m, p][tv] for tv in tiles}
                    for m, p in each
                    if not halo or step <= 2 * k + p
                }
                for t, v in tiles:
                    for m, p in each:
                        if (m, p) not in flux:
                            continue
                        n = BATCH * group + m
                        here = flux[m, p]
                        more = not halo or step < 2 * k + p
                        if more:
                            behind = carry[n, step, t, v] if p == 0 else flux[m, 0][t, v]
                        if p == 1:
                            carry[n, step, t, v] = here[t, v]
                        if not more:
                            continue
                        prev_b = here[t - 1, v] if t > 0 else pltpu.roll(here[4, v], 1, 0)
                        prev_a = here[t, 0] if v == 1 else edge * pltpu.roll(here[t, 1], 1, 1)
                        conc[m, p][t, v] = (
                            (conc[m, p][t, v] - 3.6 * here[t, v])
                            + (plane[p, 1, t, v] + behind)
                            + (prev_b + prev_a)
                        )
            if not halo:
                for p in levels:
                    for t, v in tiles:
                        part = nodes[BATCH * group, 3] * conc[0, p][t, v]
                        for m in range(1, BATCH):
                            part += nodes[BATCH * group + m, 3] * conc[m, p][t, v]
                        plane[p, 2, t, v] += part
            return 0

        lax.fori_loop(0, POINTS // BATCH, some_points, 0)
        if not halo:
            for p in levels:
                for t, v in tiles:
                    sums[v, pl.ds(16 * t + 2 * k + p - 4, 8, stride=80), :] = (
                        plane[p, 2, t, v] * (1.0 if v == 0 else 1.6)
                    )

    def wait_conc():
        for core in range(2):
            slab = pltpu.make_async_copy(
                cz.at[:, pl.ds(0, 20)], conc0.at[:, :, pl.ds(8 + 16 * core, 16)], rc.at[core]
            )
            slab.wait()

        @pl.when(u > 0)
        def _():
            pltpu.make_async_copy(
                cz.at[:, pl.ds(0, 20), pl.ds(8, 8)], conc0.at[:, :, pl.ds(0, 8)], rc.at[2]
            ).wait()

    granule = lax.broadcasted_iota(jnp.int32, (8, 128), 1) // 16
    zr = 16 * (4 * yy + 2 * xt + h)

    def home(zp, dp, half):
        to = (pts + dp) % 8
        return pltpu.make_async_remote_copy(
            src_ref=parcel.at[zp, to, half],
            dst_ref=landed.at[:, pl.ds(pl.multiple_of(zr + 8 * zp, 8), 8)],
            send_sem=so.at[3 * zp + (0 if dp else 1 + half)],
            recv_sem=ro.at[zp],
            device_id={"pts": to, "py": i, "pz": 2 * c + half},
            device_id_type=MESH,
        )

    def home_own(zp, half):
        return pltpu.make_async_copy(
            parcel.at[zp, pts, half], landed.at[:, pl.ds(pl.multiple_of(zr + 8 * zp, 8), 8)], ro.at[zp]
        )

    def go_home(zp):
        def regroup(which, _):
            half, yg = which // 4, which % 4
            arrays = []
            for y in range(4):
                for v in range(2):
                    row = pl.multiple_of(16 * (8 + 16 * half + 4 * yg + y) + 8 * zp, 8)
                    arrays.append(sums[v, pl.ds(row, 8), :])
            for bit in (4, 2, 1):
                clear = (granule // bit) % 2 == 0
                for m in range(8):
                    if m // bit % 2 == 0:
                        one, two = arrays[m], arrays[m + bit]
                        arrays[m] = jnp.where(clear, one, pltpu.roll(two, 16 * bit, 1))
                        arrays[m + bit] = jnp.where(clear, pltpu.roll(one, 128 - 16 * bit, 1), two)
            for p in range(8):
                parcel[zp, p, half, yg] = arrays[p]
            return 0

        for half in range(2):
            lax.fori_loop(4 * half, 4 * half + 4, regroup, 0)
            here = jnp.logical_and(c == h, c == half)

            @pl.when(here)
            def _():
                home_own(zp, half).start()

            @pl.when(jnp.logical_not(here))
            def _():
                home(zp, 0, half).start()

            for dp in range(1, 8):
                home(zp, dp, half).start()

    def rounds(step, _):
        @pl.when(step == 0)
        def _():
            early_come(0, 0, 2)

        @pl.when(step > 0)
        def _():
            @pl.when(step < PAIRS)
            def _():
                await_bytes(got1.at[pl.ds(2 * step, 2), pl.ds(0, 3)], r1.at[step])

        @pl.when(jnp.logical_or(step == 0, step == PAIRS - 1))
        def _():
            def one(k, _):
                for begin in (0, 1):

                    @pl.when(k == begin)
                    def _():
                        early_come(1, begin, 1)

                b_contraction(k)
                for d in (4, 5, 2, 6, 3, 7, 1):
                    single(k, d).start()
                return 0

            lax.fori_loop(2 * step, 2 * step + 2, one, 0)

        @pl.when(jnp.logical_and(step > 0, step < PAIRS - 1))
        def _():
            for sub in range(2):
                b_contraction(2 * step + sub)
            for d in (4, 5, 2, 6, 3, 7, 1):
                second(step, d).start()

        @pl.when(step == 1)
        def _():
            for k in range(2):
                single_come(k)
                a_contraction(k)
                transport(k, True)

        @pl.when(jnp.logical_and(step > 1, step < PAIRS))
        def _():
            await_bytes(got2.at[pl.ds(2 * step - 2, 2), pl.ds(0, 7)], r2.at[step - 1])
            for sub in range(2):
                a_contraction(2 * step - 2 + sub)

            def one(sub, _):
                transport(2 * step - 2 + sub, False)
                return 0

            lax.fori_loop(0, 2, one, 0)

        @pl.when(step == 3)
        def _():
            go_home(0)

        @pl.when(step == PAIRS)
        def _():
            def one(k, _):
                single_come(k)
                a_contraction(k)
                transport(k, False)
                return 0

            lax.fori_loop(2 * PAIRS - 2, 2 * PAIRS, one, 0)

        return 0

    turn_mask()
    wait_conc()
    await_bytes(listed.at[pl.ds(0, 7)], sn.at[1])
    for n in range(POINTS):
        for r in range(4):
            row = 4 * (n % 2) + r
            nodes[n, r] = jnp.broadcast_to(listed[n // 2, row : row + 1, :], (8, 128))
    lax.fori_loop(0, PAIRS + 1, rounds, 0)

    go_home(1)
    for zp in range(2):
        await_bytes(landed.at[:, pl.ds(0, 128)], ro.at[zp])

    for yg in range(4):
        for zh in range(2):
            turned = landed[yg, 128 * zh : 128 * zh + 128, :].T
            for y in range(4):
                for v in range(2):
                    e = 16 * (2 * y + v)
                    final[zh, pl.ds(16 * v + 4 * yg + y, 16, stride=32), :] = turned[e : e + 16]
    for zh in range(2):
        out[:, 128 * zh : 128 * zh + 128] = final[zh]

    await_bytes(share.at[pl.ds(0, 3 * 128 * NROUND)], s1.at[0])
    await_bytes(rows2.at[:, pl.ds(0, 7)], s2.at[0])
    await_bytes(listed.at[pl.ds(0, 7)], sn.at[0])
    for zp in range(2):
        await_bytes(parcel.at[zp, pl.ds(0, 7)], so.at[3 * zp])
    for half in range(2):

        @pl.when(jnp.logical_not(jnp.logical_and(c == h, c == half)))
        def _():
            for zp in range(2):
                home(zp, 0, half).wait_send()

    for to_h in range(2):

        @pl.when(jnp.logical_not(slab_here(to_h)))
        def _():
            slab_copy(to_h).wait_send()

    @pl.when(jnp.logical_and(halo_some(), h == 1))
    def _():
        halo_copy(0).wait_send()

    @pl.when(halo_some())
    def _():
        halo_copy(1).wait_send()


def local(xi_map, basis, point_index, conc_start, well_mask, profile):
    (tz_hi, tz_lo), (cy_hi, cy_lo), (cx_hi, cx_lo) = tables()
    tz = np.concatenate([tz_hi, tz_lo, np.zeros((8, G, 48), ml_dtypes.bfloat16)], axis=2)
    cy = np.concatenate([cy_hi, cy_lo], axis=0)
    cx = np.concatenate([cx_hi, cx_lo], axis=0)

    vmem = pl.BlockSpec(memory_space=pltpu.VMEM)
    smem = pl.BlockSpec(memory_space=pltpu.SMEM)
    dma = pltpu.SemaphoreType.DMA
    far = pl.BlockSpec(memory_space=pl.ANY)
    total = pl.pallas_call(
        kernel,
        out_shape=jax.ShapeDtypeStruct((512, 256), F32),
        in_specs=[smem, smem] + [far] * 5 + [vmem] * 2,
        out_specs=vmem,
        scratch_shapes=[
            pltpu.VMEM((64, 64, 256), F32),
            pltpu.VMEM((3, 64, 64, 256), BF16),
            pltpu.VMEM((40 * 128, 128), F32),
            pltpu.VMEM((NROUND, 4, 4, 32, 128), F32),
            pltpu.VMEM((NROUND, 8, 36, 256), F32),
            pltpu.VMEM((NROUND, 8, 36, 256), F32),
            pltpu.VMEM((2, 20, 40, 128), F32),
            pltpu.VMEM((2, 2, 4, 40, 256), F32),
            pltpu.VMEM((POINTS, STEPS, 5, 2, 8, 128), F32),
            pltpu.VMEM((2, 3, 5, 2, 8, 128), F32),
            pltpu.VMEM((64, 256), F32),
            pltpu.VMEM((8, 128), F32),
            pltpu.VMEM((8, 8, 128), F32),
            pltpu.VMEM((POINTS, 4, 8, 128), F32),
            pltpu.VMEM((2, 640, 128), F32),
            pltpu.VMEM((2, 8, 2, 4, 8, 128), F32),
            pltpu.VMEM((4, 256, 128), F32),
            pltpu.VMEM((2, 512, 128), F32),
            pltpu.VMEM((256, 128), BF16),
            pltpu.VMEM((2, 4096, 128), F32),
            pltpu.VMEM((8, 272, 128), F32),
            pltpu.VMEM((2, 640, 128), F32),
            pltpu.VMEM((2, 256, 128), jnp.int32),
            pltpu.VMEM((2, 264, 128), F32),
            pltpu.VMEM((2, 40, 128), F32),
            dma((3,)),
            dma((1,)),
            dma((PAIRS,)),
            dma((1,)),
            dma((PAIRS,)),
            dma((4,)),
            dma((4,)),
            dma((3,)),
            dma((4, 2)),
            dma((5,)),
            dma((2,)),
            dma((6,)),
            dma((2,)),
        ],
        compiler_params=pltpu.CompilerParams(
            collective_id=0, has_side_effects=True, vmem_limit_bytes=60 * 2**20
        ),
    )(point_index, profile, xi_map, basis, conc_start.reshape(4096, 256), well_mask, tz, cy, cx)
    return total.reshape(32, 16, 256)


def solution(mesh):
    placed = (
        P("py", "pz", None),
        P(None, "py", "pz", None),
        P("pts", None),
        P(None, ("py", "pz"), None),
        P(),
        P(),
    )
    return jax.shard_map(
        local, mesh=mesh, in_specs=placed, out_specs=P("pts", ("py", "pz"), None), check_vma=False
    )
```

```python
import functools

import jax
import jax.numpy as jnp
import ml_dtypes
import numpy as np
from jax import lax
from jax.experimental import pallas as pl
from jax.experimental.pallas import tpu as pltpu
from jax.sharding import PartitionSpec as P

MESH = pl.DeviceIdType.MESH
STEPS = 4
POINTS = 16
BATCH = 2
G = 256
NROUND = 10
PAIRS = 5
ROOT3 = 1.7320508075688772
F32 = jnp.float32
BF16 = jnp.bfloat16
NT = (((1,), (1,)), ((), ()))


def split_table(table):
    table = np.asarray(table, np.float64)
    high = table.astype(np.float32).astype(ml_dtypes.bfloat16)
    low = (table - high.astype(np.float64)).astype(np.float32).astype(ml_dtypes.bfloat16)
    return high, low


def tables():
    spots = np.arange(G, dtype=np.float64)
    full = np.sqrt(2.0 / G) * np.cos(np.pi * (spots[:, None] + 0.5) * spots[None, :] / G)
    full[:, 0] *= np.sqrt(0.5)
    tz = np.zeros((8, 40, G))
    for g in range(8):
        for par in range(2):
            for w in range(18):
                z = 32 * g - 4 + 2 * w + par
                if z >= 0:
                    tz[g, 20 * par + w] = full[z]
    tz = tz.transpose(0, 2, 1)
    cy = np.zeros((8, 40, G))
    for u in range(8):
        for t in range(5):
            for q in range(8):
                y = 32 * u - 8 + 5 * q + t
                if y >= 0 and (t == 4 or q > 0):
                    cy[u, q if t == 4 else 7 + 7 * t + q] = full[y]
    cx = 0.5 * np.concatenate([full[0::2], full[1::2]], axis=0).T
    return split_table(tz), split_table(cy.reshape(320, G)), split_table(cx)


def halves(value):
    high = value.astype(BF16)
    low = (value - high.astype(F32)).astype(BF16)
    return high, low


def kernel(
    point,
    prof,
    xi_far,
    basis_far,
    conc_far,
    mask_far,
    tz_far,
    cy,
    cx,
    out,
    xi,
    basis,
    share,
    got1,
    rows2,
    got2,
    conc0,
    fields,
    carry,
    plane,
    wave,
    mine,
    listed,
    nodes,
    sums,
    parcel,
    landed,
    final,
    tz,
    start,
    turned_z,
    cz_flat,
    wells,
    turned_y,
    mask,
    r0,
    s1,
    r1,
    s2,
    r3,
    sc,
    rc,
    load,
    prep,
    sn,
    so,
    ro,
):
    pts = lax.axis_index("pts")
    i = lax.axis_index("py")
    pz = lax.axis_index("pz")
    yy, x_lo = pts // 2, pts % 2
    h, c = pz // 2, pz % 2
    xt = (x_lo + h) % 2
    u = 2 * i + c
    g = 2 * yy + xt
    cz = cz_flat.reshape(2, 40, 16, 128)

    def at(i_, h_, c_):
        return {"pts": 2 * yy + (xt + h_) % 2, "py": i_, "pz": 2 * h_ + c_}

    def await_bytes(view, sem):
        pltpu.make_async_copy(view, view, sem).wait()

    barrier = pltpu.get_barrier_semaphore()
    peers = []
    for dp in range(8):
        for dh in range(2):
            for dc in range(2):
                if dp + dh + dc > 0:
                    peers.append({"pts": (pts + dp) % 8, "py": i, "pz": 2 * ((h + dh) % 2) + (c + dc) % 2})
    for di in range(1, 4):
        for dh in range(2):
            for dc in range(2):
                peers.append(at((i + di) % 4, (h + dh) % 2, (c + dc) % 2))
    for peer in peers:
        pl.semaphore_signal(barrier, inc=1, device_id=peer, device_id_type=MESH)

    def loads(q):
        copies = []
        for half in range(2):
            rows = pl.ds(pl.multiple_of(8 * q + 32 * half, 8), 8)
            copies.append(pltpu.make_async_copy(xi_far.at[rows], xi.at[rows], load.at[q, 0]))
            copies.append(
                pltpu.make_async_copy(basis_far.at[:, rows], basis.at[:, rows], load.at[q, 1])
            )
        return copies

    def start_loads(q, _):
        for copy in loads(q):
            copy.start()
        return 0

    def load_conc(zh):
        return pltpu.make_async_copy(
            conc_far.at[:, pl.ds(128 * zh, 128)], start.at[zh], prep.at[zh]
        )

    def load_mask(yh):
        return pltpu.make_async_copy(
            mask_far.at[:, pl.ds(128 * yh, 128)], wells.at[yh], prep.at[2 + yh]
        )

    load_tz = pltpu.make_async_copy(tz_far.at[g], tz, prep.at[4])
    some_z = [g <= 4, g >= 4]
    for zh in range(2):

        @pl.when(some_z[zh])
        def _():
            load_conc(zh).start()

    load_tz.start()
    lax.fori_loop(0, 4, start_loads, 0)
    for yh in range(2):
        load_mask(yh).start()

    def slab_copy(to_h):
        return pltpu.make_async_remote_copy(
            src_ref=cz.at[:, pl.ds(16 * to_h, 20)],
            dst_ref=conc0.at[:, :, pl.ds(pl.multiple_of(8 + 16 * c, 8), 16)],
            send_sem=sc.at[to_h],
            recv_sem=rc.at[c],
            device_id=at(i, to_h, h),
            device_id_type=MESH,
        )

    def slab_local(to_h):
        return pltpu.make_async_copy(
            cz.at[:, pl.ds(16 * to_h, 20)],
            conc0.at[:, :, pl.ds(pl.multiple_of(8 + 16 * c, 8), 16)],
            rc.at[c],
        )

    above = 2 * i + h + 1

    def halo_copy(to_h):
        return pltpu.make_async_remote_copy(
            src_ref=cz.at[:, pl.ds(16 * to_h, 20), pl.ds(8, 8)],
            dst_ref=conc0.at[:, :, pl.ds(0, 8)],
            send_sem=sc.at[2 + to_h],
            recv_sem=rc.at[2],
            device_id=at((above // 2) % 4, to_h, above % 2),
            device_id_type=MESH,
        )

    def halo_local(to_h):
        return pltpu.make_async_copy(
            cz.at[:, pl.ds(16 * to_h, 20), pl.ds(8, 8)], conc0.at[:, :, pl.ds(0, 8)], rc.at[2]
        )

    def slab_here(to_h):
        return jnp.logical_and(h == to_h, c == to_h)

    def halo_some():
        return jnp.logical_and(c == 1, above < 8)

    for m in range(2):
        weight = 1.0
        for r in range(3):
            index = point[m, r]
            value = jnp.where(index == 0, -ROOT3, jnp.where(index == 1, 0.0, ROOT3))
            weight = weight * jnp.where(index == 1, 2.0 / 3.0, 1.0 / 6.0)
            mine[4 * m + r : 4 * m + r + 1, :] = jnp.full((1, 128), value, F32)
        mine[4 * m + 3 : 4 * m + 4, :] = jnp.full((1, 128), weight, F32)

    def node_copy(dp):
        return pltpu.make_async_remote_copy(
            src_ref=mine,
            dst_ref=listed.at[pts],
            send_sem=sn.at[0],
            recv_sem=sn.at[1],
            device_id={"pts": (pts + dp) % 8, "py": i, "pz": pz},
            device_id_type=MESH,
        )

    turned_z[:, 0:8, :] = jnp.zeros((8, 8, 128), F32)
    for zh in range(2):

        @pl.when(some_z[zh])
        def _():
            load_conc(zh).wait()

    def turn_conc(y4, _):
        rows = [(m, v) for m in range(4) for v in range(2)]
        for zh in range(2):

            @pl.when(some_z[zh])
            def _():
                for m, v in rows:
                    turned_z[2 * m + v, 4 + 128 * zh : 132 + 128 * zh, :] = start[
                        zh, pl.ds(16 * v + 4 * y4 + m, 128, stride=32), :
                    ].T

        for m, v in rows:
            cz_flat[v, pl.ds(4 * y4 + m, 40, stride=16), :] = turned_z[
                2 * m + v, pl.ds(pl.multiple_of(32 * g, 32), 40), :
            ]
        return 0

    lax.fori_loop(0, 4, turn_conc, 0)

    def turn_mask():
        turned_y[:, 0:8, :] = jnp.zeros((2, 8, 128), F32)
        for yh in range(2):
            load_mask(yh).wait()
            for v in range(2):
                block = wells[yh, pl.ds(v, 128, stride=2), :].astype(F32)
                turned_y[v, 8 + 128 * yh : 136 + 128 * yh, :] = 0.5 * block.T
        for v in range(2):
            for t in range(5):
                mask[v, 8 * t : 8 * t + 8, :] = turned_y[v, pl.ds(32 * u + t, 8, stride=5), :]

    def greet():
        pl.semaphore_wait(barrier, len(peers))
        for dp in range(1, 8):
            node_copy(dp).start()
        listed[pts] = mine[...]
        for to_h in range(2):

            @pl.when(slab_here(to_h))
            def _():
                slab_local(to_h).start()

            @pl.when(jnp.logical_not(slab_here(to_h)))
            def _():
                slab_copy(to_h).start()

        @pl.when(jnp.logical_and(halo_some(), h == 0))
        def _():
            halo_local(0).start()

        @pl.when(jnp.logical_and(halo_some(), h == 1))
        def _():
            halo_copy(0).start()

        @pl.when(halo_some())
        def _():
            halo_copy(1).start()

        @pl.when(u == 0)
        def _():
            conc0[:, :, 0:8, :] = jnp.zeros((2, 20, 8, 128), F32)

    spot_b = (lax.broadcasted_iota(jnp.int32, (64, G), 0) + 64 * pz).astype(F32)
    spot_c = lax.broadcasted_iota(jnp.int32, (64, G), 1).astype(F32)
    wave[...] = 64.0 + spot_b * spot_b + spot_c * spot_c
    front = 64.0 * 0.9 * (32.0**1.5)

    def stage(step, _):
        amps = []
        for part in range(2):
            for half in range(2):
                a = (64 * i + 2 * step + part + 32 * half).astype(F32)
                amps.append(front / (wave[...] + a * a))
        for f in range(4):
            parts = []
            for part in range(2):
                for half in range(2):
                    row = 2 * step + part + 32 * half
                    value = xi[row] if f == 0 else basis[f - 1, row].astype(F32)
                    parts.append(value * amps[2 * part + half])
            high, low = halves(jnp.concatenate(parts, axis=0))
            both = jnp.dot(jnp.concatenate([high, low], axis=0), tz[...], preferred_element_type=F32)
            both = (both[0:256] + both[256:512]).T
            total = both[0:40] + both[40:80]
            for part in range(2):
                share[pl.ds(32 * f + 2 * step + part, 40, stride=128), :] = total[
                    :, 128 * part : 128 * part + 128
                ]
        return 0

    def stages(part, _):
        for q in range(2):
            await_bytes(xi.at[pl.ds(0, 16)], load.at[2 * part + q, 0])
            await_bytes(basis.at[:, pl.ds(0, 16)], load.at[2 * part + q, 1])
            lax.fori_loop(8 * part + 4 * q, 8 * part + 4 * q + 4, stage, 0)

        @pl.when(part == 0)
        def _():
            for d in (2, 3, 1):
                early(0, 0, 2, d).start()

        @pl.when(part == 1)
        def _():
            for begin in (0, 1):
                for d in (2, 3, 1):
                    early(1, begin, 1, d).start()

        return 0

    blocks = share.reshape(40, 4, 32, 128)

    def early(part, begin, count, d):
        to_h, to_c = (h + d // 2) % 2, (c + d % 2) % 2
        rows = pl.ds(16 * part, 16)
        return pltpu.make_async_remote_copy(
            src_ref=blocks.at[pl.ds(20 * to_c + 8 * to_h + begin, count), :, rows],
            dst_ref=got1.at[pl.ds(begin, count), pz, :, rows],
            send_sem=s1.at[0],
            recv_sem=r0.at[part + begin],
            device_id=at(i, to_h, to_c),
            device_id_type=MESH,
        )

    def early_come(part, begin, count):
        await_bytes(
            got1.at[pl.ds(begin, count), pl.ds(0, 3), :, pl.ds(16 * part, 16)], r0.at[part + begin]
        )

    greet()
    load_tz.wait()
    lax.fori_loop(0, 2, stages, 0)

    def first(pair, d):
        to_h, to_c = (h + d // 2) % 2, (c + d % 2) % 2
        return pltpu.make_async_remote_copy(
            src_ref=blocks.at[pl.ds(20 * to_c + 8 * to_h + 2 * pair, 2)],
            dst_ref=got1.at[pl.ds(2 * pair, 2), pz],
            send_sem=s1.at[0],
            recv_sem=r1.at[pair],
            device_id=at(i, to_h, to_c),
            device_id_type=MESH,
        )

    def send_first(pair, _):
        for d in (2, 3, 1):
            first(pair, d).start()
        return 0

    lax.fori_loop(1, PAIRS, send_first, 0)

    def single(k, d):
        to_i, to_c = (i + d // 2) % 4, (c + d % 2) % 2
        return pltpu.make_async_remote_copy(
            src_ref=rows2.at[k, 2 * to_i + to_c],
            dst_ref=got2.at[k, 4 * c + i],
            send_sem=s2.at[0],
            recv_sem=r3.at[k],
            device_id=at(to_i, h, to_c),
            device_id_type=MESH,
        )

    def single_come(k):
        await_bytes(got2.at[k, pl.ds(0, 7)], r3.at[k])

    lane = lax.broadcasted_iota(jnp.int32, (128, 128), 1)
    lane_low = lane < 64
    lane8 = lax.broadcasted_iota(jnp.int32, (8, 128), 1)
    edge = jnp.where(lane8 > 0, 1.6 * 1.6, 0.0).astype(F32)
    lane40 = lax.broadcasted_iota(jnp.int32, (40, 128), 1) < 64

    def b_contraction(k):
        own = share[pl.ds(pl.multiple_of((20 * c + 8 * h + k) * 128, 128), 128), :]
        got1[k, pz] = own.reshape(4, 32, 128)
        sides = [[], []]
        for pair in range(2):
            one, two = (got1[k, 2 * pair + m].reshape(128, 128) for m in range(2))
            sides[0].append(jnp.where(lane_low, one, pltpu.roll(two, 64, 1)))
            sides[1].append(jnp.where(lane_low, pltpu.roll(one, 64, 1), two))
        both = [jnp.concatenate(side, axis=1) for side in sides]
        rows = []
        for f in range(4):
            rows += [both[0][32 * f : 32 * f + 32], both[1][32 * f : 32 * f + 32]]
        high, low = halves(jnp.concatenate(rows, axis=0))
        both = lax.dot_general(cy[...], high, NT, preferred_element_type=F32)
        rest = lax.dot_general(cy[0:320], low, NT, preferred_element_type=F32)
        total = both[0:320] + both[320:640] + rest
        for slab in range(8):
            rows2[k, slab] = total[40 * slab : 40 * slab + 36]
        got2[k, 4 * c + i] = rows2[k, u]

    def a_contraction(k):
        rows = []
        for core in range(2):
            for pair in range(2):
                cols = [[], []]
                for group in range(2):
                    one, two = (
                        jnp.concatenate(
                            [
                                got2[k, 4 * core + 2 * group + m, first_row : first_row + 8, 128 * pair : 128 * pair + 128]
                                for first_row in (7, 14, 21, 28, 0)
                            ],
                            axis=0,
                        )
                        for m in range(2)
                    )
                    cols[0].append(jnp.where(lane40, one, pltpu.roll(two, 64, 1)))
                    cols[1].append(jnp.where(lane40, pltpu.roll(one, 64, 1), two))
                rows += [jnp.concatenate(col, axis=1) for col in cols]
        high, low = halves(jnp.concatenate(rows, axis=0))
        both = jnp.dot(jnp.concatenate([high, low], axis=0), cx[0:256], preferred_element_type=F32)
        total = both[0:320] + both[320:640]
        total += jnp.dot(high, cx[256:512], preferred_element_type=F32)
        for core in range(2):
            for f in range(4):
                row = 160 * core + 40 * f
                fields[k % 2, core, f] = total[row : row + 40]

    tiles = [(t, v) for t in range(5) for v in range(2)]

    def transport(k, halo):
        sub = k % 2
        levels = range(2)
        for p in levels:
            zz = 2 * k + p
            spot_z = 16 * (2 * g + h) - 4 + zz
            well = jnp.where(spot_z >= 0, prof[jnp.maximum(spot_z, 0)], 0.0)
            for t, v in tiles:
                share_v = 1.0 if v == 0 else 1.0 / 1.6
                plane[p, 0, t, v] = conc0[v, zz, pl.ds(t, 8, stride=5), :] * share_v
                plane[p, 1, t, v] = mask[v, 8 * t : 8 * t + 8, :] * (well * share_v)
                if not halo:
                    plane[p, 2, t, v] = jnp.zeros((8, 128), F32)

        def some_points(group, _):
            each = [(m, p) for m in range(BATCH) for p in levels]
            speed, conc = {e: {} for e in each}, {e: {} for e in each}
            for m, p in each:
                n = BATCH * group + m
                node = [nodes[n, r] for r in range(3)]
                for t, v in tiles:
                    logs = [
                        fields[sub, p, f, 8 * t : 8 * t + 8, 128 * v : 128 * v + 128] for f in range(4)
                    ]
                    value = logs[0] + node[0] * logs[1] + node[1] * logs[2] + node[2] * logs[3]
                    speed[m, p][t, v] = 0.125 + 0.125 * jnp.tanh(value)
                    conc[m, p][t, v] = plane[p, 0, t, v]
            for step in range(STEPS):
                flux = {
                    (m, p): {tv: speed[m, p][tv] * conc[m, p][tv] for tv in tiles}
                    for m, p in each
                    if not halo or step <= 2 * k + p
                }
                for t, v in tiles:
                    for m, p in each:
                        if (m, p) not in flux:
                            continue
                        n = BATCH * group + m
                        here = flux[m, p]
                        more = not halo or step < 2 * k + p
                        if more:
                            behind = carry[n, step, t, v] if p == 0 else flux[m, 0][t, v]
                        if p == 1:
                            carry[n, step, t, v] = here[t, v]
                        if not more:
                            continue
                        prev_b = here[t - 1, v] if t > 0 else pltpu.roll(here[4, v], 1, 0)
                        prev_a = here[t, 0] if v == 1 else edge * pltpu.roll(here[t, 1], 1, 1)
                        conc[m, p][t, v] = (
                            (conc[m, p][t, v] - 3.6 * here[t, v])
                            + (plane[p, 1, t, v] + behind)
                            + (prev_b + prev_a)
                        )
            if not halo:
                for p in levels:
                    for t, v in tiles:
                        part = nodes[BATCH * group, 3] * conc[0, p][t, v]
                        for m in range(1, BATCH):
                            part += nodes[BATCH * group + m, 3] * conc[m, p][t, v]
                        plane[p, 2, t, v] += part
            return 0

        lax.fori_loop(0, POINTS // BATCH, some_points, 0)
        if not halo:
            for p in levels:
                for t, v in tiles:
                    sums[v, pl.ds(16 * t + 2 * k + p - 4, 8, stride=80), :] = (
                        plane[p, 2, t, v] * (1.0 if v == 0 else 1.6)
                    )

    def wait_conc():
        for core in range(2):
            slab = pltpu.make_async_copy(
                cz.at[:, pl.ds(0, 20)], conc0.at[:, :, pl.ds(8 + 16 * core, 16)], rc.at[core]
            )
            slab.wait()

        @pl.when(u > 0)
        def _():
            pltpu.make_async_copy(
                cz.at[:, pl.ds(0, 20), pl.ds(8, 8)], conc0.at[:, :, pl.ds(0, 8)], rc.at[2]
            ).wait()

    granule = lax.broadcasted_iota(jnp.int32, (8, 128), 1) // 16
    zr = 16 * (4 * yy + 2 * xt + h)

    def home(zp, dp, half):
        to = (pts + dp) % 8
        return pltpu.make_async_remote_copy(
            src_ref=parcel.at[zp, to, half],
            dst_ref=landed.at[:, pl.ds(pl.multiple_of(zr + 8 * zp, 8), 8)],
            send_sem=so.at[3 * zp + (0 if dp else 1 + half)],
            recv_sem=ro.at[zp],
            device_id={"pts": to, "py": i, "pz": 2 * c + half},
            device_id_type=MESH,
        )

    def home_own(zp, half):
        return pltpu.make_async_copy(
            parcel.at[zp, pts, half], landed.at[:, pl.ds(pl.multiple_of(zr + 8 * zp, 8), 8)], ro.at[zp]
        )

    def go_home(zp):
        def regroup(which, _):
            half, yg = which // 4, which % 4
            arrays = []
            for y in range(4):
                for v in range(2):
                    row = pl.multiple_of(16 * (8 + 16 * half + 4 * yg + y) + 8 * zp, 8)
                    arrays.append(sums[v, pl.ds(row, 8), :])
            for bit in (4, 2, 1):
                clear = (granule // bit) % 2 == 0
                for m in range(8):
                    if m // bit % 2 == 0:
                        one, two = arrays[m], arrays[m + bit]
                        arrays[m] = jnp.where(clear, one, pltpu.roll(two, 16 * bit, 1))
                        arrays[m + bit] = jnp.where(clear, pltpu.roll(one, 128 - 16 * bit, 1), two)
            for p in range(8):
                parcel[zp, p, half, yg] = arrays[p]
            return 0

        for half in range(2):
            lax.fori_loop(4 * half, 4 * half + 4, regroup, 0)
            here = jnp.logical_and(c == h, c == half)

            @pl.when(here)
            def _():
                home_own(zp, half).start()

            @pl.when(jnp.logical_not(here))
            def _():
                home(zp, 0, half).start()

            for dp in range(1, 8):
                home(zp, dp, half).start()

    lag = 3

    def rounds(step, _):
        @pl.when(step == 0)
        def _():
            early_come(0, 0, 2)
            early_come(1, 0, 1)

        @pl.when(step == 1)
        def _():
            early_come(1, 1, 1)

        for pair in range(1, PAIRS):

            @pl.when(step == 2 * pair)
            def _():
                await_bytes(got1.at[pl.ds(2 * pair, 2), pl.ds(0, 3)], r1.at[pair])

        @pl.when(step < NROUND)
        def _():
            b_contraction(step)
            for d in (4, 5, 2, 6, 3, 7, 1):
                single(step, d).start()

        for k in range(2):

            @pl.when(step == lag + k)
            def _():
                single_come(k)
                a_contraction(k)
                transport(k, True)

        @pl.when(step >= lag + 2)
        def _():
            single_come(step - lag)
            a_contraction(step - lag)
            transport(step - lag, False)

        @pl.when(step == lag + 5)
        def _():
            go_home(0)

        return 0

    turn_mask()
    wait_conc()
    await_bytes(listed.at[pl.ds(0, 7)], sn.at[1])
    for n in range(POINTS):
        for r in range(4):
            row = 4 * (n % 2) + r
            nodes[n, r] = jnp.broadcast_to(listed[n // 2, row : row + 1, :], (8, 128))
    lax.fori_loop(0, NROUND + lag, rounds, 0)

    go_home(1)
    for zp in range(2):
        await_bytes(landed.at[:, pl.ds(0, 128)], ro.at[zp])

    for yg in range(4):
        for zh in range(2):
            turned = landed[yg, 128 * zh : 128 * zh + 128, :].T
            for y in range(4):
                for v in range(2):
                    e = 16 * (2 * y + v)
                    final[zh, pl.ds(16 * v + 4 * yg + y, 16, stride=32), :] = turned[e : e + 16]
    for zh in range(2):
        out[:, 128 * zh : 128 * zh + 128] = final[zh]

    await_bytes(share.at[pl.ds(0, 3 * 128 * NROUND)], s1.at[0])
    await_bytes(rows2.at[:, pl.ds(0, 7)], s2.at[0])
    await_bytes(listed.at[pl.ds(0, 7)], sn.at[0])
    for zp in range(2):
        await_bytes(parcel.at[zp, pl.ds(0, 7)], so.at[3 * zp])
    for half in range(2):

        @pl.when(jnp.logical_not(jnp.logical_and(c == h, c == half)))
        def _():
            for zp in range(2):
                home(zp, 0, half).wait_send()

    for to_h in range(2):

        @pl.when(jnp.logical_not(slab_here(to_h)))
        def _():
            slab_copy(to_h).wait_send()

    @pl.when(jnp.logical_and(halo_some(), h == 1))
    def _():
        halo_copy(0).wait_send()

    @pl.when(halo_some())
    def _():
        halo_copy(1).wait_send()


def local(xi_map, basis, point_index, conc_start, well_mask, profile):
    (tz_hi, tz_lo), (cy_hi, cy_lo), (cx_hi, cx_lo) = tables()
    tz = np.concatenate([tz_hi, tz_lo, np.zeros((8, G, 48), ml_dtypes.bfloat16)], axis=2)
    cy = np.concatenate([cy_hi, cy_lo], axis=0)
    cx = np.concatenate([cx_hi, cx_lo], axis=0)

    vmem = pl.BlockSpec(memory_space=pltpu.VMEM)
    smem = pl.BlockSpec(memory_space=pltpu.SMEM)
    dma = pltpu.SemaphoreType.DMA
    far = pl.BlockSpec(memory_space=pl.ANY)
    total = pl.pallas_call(
        kernel,
        out_shape=jax.ShapeDtypeStruct((512, 256), F32),
        in_specs=[smem, smem] + [far] * 5 + [vmem] * 2,
        out_specs=vmem,
        scratch_shapes=[
            pltpu.VMEM((64, 64, 256), F32),
            pltpu.VMEM((3, 64, 64, 256), BF16),
            pltpu.VMEM((40 * 128, 128), F32),
            pltpu.VMEM((NROUND, 4, 4, 32, 128), F32),
            pltpu.VMEM((NROUND, 8, 36, 256), F32),
            pltpu.VMEM((NROUND, 8, 36, 256), F32),
            pltpu.VMEM((2, 20, 40, 128), F32),
            pltpu.VMEM((2, 2, 4, 40, 256), F32),
            pltpu.VMEM((POINTS, STEPS, 5, 2, 8, 128), F32),
            pltpu.VMEM((2, 3, 5, 2, 8, 128), F32),
            pltpu.VMEM((64, 256), F32),
            pltpu.VMEM((8, 128), F32),
            pltpu.VMEM((8, 8, 128), F32),
            pltpu.VMEM((POINTS, 4, 8, 128), F32),
            pltpu.VMEM((2, 640, 128), F32),
            pltpu.VMEM((2, 8, 2, 4, 8, 128), F32),
            pltpu.VMEM((4, 256, 128), F32),
            pltpu.VMEM((2, 512, 128), F32),
            pltpu.VMEM((256, 128), BF16),
            pltpu.VMEM((2, 4096, 128), F32),
            pltpu.VMEM((8, 272, 128), F32),
            pltpu.VMEM((2, 640, 128), F32),
            pltpu.VMEM((2, 256, 128), jnp.int32),
            pltpu.VMEM((2, 264, 128), F32),
            pltpu.VMEM((2, 40, 128), F32),
            dma((3,)),
            dma((1,)),
            dma((PAIRS,)),
            dma((1,)),
            dma((NROUND,)),
            dma((4,)),
            dma((3,)),
            dma((4, 2)),
            dma((5,)),
            dma((2,)),
            dma((6,)),
            dma((2,)),
        ],
        compiler_params=pltpu.CompilerParams(
            collective_id=0, has_side_effects=True, vmem_limit_bytes=60 * 2**20
        ),
    )(point_index, profile, xi_map, basis, conc_start.reshape(4096, 256), well_mask, tz, cy, cx)
    return total.reshape(32, 16, 256)


def solution(mesh):
    placed = (
        P("py", "pz", None),
        P(None, "py", "pz", None),
        P("pts", None),
        P(None, ("py", "pz"), None),
        P(),
        P(),
    )
    return jax.shard_map(
        local, mesh=mesh, in_specs=placed, out_specs=P("pts", ("py", "pz"), None), check_vma=False
    )
```

```python
import functools

import jax
import jax.numpy as jnp
import ml_dtypes
import numpy as np
from jax import lax
from jax.experimental import pallas as pl
from jax.experimental.pallas import tpu as pltpu
from jax.sharding import PartitionSpec as P

MESH = pl.DeviceIdType.MESH
STEPS = 4
POINTS = 16
BATCH = 2
G = 256
NROUND = 10
PAIRS = 5
ROOT3 = 1.7320508075688772
F32 = jnp.float32
BF16 = jnp.bfloat16
NT = (((1,), (1,)), ((), ()))


def split_table(table):
    table = np.asarray(table, np.float64)
    high = table.astype(np.float32).astype(ml_dtypes.bfloat16)
    low = (table - high.astype(np.float64)).astype(np.float32).astype(ml_dtypes.bfloat16)
    return high, low


def tables():
    spots = np.arange(G, dtype=np.float64)
    full = np.sqrt(2.0 / G) * np.cos(np.pi * (spots[:, None] + 0.5) * spots[None, :] / G)
    full[:, 0] *= np.sqrt(0.5)
    tz = np.zeros((8, 40, G))
    for g in range(8):
        for par in range(2):
            for w in range(18):
                z = 32 * g - 4 + 2 * w + par
                if z >= 0:
                    tz[g, 20 * par + w] = full[z]
    tz = tz.transpose(0, 2, 1)
    cy = np.zeros((8, 40, G))
    for u in range(8):
        for t in range(5):
            for q in range(8):
                y = 32 * u - 8 + 5 * q + t
                if y >= 0 and (t == 4 or q > 0):
                    cy[u, q if t == 4 else 7 + 7 * t + q] = full[y]
    cx = 0.5 * np.concatenate([full[0::2], full[1::2]], axis=0).T
    return split_table(tz), split_table(cy.reshape(320, G)), split_table(cx)


def halves(value):
    high = value.astype(BF16)
    low = (value - high.astype(F32)).astype(BF16)
    return high, low


def kernel(
    point,
    prof,
    xi_far,
    basis_far,
    conc_far,
    mask_far,
    tz_far,
    cy,
    cx,
    out,
    xi,
    basis,
    share,
    got1,
    rows2,
    got2,
    conc0,
    fields,
    carry,
    plane,
    wave,
    mine,
    listed,
    nodes,
    sums,
    parcel,
    landed,
    final,
    tz,
    start,
    turned_z,
    cz_flat,
    wells,
    turned_y,
    mask,
    r0,
    s1,
    r1,
    s2,
    r3,
    sc,
    rc,
    load,
    prep,
    sn,
    so,
    ro,
):
    pts = lax.axis_index("pts")
    i = lax.axis_index("py")
    pz = lax.axis_index("pz")
    yy, x_lo = pts // 2, pts % 2
    h, c = pz // 2, pz % 2
    xt = (x_lo + h) % 2
    u = 2 * i + c
    g = 2 * yy + xt
    cz = cz_flat.reshape(2, 40, 16, 128)

    def at(i_, h_, c_):
        return {"pts": 2 * yy + (xt + h_) % 2, "py": i_, "pz": 2 * h_ + c_}

    def await_bytes(view, sem):
        pltpu.make_async_copy(view, view, sem).wait()

    barrier = pltpu.get_barrier_semaphore()
    peers = []
    for dp in range(8):
        for dh in range(2):
            for dc in range(2):
                if dp + dh + dc > 0:
                    peers.append({"pts": (pts + dp) % 8, "py": i, "pz": 2 * ((h + dh) % 2) + (c + dc) % 2})
    for di in range(1, 4):
        for dh in range(2):
            for dc in range(2):
                peers.append(at((i + di) % 4, (h + dh) % 2, (c + dc) % 2))
    for peer in peers:
        pl.semaphore_signal(barrier, inc=1, device_id=peer, device_id_type=MESH)

    def loads(q):
        copies = []
        for half in range(2):
            rows = pl.ds(pl.multiple_of(8 * q + 32 * half, 8), 8)
            copies.append(pltpu.make_async_copy(xi_far.at[rows], xi.at[rows], load.at[q, 0]))
            copies.append(
                pltpu.make_async_copy(basis_far.at[:, rows], basis.at[:, rows], load.at[q, 1])
            )
        return copies

    def start_loads(q, _):
        for copy in loads(q):
            copy.start()
        return 0

    def load_conc(zh):
        return pltpu.make_async_copy(
            conc_far.at[:, pl.ds(128 * zh, 128)], start.at[zh], prep.at[zh]
        )

    def load_mask(yh):
        return pltpu.make_async_copy(
            mask_far.at[:, pl.ds(128 * yh, 128)], wells.at[yh], prep.at[2 + yh]
        )

    load_tz = pltpu.make_async_copy(tz_far.at[g], tz, prep.at[4])
    some_z = [g <= 4, g >= 4]
    for zh in range(2):

        @pl.when(some_z[zh])
        def _():
            load_conc(zh).start()

    load_tz.start()
    lax.fori_loop(0, 4, start_loads, 0)
    for yh in range(2):
        load_mask(yh).start()

    def slab_copy(to_h):
        return pltpu.make_async_remote_copy(
            src_ref=cz.at[:, pl.ds(16 * to_h, 20)],
            dst_ref=conc0.at[:, :, pl.ds(pl.multiple_of(8 + 16 * c, 8), 16)],
            send_sem=sc.at[to_h],
            recv_sem=rc.at[c],
            device_id=at(i, to_h, h),
            device_id_type=MESH,
        )

    def slab_local(to_h):
        return pltpu.make_async_copy(
            cz.at[:, pl.ds(16 * to_h, 20)],
            conc0.at[:, :, pl.ds(pl.multiple_of(8 + 16 * c, 8), 16)],
            rc.at[c],
        )

    above = 2 * i + h + 1

    def halo_copy(to_h):
        return pltpu.make_async_remote_copy(
            src_ref=cz.at[:, pl.ds(16 * to_h, 20), pl.ds(8, 8)],
            dst_ref=conc0.at[:, :, pl.ds(0, 8)],
            send_sem=sc.at[2 + to_h],
            recv_sem=rc.at[2],
            device_id=at((above // 2) % 4, to_h, above % 2),
            device_id_type=MESH,
        )

    def halo_local(to_h):
        return pltpu.make_async_copy(
            cz.at[:, pl.ds(16 * to_h, 20), pl.ds(8, 8)], conc0.at[:, :, pl.ds(0, 8)], rc.at[2]
        )

    def slab_here(to_h):
        return jnp.logical_and(h == to_h, c == to_h)

    def halo_some():
        return jnp.logical_and(c == 1, above < 8)

    for m in range(2):
        weight = 1.0
        for r in range(3):
            index = point[m, r]
            value = jnp.where(index == 0, -ROOT3, jnp.where(index == 1, 0.0, ROOT3))
            weight = weight * jnp.where(index == 1, 2.0 / 3.0, 1.0 / 6.0)
            mine[4 * m + r : 4 * m + r + 1, :] = jnp.full((1, 128), value, F32)
        mine[4 * m + 3 : 4 * m + 4, :] = jnp.full((1, 128), weight, F32)

    def node_copy(dp):
        return pltpu.make_async_remote_copy(
            src_ref=mine,
            dst_ref=listed.at[pts],
            send_sem=sn.at[0],
            recv_sem=sn.at[1],
            device_id={"pts": (pts + dp) % 8, "py": i, "pz": pz},
            device_id_type=MESH,
        )

    turned_z[:, 0:8, :] = jnp.zeros((8, 8, 128), F32)
    for zh in range(2):

        @pl.when(some_z[zh])
        def _():
            load_conc(zh).wait()

    def turn_conc(y4, _):
        rows = [(m, v) for m in range(4) for v in range(2)]
        for zh in range(2):

            @pl.when(some_z[zh])
            def _():
                for m, v in rows:
                    turned_z[2 * m + v, 4 + 128 * zh : 132 + 128 * zh, :] = start[
                        zh, pl.ds(16 * v + 4 * y4 + m, 128, stride=32), :
                    ].T

        for m, v in rows:
            cz_flat[v, pl.ds(4 * y4 + m, 40, stride=16), :] = turned_z[
                2 * m + v, pl.ds(pl.multiple_of(32 * g, 32), 40), :
            ]
        return 0

    lax.fori_loop(0, 4, turn_conc, 0)

    def turn_mask():
        turned_y[:, 0:8, :] = jnp.zeros((2, 8, 128), F32)
        for yh in range(2):
            load_mask(yh).wait()
            for v in range(2):
                block = wells[yh, pl.ds(v, 128, stride=2), :].astype(F32)
                turned_y[v, 8 + 128 * yh : 136 + 128 * yh, :] = 0.5 * block.T
        for v in range(2):
            for t in range(5):
                mask[v, 8 * t : 8 * t + 8, :] = turned_y[v, pl.ds(32 * u + t, 8, stride=5), :]

    def greet():
        pl.semaphore_wait(barrier, len(peers))
        for dp in range(1, 8):
            node_copy(dp).start()
        listed[pts] = mine[...]
        for to_h in range(2):

            @pl.when(slab_here(to_h))
            def _():
                slab_local(to_h).start()

            @pl.when(jnp.logical_not(slab_here(to_h)))
            def _():
                slab_copy(to_h).start()

        @pl.when(jnp.logical_and(halo_some(), h == 0))
        def _():
            halo_local(0).start()

        @pl.when(jnp.logical_and(halo_some(), h == 1))
        def _():
            halo_copy(0).start()

        @pl.when(halo_some())
        def _():
            halo_copy(1).start()

        @pl.when(u == 0)
        def _():
            conc0[:, :, 0:8, :] = jnp.zeros((2, 20, 8, 128), F32)

    spot_b = (lax.broadcasted_iota(jnp.int32, (64, G), 0) + 64 * pz).astype(F32)
    spot_c = lax.broadcasted_iota(jnp.int32, (64, G), 1).astype(F32)
    wave[...] = 64.0 + spot_b * spot_b + spot_c * spot_c
    front = 64.0 * 0.9 * (32.0**1.5)

    def stage(step, _):
        amps = []
        for part in range(2):
            for half in range(2):
                a = (64 * i + 2 * step + part + 32 * half).astype(F32)
                amps.append(front / (wave[...] + a * a))
        for f in range(4):
            parts = []
            for part in range(2):
                for half in range(2):
                    row = 2 * step + part + 32 * half
                    value = xi[row] if f == 0 else basis[f - 1, row].astype(F32)
                    parts.append(value * amps[2 * part + half])
            high, low = halves(jnp.concatenate(parts, axis=0))
            both = jnp.dot(jnp.concatenate([high, low], axis=0), tz[...], preferred_element_type=F32)
            both = (both[0:256] + both[256:512]).T
            total = both[0:40] + both[40:80]
            for part in range(2):
                share[pl.ds(32 * f + 2 * step + part, 40, stride=128), :] = total[
                    :, 128 * part : 128 * part + 128
                ]
        return 0

    def stages(part, _):
        for q in range(2):
            await_bytes(xi.at[pl.ds(0, 16)], load.at[2 * part + q, 0])
            await_bytes(basis.at[:, pl.ds(0, 16)], load.at[2 * part + q, 1])
            lax.fori_loop(8 * part + 4 * q, 8 * part + 4 * q + 4, stage, 0)

        @pl.when(part == 0)
        def _():
            for d in (2, 3, 1):
                early(0, 0, 2, d).start()

        @pl.when(part == 1)
        def _():
            for begin in (0, 1):
                for d in (2, 3, 1):
                    early(1, begin, 1, d).start()
            for k in (2, 3):
                for d in (2, 3, 1):
                    lone(k, d).start()

        return 0

    blocks = share.reshape(40, 4, 32, 128)

    def early(part, begin, count, d):
        to_h, to_c = (h + d // 2) % 2, (c + d % 2) % 2
        rows = pl.ds(16 * part, 16)
        return pltpu.make_async_remote_copy(
            src_ref=blocks.at[pl.ds(20 * to_c + 8 * to_h + begin, count), :, rows],
            dst_ref=got1.at[pl.ds(begin, count), pz, :, rows],
            send_sem=s1.at[0],
            recv_sem=r0.at[part + begin],
            device_id=at(i, to_h, to_c),
            device_id_type=MESH,
        )

    def lone(k, d):
        to_h, to_c = (h + d // 2) % 2, (c + d % 2) % 2
        return pltpu.make_async_remote_copy(
            src_ref=blocks.at[20 * to_c + 8 * to_h + k],
            dst_ref=got1.at[k, pz],
            send_sem=s1.at[0],
            recv_sem=r0.at[1 + k],
            device_id=at(i, to_h, to_c),
            device_id_type=MESH,
        )

    def early_come(part, begin, count):
        await_bytes(
            got1.at[pl.ds(begin, count), pl.ds(0, 3), :, pl.ds(16 * part, 16)], r0.at[part + begin]
        )

    greet()
    load_tz.wait()
    lax.fori_loop(0, 2, stages, 0)

    def first(pair, d):
        to_h, to_c = (h + d // 2) % 2, (c + d % 2) % 2
        return pltpu.make_async_remote_copy(
            src_ref=blocks.at[pl.ds(20 * to_c + 8 * to_h + 2 * pair, 2)],
            dst_ref=got1.at[pl.ds(2 * pair, 2), pz],
            send_sem=s1.at[0],
            recv_sem=r1.at[pair],
            device_id=at(i, to_h, to_c),
            device_id_type=MESH,
        )

    def send_first(pair, _):
        for d in (2, 3, 1):
            first(pair, d).start()
        return 0

    lax.fori_loop(2, PAIRS, send_first, 0)

    def single(k, d):
        to_i, to_c = (i + d // 2) % 4, (c + d % 2) % 2
        return pltpu.make_async_remote_copy(
            src_ref=rows2.at[k, 2 * to_i + to_c],
            dst_ref=got2.at[k, 4 * c + i],
            send_sem=s2.at[0],
            recv_sem=r3.at[k],
            device_id=at(to_i, h, to_c),
            device_id_type=MESH,
        )

    def single_come(k):
        await_bytes(got2.at[k, pl.ds(0, 7)], r3.at[k])

    lane = lax.broadcasted_iota(jnp.int32, (128, 128), 1)
    lane_low = lane < 64
    lane8 = lax.broadcasted_iota(jnp.int32, (8, 128), 1)
    edge = jnp.where(lane8 > 0, 1.6 * 1.6, 0.0).astype(F32)
    lane40 = lax.broadcasted_iota(jnp.int32, (40, 128), 1) < 64

    def b_contraction(k):
        own = share[pl.ds(pl.multiple_of((20 * c + 8 * h + k) * 128, 128), 128), :]
        got1[k, pz] = own.reshape(4, 32, 128)
        sides = [[], []]
        for pair in range(2):
            one, two = (got1[k, 2 * pair + m].reshape(128, 128) for m in range(2))
            sides[0].append(jnp.where(lane_low, one, pltpu.roll(two, 64, 1)))
            sides[1].append(jnp.where(lane_low, pltpu.roll(one, 64, 1), two))
        both = [jnp.concatenate(side, axis=1) for side in sides]
        rows = []
        for f in range(4):
            rows += [both[0][32 * f : 32 * f + 32], both[1][32 * f : 32 * f + 32]]
        high, low = halves(jnp.concatenate(rows, axis=0))
        both = lax.dot_general(cy[...], high, NT, preferred_element_type=F32)
        rest = lax.dot_general(cy[0:320], low, NT, preferred_element_type=F32)
        total = both[0:320] + both[320:640] + rest
        for slab in range(8):
            rows2[k, slab] = total[40 * slab : 40 * slab + 36]
        got2[k, 4 * c + i] = rows2[k, u]

    def a_contraction(k):
        rows = []
        for core in range(2):
            for pair in range(2):
                cols = [[], []]
                for group in range(2):
                    one, two = (
                        jnp.concatenate(
                            [
                                got2[k, 4 * core + 2 * group + m, first_row : first_row + 8, 128 * pair : 128 * pair + 128]
                                for first_row in (7, 14, 21, 28, 0)
                            ],
                            axis=0,
                        )
                        for m in range(2)
                    )
                    cols[0].append(jnp.where(lane40, one, pltpu.roll(two, 64, 1)))
                    cols[1].append(jnp.where(lane40, pltpu.roll(one, 64, 1), two))
                rows += [jnp.concatenate(col, axis=1) for col in cols]
        high, low = halves(jnp.concatenate(rows, axis=0))
        both = jnp.dot(jnp.concatenate([high, low], axis=0), cx[0:256], preferred_element_type=F32)
        total = both[0:320] + both[320:640]
        total += jnp.dot(high, cx[256:512], preferred_element_type=F32)
        for core in range(2):
            for f in range(4):
                row = 160 * core + 40 * f
                fields[k % 2, core, f] = total[row : row + 40]

    tiles = [(t, v) for t in range(5) for v in range(2)]

    def transport(k, halo):
        sub = k % 2
        levels = range(2)
        for p in levels:
            zz = 2 * k + p
            spot_z = 16 * (2 * g + h) - 4 + zz
            well = jnp.where(spot_z >= 0, prof[jnp.maximum(spot_z, 0)], 0.0)
            for t, v in tiles:
                share_v = 1.0 if v == 0 else 1.0 / 1.6
                plane[p, 0, t, v] = conc0[v, zz, pl.ds(t, 8, stride=5), :] * share_v
                plane[p, 1, t, v] = mask[v, 8 * t : 8 * t + 8, :] * (well * share_v)
                if not halo:
                    plane[p, 2, t, v] = jnp.zeros((8, 128), F32)

        def some_points(group, _):
            each = [(m, p) for m in range(BATCH) for p in levels]
            speed, conc = {e: {} for e in each}, {e: {} for e in each}
            for m, p in each:
                n = BATCH * group + m
                node = [nodes[n, r] for r in range(3)]
                for t, v in tiles:
                    logs = [
                        fields[sub, p, f, 8 * t : 8 * t + 8, 128 * v : 128 * v + 128] for f in range(4)
                    ]
                    value = logs[0] + node[0] * logs[1] + node[1] * logs[2] + node[2] * logs[3]
                    speed[m, p][t, v] = 0.125 + 0.125 * jnp.tanh(value)
                    conc[m, p][t, v] = plane[p, 0, t, v]
            for step in range(STEPS):
                flux = {
                    (m, p): {tv: speed[m, p][tv] * conc[m, p][tv] for tv in tiles}
                    for m, p in each
                    if not halo or step <= 2 * k + p
                }
                for t, v in tiles:
                    for m, p in each:
                        if (m, p) not in flux:
                            continue
                        n = BATCH * group + m
                        here = flux[m, p]
                        more = not halo or step < 2 * k + p
                        if more:
                            behind = carry[n, step, t, v] if p == 0 else flux[m, 0][t, v]
                        if p == 1:
                            carry[n, step, t, v] = here[t, v]
                        if not more:
                            continue
                        prev_b = here[t - 1, v] if t > 0 else pltpu.roll(here[4, v], 1, 0)
                        prev_a = here[t, 0] if v == 1 else edge * pltpu.roll(here[t, 1], 1, 1)
                        conc[m, p][t, v] = (
                            (conc[m, p][t, v] - 3.6 * here[t, v])
                            + (plane[p, 1, t, v] + behind)
                            + (prev_b + prev_a)
                        )
            if not halo:
                for p in levels:
                    for t, v in tiles:
                        part = nodes[BATCH * group, 3] * conc[0, p][t, v]
                        for m in range(1, BATCH):
                            part += nodes[BATCH * group + m, 3] * conc[m, p][t, v]
                        plane[p, 2, t, v] += part
            return 0

        lax.fori_loop(0, POINTS // BATCH, some_points, 0)
        if not halo:
            for p in levels:
                for t, v in tiles:
                    sums[v, pl.ds(16 * t + 2 * k + p - 4, 8, stride=80), :] = (
                        plane[p, 2, t, v] * (1.0 if v == 0 else 1.6)
                    )

    def wait_conc():
        for core in range(2):
            slab = pltpu.make_async_copy(
                cz.at[:, pl.ds(0, 20)], conc0.at[:, :, pl.ds(8 + 16 * core, 16)], rc.at[core]
            )
            slab.wait()

        @pl.when(u > 0)
        def _():
            pltpu.make_async_copy(
                cz.at[:, pl.ds(0, 20), pl.ds(8, 8)], conc0.at[:, :, pl.ds(0, 8)], rc.at[2]
            ).wait()

    granule = lax.broadcasted_iota(jnp.int32, (8, 128), 1) // 16
    zr = 16 * (4 * yy + 2 * xt + h)

    def home(zp, dp, half):
        to = (pts + dp) % 8
        return pltpu.make_async_remote_copy(
            src_ref=parcel.at[zp, to, half],
            dst_ref=landed.at[:, pl.ds(pl.multiple_of(zr + 8 * zp, 8), 8)],
            send_sem=so.at[3 * zp + (0 if dp else 1 + half)],
            recv_sem=ro.at[zp],
            device_id={"pts": to, "py": i, "pz": 2 * c + half},
            device_id_type=MESH,
        )

    def home_own(zp, half):
        return pltpu.make_async_copy(
            parcel.at[zp, pts, half], landed.at[:, pl.ds(pl.multiple_of(zr + 8 * zp, 8), 8)], ro.at[zp]
        )

    def go_home(zp):
        def regroup(which, _):
            half, yg = which // 4, which % 4
            arrays = []
            for y in range(4):
                for v in range(2):
                    row = pl.multiple_of(16 * (8 + 16 * half + 4 * yg + y) + 8 * zp, 8)
                    arrays.append(sums[v, pl.ds(row, 8), :])
            for bit in (4, 2, 1):
                clear = (granule // bit) % 2 == 0
                for m in range(8):
                    if m // bit % 2 == 0:
                        one, two = arrays[m], arrays[m + bit]
                        arrays[m] = jnp.where(clear, one, pltpu.roll(two, 16 * bit, 1))
                        arrays[m + bit] = jnp.where(clear, pltpu.roll(one, 128 - 16 * bit, 1), two)
            for p in range(8):
                parcel[zp, p, half, yg] = arrays[p]
            return 0

        for half in range(2):
            lax.fori_loop(4 * half, 4 * half + 4, regroup, 0)
            here = jnp.logical_and(c == h, c == half)

            @pl.when(here)
            def _():
                home_own(zp, half).start()

            @pl.when(jnp.logical_not(here))
            def _():
                home(zp, 0, half).start()

            for dp in range(1, 8):
                home(zp, dp, half).start()

    lag = 3

    def rounds(step, _):
        @pl.when(step == 0)
        def _():
            early_come(0, 0, 2)
            early_come(1, 0, 1)

        @pl.when(step == 1)
        def _():
            early_come(1, 1, 1)

        for k in (2, 3):

            @pl.when(step == k)
            def _():
                await_bytes(got1.at[k, pl.ds(0, 3)], r0.at[1 + k])

        for pair in range(2, PAIRS):

            @pl.when(step == 2 * pair)
            def _():
                await_bytes(got1.at[pl.ds(2 * pair, 2), pl.ds(0, 3)], r1.at[pair])

        @pl.when(step < NROUND)
        def _():
            b_contraction(step)
            for d in (4, 5, 2, 6, 3, 7, 1):
                single(step, d).start()

        for k in range(2):

            @pl.when(step == lag + k)
            def _():
                single_come(k)
                a_contraction(k)
                transport(k, True)

        @pl.when(step >= lag + 2)
        def _():
            single_come(step - lag)
            a_contraction(step - lag)
            transport(step - lag, False)

        @pl.when(step == lag + 5)
        def _():
            go_home(0)

        return 0

    turn_mask()
    wait_conc()
    await_bytes(listed.at[pl.ds(0, 7)], sn.at[1])
    for n in range(POINTS):
        for r in range(4):
            row = 4 * (n % 2) + r
            nodes[n, r] = jnp.broadcast_to(listed[n // 2, row : row + 1, :], (8, 128))
    lax.fori_loop(0, NROUND + lag, rounds, 0)

    go_home(1)
    for zp in range(2):
        await_bytes(landed.at[:, pl.ds(0, 128)], ro.at[zp])

    for yg in range(4):
        for zh in range(2):
            turned = landed[yg, 128 * zh : 128 * zh + 128, :].T
            for y in range(4):
                for v in range(2):
                    e = 16 * (2 * y + v)
                    final[zh, pl.ds(16 * v + 4 * yg + y, 16, stride=32), :] = turned[e : e + 16]
    for zh in range(2):
        out[:, 128 * zh : 128 * zh + 128] = final[zh]

    await_bytes(share.at[pl.ds(0, 3 * 128 * NROUND)], s1.at[0])
    await_bytes(rows2.at[:, pl.ds(0, 7)], s2.at[0])
    await_bytes(listed.at[pl.ds(0, 7)], sn.at[0])
    for zp in range(2):
        await_bytes(parcel.at[zp, pl.ds(0, 7)], so.at[3 * zp])
    for half in range(2):

        @pl.when(jnp.logical_not(jnp.logical_and(c == h, c == half)))
        def _():
            for zp in range(2):
                home(zp, 0, half).wait_send()

    for to_h in range(2):

        @pl.when(jnp.logical_not(slab_here(to_h)))
        def _():
            slab_copy(to_h).wait_send()

    @pl.when(jnp.logical_and(halo_some(), h == 1))
    def _():
        halo_copy(0).wait_send()

    @pl.when(halo_some())
    def _():
        halo_copy(1).wait_send()


def local(xi_map, basis, point_index, conc_start, well_mask, profile):
    (tz_hi, tz_lo), (cy_hi, cy_lo), (cx_hi, cx_lo) = tables()
    tz = np.concatenate([tz_hi, tz_lo, np.zeros((8, G, 48), ml_dtypes.bfloat16)], axis=2)
    cy = np.concatenate([cy_hi, cy_lo], axis=0)
    cx = np.concatenate([cx_hi, cx_lo], axis=0)

    vmem = pl.BlockSpec(memory_space=pltpu.VMEM)
    smem = pl.BlockSpec(memory_space=pltpu.SMEM)
    dma = pltpu.SemaphoreType.DMA
    far = pl.BlockSpec(memory_space=pl.ANY)
    total = pl.pallas_call(
        kernel,
        out_shape=jax.ShapeDtypeStruct((512, 256), F32),
        in_specs=[smem, smem] + [far] * 5 + [vmem] * 2,
        out_specs=vmem,
        scratch_shapes=[
            pltpu.VMEM((64, 64, 256), F32),
            pltpu.VMEM((3, 64, 64, 256), BF16),
            pltpu.VMEM((40 * 128, 128), F32),
            pltpu.VMEM((NROUND, 4, 4, 32, 128), F32),
            pltpu.VMEM((NROUND, 8, 36, 256), F32),
            pltpu.VMEM((NROUND, 8, 36, 256), F32),
            pltpu.VMEM((2, 20, 40, 128), F32),
            pltpu.VMEM((2, 2, 4, 40, 256), F32),
            pltpu.VMEM((POINTS, STEPS, 5, 2, 8, 128), F32),
            pltpu.VMEM((2, 3, 5, 2, 8, 128), F32),
            pltpu.VMEM((64, 256), F32),
            pltpu.VMEM((8, 128), F32),
            pltpu.VMEM((8, 8, 128), F32),
            pltpu.VMEM((POINTS, 4, 8, 128), F32),
            pltpu.VMEM((2, 640, 128), F32),
            pltpu.VMEM((2, 8, 2, 4, 8, 128), F32),
            pltpu.VMEM((4, 256, 128), F32),
            pltpu.VMEM((2, 512, 128), F32),
            pltpu.VMEM((256, 128), BF16),
            pltpu.VMEM((2, 4096, 128), F32),
            pltpu.VMEM((8, 272, 128), F32),
            pltpu.VMEM((2, 640, 128), F32),
            pltpu.VMEM((2, 256, 128), jnp.int32),
            pltpu.VMEM((2, 264, 128), F32),
            pltpu.VMEM((2, 40, 128), F32),
            dma((5,)),
            dma((1,)),
            dma((PAIRS,)),
            dma((1,)),
            dma((NROUND,)),
            dma((4,)),
            dma((3,)),
            dma((4, 2)),
            dma((5,)),
            dma((2,)),
            dma((6,)),
            dma((2,)),
        ],
        compiler_params=pltpu.CompilerParams(
            collective_id=0, has_side_effects=True, vmem_limit_bytes=60 * 2**20
        ),
    )(point_index, profile, xi_map, basis, conc_start.reshape(4096, 256), well_mask, tz, cy, cx)
    return total.reshape(32, 16, 256)


def solution(mesh):
    placed = (
        P("py", "pz", None),
        P(None, "py", "pz", None),
        P("pts", None),
        P(None, ("py", "pz"), None),
        P(),
        P(),
    )
    return jax.shard_map(
        local, mesh=mesh, in_specs=placed, out_specs=P("pts", ("py", "pz"), None), check_vma=False
    )
```
